32 devices in a mesh: req: 8 (over z, core), tensor: 4 (over y, x).
Axes of the slice: x: 2, y: 2, z: 4, core: 2. Of those that a mesh axis runs over, the one named last changes fastest.
Arguments:
- text: bfloat16 [3072, 4096], P('req', 'tensor'), may hold values from -6 to 6
- patches: bfloat16 [64, 6, 6, 4096], P('req', None, None, 'tensor'), may hold values from -6 to 6
- grids: int32 [64, 2], replicated, may hold values from 2 to 6, as said below
- image_request: int32 [64], replicated, may hold values from 0 to 7, as said below
- slot_start: int32 [64], replicated, may hold values from 1 to 375, as said below
- vis_gain: bfloat16 [4096], P('tensor'), may hold values from 0.099609375 to 1.8984375
- dec_gain: bfloat16 [4096], replicated, may hold values from 0.099609375 to 1.8984375
- w_qkv: bfloat16 [4096, 3, 2048], P(None, None, 'tensor'), may hold values from -0.09375 to 0.09375
- w_out: bfloat16 [2048, 4096], P('tensor'), may hold values from -0.125 to 0.125
Outputs:
- layer_out: bfloat16 [3072, 4096], P('req', 'tensor')
The draws below stay inside these ranges and needn't reach their ends.
Inputs may be any that keep to these rules, and one draw needn't show every extreme that they name: `grids`: heights and widths are even; some image has a 6 x 6 grid and some a 2 x 2 grid. `image_request`: the images of one index of req go to distinct requests, one to each. `slot_start`: the regions of 9 positions of the images of one request don't intersect and lie within the prompt; position 0 of every prompt lies outside them.
All inputs are finite; a program needn't handle non-finite values.
Results may differ from the reference program's by a relative error of at most 0.011.
Values may be sent and summed in bfloat16 or wider, within the bound.
No kernel may reach another device: no remote copies, remote signals or barrier semaphores. Data moves between devices by JAX's collectives and lax.ppermute only.
A program may use at most 64 MiB of HBM per device.

```python
import jax
import jax.numpy as jnp
from jax import lax

D = 4096
HEADS = 16
HD = 128
G = 6
REGION = 9
IMG_DEV = 8
L = 384
IMAGES = 64
TOKENS = 3072
N_REQ = 8
N_TENSOR = 4


def shared_layout(key):
    offsets = jax.random.permutation(jax.random.fold_in(key, 11), N_REQ)
    index = jnp.arange(IMAGES, dtype=jnp.int32)
    device = index // IMG_DEV
    within = index % IMG_DEV
    request = (device + offsets[within]) % N_REQ
    base = jax.random.randint(jax.random.fold_in(key, 12), (N_REQ,), 1, L - IMG_DEV * REGION + 1)
    base = base.at[0].set(L - IMG_DEV * REGION).at[1].set(1)
    start = base[request] + within * REGION
    return (request.astype(jnp.int32), start.astype(jnp.int32))


def draw_image_request(key, part):
    return shared_layout(key)[0]


def draw_slot_start(key, part):
    return shared_layout(key)[1]


def draw_grids(key, part):
    low = max(1, G // 4)
    sides = 2 * jax.random.randint(jax.random.fold_in(key, 13), (IMAGES, 2), low, G // 2 + 1)
    sides = sides.at[0].set(G).at[1].set(2)
    return sides.astype(jnp.int32)


def block_levels(key, shape, cuts, low, largest):
    def one(dim, blocks):
        steps = jax.random.uniform(jax.random.fold_in(jax.random.fold_in(key, 6), dim), (blocks,), jnp.float32, low / len(cuts), largest / len(cuts))
        return jnp.repeat(jnp.exp(steps), shape[dim] // blocks).reshape((-1,) + (1,) * (len(shape) - dim - 1))

    level = one(*cuts[0])
    for cut in cuts[1:]:
        level = level * one(*cut)
    return level


def noise(rng, dims, scale, limit, shards=(), kind=jnp.bfloat16):
    values = scale * jax.random.normal(rng, dims, jnp.float32)
    if shards:
        values = values * block_levels(rng, dims, shards, -0.22, 0.18)
    return jnp.clip(values, -limit, limit).astype(kind)


def setup_inputs(seed: int = 0) -> dict:
    streams_of = jax.random.split(jax.random.key(seed), 10)
    return {
        "text": noise(streams_of[0], (TOKENS, D), 1.0, 6.0, ((0, 8), (1, 4))),
        "patches": noise(streams_of[1], (IMAGES, G, G, D), 1.0, 6.0, ((0, 8), (3, 4))),
        "grids": draw_grids(jax.random.fold_in(streams_of[9], 71), 0),
        "image_request": draw_image_request(jax.random.fold_in(streams_of[9], 71), 0),
        "slot_start": draw_slot_start(jax.random.fold_in(streams_of[9], 71), 0),
        "vis_gain": jnp.clip(1.0 + 0.18 * jax.random.normal(streams_of[5], (D,), jnp.float32), 0.099609375, 1.8984375).astype(jnp.bfloat16),
        "dec_gain": jnp.clip(1.0 + 0.18 * jax.random.normal(streams_of[6], (D,), jnp.float32), 0.099609375, 1.8984375).astype(jnp.bfloat16),
        "w_qkv": noise(streams_of[7], (D, 3, HEADS * HD), D ** -0.5, 0.09375, ((2, 4),)),
        "w_out": noise(streams_of[8], (HEADS * HD, D), (HEADS * HD) ** -0.5, 0.125, ((0, 4),)),
    }


def merge_one(block):
    half = G // 2
    f = block.astype(jnp.float32).reshape(half, 2, half, 2, D).mean(axis=(1, 3)).reshape(REGION, D)
    return f

def reference(text, patches, grids, image_request, slot_start, vis_gain, dec_gain, w_qkv, w_out):
    half = G // 2
    gain_v = vis_gain.astype(jnp.float32)

    def merge_norm(block):
        f = merge_one(block)
        ms = lax.optimization_barrier(jnp.mean(f * f, axis=-1, keepdims=True))
        return (f * lax.rsqrt(ms + 1e-05) * gain_v).astype(jnp.bfloat16)
    merged = lax.map(merge_norm, patches)
    cells = jnp.arange(REGION, dtype=jnp.int32)
    row_i = cells // half
    col_j = cells % half
    height = grids[:, 0][:, None] // 2
    width = grids[:, 1][:, None] // 2
    valid = (row_i[None, :] < height) & (col_j[None, :] < width)
    base = image_request[:, None] * L + slot_start[:, None]
    pos = jnp.where(valid, base + row_i[None, :] * width + col_j[None, :], TOKENS).astype(jnp.int32)
    rpos = (base + cells[None, :]).astype(jnp.int32)
    img_rows = jnp.zeros((TOKENS, D), jnp.bfloat16).at[pos.reshape(-1)].set(merged.reshape(-1, D), mode='drop')
    is_img = jnp.zeros((TOKENS,), bool).at[pos.reshape(-1)].set(True, mode='drop')
    in_region = jnp.zeros((TOKENS,), bool).at[rpos.reshape(-1)].set(True, mode='drop')
    key_ok = ~in_region | is_img
    x_in = jnp.where(is_img[:, None], img_rows, text)
    heads_local = HEADS // N_TENSOR
    gain_d = dec_gain.astype(jnp.float32)
    w_flat = w_qkv.reshape(D, 3 * HEADS * HD)
    w_groups = w_out.reshape(N_TENSOR, heads_local * HD, D).astype(jnp.float32)
    causal = jnp.arange(L)[:, None] >= jnp.arange(L)[None, :]

    def one_prompt(item):
        rows, ok = item
        xf = rows.astype(jnp.float32)
        ms = lax.optimization_barrier(jnp.mean(xf * xf, axis=-1, keepdims=True))
        normed = (xf * lax.rsqrt(ms + 1e-05) * gain_d).astype(jnp.bfloat16)
        qkv = jnp.dot(normed, w_flat, preferred_element_type=jnp.float32).astype(jnp.bfloat16)
        qkv = qkv.reshape(L, 3, HEADS, HD).astype(jnp.float32)
        scores = jnp.einsum('qhd,khd->hqk', qkv[:, 0], qkv[:, 1]) / jnp.sqrt(jnp.float32(HD))
        mask = causal & ok[None, :]
        scores = jnp.where(mask[None], scores, jnp.float32(-1e+30))
        top = lax.optimization_barrier(jnp.max(scores, axis=-1, keepdims=True))
        ex = jnp.exp(scores - top)
        probs = (ex / lax.optimization_barrier(jnp.sum(ex, axis=-1, keepdims=True))).astype(jnp.bfloat16)
        context = jnp.einsum('hqk,khd->qhd', probs.astype(jnp.float32), qkv[:, 2]).astype(jnp.bfloat16)
        context = context.reshape(L, N_TENSOR, heads_local * HD).astype(jnp.float32)
        partial_value = jnp.einsum('lta,tad->tld', context, w_groups).astype(jnp.bfloat16)
        summed = lax.optimization_barrier(jnp.sum(partial_value.astype(jnp.float32), axis=0))
        return (xf + summed).astype(jnp.bfloat16)
    out = lax.map(one_prompt, (x_in.reshape(N_REQ, L, D), key_ok.reshape(N_REQ, L)))
    return out.reshape(TOKENS, D)
```

```python
import functools

import jax
import jax.numpy as jnp
from jax import lax
from jax.experimental import pallas as pl
from jax.experimental.pallas import tpu as pltpu
from jax.sharding import PartitionSpec as P

D = 4096
HD = 128
EPS = 1e-05
VMEM_LIMIT = 48 * 1024 * 1024


def round_up(n, m):
    return -(-n // m) * m


def swap(x, s):
    n = lax.axis_size("tensor")
    return lax.ppermute(x, "tensor", [(i, i ^ s) for i in range(n)])


def low_bit(s):
    return s & -s


def high_bit(s):
    return 1 << (s.bit_length() - 1)


def by_bits(n, reverse=False):
    return sorted(range(1, n), key=lambda s: (bin(s).count("1"), s), reverse=reverse)


def gather_blocks(x, n):
    half = x.shape[0] // 2
    blocks = {0: x}
    for s in by_bits(n):
        if s & (s - 1) == 0:
            blocks[s] = swap(x, s)
        else:
            low, high = low_bit(s), high_bit(s)
            top = swap(blocks[s ^ low][:half], low)
            bottom = swap(blocks[s ^ high][half:], high)
            blocks[s] = (top, bottom)
            if n > 4:
                blocks[s] = jnp.concatenate(blocks[s], axis=0)
    return blocks


def qkv_kernel(has_acc, idx_ref, x_ref, gain_ref, w_ref, *refs):
    if has_acc:
        acc_in, ss_in, acc_ref, ss_ref, xs_ref = refs
    else:
        acc_ref, ss_ref, xs_ref = refs
    j, s = pl.program_id(0), pl.program_id(1)

    @pl.when(j == 0)
    def _():
        xf = x_ref[0].astype(jnp.float32)
        xs_ref[s] = (xf * gain_ref[0]).astype(jnp.bfloat16)
        part = jnp.broadcast_to(jnp.sum(xf * xf, axis=1, keepdims=True), ss_ref.shape)

        @pl.when(s == 0)
        def _():
            ss_ref[...] = part + ss_in[...] if has_acc else part

        @pl.when(s > 0)
        def _():
            ss_ref[...] += part

    prod = jnp.dot(xs_ref[s], w_ref[0], preferred_element_type=jnp.float32)

    @pl.when(s == 0)
    def _():
        acc_ref[0] = prod + acc_in[0] if has_acc else prod

    @pl.when(s > 0)
    def _():
        acc_ref[0] += prod


def qkv_part(idx, x, gain, w, acc=None, ss=None):
    n_blk, rows, width = x.shape
    cols = w.shape[2]
    has_acc = acc is not None
    in_specs = [
        pl.BlockSpec((1, rows, width), lambda j, s, idx: (jnp.where(j == 0, s, n_blk - 1), 0, 0)),
        pl.BlockSpec((1, 1, width), lambda j, s, idx: (s, 0, 0)),
        pl.BlockSpec((1, width, cols), lambda j, s, idx: (j, idx[s], 0)),
    ]
    args = [x, gain, w]
    if has_acc:
        in_specs += [
            pl.BlockSpec((1, rows, cols), lambda j, s, idx: (j, 0, 0)),
            pl.BlockSpec((rows, 128), lambda j, s, idx: (0, 0)),
        ]
        args += [acc, ss]
    return pl.pallas_call(
        functools.partial(qkv_kernel, has_acc),
        out_shape=(
            jax.ShapeDtypeStruct((3, rows, cols), jnp.float32),
            jax.ShapeDtypeStruct((rows, 128), jnp.float32),
        ),
        grid_spec=pltpu.PrefetchScalarGridSpec(
            num_scalar_prefetch=1,
            grid=(3, n_blk),
            in_specs=in_specs,
            out_specs=(
                pl.BlockSpec((1, rows, cols), lambda j, s, idx: (j, 0, 0)),
                pl.BlockSpec((rows, 128), lambda j, s, idx: (0, 0)),
            ),
            scratch_shapes=[pltpu.VMEM((n_blk, rows, width), jnp.bfloat16)],
        ),
        compiler_params=pltpu.CompilerParams(vmem_limit_bytes=VMEM_LIMIT),
        cost_estimate=pl.CostEstimate(
            flops=2 * n_blk * rows * width * 3 * cols,
            bytes_accessed=2 * n_blk * width * 3 * cols + 4 * rows * 3 * cols,
            transcendentals=0,
        ),
    )(idx, *args)


def attention_kernel(acc_ref, ss_ref, img_ref, img_ss_ref, place_ref, is_img_ref, key_ref, out_ref):
    rows = acc_ref.shape[1]
    scale = lax.rsqrt(ss_ref[...] / D + EPS)
    img_scale = lax.rsqrt(img_ss_ref[...] / D + EPS)
    is_img = is_img_ref[...] > 0.5
    place = place_ref[...]
    parts = []
    for j in range(3):
        img = (img_ref[j] * img_scale).astype(jnp.bfloat16)
        put = jnp.dot(place, img, preferred_element_type=jnp.float32)
        parts.append(jnp.where(is_img, put, acc_ref[j] * scale).astype(jnp.bfloat16))
    q, k, v = parts
    scores = lax.dot_general(q, k, (((1,), (1,)), ((), ())), preferred_element_type=jnp.float32)
    scores = scores * (1.0 / HD**0.5)
    row = lax.broadcasted_iota(jnp.int32, (rows, rows), 0)
    col = lax.broadcasted_iota(jnp.int32, (rows, rows), 1)
    mask = (row >= col) & (key_ref[0:1, :] > 0.5)
    scores = jnp.where(mask, scores, -1e30)
    top = jnp.max(scores, axis=1, keepdims=True)
    expo = jnp.exp(scores - top)
    probs = (expo / jnp.sum(expo, axis=1, keepdims=True)).astype(jnp.bfloat16)
    out_ref[...] = jnp.dot(probs, v, preferred_element_type=jnp.float32).astype(jnp.bfloat16)


def attention(acc, ss, img_acc, img_ss, place, is_img, key_ok):
    rows, cols = acc.shape[1:]
    n_img = img_acc.shape[1]
    heads = cols // HD
    whole = lambda h: (0, 0)
    return pl.pallas_call(
        attention_kernel,
        out_shape=jax.ShapeDtypeStruct((rows, cols), jnp.bfloat16),
        grid=(heads,),
        in_specs=[
            pl.BlockSpec((3, rows, HD), lambda h: (0, 0, h)),
            pl.BlockSpec((rows, 128), whole),
            pl.BlockSpec((3, n_img, HD), lambda h: (0, 0, h)),
            pl.BlockSpec((n_img, 128), whole),
            pl.BlockSpec((rows, n_img), whole),
            pl.BlockSpec((rows, 128), whole),
            pl.BlockSpec((8, rows), whole),
        ],
        out_specs=pl.BlockSpec((rows, HD), lambda h: (0, h)),
        compiler_params=pltpu.CompilerParams(vmem_limit_bytes=VMEM_LIMIT),
        cost_estimate=pl.CostEstimate(
            flops=4 * heads * rows * rows * HD,
            bytes_accessed=4 * rows * 3 * cols,
            transcendentals=heads * rows * rows,
        ),
    )(acc, ss, img_acc, img_ss, place, is_img, key_ok)


def out_kernel(idx_ref, x_ref, w_ref, out_ref):
    out_ref[...] = jnp.dot(x_ref[...], w_ref[...], preferred_element_type=jnp.float32).astype(out_ref.dtype)


def out_part(idx, x, w, width, dtype=jnp.bfloat16):
    rows, depth = x.shape
    return pl.pallas_call(
        out_kernel,
        out_shape=jax.ShapeDtypeStruct((rows, width), dtype),
        grid_spec=pltpu.PrefetchScalarGridSpec(
            num_scalar_prefetch=1,
            grid=(1,),
            in_specs=[
                pl.BlockSpec((rows, depth), lambda i, idx: (0, 0)),
                pl.BlockSpec((depth, width), lambda i, idx: (0, idx[0])),
            ],
            out_specs=pl.BlockSpec((rows, width), lambda i, idx: (0, 0)),
        ),
        compiler_params=pltpu.CompilerParams(vmem_limit_bytes=VMEM_LIMIT),
        cost_estimate=pl.CostEstimate(
            flops=2 * rows * depth * width,
            bytes_accessed=2 * (rows * depth + depth * width + rows * width),
            transcendentals=0,
        ),
    )(idx, x, w)


def scatter_sum(parts, n):
    rows = parts[0].shape[0]
    half = rows // 2
    acc = {s: [[parts[s][:half]], [parts[s][half:]]] for s in range(n)}
    add = lambda terms: functools.reduce(lambda a, b: a + b, [t.astype(jnp.float32) for t in terms])
    for s in by_bits(n, reverse=True):
        for side, bit in ((0, low_bit(s)), (1, high_bit(s))):
            terms = acc[s][side]
            out = terms[0] if len(terms) == 1 else add(terms).astype(jnp.bfloat16)
            acc[s ^ bit][side].append(swap(out, bit))
    return jnp.concatenate([add(acc[0][0]), add(acc[0][1])], axis=0)


def body(text, patches, grids, image_request, slot_start, vis_gain, dec_gain, w_qkv, w_out):
    n_req = lax.axis_size("req")
    n_ten = lax.axis_size("tensor")
    me_req = lax.axis_index("req")
    me_ten = lax.axis_index("tensor")
    img_dev, side, _, width = patches.shape
    half = side // 2
    region = half * half
    length = text.shape[0]
    w3 = jnp.transpose(w_qkv, (1, 0, 2))
    owners = [(me_ten ^ s).astype(jnp.int32) for s in range(n_ten)]
    gains = [
        lax.dynamic_slice_in_dim(dec_gain, o * width, width).astype(jnp.float32).reshape(1, 1, width)
        for o in owners
    ]

    blocks = gather_blocks(text, n_ten)

    grid6 = jnp.transpose(patches, (1, 2, 0, 3)).astype(jnp.float32)
    pooled = grid6.reshape(half, 2, half, 2, img_dev, width).mean(axis=(1, 3))
    pooled = pooled.reshape(region, img_dev, width).astype(jnp.bfloat16)
    own_map = lax.dynamic_slice_in_dim(image_request, me_req * img_dev, img_dev)
    onehot = (jnp.arange(n_req, dtype=jnp.int32)[:, None] == own_map[None, :]).astype(jnp.bfloat16)
    outgoing = jnp.einsum("nk,rkd->nrd", onehot, pooled, preferred_element_type=jnp.float32).astype(jnp.bfloat16)
    received = lax.all_to_all(outgoing, "req", split_axis=0, concat_axis=0, tiled=True)
    n_rows = n_req * region
    n_img = round_up(n_rows + 1, 16)
    img_own = jnp.concatenate(
        [
            received.reshape(n_rows, width),
            jnp.broadcast_to(vis_gain[None, :], (n_img - n_rows, width)),
        ],
        axis=0,
    )
    img_blocks = [img_own] + [swap(img_own, s) for s in range(1, n_ten)]
    img_f = [b.astype(jnp.float32) for b in img_blocks]
    img_sq = functools.reduce(lambda a, b: a + b, [jnp.sum(f * f, axis=1, keepdims=True) for f in img_f])
    img_scale = lax.rsqrt(img_sq / D + EPS)
    merged = [(f * img_scale * f[n_rows : n_rows + 1]).astype(jnp.bfloat16) for f in img_f]
    img_acc, img_ss = qkv_part(jnp.stack(owners), jnp.stack(merged), jnp.concatenate(gains, axis=0), w3)

    pick = image_request.reshape(n_req, img_dev) == me_req
    has_img = jnp.any(pick, axis=1)
    start_src = jnp.sum(jnp.where(pick, slot_start.reshape(n_req, img_dev), 0), axis=1)
    grid_src = jnp.sum(jnp.where(pick[:, :, None], grids.reshape(n_req, img_dev, 2), 0), axis=1)
    cells = jnp.arange(region, dtype=jnp.int32)
    row_i = cells // half
    col_j = cells % half
    height = grid_src[:, 0][:, None] // 2
    grid_w = grid_src[:, 1][:, None] // 2
    valid = has_img[:, None] & (row_i[None, :] < height) & (col_j[None, :] < grid_w)
    pos = jnp.where(valid, start_src[:, None] + row_i[None, :] * grid_w + col_j[None, :], -1)
    rpos = jnp.where(has_img[:, None], start_src[:, None] + cells[None, :], -1)
    pos = jnp.pad(pos.reshape(-1), (0, n_img - n_rows), constant_values=-1)
    spots = jnp.arange(length, dtype=jnp.int32)
    hit = spots[:, None] == pos[None, :]
    place = hit.astype(jnp.bfloat16)
    is_img = jnp.any(hit, axis=1)
    in_region = jnp.any(rpos.reshape(-1)[:, None] == spots[None, :], axis=0)
    is_key = jnp.any(pos[:, None] == spots[None, :], axis=0)
    key_ok = jnp.broadcast_to((~in_region | is_key).astype(jnp.float32)[None, :], (8, length))
    is_img_w = jnp.broadcast_to(is_img.astype(jnp.float32)[:, None], (length, 128))
    img_here = jnp.dot(place, merged[0], preferred_element_type=jnp.float32)
    x_in = jnp.where(is_img[:, None], img_here, text.astype(jnp.float32))

    acc, ss = None, None
    for s in [0] + by_bits(n_ten):
        x = blocks[s] if not isinstance(blocks[s], tuple) else jnp.concatenate(blocks[s], axis=0)
        acc, ss = qkv_part(owners[s].reshape(1), x[None], gains[s], w3, acc, ss)
    context = attention(acc, ss, img_acc, img_ss, place, is_img_w, key_ok)

    parts = {s: out_part(owners[s].reshape(1), context, w_out, width) for s in by_bits(n_ten, reverse=True) + [0]}
    return (x_in + scatter_sum(parts, n_ten)).astype(jnp.bfloat16)


def solution(mesh):
    in_specs = (
        P("req", "tensor"),
        P("req", None, None, "tensor"),
        P(),
        P(),
        P(),
        P("tensor"),
        P(),
        P(None, None, "tensor"),
        P("tensor", None),
    )
    out_specs = P("req", "tensor")
    return jax.shard_map(body, mesh=mesh, in_specs=in_specs, out_specs=out_specs, check_vma=False)
```

```python
import functools

import jax
import jax.numpy as jnp
from jax import lax
from jax.experimental import pallas as pl
from jax.experimental.pallas import tpu as pltpu
from jax.sharding import PartitionSpec as P

D = 4096
HD = 128
EPS = 1e-05


def round_up(n, m):
    return -(-n // m) * m


def swap(x, s):
    n = lax.axis_size("tensor")
    return lax.ppermute(x, "tensor", [(i, i ^ s) for i in range(n)])


def low_bit(s):
    return s & -s


def high_bit(s):
    return 1 << (s.bit_length() - 1)


def by_bits(n, reverse=False):
    return sorted(range(1, n), key=lambda s: (bin(s).count("1"), s), reverse=reverse)


def gather_halves(top, bottom, n):
    blocks = {0: (top, bottom)}
    for s in by_bits(n):
        low, high = low_bit(s), high_bit(s)
        if low == high:
            other = (swap(top, s), swap(bottom, s))
        else:
            other = (swap(blocks[s ^ low][0], low), swap(blocks[s ^ high][1], high))
        blocks[s] = other
    return blocks


def vmem_specs(n):
    return [pl.BlockSpec(memory_space=pltpu.VMEM)] * n


def params(mib):
    return pltpu.CompilerParams(vmem_limit_bytes=mib * 1024 * 1024)


def pool_kernel(map_ref, x_ref, out_ref, tmp_ref):
    n_req, region = out_ref.shape[0], tmp_ref.shape[1]
    side, img_dev = x_ref.shape[0], x_ref.shape[2]
    half = side // 2
    rows = lax.broadcasted_iota(jnp.int32, (n_req, img_dev), 0)
    onehot = (rows == map_ref[0:1, :]).astype(jnp.bfloat16)
    tmp_ref[...] = jnp.zeros_like(tmp_ref)
    for i in range(half):
        for j in range(half):
            total = x_ref[2 * i, 2 * j].astype(jnp.float32)
            for a, b in ((0, 1), (1, 0), (1, 1)):
                total += x_ref[2 * i + a, 2 * j + b].astype(jnp.float32)
            pooled = (total * 0.25).astype(jnp.bfloat16)
            tmp_ref[:, i * half + j, :] = jnp.dot(onehot, pooled, preferred_element_type=jnp.float32)
    out_ref[...] = tmp_ref[...].astype(jnp.bfloat16)


def pool_images(own_map, patches, n_req):
    side, _, img_dev, width = patches.shape
    padded = round_up((side // 2) ** 2, 16)
    return pl.pallas_call(
        pool_kernel,
        out_shape=jax.ShapeDtypeStruct((n_req, padded, width), jnp.bfloat16),
        in_specs=vmem_specs(2),
        out_specs=pl.BlockSpec(memory_space=pltpu.VMEM),
        scratch_shapes=[pltpu.VMEM((n_req, padded, width), jnp.float32)],
        compiler_params=params(24),
        cost_estimate=pl.CostEstimate(flops=0, bytes_accessed=4 * side * side * img_dev * width, transcendentals=0),
    )(jnp.broadcast_to(own_map[None, :], (8, img_dev)), patches)


def pack_kernel(region, rec_ref, gain_ref, out_ref, tmp_ref):
    n_req = rec_ref.shape[0]
    for r in range(n_req):
        tmp_ref[region * r : region * (r + 1)] = rec_ref[r].astype(jnp.float32)[:region]
    rest = tmp_ref.shape[0] - region * n_req
    tmp_ref[region * n_req :] = jnp.broadcast_to(gain_ref[0:1, :], (rest, gain_ref.shape[1]))
    out_ref[...] = tmp_ref[...].astype(jnp.bfloat16)


def pack_images(received, gain, region, n_img):
    width = received.shape[2]
    return pl.pallas_call(
        functools.partial(pack_kernel, region),
        out_shape=jax.ShapeDtypeStruct((n_img, width), jnp.bfloat16),
        in_specs=vmem_specs(2),
        out_specs=pl.BlockSpec(memory_space=pltpu.VMEM),
        scratch_shapes=[pltpu.VMEM((n_img, width), jnp.float32)],
        compiler_params=params(24),
        cost_estimate=pl.CostEstimate(flops=0, bytes_accessed=4 * n_img * width, transcendentals=0),
    )(received, gain)


def weight_copies(n_blk, idx_ref, w_ref, wbuf_ref, sem_ref):
    width = wbuf_ref.shape[2]
    copies = []
    for s in range(n_blk):
        first = pl.multiple_of(idx_ref[s] * width, width)
        copies.append(
            [
                pltpu.make_async_copy(w_ref.at[j, pl.ds(first, width)], wbuf_ref.at[s, j], sem_ref.at[s, j])
                for j in range(3)
            ]
        )
    for row in copies:
        for copy in row:
            copy.start()
    return copies


def weight_scratch(n_blk, width, cols):
    return [pltpu.VMEM((n_blk, 3, width, cols), jnp.bfloat16), pltpu.SemaphoreType.DMA((n_blk, 3))]


def text_kernel(n_blk, has_acc, idx_ref, *refs):
    x_refs, refs = refs[: 2 * n_blk], refs[2 * n_blk :]
    if has_acc:
        gain_ref, w_ref, acc_in, ss_in, acc_ref, ss_ref, wbuf_ref, sem_ref = refs
    else:
        gain_ref, w_ref, acc_ref, ss_ref, wbuf_ref, sem_ref = refs
    half = x_refs[0].shape[0]
    copies = weight_copies(n_blk, idx_ref, w_ref, wbuf_ref, sem_ref)
    scaled = []
    for side in range(2):
        rows = pl.ds(side * half, half)
        total = ss_in[rows] if has_acc else jnp.zeros((half, 128), jnp.float32)
        for s in range(n_blk):
            xf = x_refs[2 * s + side][...].astype(jnp.float32)
            scaled.append((xf * gain_ref[s]).astype(jnp.bfloat16))
            total += jnp.sum(xf * xf, axis=1, keepdims=True)
        ss_ref[rows] = total
    for s in range(n_blk):
        for j in range(3):
            copies[s][j].wait()
            for side in range(2):
                rows = pl.ds(side * half, half)
                prod = jnp.dot(scaled[side * n_blk + s], wbuf_ref[s, j], preferred_element_type=jnp.float32)
                if s > 0:
                    prod += acc_ref[j, rows]
                elif has_acc:
                    prod += acc_in[j, rows]
                acc_ref[j, rows] = prod


def text_part(idx, blocks, gain, w, acc=None, ss=None):
    n_blk = len(blocks)
    half, width = blocks[0][0].shape
    rows, cols = 2 * half, w.shape[2]
    has_acc = acc is not None
    args = [h for b in blocks for h in b] + [gain, w]
    in_specs = vmem_specs(2 * n_blk + 1) + [pl.BlockSpec(memory_space=pl.ANY)]
    if has_acc:
        args += [acc, ss]
        in_specs += vmem_specs(2)
    return pl.pallas_call(
        functools.partial(text_kernel, n_blk, has_acc),
        out_shape=(
            jax.ShapeDtypeStruct((3, rows, cols), jnp.float32),
            jax.ShapeDtypeStruct((rows, 128), jnp.float32),
        ),
        in_specs=[pl.BlockSpec(memory_space=pltpu.SMEM)] + in_specs,
        out_specs=tuple(vmem_specs(2)),
        scratch_shapes=weight_scratch(n_blk, width, cols),
        compiler_params=params(28),
        cost_estimate=pl.CostEstimate(
            flops=2 * n_blk * rows * width * 3 * cols,
            bytes_accessed=2 * n_blk * width * 3 * cols,
            transcendentals=0,
        ),
    )(idx, *args)


def image_kernel(n_blk, n_rows, idx_ref, *refs):
    x_refs, (gain_ref, w_ref, qkv_ref, own_ref, wbuf_ref, sem_ref) = refs[:n_blk], refs[n_blk:]
    copies = weight_copies(n_blk, idx_ref, w_ref, wbuf_ref, sem_ref)
    total = 0.0
    for s in range(n_blk):
        xf = x_refs[s][...].astype(jnp.float32)
        total += jnp.sum(xf * xf, axis=1, keepdims=True)
    scale = lax.rsqrt(total / D + EPS)
    total = 0.0
    scaled = []
    for s in range(n_blk):
        xf = x_refs[s][...].astype(jnp.float32)
        merged = (xf * scale * xf[n_rows : n_rows + 1]).astype(jnp.bfloat16)
        if s == 0:
            own_ref[...] = merged
        mf = merged.astype(jnp.float32)
        total += jnp.sum(mf * mf, axis=1, keepdims=True)
        scaled.append((mf * gain_ref[s]).astype(jnp.bfloat16))
    scale = lax.rsqrt(total / D + EPS)
    for j in range(3):
        acc = 0.0
        for s in range(n_blk):
            copies[s][j].wait()
            acc += jnp.dot(scaled[s], wbuf_ref[s, j], preferred_element_type=jnp.float32)
        qkv_ref[j] = (acc * scale).astype(jnp.bfloat16)


def image_part(idx, blocks, gain, w, n_rows):
    n_blk = len(blocks)
    n_img, width = blocks[0].shape
    cols = w.shape[2]
    return pl.pallas_call(
        functools.partial(image_kernel, n_blk, n_rows),
        out_shape=(
            jax.ShapeDtypeStruct((3, n_img, cols), jnp.bfloat16),
            jax.ShapeDtypeStruct((n_img, width), jnp.bfloat16),
        ),
        in_specs=[pl.BlockSpec(memory_space=pltpu.SMEM)]
        + vmem_specs(n_blk + 1)
        + [pl.BlockSpec(memory_space=pl.ANY)],
        out_specs=tuple(vmem_specs(2)),
        scratch_shapes=weight_scratch(n_blk, width, cols),
        compiler_params=params(28),
        cost_estimate=pl.CostEstimate(
            flops=2 * n_blk * n_img * width * 3 * cols,
            bytes_accessed=2 * n_blk * width * 3 * cols,
            transcendentals=0,
        ),
    )(idx, *blocks, gain, w)


def final_kernel(idx_ref, top_ref, bottom_ref, gain_ref, w_ref, acc_ref, ss_ref, img_ref, place_ref, text_row_ref,
                 key_ref, w_out_ref, ctx_ref, far_top_ref, far_bottom_ref, wbuf_ref, sem_ref, qkv_ref, wo_ref, wo_sem):
    half = top_ref.shape[0]
    rows, cols = 2 * half, ctx_ref.shape[1]
    width = wo_ref.shape[1]
    copies = weight_copies(1, idx_ref, w_ref, wbuf_ref, sem_ref)
    first = pl.multiple_of(idx_ref[0] * width, width)
    wo_copy = pltpu.make_async_copy(w_out_ref.at[:, pl.ds(first, width)], wo_ref, wo_sem)
    wo_copy.start()
    scaled, scales = [], []
    for side, x_ref in enumerate((top_ref, bottom_ref)):
        part = pl.ds(side * half, half)
        xf = x_ref[...].astype(jnp.float32)
        scaled.append((xf * gain_ref[0]).astype(jnp.bfloat16))
        total = ss_ref[part] + jnp.sum(xf * xf, axis=1, keepdims=True)
        scales.append((lax.rsqrt(total / D + EPS) * text_row_ref[part])[:, :1])
    for j in range(3):
        copies[0][j].wait()
        for side in range(2):
            part = pl.ds(side * half, half)
            prod = jnp.dot(scaled[side], wbuf_ref[0, j], preferred_element_type=jnp.float32)
            put = jnp.dot(place_ref[part], img_ref[j], preferred_element_type=jnp.float32)
            qkv_ref[j, part] = ((prod + acc_ref[j, part]) * scales[side] + put).astype(jnp.bfloat16)
    step = 128
    for h in range(cols // HD):
        lanes = pl.ds(h * HD, HD)
        for r in range(rows // step):
            last = (r + 1) * step
            q = qkv_ref[0, pl.ds(r * step, step), lanes]
            k = qkv_ref[1, pl.ds(0, last), lanes]
            v = qkv_ref[2, pl.ds(0, last), lanes]
            scores = lax.dot_general(q, k, (((1,), (1,)), ((), ())), preferred_element_type=jnp.float32)
            scores = scores * (1.0 / HD**0.5)
            row = lax.broadcasted_iota(jnp.int32, (step, last), 0) + r * step
            col = lax.broadcasted_iota(jnp.int32, (step, last), 1)
            mask = (row >= col) & (key_ref[0:1, pl.ds(0, last)] > 0.5)
            scores = jnp.where(mask, scores, -1e30)
            top = jnp.max(scores, axis=1, keepdims=True)
            expo = jnp.exp(scores - top)
            probs = (expo / jnp.sum(expo, axis=1, keepdims=True)).astype(jnp.bfloat16)
            ctx_ref[pl.ds(r * step, step), lanes] = jnp.dot(
                probs, v, preferred_element_type=jnp.float32
            ).astype(jnp.bfloat16)
    wo_copy.wait()
    for side, out_ref in enumerate((far_top_ref, far_bottom_ref)):
        out_ref[...] = jnp.dot(
            ctx_ref[pl.ds(side * half, half)], wo_ref[...], preferred_element_type=jnp.float32
        ).astype(jnp.bfloat16)


def final_part(idx, block, gain, w, acc, ss, img, place, text_row, key_ok, w_out):
    half, width = block[0].shape
    rows, cols = 2 * half, w.shape[2]
    any_spec = pl.BlockSpec(memory_space=pl.ANY)
    return pl.pallas_call(
        final_kernel,
        out_shape=(
            jax.ShapeDtypeStruct((rows, cols), jnp.bfloat16),
            jax.ShapeDtypeStruct((half, width), jnp.bfloat16),
            jax.ShapeDtypeStruct((half, width), jnp.bfloat16),
        ),
        in_specs=[pl.BlockSpec(memory_space=pltpu.SMEM)]
        + vmem_specs(3)
        + [any_spec]
        + vmem_specs(6)
        + [any_spec],
        out_specs=tuple(vmem_specs(3)),
        scratch_shapes=weight_scratch(1, width, cols)
        + [
            pltpu.VMEM((3, rows, cols), jnp.bfloat16),
            pltpu.VMEM((cols, width), jnp.bfloat16),
            pltpu.SemaphoreType.DMA,
        ],
        compiler_params=params(28),
        cost_estimate=pl.CostEstimate(
            flops=2 * rows * width * 4 * cols + 4 * cols * rows * rows,
            bytes_accessed=2 * width * 4 * cols,
            transcendentals=cols // HD * rows * rows,
        ),
    )(idx, *block, gain, w, acc, ss, img, place, text_row, key_ok, w_out)


def out_kernel(idx_ref, ctx_ref, w_ref, top_ref, bottom_ref, wo_ref, wo_sem):
    half, width = top_ref.shape
    first = pl.multiple_of(idx_ref[0] * width, width)
    wo_copy = pltpu.make_async_copy(w_ref.at[:, pl.ds(first, width)], wo_ref, wo_sem)
    wo_copy.start()
    wo_copy.wait()
    for side, out_ref in enumerate((top_ref, bottom_ref)):
        out_ref[...] = jnp.dot(
            ctx_ref[pl.ds(side * half, half)], wo_ref[...], preferred_element_type=jnp.float32
        ).astype(out_ref.dtype)


def out_part(idx, ctx, w, width, dtype=jnp.bfloat16):
    rows, depth = ctx.shape
    return pl.pallas_call(
        out_kernel,
        out_shape=(
            jax.ShapeDtypeStruct((rows // 2, width), dtype),
            jax.ShapeDtypeStruct((rows // 2, width), dtype),
        ),
        in_specs=[pl.BlockSpec(memory_space=pltpu.SMEM)] + vmem_specs(1) + [pl.BlockSpec(memory_space=pl.ANY)],
        out_specs=tuple(vmem_specs(2)),
        scratch_shapes=[pltpu.VMEM((depth, width), jnp.bfloat16), pltpu.SemaphoreType.DMA],
        compiler_params=params(16),
        cost_estimate=pl.CostEstimate(
            flops=2 * rows * depth * width,
            bytes_accessed=2 * depth * width,
            transcendentals=0,
        ),
    )(idx, ctx, w)


def add_kernel(n_top, base_ref, *refs):
    out_ref = refs[-1]
    half = out_ref.shape[0] // 2
    for side, terms in enumerate((refs[:n_top], refs[n_top:-1])):
        part = pl.ds(side * half, half)
        total = terms[0][...].astype(jnp.float32)
        for term in terms[1:]:
            total += term[...].astype(jnp.float32)
        out_ref[part] = (base_ref[part].astype(jnp.float32) + total).astype(out_ref.dtype)


def add_all(base, top, bottom):
    return pl.pallas_call(
        functools.partial(add_kernel, len(top)),
        out_shape=jax.ShapeDtypeStruct(base.shape, jnp.bfloat16),
        in_specs=vmem_specs(1 + len(top) + len(bottom)),
        out_specs=pl.BlockSpec(memory_space=pltpu.VMEM),
        compiler_params=params(16),
        cost_estimate=pl.CostEstimate(
            flops=0, bytes_accessed=2 * base.size * (2 + len(top)), transcendentals=0
        ),
    )(base, *top, *bottom)


def scatter_terms(parts, n):
    acc = {s: [[parts[s][0]], [parts[s][1]]] for s in range(n)}
    for s in by_bits(n, reverse=True):
        for side, bit in ((0, low_bit(s)), (1, high_bit(s))):
            terms = [t.astype(jnp.float32) for t in acc[s][side]]
            out = functools.reduce(lambda a, b: a + b, terms).astype(jnp.bfloat16)
            acc[s ^ bit][side].append(swap(out, bit))
    return acc[0]


def body(text, patches, grids, image_request, slot_start, vis_gain, dec_gain, w_qkv, w_out):
    n_req = lax.axis_size("req")
    n_ten = lax.axis_size("tensor")
    me_req = lax.axis_index("req")
    me_ten = lax.axis_index("tensor")
    img_dev, side, _, width = patches.shape
    half = side // 2
    region = half * half
    length = text.shape[0]
    w3 = jnp.transpose(w_qkv, (1, 0, 2))
    owners = jnp.stack([(me_ten ^ s).astype(jnp.int32) for s in range(n_ten)])
    gains = dec_gain.astype(jnp.float32).reshape(n_ten, 1, width)[owners]

    blocks = gather_halves(text[: length // 2], text[length // 2 :], n_ten)

    own_map = lax.dynamic_slice_in_dim(image_request, me_req * img_dev, img_dev)
    outgoing = pool_images(own_map, jnp.transpose(patches, (1, 2, 0, 3)), n_req)
    received = lax.all_to_all(outgoing, "req", split_axis=0, concat_axis=0, tiled=True)
    n_rows = n_req * region
    n_img = round_up(n_rows + 1, 16)
    img_own = pack_images(received, vis_gain.astype(jnp.float32).reshape(1, width), region, n_img)
    img_blocks = [img_own] + [swap(img_own, s) for s in range(1, n_ten)]
    near = [blocks[s] for s in by_bits(n_ten)[:-1]]
    img_blocks, near = lax.optimization_barrier((img_blocks, near))
    img_qkv, merged = image_part(owners, img_blocks, gains, w3, n_rows)

    pick = image_request.reshape(n_req, img_dev) == me_req
    has_img = jnp.any(pick, axis=1)
    start_src = jnp.sum(jnp.where(pick, slot_start.reshape(n_req, img_dev), 0), axis=1)
    grid_src = jnp.sum(jnp.where(pick[:, :, None], grids.reshape(n_req, img_dev, 2), 0), axis=1)
    cells = jnp.arange(region, dtype=jnp.int32)
    row_i = cells // half
    col_j = cells % half
    height = grid_src[:, 0][:, None] // 2
    grid_w = grid_src[:, 1][:, None] // 2
    valid = has_img[:, None] & (row_i[None, :] < height) & (col_j[None, :] < grid_w)
    pos = jnp.where(valid, start_src[:, None] + row_i[None, :] * grid_w + col_j[None, :], -1)
    rpos = jnp.where(has_img[:, None], start_src[:, None] + cells[None, :], -1)
    pos = jnp.pad(pos.reshape(-1), (0, n_img - n_rows), constant_values=-1)
    spots = jnp.arange(length, dtype=jnp.int32)
    hit = spots[:, None] == pos[None, :]
    place = hit.astype(jnp.bfloat16)
    is_img = jnp.any(hit, axis=1)
    in_region = jnp.any(rpos.reshape(-1)[:, None] == spots[None, :], axis=0)
    is_key = jnp.any(pos[:, None] == spots[None, :], axis=0)
    key_ok = jnp.broadcast_to((~in_region | is_key).astype(jnp.float32)[None, :], (8, length))
    text_row = jnp.broadcast_to(1.0 - is_img.astype(jnp.float32)[:, None], (length, 128))
    img_here = jnp.dot(place, merged, preferred_element_type=jnp.float32).astype(jnp.bfloat16)
    x_in = jnp.where(is_img[:, None], img_here, text)

    order = by_bits(n_ten)
    acc, ss = text_part(owners[:1], [blocks[0]], gains[:1], w3)
    near_at = jnp.array(order[:-1])
    acc, ss = text_part(owners[near_at], near, gains[near_at], w3, acc, ss)
    far = order[-1]
    context, far_top, far_bottom = final_part(
        owners[far][None], blocks[far], gains[far][None], w3, acc, ss, img_qkv, place, text_row, key_ok, w_out
    )
    parts = {far: (far_top, far_bottom)}
    for s in reversed([0] + order[:-1]):
        parts[s] = out_part(owners[s][None], context, w_out, width, jnp.float32 if s == 0 else jnp.bfloat16)
    top, bottom = scatter_terms(parts, n_ten)
    return add_all(x_in, top, bottom)


def solution(mesh):
    in_specs = (
        P("req", "tensor"),
        P("req", None, None, "tensor"),
        P(),
        P(),
        P(),
        P("tensor"),
        P(),
        P(None, None, "tensor"),
        P("tensor", None),
    )
    out_specs = P("req", "tensor")
    return jax.shard_map(body, mesh=mesh, in_specs=in_specs, out_specs=out_specs, check_vma=False)
```

```python
import functools

import jax
import jax.numpy as jnp
from jax import lax
from jax.experimental import pallas as pl
from jax.experimental.pallas import tpu as pltpu
from jax.sharding import PartitionSpec as P

D = 4096
HD = 128
EPS = 1e-05
LOG2E = 1.4426950408889634
TINY = pl.CostEstimate(flops=0, bytes_accessed=0, transcendentals=0)


def round_up(n, m):
    return -(-n // m) * m


def swap(x, s):
    n = lax.axis_size("tensor")
    return lax.ppermute(x, "tensor", [(i, i ^ s) for i in range(n)])


def low_bit(s):
    return s & -s


def high_bit(s):
    return 1 << (s.bit_length() - 1)


def by_bits(n, reverse=False):
    return sorted(range(1, n), key=lambda s: (bin(s).count("1"), s), reverse=reverse)


def gather_halves(top, bottom, n):
    blocks = {0: (top, bottom)}
    for s in by_bits(n):
        low, high = low_bit(s), high_bit(s)
        if low == high:
            other = (swap(top, s), swap(bottom, s))
        else:
            other = (swap(blocks[s ^ low][0], low), swap(blocks[s ^ high][1], high))
        blocks[s] = other
    return blocks


def vmem_specs(n):
    return [pl.BlockSpec(memory_space=pltpu.VMEM)] * n


def params(mib):
    return pltpu.CompilerParams(vmem_limit_bytes=mib * 1024 * 1024)


def pool_kernel(me_ref, map_ref, x_ref, out_ref, tmp_ref):
    n_req, region = out_ref.shape[0], tmp_ref.shape[1]
    side, img_dev = x_ref.shape[0], x_ref.shape[2]
    half = side // 2
    rows = lax.broadcasted_iota(jnp.int32, (n_req, img_dev), 0)
    onehot = (rows == map_ref[pl.ds(me_ref[0], 1), :]).astype(jnp.bfloat16)
    tmp_ref[...] = jnp.zeros_like(tmp_ref)
    for i in range(half):
        for j in range(half):
            total = x_ref[2 * i, 2 * j].astype(jnp.float32)
            for a, b in ((0, 1), (1, 0), (1, 1)):
                total += x_ref[2 * i + a, 2 * j + b].astype(jnp.float32)
            pooled = (total * 0.25).astype(jnp.bfloat16)
            tmp_ref[:, i * half + j, :] = jnp.dot(onehot, pooled, preferred_element_type=jnp.float32)
    out_ref[...] = tmp_ref[...].astype(jnp.bfloat16)


def pool_images(me, req_map, patches):
    n_req = req_map.shape[0]
    side, _, img_dev, width = patches.shape
    padded = round_up((side // 2) ** 2, 16)
    return pl.pallas_call(
        pool_kernel,
        out_shape=jax.ShapeDtypeStruct((n_req, padded, width), jnp.bfloat16),
        in_specs=[pl.BlockSpec(memory_space=pltpu.SMEM)] + vmem_specs(2),
        out_specs=pl.BlockSpec(memory_space=pltpu.VMEM),
        scratch_shapes=[pltpu.VMEM((n_req, padded, width), jnp.float32)],
        compiler_params=params(24),
        cost_estimate=TINY,
    )(me[None], req_map, patches)


def pack_kernel(region, rec_ref, gain_ref, out_ref, tmp_ref):
    n_req = rec_ref.shape[0]
    for r in range(n_req):
        tmp_ref[region * r : region * (r + 1)] = rec_ref[r].astype(jnp.float32)[:region]
    rest = tmp_ref.shape[0] - region * n_req
    tmp_ref[region * n_req :] = jnp.broadcast_to(gain_ref[0:1, :], (rest, gain_ref.shape[1]))
    out_ref[...] = tmp_ref[...].astype(jnp.bfloat16)


def pack_images(received, gain, region, n_img):
    width = received.shape[2]
    return pl.pallas_call(
        functools.partial(pack_kernel, region),
        out_shape=jax.ShapeDtypeStruct((n_img, width), jnp.bfloat16),
        in_specs=vmem_specs(2),
        out_specs=pl.BlockSpec(memory_space=pltpu.VMEM),
        scratch_shapes=[pltpu.VMEM((n_img, width), jnp.float32)],
        compiler_params=params(24),
        cost_estimate=TINY,
    )(received, gain)


def load_kernel(qkv_ref, out_ref, qkv_vmem, out_vmem, sem_ref):
    copies = [
        pltpu.make_async_copy(qkv_ref, qkv_vmem, sem_ref.at[0]),
        pltpu.make_async_copy(out_ref, out_vmem, sem_ref.at[1]),
    ]
    for copy in copies:
        copy.start()
    for copy in copies:
        copy.wait()


def load_weights(w_qkv, w_out):
    return pl.pallas_call(
        load_kernel,
        out_shape=(pltpu.VMEM(w_qkv.shape, w_qkv.dtype), pltpu.VMEM(w_out.shape, w_out.dtype)),
        in_specs=[pl.BlockSpec(memory_space=pltpu.HBM)] * 2,
        out_specs=tuple(vmem_specs(2)),
        scratch_shapes=[pltpu.SemaphoreType.DMA((2,))],
        compiler_params=params(4),
        cost_estimate=TINY,
    )(w_qkv, w_out)


def cols_of(ref, owner, width):
    return ref[:, pl.ds(pl.multiple_of(owner * width, width), width)]


def rows_of(ref, j, owner, width):
    return ref[j, pl.ds(pl.multiple_of(owner * width, width), width)]


def text_kernel(n_blk, has_acc, idx_ref, *refs):
    x_refs, refs = refs[: 2 * n_blk], refs[2 * n_blk :]
    if has_acc:
        gain_ref, w_ref, acc_in, ss_in, acc_ref, ss_ref = refs
    else:
        gain_ref, w_ref, acc_ref, ss_ref = refs
    half, width = x_refs[0].shape
    scaled = []
    for side in range(2):
        rows = pl.ds(side * half, half)
        total = ss_in[rows] if has_acc else jnp.zeros((half, 128), jnp.float32)
        for s in range(n_blk):
            xf = x_refs[2 * s + side][...].astype(jnp.float32)
            scaled.append((xf * gain_ref[idx_ref[s]]).astype(jnp.bfloat16))
            total += jnp.sum(xf * xf, axis=1, keepdims=True)
        ss_ref[rows] = total
    for s in range(n_blk):
        for j in range(3):
            weight = rows_of(w_ref, j, idx_ref[s], width)
            for side in range(2):
                rows = pl.ds(side * half, half)
                prod = jnp.dot(scaled[side * n_blk + s], weight, preferred_element_type=jnp.float32)
                if s > 0:
                    prod += acc_ref[j, rows]
                elif has_acc:
                    prod += acc_in[j, rows]
                acc_ref[j, rows] = prod


def text_part(idx, blocks, gain, w, acc=None, ss=None):
    n_blk = len(blocks)
    half, width = blocks[0][0].shape
    rows, cols = 2 * half, w.shape[2]
    has_acc = acc is not None
    args = [h for b in blocks for h in b] + [gain, w]
    in_specs = vmem_specs(2 * n_blk + 2)
    if has_acc:
        args += [acc, ss]
        in_specs += vmem_specs(2)
    return pl.pallas_call(
        functools.partial(text_kernel, n_blk, has_acc),
        out_shape=(
            jax.ShapeDtypeStruct((3, rows, cols), jnp.float32),
            jax.ShapeDtypeStruct((rows, 128), jnp.float32),
        ),
        in_specs=[pl.BlockSpec(memory_space=pltpu.SMEM)] + in_specs,
        out_specs=tuple(vmem_specs(2)),
        compiler_params=params(16),
        cost_estimate=TINY,
    )(idx, *args)


def image_kernel(n_blk, n_rows, idx_ref, *refs):
    x_refs, (gain_ref, w_ref, qkv_ref, own_ref) = refs[:n_blk], refs[n_blk:]
    width = gain_ref.shape[2]
    total = 0.0
    for s in range(n_blk):
        xf = x_refs[s][...].astype(jnp.float32)
        total += jnp.sum(xf * xf, axis=1, keepdims=True)
    scale = lax.rsqrt(total / D + EPS)
    total = 0.0
    scaled = []
    for s in range(n_blk):
        xf = x_refs[s][...].astype(jnp.float32)
        merged = (xf * scale * xf[n_rows : n_rows + 1]).astype(jnp.bfloat16)
        if s == 0:
            own_ref[...] = merged
        mf = merged.astype(jnp.float32)
        total += jnp.sum(mf * mf, axis=1, keepdims=True)
        scaled.append((mf * gain_ref[idx_ref[s]]).astype(jnp.bfloat16))
    scale = lax.rsqrt(total / D + EPS)
    for j in range(3):
        acc = 0.0
        for s in range(n_blk):
            weight = rows_of(w_ref, j, idx_ref[s], width)
            acc += jnp.dot(scaled[s], weight, preferred_element_type=jnp.float32)
        qkv_ref[j] = (acc * scale).astype(jnp.bfloat16)


def image_part(idx, blocks, gain, w, n_rows):
    n_blk = len(blocks)
    n_img, width = blocks[0].shape
    cols = w.shape[2]
    return pl.pallas_call(
        functools.partial(image_kernel, n_blk, n_rows),
        out_shape=(
            jax.ShapeDtypeStruct((3, n_img, cols), jnp.bfloat16),
            jax.ShapeDtypeStruct((n_img, width), jnp.bfloat16),
        ),
        in_specs=[pl.BlockSpec(memory_space=pltpu.SMEM)]
        + vmem_specs(n_blk + 2),
        out_specs=tuple(vmem_specs(2)),
        compiler_params=params(16),
        cost_estimate=TINY,
    )(idx, *blocks, gain, w)


def final_kernel(idx_ref, top_ref, bottom_ref, gain_ref, w_ref, acc_ref, ss_ref, img_ref, place_ref, text_row_ref,
                 key_ref, w_out_ref, ctx_ref, far_top_ref, far_bottom_ref, qkv_ref):
    half, width = top_ref.shape
    rows, cols = 2 * half, ctx_ref.shape[1]
    owner = idx_ref[0]
    scaled, scales = [], []
    for side, x_ref in enumerate((top_ref, bottom_ref)):
        part = pl.ds(side * half, half)
        xf = x_ref[...].astype(jnp.float32)
        scaled.append((xf * gain_ref[owner]).astype(jnp.bfloat16))
        total = ss_ref[part] + jnp.sum(xf * xf, axis=1, keepdims=True)
        scales.append((lax.rsqrt(total / D + EPS) * text_row_ref[part])[:, :1])
    for j in range(3):
        weight = rows_of(w_ref, j, owner, width)
        for side in range(2):
            part = pl.ds(side * half, half)
            prod = jnp.dot(scaled[side], weight, preferred_element_type=jnp.float32)
            put = jnp.dot(place_ref[part], img_ref[j], preferred_element_type=jnp.float32)
            qkv_ref[j, part] = ((prod + acc_ref[j, part]) * scales[side] + put).astype(jnp.bfloat16)
    step = 128
    heads = [pl.ds(h * HD, HD) for h in range(cols // HD)]
    for r in range(rows // step):
        here, last = pl.ds(r * step, step), (r + 1) * step
        row = lax.broadcasted_iota(jnp.int32, (step, last), 0) + r * step
        col = lax.broadcasted_iota(jnp.int32, (step, last), 1)
        bias = jnp.where((row >= col) & (key_ref[0:1, pl.ds(0, last)] > 0.5), 0.0, -1e30)
        scores = [
            lax.dot_general(
                qkv_ref[0, here, lanes],
                qkv_ref[1, pl.ds(0, last), lanes],
                (((1,), (1,)), ((), ())),
                preferred_element_type=jnp.float32,
            )
            for lanes in heads
        ]
        scores = [x * (LOG2E / HD**0.5) + bias for x in scores]
        tops = [jnp.max(x, axis=1, keepdims=True) for x in scores]
        expo = [jnp.exp2(x - top) for x, top in zip(scores, tops)]
        sums = [jnp.sum(x, axis=1, keepdims=True) for x in expo]
        outs = [
            jnp.dot(x.astype(jnp.bfloat16), qkv_ref[2, pl.ds(0, last), lanes], preferred_element_type=jnp.float32)
            for x, lanes in zip(expo, heads)
        ]
        for lanes, out, total in zip(heads, outs, sums):
            ctx_ref[here, lanes] = (out / total).astype(jnp.bfloat16)
    weight = cols_of(w_out_ref, owner, width)
    for side, out_ref in enumerate((far_top_ref, far_bottom_ref)):
        out_ref[...] = jnp.dot(
            ctx_ref[pl.ds(side * half, half)], weight, preferred_element_type=jnp.float32
        ).astype(jnp.bfloat16)


def final_part(idx, block, gain, w, acc, ss, img, place, text_row, key_ok, w_out):
    half, width = block[0].shape
    rows, cols = 2 * half, w.shape[2]
    return pl.pallas_call(
        final_kernel,
        out_shape=(
            jax.ShapeDtypeStruct((rows, cols), jnp.bfloat16),
            jax.ShapeDtypeStruct((half, width), jnp.bfloat16),
            jax.ShapeDtypeStruct((half, width), jnp.bfloat16),
        ),
        in_specs=[pl.BlockSpec(memory_space=pltpu.SMEM)]
        + vmem_specs(11),
        out_specs=tuple(vmem_specs(3)),
        scratch_shapes=[pltpu.VMEM((3, rows, cols), jnp.bfloat16)],
        compiler_params=params(16),
        cost_estimate=TINY,
    )(idx, *block, gain, w, acc, ss, img, place, text_row, key_ok, w_out)


def out_kernel(idx_ref, ctx_ref, w_ref, top_ref, bottom_ref):
    half, width = top_ref.shape
    weight = cols_of(w_ref, idx_ref[0], width)
    for side, out_ref in enumerate((top_ref, bottom_ref)):
        out_ref[...] = jnp.dot(
            ctx_ref[pl.ds(side * half, half)], weight, preferred_element_type=jnp.float32
        ).astype(out_ref.dtype)


def out_part(idx, ctx, w, width, dtype=jnp.bfloat16):
    rows, depth = ctx.shape
    return pl.pallas_call(
        out_kernel,
        out_shape=(
            jax.ShapeDtypeStruct((rows // 2, width), dtype),
            jax.ShapeDtypeStruct((rows // 2, width), dtype),
        ),
        in_specs=[pl.BlockSpec(memory_space=pltpu.SMEM)] + vmem_specs(2),
        out_specs=tuple(vmem_specs(2)),
        compiler_params=params(16),
        cost_estimate=TINY,
    )(idx, ctx, w)


def add_kernel(n_top, base_ref, *refs):
    out_ref = refs[-1]
    half = out_ref.shape[0] // 2
    for side, terms in enumerate((refs[:n_top], refs[n_top:-1])):
        part = pl.ds(side * half, half)
        total = terms[0][...].astype(jnp.float32)
        for term in terms[1:]:
            total += term[...].astype(jnp.float32)
        out_ref[part] = (base_ref[part].astype(jnp.float32) + total).astype(out_ref.dtype)


def add_all(base, top, bottom):
    return pl.pallas_call(
        functools.partial(add_kernel, len(top)),
        out_shape=jax.ShapeDtypeStruct(base.shape, jnp.bfloat16),
        in_specs=vmem_specs(1 + len(top) + len(bottom)),
        out_specs=pl.BlockSpec(memory_space=pltpu.VMEM),
        compiler_params=params(16),
        cost_estimate=pl.CostEstimate(
            flops=0, bytes_accessed=2 * base.size * (2 + len(top)), transcendentals=0
        ),
    )(base, *top, *bottom)


def scatter_terms(parts, n):
    acc = {s: [[parts[s][0]], [parts[s][1]]] for s in range(n)}
    for s in by_bits(n, reverse=True):
        for side, bit in ((0, low_bit(s)), (1, high_bit(s))):
            terms = [t.astype(jnp.float32) for t in acc[s][side]]
            out = functools.reduce(lambda a, b: a + b, terms).astype(jnp.bfloat16)
            acc[s ^ bit][side].append(swap(out, bit))
    return acc[0]


def body(text, patches, grids, image_request, slot_start, vis_gain, dec_gain, w_qkv, w_out):
    n_req = lax.axis_size("req")
    n_ten = lax.axis_size("tensor")
    me_req = lax.axis_index("req")
    me_ten = lax.axis_index("tensor")
    img_dev, side, _, width = patches.shape
    half = side // 2
    region = half * half
    length = text.shape[0]
    w3 = jnp.transpose(w_qkv, (1, 0, 2))
    owners = [(me_ten ^ s).astype(jnp.int32) for s in range(n_ten)]
    gains = dec_gain.astype(jnp.float32).reshape(n_ten, 1, width)

    blocks = gather_halves(text[: length // 2], text[length // 2 :], n_ten)

    req_map = image_request.reshape(n_req, img_dev)
    outgoing = pool_images(me_req.astype(jnp.int32), req_map, jnp.transpose(patches, (1, 2, 0, 3)))
    w3, w_out, outgoing = lax.optimization_barrier((w3, w_out, outgoing))
    w3, w_out = load_weights(w3, w_out)
    received = lax.all_to_all(outgoing, "req", split_axis=0, concat_axis=0, tiled=True)
    n_rows = n_req * region
    n_img = round_up(n_rows + 1, 16)
    img_own = pack_images(received, vis_gain.astype(jnp.float32).reshape(1, width), region, n_img)
    img_blocks = [img_own] + [swap(img_own, s) for s in range(1, n_ten)]
    near = [blocks[s] for s in by_bits(n_ten)[:-1]]
    img_blocks, near = lax.optimization_barrier((img_blocks, near))
    img_qkv, merged = image_part(jnp.stack(owners), img_blocks, gains, w3, n_rows)

    pick = req_map == me_req
    has_img = jnp.any(pick, axis=1)
    start_src = jnp.sum(jnp.where(pick, slot_start.reshape(n_req, img_dev), 0), axis=1)
    grid_src = jnp.sum(jnp.where(pick[:, :, None], grids.reshape(n_req, img_dev, 2), 0), axis=1)
    cells = jnp.arange(region, dtype=jnp.int32)
    row_i = cells // half
    col_j = cells % half
    height = grid_src[:, 0][:, None] // 2
    grid_w = grid_src[:, 1][:, None] // 2
    valid = has_img[:, None] & (row_i[None, :] < height) & (col_j[None, :] < grid_w)
    pos = jnp.where(valid, start_src[:, None] + row_i[None, :] * grid_w + col_j[None, :], -1)
    rpos = jnp.where(has_img[:, None], start_src[:, None] + cells[None, :], -1)
    pos = jnp.pad(pos.reshape(-1), (0, n_img - n_rows), constant_values=-1)
    spots = jnp.arange(length, dtype=jnp.int32)
    hit = spots[:, None] == pos[None, :]
    place = hit.astype(jnp.bfloat16)
    is_img = jnp.any(hit, axis=1)
    in_region = jnp.any(rpos.reshape(-1)[:, None] == spots[None, :], axis=0)
    is_key = jnp.any(pos[:, None] == spots[None, :], axis=0)
    key_ok = jnp.broadcast_to((~in_region | is_key).astype(jnp.float32)[None, :], (8, length))
    text_row = jnp.broadcast_to(1.0 - is_img.astype(jnp.float32)[:, None], (length, 128))
    img_here = jnp.dot(place, merged, preferred_element_type=jnp.float32).astype(jnp.bfloat16)
    x_in = jnp.where(is_img[:, None], img_here, text)

    order = by_bits(n_ten)
    acc, ss = text_part(owners[0][None], [blocks[0]], gains, w3)
    acc, ss = text_part(jnp.stack([owners[s] for s in order[:-1]]), near, gains, w3, acc, ss)
    far = order[-1]
    context, far_top, far_bottom = final_part(
        owners[far][None], blocks[far], gains, w3, acc, ss, img_qkv, place, text_row, key_ok, w_out
    )
    parts = {far: (far_top, far_bottom)}
    for s in reversed([0] + order[:-1]):
        parts[s] = out_part(owners[s][None], context, w_out, width, jnp.float32 if s == 0 else jnp.bfloat16)
    top, bottom = scatter_terms(parts, n_ten)
    return add_all(x_in, top, bottom)


def solution(mesh):
    in_specs = (
        P("req", "tensor"),
        P("req", None, None, "tensor"),
        P(),
        P(),
        P(),
        P("tensor"),
        P(),
        P(None, None, "tensor"),
        P("tensor", None),
    )
    out_specs = P("req", "tensor")
    return jax.shard_map(body, mesh=mesh, in_specs=in_specs, out_specs=out_specs, check_vma=False)
```

```python
import functools

import jax
import jax.numpy as jnp
from jax import lax
from jax.experimental import pallas as pl
from jax.experimental.pallas import tpu as pltpu
from jax.sharding import PartitionSpec as P

D = 4096
HD = 128
EPS = 1e-05
LOG2E = 1.4426950408889634
TINY = pl.CostEstimate(flops=0, bytes_accessed=0, transcendentals=0)


def round_up(n, m):
    return -(-n // m) * m


def swap(x, s, axis="tensor"):
    n = lax.axis_size(axis)
    return lax.ppermute(x, axis, [(i, i ^ s) for i in range(n)])


def in_hbm(x):
    return pltpu.with_memory_space_constraint(x, pltpu.HBM)


def low_bit(s):
    return s & -s


def high_bit(s):
    return 1 << (s.bit_length() - 1)


def by_bits(n, reverse=False):
    return sorted(range(1, n), key=lambda s: (bin(s).count("1"), s), reverse=reverse)


def gather_halves(top, bottom, n):
    blocks = {0: (top, bottom)}
    for s in by_bits(n):
        low, high = low_bit(s), high_bit(s)
        if low == high:
            other = (swap(top, s), swap(bottom, s))
        else:
            other = (swap(blocks[s ^ low][0], low), swap(blocks[s ^ high][1], high))
        blocks[s] = other
    return blocks


def vmem_specs(n):
    return [pl.BlockSpec(memory_space=pltpu.VMEM)] * n


def params(mib):
    return pltpu.CompilerParams(vmem_limit_bytes=mib * 1024 * 1024)


def split_kernel(x_ref, top_ref, bottom_ref, sem_ref):
    half = top_ref.shape[0]
    copies = [
        pltpu.make_async_copy(x_ref.at[pl.ds(side * half, half)], out_ref, sem_ref.at[side])
        for side, out_ref in enumerate((top_ref, bottom_ref))
    ]
    for copy in copies:
        copy.start()
    for copy in copies:
        copy.wait()


def split_rows(x):
    half = pltpu.VMEM((x.shape[0] // 2, x.shape[1]), x.dtype)
    return pl.pallas_call(
        split_kernel,
        out_shape=(half, half),
        in_specs=[pl.BlockSpec(memory_space=pltpu.HBM)],
        out_specs=tuple(vmem_specs(2)),
        scratch_shapes=[pltpu.SemaphoreType.DMA((2,))],
        compiler_params=params(4),
        cost_estimate=TINY,
    )(in_hbm(x))


def pool_kernel(me_ref, req_ref, x_ref, *refs):
    outs, tmp_ref = refs[:-1], refs[-1]
    n_req = len(outs)
    side, img_dev = x_ref.shape[0], x_ref.shape[2]
    half = side // 2
    me = me_ref[0]
    rows = lax.broadcasted_iota(jnp.int32, (n_req, img_dev), 0)
    cols = lax.broadcasted_iota(jnp.int32, (n_req, img_dev), 1)
    away = jnp.full((n_req, img_dev), -1, jnp.int32)
    for k in range(img_dev):
        away = jnp.where(cols == k, req_ref[me * img_dev + k] ^ me, away)
    onehot = (rows == away).astype(jnp.bfloat16)
    tmp_ref[...] = jnp.zeros_like(tmp_ref)
    for i in range(half):
        for j in range(half):
            total = x_ref[2 * i, 2 * j].astype(jnp.float32)
            for a, b in ((0, 1), (1, 0), (1, 1)):
                total += x_ref[2 * i + a, 2 * j + b].astype(jnp.float32)
            pooled = (total * 0.25).astype(jnp.bfloat16)
            tmp_ref[:, i * half + j, :] = jnp.dot(onehot, pooled, preferred_element_type=jnp.float32)
    for s in range(n_req):
        outs[s][...] = tmp_ref[s].astype(jnp.bfloat16)


def pool_images(me, image_request, patches, n_req):
    side, _, img_dev, width = patches.shape
    padded = round_up((side // 2) ** 2, 16)
    return pl.pallas_call(
        pool_kernel,
        out_shape=(jax.ShapeDtypeStruct((padded, width), jnp.bfloat16),) * n_req,
        in_specs=[pl.BlockSpec(memory_space=pltpu.SMEM)] * 2 + vmem_specs(1),
        out_specs=tuple(vmem_specs(n_req)),
        scratch_shapes=[pltpu.VMEM((n_req, padded, width), jnp.float32)],
        compiler_params=params(24),
        cost_estimate=TINY,
    )(me, image_request, patches)


def pack_kernel(region, gain_ref, *refs):
    recs, (out_ref, tmp_ref) = refs[:-2], refs[-2:]
    for r, rec_ref in enumerate(recs):
        tmp_ref[region * r : region * (r + 1)] = rec_ref[...].astype(jnp.float32)[:region]
    done = region * len(recs)
    rest = tmp_ref.shape[0] - done
    tmp_ref[done:] = jnp.broadcast_to(gain_ref[0:1, :], (rest, gain_ref.shape[1]))
    out_ref[...] = tmp_ref[...].astype(jnp.bfloat16)


def pack_images(received, gain, region, n_img):
    width = gain.shape[1]
    return pl.pallas_call(
        functools.partial(pack_kernel, region),
        out_shape=jax.ShapeDtypeStruct((n_img, width), jnp.bfloat16),
        in_specs=vmem_specs(1 + len(received)),
        out_specs=pl.BlockSpec(memory_space=pltpu.VMEM),
        scratch_shapes=[pltpu.VMEM((n_img, width), jnp.float32)],
        compiler_params=params(24),
        cost_estimate=TINY,
    )(gain, *received)


def place_kernel(n_req, half, me_ref, req_ref, start_ref, high_ref, wide_ref, place_ref, text_row_ref, key_ref):
    rows, n_img = place_ref.shape
    img_dev = req_ref.shape[0] // n_req
    me = me_ref[0]
    lane = lax.broadcasted_iota(jnp.int32, (1, n_img), 1)

    def one_source(s, carry):
        pos, spot = carry
        source = me ^ s

        def one_image(k, found):
            i = source * img_dev + k
            hit = req_ref[i] == me
            values = (start_ref[i], high_ref[i] // 2, wide_ref[i] // 2)
            return tuple(jnp.where(hit, new, old) for new, old in zip(values, found))

        none = jnp.int32(-1)
        start, high, wide = lax.fori_loop(0, img_dev, one_image, (none, none, none), unroll=img_dev <= 8)
        for i in range(half):
            for j in range(half):
                cell = i * half + j
                here = lane == s * half * half + cell
                has = start >= 0
                valid = has & (i < high) & (j < wide)
                pos = jnp.where(here, jnp.where(valid, start + i * wide + j, none), pos)
                spot = jnp.where(here, jnp.where(has, start + cell, none), spot)
        return pos, spot

    empty = jnp.full((1, n_img), -1, jnp.int32)
    pos, spot = lax.fori_loop(0, n_req, one_source, (empty, empty))
    row = lax.broadcasted_iota(jnp.int32, (rows, n_img), 0)
    placed = (row == pos).astype(jnp.float32)
    region = (row == spot).astype(jnp.float32)
    place = placed.astype(jnp.bfloat16)
    place_ref[...] = place
    text_row_ref[...] = jnp.broadcast_to(1.0 - jnp.sum(placed, axis=1, keepdims=True), text_row_ref.shape)
    ones = jnp.ones((8, n_img), jnp.bfloat16)
    open_keys = (placed - region).astype(jnp.bfloat16)
    count = lax.dot_general(ones, open_keys, (((1,), (1,)), ((), ())), preferred_element_type=jnp.float32)
    key_ref[...] = 1.0 + count


def placement(me, image_request, slot_start, grids, n_req, half, rows, n_img):
    return pl.pallas_call(
        functools.partial(place_kernel, n_req, half),
        out_shape=(
            jax.ShapeDtypeStruct((rows, n_img), jnp.bfloat16),
            jax.ShapeDtypeStruct((rows, 128), jnp.float32),
            jax.ShapeDtypeStruct((8, rows), jnp.float32),
        ),
        in_specs=[pl.BlockSpec(memory_space=pltpu.SMEM)] * 5,
        out_specs=tuple(vmem_specs(3)),
        compiler_params=params(8),
        cost_estimate=TINY,
    )(me, image_request, slot_start, grids[:, 0], grids[:, 1])


def cols_of(ref, owner, width):
    return ref[:, pl.ds(pl.multiple_of(owner * width, width), width)]


def rows_of(ref, j, owner, width):
    return ref[j, pl.ds(pl.multiple_of(owner * width, width), width)]


def scale_rows(x_ref, gain):
    xf = x_ref[...].astype(jnp.float32)
    return (xf * gain).astype(jnp.bfloat16), jnp.sum(xf * xf, axis=1, keepdims=True)


def own_kernel(owners, me_ref, top_ref, bottom_ref, gain_ref, w_ref, acc_ref, ss_ref, held_ref, sem_ref):
    half, width = top_ref.shape
    me = me_ref[0]
    copies = []
    for s in range(owners):
        rows = pl.ds(pl.multiple_of((me ^ s) * width, width), width)
        for j in range(3):
            copies.append(pltpu.make_async_copy(w_ref.at[j, rows], held_ref.at[j, rows], sem_ref.at[s, j]))
    for copy in copies:
        copy.start()
    scaled = []
    for side, x_ref in enumerate((top_ref, bottom_ref)):
        x, total = scale_rows(x_ref, gain_ref[me])
        scaled.append(x)
        ss_ref[pl.ds(side * half, half)] = jnp.broadcast_to(total, (half, 128))
    for j in range(3):
        copies[j].wait()
        weight = rows_of(held_ref, j, me, width)
        for side in range(2):
            acc_ref[j, pl.ds(side * half, half)] = jnp.dot(scaled[side], weight, preferred_element_type=jnp.float32)
    for copy in copies[3:]:
        copy.wait()


def own_part(me, block, gain, w, n_ten):
    half, width = block[0].shape
    rows, cols = 2 * half, w.shape[2]
    return pl.pallas_call(
        functools.partial(own_kernel, n_ten),
        out_shape=(
            jax.ShapeDtypeStruct((3, rows, cols), jnp.float32),
            jax.ShapeDtypeStruct((rows, 128), jnp.float32),
            pltpu.VMEM(w.shape, w.dtype),
        ),
        in_specs=[pl.BlockSpec(memory_space=pltpu.SMEM)] + vmem_specs(3) + [pl.BlockSpec(memory_space=pltpu.HBM)],
        out_specs=tuple(vmem_specs(3)),
        scratch_shapes=[pltpu.SemaphoreType.DMA((n_ten, 3))],
        compiler_params=params(12),
        cost_estimate=TINY,
    )(me, *block, gain, in_hbm(w))


def near_kernel(near, me_ref, *refs):
    n_blk = len(near)
    x_refs, refs = refs[: 2 * n_blk], refs[2 * n_blk :]
    gain_ref, w_ref, acc_in, ss_in, w_out_ref, acc_ref, ss_ref, held_ref, sem_ref = refs
    half, width = x_refs[0].shape
    me = me_ref[0]
    copy = pltpu.make_async_copy(w_out_ref, held_ref, sem_ref)
    copy.start()
    scaled = {}
    for side in range(2):
        rows = pl.ds(side * half, half)
        total = ss_in[rows]
        for b, s in enumerate(near):
            scaled[side, b], part = scale_rows(x_refs[2 * b + side], gain_ref[me ^ s])
            total += part
        ss_ref[rows] = total
    for j in range(3):
        for side in range(2):
            rows = pl.ds(side * half, half)
            acc = acc_in[j, rows]
            for b, s in enumerate(near):
                weight = rows_of(w_ref, j, me ^ s, width)
                acc += jnp.dot(scaled[side, b], weight, preferred_element_type=jnp.float32)
            acc_ref[j, rows] = acc
    copy.wait()


def near_part(near, me, blocks, gain, w, acc, ss, w_out):
    return pl.pallas_call(
        functools.partial(near_kernel, near),
        out_shape=(
            jax.ShapeDtypeStruct(acc.shape, jnp.float32),
            jax.ShapeDtypeStruct(ss.shape, jnp.float32),
            pltpu.VMEM(w_out.shape, w_out.dtype),
        ),
        in_specs=[pl.BlockSpec(memory_space=pltpu.SMEM)]
        + vmem_specs(2 * len(near) + 4)
        + [pl.BlockSpec(memory_space=pltpu.HBM)],
        out_specs=tuple(vmem_specs(3)),
        scratch_shapes=[pltpu.SemaphoreType.DMA],
        compiler_params=params(16),
        cost_estimate=TINY,
    )(me, *[h for b in blocks for h in b], gain, w, acc, ss, in_hbm(w_out))


def image_kernel(n_blk, n_rows, me_ref, *refs):
    x_refs, (gain_ref, w_ref, qkv_ref, own_ref) = refs[:n_blk], refs[n_blk:]
    width = gain_ref.shape[2]
    me = me_ref[0]
    total = 0.0
    for s in range(n_blk):
        xf = x_refs[s][...].astype(jnp.float32)
        total += jnp.sum(xf * xf, axis=1, keepdims=True)
    scale = lax.rsqrt(total / D + EPS)
    total = 0.0
    scaled = []
    for s in range(n_blk):
        xf = x_refs[s][...].astype(jnp.float32)
        merged = (xf * scale * xf[n_rows : n_rows + 1]).astype(jnp.bfloat16)
        if s == 0:
            own_ref[...] = merged
        mf = merged.astype(jnp.float32)
        total += jnp.sum(mf * mf, axis=1, keepdims=True)
        scaled.append((mf * gain_ref[me ^ s]).astype(jnp.bfloat16))
    scale = lax.rsqrt(total / D + EPS)
    for j in range(3):
        acc = 0.0
        for s in range(n_blk):
            weight = rows_of(w_ref, j, me ^ s, width)
            acc += jnp.dot(scaled[s], weight, preferred_element_type=jnp.float32)
        qkv_ref[j] = (acc * scale).astype(jnp.bfloat16)


def image_part(me, blocks, gain, w, n_rows):
    n_blk = len(blocks)
    n_img, width = blocks[0].shape
    cols = w.shape[2]
    return pl.pallas_call(
        functools.partial(image_kernel, n_blk, n_rows),
        out_shape=(
            jax.ShapeDtypeStruct((3, n_img, cols), jnp.bfloat16),
            jax.ShapeDtypeStruct((n_img, width), jnp.bfloat16),
        ),
        in_specs=[pl.BlockSpec(memory_space=pltpu.SMEM)]
        + vmem_specs(n_blk + 2),
        out_specs=tuple(vmem_specs(2)),
        compiler_params=params(16),
        cost_estimate=TINY,
    )(me, *blocks, gain, w)


def final_kernel(far, me_ref, top_ref, bottom_ref, gain_ref, w_ref, acc_ref, ss_ref, img_ref, place_ref, text_row_ref,
                 key_ref, w_out_ref, ctx_ref, far_top_ref, far_bottom_ref, qkv_ref):
    half, width = top_ref.shape
    rows, cols = 2 * half, ctx_ref.shape[1]
    owner = me_ref[0] ^ far
    scaled, scales = [], []
    for side, x_ref in enumerate((top_ref, bottom_ref)):
        part = pl.ds(side * half, half)
        x, total = scale_rows(x_ref, gain_ref[owner])
        scaled.append(x)
        total = ss_ref[part] + total
        scales.append((lax.rsqrt(total / D + EPS) * text_row_ref[part])[:, :1])
    for j in range(3):
        weight = rows_of(w_ref, j, owner, width)
        for side in range(2):
            part = pl.ds(side * half, half)
            prod = jnp.dot(scaled[side], weight, preferred_element_type=jnp.float32)
            put = jnp.dot(place_ref[part], img_ref[j], preferred_element_type=jnp.float32)
            qkv_ref[j, part] = ((prod + acc_ref[j, part]) * scales[side] + put).astype(jnp.bfloat16)
    step = 128
    heads = [pl.ds(h * HD, HD) for h in range(cols // HD)]
    for r in range(rows // step):
        here, last = pl.ds(r * step, step), (r + 1) * step
        row = lax.broadcasted_iota(jnp.int32, (step, last), 0) + r * step
        col = lax.broadcasted_iota(jnp.int32, (step, last), 1)
        bias = jnp.where((row >= col) & (key_ref[0:1, pl.ds(0, last)] > 0.5), 0.0, -1e30)
        scores = [
            lax.dot_general(
                qkv_ref[0, here, lanes],
                qkv_ref[1, pl.ds(0, last), lanes],
                (((1,), (1,)), ((), ())),
                preferred_element_type=jnp.float32,
            )
            for lanes in heads
        ]
        scores = [x * (LOG2E / HD**0.5) + bias for x in scores]
        tops = [jnp.max(x, axis=1, keepdims=True) for x in scores]
        expo = [jnp.exp2(x - top) for x, top in zip(scores, tops)]
        sums = [jnp.sum(x, axis=1, keepdims=True) for x in expo]
        outs = [
            jnp.dot(x.astype(jnp.bfloat16), qkv_ref[2, pl.ds(0, last), lanes], preferred_element_type=jnp.float32)
            for x, lanes in zip(expo, heads)
        ]
        for lanes, out, total in zip(heads, outs, sums):
            ctx_ref[here, lanes] = (out / total).astype(jnp.bfloat16)
    weight = cols_of(w_out_ref, owner, width)
    for side, out_ref in enumerate((far_top_ref, far_bottom_ref)):
        out_ref[...] = jnp.dot(
            ctx_ref[pl.ds(side * half, half)], weight, preferred_element_type=jnp.float32
        ).astype(jnp.bfloat16)


def final_part(far, me, block, gain, w, acc, ss, img, place, text_row, key_ok, w_out):
    half, width = block[0].shape
    rows, cols = 2 * half, w.shape[2]
    return pl.pallas_call(
        functools.partial(final_kernel, far),
        out_shape=(
            jax.ShapeDtypeStruct((rows, cols), jnp.bfloat16),
            jax.ShapeDtypeStruct((half, width), jnp.bfloat16),
            jax.ShapeDtypeStruct((half, width), jnp.bfloat16),
        ),
        in_specs=[pl.BlockSpec(memory_space=pltpu.SMEM)]
        + vmem_specs(11),
        out_specs=tuple(vmem_specs(3)),
        scratch_shapes=[pltpu.VMEM((3, rows, cols), jnp.bfloat16)],
        compiler_params=params(16),
        cost_estimate=TINY,
    )(me, *block, gain, w, acc, ss, img, place, text_row, key_ok, w_out)


def out_kernel(away, me_ref, ctx_ref, w_ref, top_ref, bottom_ref):
    half, width = top_ref.shape
    weight = cols_of(w_ref, me_ref[0] ^ away, width)
    for side, out_ref in enumerate((top_ref, bottom_ref)):
        out_ref[...] = jnp.dot(
            ctx_ref[pl.ds(side * half, half)], weight, preferred_element_type=jnp.float32
        ).astype(out_ref.dtype)


def out_part(away, me, ctx, w, width, dtype=jnp.bfloat16):
    rows, depth = ctx.shape
    return pl.pallas_call(
        functools.partial(out_kernel, away),
        out_shape=(
            jax.ShapeDtypeStruct((rows // 2, width), dtype),
            jax.ShapeDtypeStruct((rows // 2, width), dtype),
        ),
        in_specs=[pl.BlockSpec(memory_space=pltpu.SMEM)] + vmem_specs(2),
        out_specs=tuple(vmem_specs(2)),
        compiler_params=params(16),
        cost_estimate=TINY,
    )(me, ctx, w)


def add_kernel(n_top, base_ref, *refs):
    out_ref, tmp_ref, sem_ref = refs[-3:]
    refs = refs[:-3]
    half = base_ref.shape[0] // 2
    copies = []
    for side, terms in enumerate((refs[:n_top], refs[n_top:])):
        part = pl.ds(side * half, half)
        total = terms[0][...].astype(jnp.float32)
        for term in terms[1:]:
            total += term[...].astype(jnp.float32)
        tmp_ref[part] = (base_ref[part].astype(jnp.float32) + total).astype(tmp_ref.dtype)
        copy = pltpu.make_async_copy(tmp_ref.at[part], out_ref.at[part], sem_ref.at[side])
        copy.start()
        copies.append(copy)
    for copy in copies:
        copy.wait()


def add_all(base, top, bottom):
    return pl.pallas_call(
        functools.partial(add_kernel, len(top)),
        out_shape=jax.ShapeDtypeStruct(base.shape, jnp.bfloat16),
        in_specs=vmem_specs(1 + len(top) + len(bottom)),
        out_specs=pl.BlockSpec(memory_space=pl.ANY),
        scratch_shapes=[pltpu.VMEM(base.shape, jnp.bfloat16), pltpu.SemaphoreType.DMA((2,))],
        compiler_params=params(16),
        cost_estimate=TINY,
    )(base, *top, *bottom)


def scatter_terms(parts, n):
    acc = {s: [[parts[s][0]], [parts[s][1]]] for s in range(n)}
    for s in by_bits(n, reverse=True):
        for side, bit in ((0, low_bit(s)), (1, high_bit(s))):
            terms = [t.astype(jnp.float32) for t in acc[s][side]]
            out = functools.reduce(lambda a, b: a + b, terms).astype(jnp.bfloat16)
            acc[s ^ bit][side].append(swap(out, bit))
    return acc[0]


def body(text, patches, grids, image_request, slot_start, vis_gain, dec_gain, w_qkv, w_out):
    n_req = lax.axis_size("req")
    n_ten = lax.axis_size("tensor")
    me_req = lax.axis_index("req")
    me_ten = lax.axis_index("tensor")
    img_dev, side, _, width = patches.shape
    half = side // 2
    region = half * half
    length = text.shape[0]
    w3 = jnp.transpose(w_qkv, (1, 0, 2))
    req_at = me_req.astype(jnp.int32)[None]
    ten_at = me_ten.astype(jnp.int32)[None]
    gains = dec_gain.astype(jnp.float32).reshape(n_ten, 1, width)
    order = by_bits(n_ten)
    near_at, far = order[:-1], order[-1]

    text_halves = split_rows(text)
    blocks = gather_halves(*text_halves, n_ten)

    outgoing = pool_images(req_at, image_request, jnp.transpose(patches, (1, 2, 0, 3)), n_req)
    received = [outgoing[0]] + [swap(outgoing[s], s, "req") for s in range(1, n_req)]

    n_rows = n_req * region
    n_img = round_up(n_rows + 1, 16)
    place, text_row, key_ok = placement(
        req_at, image_request, slot_start, grids, n_req, half, length, n_img
    )
    text_halves, outgoing = lax.optimization_barrier((text_halves, outgoing))
    acc, ss, w3 = own_part(ten_at, text_halves, gains, w3, n_ten)
    received, place, acc = lax.optimization_barrier((received, place, acc))

    img_own = pack_images(received, vis_gain.astype(jnp.float32).reshape(1, width), region, n_img)
    img_blocks = [img_own] + [swap(img_own, s) for s in range(1, n_ten)]

    near = [blocks[s] for s in near_at]
    acc, ss, w_out = near_part(near_at, ten_at, near, gains, w3, acc, ss, w_out)
    img_blocks, near = lax.optimization_barrier((img_blocks, near))
    img_qkv, merged = image_part(ten_at, img_blocks, gains, w3, n_rows)
    context, far_top, far_bottom = final_part(
        far, ten_at, blocks[far], gains, w3, acc, ss, img_qkv, place, text_row, key_ok, w_out
    )
    img_here = jnp.dot(place, merged, preferred_element_type=jnp.float32)
    x_in = (text.astype(jnp.float32) * text_row[:, :1] + img_here).astype(jnp.bfloat16)

    parts = {far: (far_top, far_bottom)}
    for s in reversed([0] + near_at):
        parts[s] = out_part(s, ten_at, context, w_out, width, jnp.float32 if s == 0 else jnp.bfloat16)
    top, bottom = scatter_terms(parts, n_ten)
    return add_all(x_in, top, bottom)


def solution(mesh):
    in_specs = (
        P("req", "tensor"),
        P("req", None, None, "tensor"),
        P(),
        P(),
        P(),
        P("tensor"),
        P(),
        P(None, None, "tensor"),
        P("tensor", None),
    )
    out_specs = P("req", "tensor")
    return jax.shard_map(body, mesh=mesh, in_specs=in_specs, out_specs=out_specs, check_vma=False)
```

```python
import functools

import jax
import jax.numpy as jnp
from jax import lax
from jax.experimental import pallas as pl
from jax.experimental.pallas import tpu as pltpu
from jax.sharding import PartitionSpec as P

D = 4096
HD = 128
EPS = 1e-05
LOG2E = 1.4426950408889634
TINY = pl.CostEstimate(flops=0, bytes_accessed=0, transcendentals=0)


def round_up(n, m):
    return -(-n // m) * m


def swap(x, s, axis="tensor"):
    n = lax.axis_size(axis)
    return lax.ppermute(x, axis, [(i, i ^ s) for i in range(n)])


def in_hbm(x):
    return pltpu.with_memory_space_constraint(x, pltpu.HBM)


def low_bit(s):
    return s & -s


def high_bit(s):
    return 1 << (s.bit_length() - 1)


def by_bits(n, reverse=False):
    return sorted(range(1, n), key=lambda s: (bin(s).count("1"), s), reverse=reverse)


def halves(block):
    if isinstance(block, tuple):
        return block
    half = block.shape[0] // 2
    return block[:half], block[half:]


def near_blocks(x, n):
    return {s: swap(x, s) for s in by_bits(n) if s & (s - 1) == 0}


def far_blocks(blocks, n):
    blocks = dict(blocks)
    for s in by_bits(n):
        if s not in blocks:
            low, high = low_bit(s), high_bit(s)
            blocks[s] = (swap(halves(blocks[s ^ low])[0], low), swap(halves(blocks[s ^ high])[1], high))
    return blocks


def vmem_specs(n):
    return [pl.BlockSpec(memory_space=pltpu.VMEM)] * n


def params(mib):
    return pltpu.CompilerParams(vmem_limit_bytes=mib * 1024 * 1024)


def pool_kernel(me_ref, req_ref, x_ref, dec_ref, vis_ref, *refs):
    outs, (dec_out, vis_out, tmp_ref) = refs[:-3], refs[-3:]
    per = vis_ref.shape[0]
    for i in range(per):
        lanes = pl.ds(i * 128, 128)
        vis_out[:, lanes] = vis_ref[i : i + 1, :].astype(jnp.float32)
        for t in range(dec_out.shape[0]):
            at = t * per + i
            dec_out[t, :, lanes] = dec_ref[at : at + 1, :].astype(jnp.float32)
    n_req = len(outs)
    side, img_dev = x_ref.shape[0], x_ref.shape[2]
    half = side // 2
    me = me_ref[0]
    rows = lax.broadcasted_iota(jnp.int32, (n_req, img_dev), 0)
    cols = lax.broadcasted_iota(jnp.int32, (n_req, img_dev), 1)
    away = jnp.full((n_req, img_dev), -1, jnp.int32)
    for k in range(img_dev):
        away = jnp.where(cols == k, req_ref[me * img_dev + k] ^ me, away)
    onehot = (rows == away).astype(jnp.bfloat16)
    tmp_ref[...] = jnp.zeros_like(tmp_ref)
    for i in range(half):
        for j in range(half):
            total = x_ref[2 * i, 2 * j].astype(jnp.float32)
            for a, b in ((0, 1), (1, 0), (1, 1)):
                total += x_ref[2 * i + a, 2 * j + b].astype(jnp.float32)
            pooled = (total * 0.25).astype(jnp.bfloat16)
            tmp_ref[:, i * half + j, :] = jnp.dot(onehot, pooled, preferred_element_type=jnp.float32)
    for s in range(n_req):
        outs[s][...] = tmp_ref[s].astype(jnp.bfloat16)


def pool_images(me, image_request, patches, dec_gain, vis_gain, n_req):
    side, _, img_dev, width = patches.shape
    padded = round_up((side // 2) ** 2, 16)
    return pl.pallas_call(
        pool_kernel,
        out_shape=(jax.ShapeDtypeStruct((padded, width), jnp.bfloat16),) * n_req
        + (
            jax.ShapeDtypeStruct((dec_gain.size // width, 1, width), jnp.float32),
            jax.ShapeDtypeStruct((1, width), jnp.float32),
        ),
        in_specs=[pl.BlockSpec(memory_space=pltpu.SMEM)] * 2 + vmem_specs(3),
        out_specs=tuple(vmem_specs(n_req + 2)),
        scratch_shapes=[pltpu.VMEM((n_req, padded, width), jnp.float32)],
        compiler_params=params(24),
        cost_estimate=TINY,
    )(me, image_request, patches, dec_gain.reshape(-1, 128), vis_gain.reshape(-1, 128))


def pack_kernel(region, gain_ref, *refs):
    recs, (out_ref, tmp_ref) = refs[:-2], refs[-2:]
    for r, rec_ref in enumerate(recs):
        tmp_ref[region * r : region * (r + 1)] = rec_ref[...].astype(jnp.float32)[:region]
    done = region * len(recs)
    rest = tmp_ref.shape[0] - done
    tmp_ref[done:] = jnp.broadcast_to(gain_ref[0:1, :], (rest, gain_ref.shape[1]))
    out_ref[...] = tmp_ref[...].astype(jnp.bfloat16)


def pack_images(received, gain, region, n_img):
    width = gain.shape[1]
    return pl.pallas_call(
        functools.partial(pack_kernel, region),
        out_shape=jax.ShapeDtypeStruct((n_img, width), jnp.bfloat16),
        in_specs=vmem_specs(1 + len(received)),
        out_specs=pl.BlockSpec(memory_space=pltpu.VMEM),
        scratch_shapes=[pltpu.VMEM((n_img, width), jnp.float32)],
        compiler_params=params(24),
        cost_estimate=TINY,
    )(gain, *received)


def place_kernel(n_req, half, me_ref, req_ref, start_ref, grid_ref, place_ref, text_row_ref, key_ref):
    rows, n_img = place_ref.shape
    img_dev = req_ref.shape[0] // n_req
    me = me_ref[0]
    lane = lax.broadcasted_iota(jnp.int32, (1, n_img), 1)

    def one_source(s, carry):
        pos, spot = carry
        source = me ^ s

        def one_image(k, found):
            i = source * img_dev + k
            hit = req_ref[i] == me
            values = (start_ref[i], grid_ref[0, i] // 2, grid_ref[1, i] // 2)
            return tuple(jnp.where(hit, new, old) for new, old in zip(values, found))

        none = jnp.int32(-1)
        start, high, wide = lax.fori_loop(0, img_dev, one_image, (none, none, none), unroll=img_dev <= 8)
        for i in range(half):
            for j in range(half):
                cell = i * half + j
                here = lane == s * half * half + cell
                has = start >= 0
                valid = has & (i < high) & (j < wide)
                pos = jnp.where(here, jnp.where(valid, start + i * wide + j, none), pos)
                spot = jnp.where(here, jnp.where(has, start + cell, none), spot)
        return pos, spot

    empty = jnp.full((1, n_img), -1, jnp.int32)
    pos, spot = lax.fori_loop(0, n_req, one_source, (empty, empty))
    row = lax.broadcasted_iota(jnp.int32, (rows, n_img), 0)
    placed = (row == pos).astype(jnp.float32)
    region = (row == spot).astype(jnp.float32)
    place = placed.astype(jnp.bfloat16)
    place_ref[...] = place
    text_row_ref[...] = jnp.broadcast_to(1.0 - jnp.sum(placed, axis=1, keepdims=True), text_row_ref.shape)
    ones = jnp.ones((8, n_img), jnp.bfloat16)
    open_keys = (placed - region).astype(jnp.bfloat16)
    count = lax.dot_general(ones, open_keys, (((1,), (1,)), ((), ())), preferred_element_type=jnp.float32)
    key_ref[...] = 1.0 + count


def placement(me, image_request, slot_start, grids, n_req, half, rows, n_img):
    return pl.pallas_call(
        functools.partial(place_kernel, n_req, half),
        out_shape=(
            jax.ShapeDtypeStruct((rows, n_img), jnp.bfloat16),
            jax.ShapeDtypeStruct((rows, 128), jnp.float32),
            jax.ShapeDtypeStruct((8, rows), jnp.float32),
        ),
        in_specs=[pl.BlockSpec(memory_space=pltpu.SMEM)] * 4,
        out_specs=tuple(vmem_specs(3)),
        compiler_params=params(8),
        cost_estimate=TINY,
    )(me, image_request, slot_start, grids.T)


def cols_of(ref, owner, width):
    return ref[:, pl.ds(pl.multiple_of(owner * width, width), width)]


def scale_rows(x, gain):
    xf = x.astype(jnp.float32)
    return (xf * gain).astype(jnp.bfloat16), jnp.sum(xf * xf, axis=1, keepdims=True)


def weight_copies(away, me_ref, w_ref, held_ref, sem_ref):
    width = held_ref.shape[2]
    copies = []
    for i, s in enumerate(away):
        rows = pl.ds(pl.multiple_of((me_ref[0] ^ s) * width, width), width)
        copies.append([pltpu.make_async_copy(w_ref.at[j, rows], held_ref.at[i, j], sem_ref.at[i, j]) for j in range(3)])
    for row in copies:
        for copy in row:
            copy.start()
    return copies


def held_weights(n, w, width):
    return pltpu.VMEM((n, 3, width, w.shape[2]), w.dtype)


def own_kernel(far, me_ref, x_ref, gain_ref, w_ref, acc_ref, ss_ref, held_ref, sem_ref):
    half = x_ref.shape[0] // 2
    copies = weight_copies((0, far), me_ref, w_ref, held_ref, sem_ref)
    scaled = []
    for side in range(2):
        rows = pl.ds(side * half, half)
        x, total = scale_rows(x_ref[rows], gain_ref[me_ref[0]])
        scaled.append(x)
        ss_ref[rows] = jnp.broadcast_to(total, (half, 128))
    for j in range(3):
        copies[0][j].wait()
        for side in range(2):
            acc_ref[j, pl.ds(side * half, half)] = jnp.dot(
                scaled[side], held_ref[0, j], preferred_element_type=jnp.float32
            )
    for copy in copies[1]:
        copy.wait()


def own_part(far, me, x, gain, w):
    rows, width = x.shape
    return pl.pallas_call(
        functools.partial(own_kernel, far),
        out_shape=(
            jax.ShapeDtypeStruct((3, rows, w.shape[2]), jnp.float32),
            jax.ShapeDtypeStruct((rows, 128), jnp.float32),
            held_weights(2, w, width),
        ),
        in_specs=[pl.BlockSpec(memory_space=pltpu.SMEM)] + vmem_specs(2) + [pl.BlockSpec(memory_space=pltpu.HBM)],
        out_specs=tuple(vmem_specs(3)),
        scratch_shapes=[pltpu.SemaphoreType.DMA((2, 3))],
        compiler_params=params(12),
        cost_estimate=TINY,
    )(me, x, gain, in_hbm(w))


def near_kernel(near, pieces, me_ref, *refs):
    n_x = sum(pieces)
    x_refs, refs = list(refs[:n_x]), refs[n_x:]
    gain_ref, acc_in, ss_in, w_ref, acc_ref, ss_ref, held_ref, sem_ref = refs
    half = acc_ref.shape[1] // 2
    copies = weight_copies(near, me_ref, w_ref, held_ref, sem_ref)
    views = []
    for n in pieces:
        mine, x_refs = x_refs[:n], x_refs[n:]
        views.append([mine[0].at[pl.ds(side * half, half)] if n == 1 else mine[side] for side in range(2)])
    scaled = {}
    for side in range(2):
        rows = pl.ds(side * half, half)
        total = ss_in[rows]
        for b, s in enumerate(near):
            scaled[side, b], part = scale_rows(views[b][side][...], gain_ref[me_ref[0] ^ s])
            total += part
        ss_ref[rows] = total
    for j in range(3):
        for b in range(len(near)):
            copies[b][j].wait()
        for side in range(2):
            rows = pl.ds(side * half, half)
            acc = acc_in[j, rows]
            for b in range(len(near)):
                acc += jnp.dot(scaled[side, b], held_ref[b, j], preferred_element_type=jnp.float32)
            acc_ref[j, rows] = acc


def near_part(near, me, blocks, gain, acc, ss, w):
    width = gain.shape[2]
    blocks = [b if isinstance(b, tuple) else (b,) for b in blocks]
    pieces = [len(b) for b in blocks]
    return pl.pallas_call(
        functools.partial(near_kernel, near, pieces),
        out_shape=(
            jax.ShapeDtypeStruct(acc.shape, jnp.float32),
            jax.ShapeDtypeStruct(ss.shape, jnp.float32),
            held_weights(len(near), w, width),
        ),
        in_specs=[pl.BlockSpec(memory_space=pltpu.SMEM)]
        + vmem_specs(sum(pieces) + 3)
        + [pl.BlockSpec(memory_space=pltpu.HBM)],
        out_specs=tuple(vmem_specs(3)),
        scratch_shapes=[pltpu.SemaphoreType.DMA((len(near), 3))],
        compiler_params=params(16),
        cost_estimate=TINY,
    )(me, *[h for b in blocks for h in b], gain, acc, ss, in_hbm(w))


def image_kernel(n_rows, far, near, me_ref, *refs):
    n_blk = len(near) + 2
    x_refs, refs = refs[:n_blk], refs[n_blk:]
    gain_ref, held_ref, near_ref, w_out_ref, qkv_ref, own_ref, w_out_held, sem_ref = refs
    copy = pltpu.make_async_copy(w_out_ref, w_out_held, sem_ref)
    copy.start()
    total = 0.0
    for s in range(n_blk):
        xf = x_refs[s][...].astype(jnp.float32)
        total += jnp.sum(xf * xf, axis=1, keepdims=True)
    scale = lax.rsqrt(total / D + EPS)
    total = 0.0
    scaled = []
    for s in range(n_blk):
        xf = x_refs[s][...].astype(jnp.float32)
        merged = (xf * scale * xf[n_rows : n_rows + 1]).astype(jnp.bfloat16)
        if s == 0:
            own_ref[...] = merged
        mf = merged.astype(jnp.float32)
        total += jnp.sum(mf * mf, axis=1, keepdims=True)
        scaled.append((mf * gain_ref[me_ref[0] ^ s]).astype(jnp.bfloat16))
    scale = lax.rsqrt(total / D + EPS)
    for j in range(3):
        weights = [(0, held_ref[0, j]), (far, held_ref[1, j])] + [(s, near_ref[i, j]) for i, s in enumerate(near)]
        acc = 0.0
        for s, weight in weights:
            acc += jnp.dot(scaled[s], weight, preferred_element_type=jnp.float32)
        qkv_ref[j] = (acc * scale).astype(jnp.bfloat16)
    copy.wait()


def image_part(far, near, me, blocks, gain, held, near_held, w_out, n_rows):
    n_img, width = blocks[0].shape
    return pl.pallas_call(
        functools.partial(image_kernel, n_rows, far, near),
        out_shape=(
            jax.ShapeDtypeStruct((3, n_img, held.shape[3]), jnp.bfloat16),
            jax.ShapeDtypeStruct((n_img, width), jnp.bfloat16),
            pltpu.VMEM(w_out.shape, w_out.dtype),
        ),
        in_specs=[pl.BlockSpec(memory_space=pltpu.SMEM)]
        + vmem_specs(len(blocks) + 3)
        + [pl.BlockSpec(memory_space=pltpu.HBM)],
        out_specs=tuple(vmem_specs(3)),
        scratch_shapes=[pltpu.SemaphoreType.DMA],
        compiler_params=params(16),
        cost_estimate=TINY,
    )(me, *blocks, gain, held, near_held, in_hbm(w_out))


def final_kernel(far, me_ref, top_ref, bottom_ref, gain_ref, held_ref, acc_ref, ss_ref, img_ref, place_ref, text_row_ref,
                 key_ref, w_out_ref, ctx_ref, far_top_ref, far_bottom_ref, qkv_ref):
    half, width = top_ref.shape
    rows, cols = 2 * half, ctx_ref.shape[1]
    owner = me_ref[0] ^ far
    scaled, scales = [], []
    for side, x_ref in enumerate((top_ref, bottom_ref)):
        part = pl.ds(side * half, half)
        x, total = scale_rows(x_ref[...], gain_ref[owner])
        scaled.append(x)
        total = ss_ref[part] + total
        scales.append((lax.rsqrt(total / D + EPS) * text_row_ref[part])[:, :1])
    for j in range(3):
        weight = held_ref[1, j]
        for side in range(2):
            part = pl.ds(side * half, half)
            prod = jnp.dot(scaled[side], weight, preferred_element_type=jnp.float32)
            put = jnp.dot(place_ref[part], img_ref[j], preferred_element_type=jnp.float32)
            qkv_ref[j, part] = ((prod + acc_ref[j, part]) * scales[side] + put).astype(jnp.bfloat16)
    step = 128
    heads = [pl.ds(h * HD, HD) for h in range(cols // HD)]
    for r in range(rows // step):
        here, last = pl.ds(r * step, step), (r + 1) * step
        row = lax.broadcasted_iota(jnp.int32, (step, last), 0) + r * step
        col = lax.broadcasted_iota(jnp.int32, (step, last), 1)
        bias = jnp.where((row >= col) & (key_ref[0:1, pl.ds(0, last)] > 0.5), 0.0, -1e30)
        scores = [
            lax.dot_general(
                qkv_ref[0, here, lanes],
                qkv_ref[1, pl.ds(0, last), lanes],
                (((1,), (1,)), ((), ())),
                preferred_element_type=jnp.float32,
            )
            for lanes in heads
        ]
        scores = [x * (LOG2E / HD**0.5) + bias for x in scores]
        tops = [jnp.max(x, axis=1, keepdims=True) for x in scores]
        expo = [jnp.exp2(x - top) for x, top in zip(scores, tops)]
        sums = [jnp.sum(x, axis=1, keepdims=True) for x in expo]
        outs = [
            jnp.dot(x.astype(jnp.bfloat16), qkv_ref[2, pl.ds(0, last), lanes], preferred_element_type=jnp.float32)
            for x, lanes in zip(expo, heads)
        ]
        for lanes, out, total in zip(heads, outs, sums):
            ctx_ref[here, lanes] = (out / total).astype(jnp.bfloat16)
    weight = cols_of(w_out_ref, owner, width)
    for side, out_ref in enumerate((far_top_ref, far_bottom_ref)):
        out_ref[...] = jnp.dot(
            ctx_ref[pl.ds(side * half, half)], weight, preferred_element_type=jnp.float32
        ).astype(jnp.bfloat16)


def final_part(far, me, block, gain, held, acc, ss, img, place, text_row, key_ok, w_out):
    half, width = block[0].shape
    rows, cols = 2 * half, held.shape[3]
    return pl.pallas_call(
        functools.partial(final_kernel, far),
        out_shape=(
            jax.ShapeDtypeStruct((rows, cols), jnp.bfloat16),
            jax.ShapeDtypeStruct((half, width), jnp.bfloat16),
            jax.ShapeDtypeStruct((half, width), jnp.bfloat16),
        ),
        in_specs=[pl.BlockSpec(memory_space=pltpu.SMEM)]
        + vmem_specs(11),
        out_specs=tuple(vmem_specs(3)),
        scratch_shapes=[pltpu.VMEM((3, rows, cols), jnp.bfloat16)],
        compiler_params=params(16),
        cost_estimate=TINY,
    )(me, *block, gain, held, acc, ss, img, place, text_row, key_ok, w_out)


def out_kernel(away, me_ref, ctx_ref, w_ref, top_ref, bottom_ref):
    half, width = top_ref.shape
    weight = cols_of(w_ref, me_ref[0] ^ away, width)
    for side, out_ref in enumerate((top_ref, bottom_ref)):
        out_ref[...] = jnp.dot(
            ctx_ref[pl.ds(side * half, half)], weight, preferred_element_type=jnp.float32
        ).astype(out_ref.dtype)


def out_part(away, me, ctx, w, width, dtype=jnp.bfloat16):
    rows, depth = ctx.shape
    return pl.pallas_call(
        functools.partial(out_kernel, away),
        out_shape=(
            jax.ShapeDtypeStruct((rows // 2, width), dtype),
            jax.ShapeDtypeStruct((rows // 2, width), dtype),
        ),
        in_specs=[pl.BlockSpec(memory_space=pltpu.SMEM)] + vmem_specs(2),
        out_specs=tuple(vmem_specs(2)),
        compiler_params=params(16),
        cost_estimate=TINY,
    )(me, ctx, w)


def add_kernel(n_top, base_ref, *refs):
    out_ref, tmp_ref, sem_ref = refs[-3:]
    refs = refs[:-3]
    half = base_ref.shape[0] // 2
    copies = []
    for side, terms in enumerate((refs[:n_top], refs[n_top:])):
        part = pl.ds(side * half, half)
        total = terms[0][...].astype(jnp.float32)
        for term in terms[1:]:
            total += term[...].astype(jnp.float32)
        tmp_ref[part] = (base_ref[part].astype(jnp.float32) + total).astype(tmp_ref.dtype)
        copy = pltpu.make_async_copy(tmp_ref.at[part], out_ref.at[part], sem_ref.at[side])
        copy.start()
        copies.append(copy)
    for copy in copies:
        copy.wait()


def add_all(base, top, bottom):
    return pl.pallas_call(
        functools.partial(add_kernel, len(top)),
        out_shape=jax.ShapeDtypeStruct(base.shape, jnp.bfloat16),
        in_specs=vmem_specs(1 + len(top) + len(bottom)),
        out_specs=pl.BlockSpec(memory_space=pl.ANY),
        scratch_shapes=[pltpu.VMEM(base.shape, jnp.bfloat16), pltpu.SemaphoreType.DMA((2,))],
        compiler_params=params(16),
        cost_estimate=TINY,
    )(base, *top, *bottom)


def scatter_terms(parts, n):
    acc = {s: [[parts[s][0]], [parts[s][1]]] for s in range(n)}
    for s in by_bits(n, reverse=True):
        for side, bit in ((0, low_bit(s)), (1, high_bit(s))):
            terms = [t.astype(jnp.float32) for t in acc[s][side]]
            out = functools.reduce(lambda a, b: a + b, terms).astype(jnp.bfloat16)
            acc[s ^ bit][side].append(swap(out, bit))
    return acc[0]


def body(text, patches, grids, image_request, slot_start, vis_gain, dec_gain, w_qkv, w_out):
    n_req = lax.axis_size("req")
    n_ten = lax.axis_size("tensor")
    me_req = lax.axis_index("req")
    me_ten = lax.axis_index("tensor")
    img_dev, side, _, width = patches.shape
    half = side // 2
    region = half * half
    length = text.shape[0]
    w3 = jnp.transpose(w_qkv, (1, 0, 2))
    req_at = me_req.astype(jnp.int32)[None]
    ten_at = me_ten.astype(jnp.int32)[None]
    order = by_bits(n_ten)
    near_at, far = order[:-1], order[-1]

    blocks = near_blocks(text, n_ten)

    *outgoing, gains, vis_row = pool_images(
        req_at, image_request, jnp.transpose(patches, (1, 2, 0, 3)), dec_gain, vis_gain, n_req
    )
    received = [outgoing[0]] + [swap(outgoing[s], s, "req") for s in range(1, n_req)]
    n_rows = n_req * region
    n_img = round_up(n_rows + 1, 16)
    img_own = pack_images(received, vis_row, region, n_img)
    img_blocks = [img_own] + [swap(img_own, s) for s in range(1, n_ten)]

    own, gains, starts, _ = lax.optimization_barrier((text, gains, slot_start, img_own))
    place, text_row, key_ok = placement(req_at, image_request, starts, grids, n_req, half, length, n_img)
    acc, ss, held = own_part(far, ten_at, own, gains, w3)
    blocks, acc, place = lax.optimization_barrier((blocks, acc, place))
    blocks = far_blocks(blocks, n_ten)

    near = [blocks[s] for s in near_at]
    acc, ss, near_held = near_part(near_at, ten_at, near, gains, acc, ss, w3)
    img_qkv, merged, w_out = image_part(far, near_at, ten_at, img_blocks, gains, held, near_held, w_out, n_rows)
    context, far_top, far_bottom = final_part(
        far, ten_at, blocks[far], gains, held, acc, ss, img_qkv, place, text_row, key_ok, w_out
    )
    img_here = jnp.dot(place, merged, preferred_element_type=jnp.float32)
    x_in = (text.astype(jnp.float32) * text_row[:, :1] + img_here).astype(jnp.bfloat16)

    parts = {far: (far_top, far_bottom)}
    for s in reversed([0] + near_at):
        parts[s] = out_part(s, ten_at, context, w_out, width, jnp.float32 if s == 0 else jnp.bfloat16)
    top, bottom = scatter_terms(parts, n_ten)
    return add_all(x_in, top, bottom)


def solution(mesh):
    in_specs = (
        P("req", "tensor"),
        P("req", None, None, "tensor"),
        P(),
        P(),
        P(),
        P("tensor"),
        P(),
        P(None, None, "tensor"),
        P("tensor", None),
    )
    out_specs = P("req", "tensor")
    return jax.shard_map(body, mesh=mesh, in_specs=in_specs, out_specs=out_specs, check_vma=False)
```

```python
import functools

import jax
import jax.numpy as jnp
from jax import lax
from jax.experimental import pallas as pl
from jax.experimental.pallas import tpu as pltpu
from jax.sharding import PartitionSpec as P

D = 4096
HD = 128
EPS = 1e-05
LOG2E = 1.4426950408889634
TINY = pl.CostEstimate(flops=0, bytes_accessed=0, transcendentals=0)


def round_up(n, m):
    return -(-n // m) * m


def swap(x, s, axis="tensor"):
    n = lax.axis_size(axis)
    return lax.ppermute(x, axis, [(i, i ^ s) for i in range(n)])


def in_hbm(x):
    return pltpu.with_memory_space_constraint(x, pltpu.HBM)


def low_bit(s):
    return s & -s


def high_bit(s):
    return 1 << (s.bit_length() - 1)


def by_bits(n, reverse=False):
    return sorted(range(1, n), key=lambda s: (bin(s).count("1"), s), reverse=reverse)


def halves(block):
    if isinstance(block, tuple):
        return block
    half = block.shape[0] // 2
    return block[:half], block[half:]


def near_blocks(x, n):
    return {s: swap(x, s) for s in by_bits(n) if s & (s - 1) == 0}


def far_blocks(blocks, n):
    blocks = dict(blocks)
    for s in by_bits(n):
        if s not in blocks:
            low, high = low_bit(s), high_bit(s)
            blocks[s] = (swap(halves(blocks[s ^ low])[0], low), swap(halves(blocks[s ^ high])[1], high))
    return blocks


def vmem_specs(n):
    return [pl.BlockSpec(memory_space=pltpu.VMEM)] * n


def params(mib):
    return pltpu.CompilerParams(vmem_limit_bytes=mib * 1024 * 1024)


def fetch(pairs, sem_ref):
    copies = [pltpu.make_async_copy(src, dst, sem_ref.at[i]) for i, (src, dst) in enumerate(pairs)]
    for copy in copies:
        copy.start()
    return copies


def pool_kernel(me_ref, req_hbm, x_hbm, dec_hbm, vis_hbm, out_ref, dec_out, vis_out, req_ref, x_ref, dec_ref, vis_ref,
                tmp_ref, sem_ref):
    pairs = ((req_hbm, req_ref), (x_hbm, x_ref), (dec_hbm, dec_ref), (vis_hbm, vis_ref))
    copies = fetch(pairs, sem_ref)
    n_req = out_ref.shape[0]
    side, img_dev = x_ref.shape[0], x_ref.shape[2]
    half = side // 2
    me = me_ref[0]
    rows = lax.broadcasted_iota(jnp.int32, (n_req, img_dev), 0)
    cols = lax.broadcasted_iota(jnp.int32, (n_req, img_dev), 1)
    goal = jnp.full((n_req, img_dev), -1, jnp.int32)
    tmp_ref[...] = jnp.zeros_like(tmp_ref)
    copies[0].wait()
    for k in range(img_dev):
        goal = jnp.where(cols == k, req_ref[me * img_dev + k], goal)
    onehot = (rows == goal).astype(jnp.bfloat16)
    copies[2].wait()
    copies[3].wait()
    per = vis_ref.shape[0]
    for i in range(per):
        lanes = pl.ds(i * 128, 128)
        vis_out[:, lanes] = vis_ref[i : i + 1, :].astype(jnp.float32)
        for t in range(dec_out.shape[0]):
            at = t * per + i
            dec_out[t, :, lanes] = dec_ref[at : at + 1, :].astype(jnp.float32)
    copies[1].wait()
    for i in range(half):
        for j in range(half):
            total = x_ref[2 * i, 2 * j].astype(jnp.float32)
            for a, b in ((0, 1), (1, 0), (1, 1)):
                total += x_ref[2 * i + a, 2 * j + b].astype(jnp.float32)
            pooled = (total * 0.25).astype(jnp.bfloat16)
            tmp_ref[:, i * half + j, :] = jnp.dot(onehot, pooled, preferred_element_type=jnp.float32)
    out_ref[...] = tmp_ref[...].astype(jnp.bfloat16)


def pool_images(me, image_request, patches, dec_gain, vis_gain, n_req):
    side, _, img_dev, width = patches.shape
    padded = round_up((side // 2) ** 2, 16)
    inputs = (image_request, patches, dec_gain.reshape(-1, 128), vis_gain.reshape(-1, 128))
    return pl.pallas_call(
        pool_kernel,
        out_shape=(
            jax.ShapeDtypeStruct((n_req, padded, width), jnp.bfloat16),
            jax.ShapeDtypeStruct((dec_gain.size // width, 1, width), jnp.float32),
            jax.ShapeDtypeStruct((1, width), jnp.float32),
        ),
        in_specs=[pl.BlockSpec(memory_space=pltpu.SMEM)] + [pl.BlockSpec(memory_space=pltpu.HBM)] * 4,
        out_specs=tuple(vmem_specs(3)),
        scratch_shapes=[pltpu.SMEM(image_request.shape, jnp.int32)]
        + [pltpu.VMEM(x.shape, x.dtype) for x in inputs[1:]]
        + [pltpu.VMEM((n_req, padded, width), jnp.float32), pltpu.SemaphoreType.DMA((4,))],
        compiler_params=params(24),
        cost_estimate=TINY,
    )(me, *[in_hbm(x) for x in inputs])


def pack_kernel(region, rec_ref, gain_ref, out_ref, tmp_ref):
    n_req = rec_ref.shape[0]
    for r in range(n_req):
        tmp_ref[region * r : region * (r + 1)] = rec_ref[r].astype(jnp.float32)[:region]
    rest = tmp_ref.shape[0] - region * n_req
    tmp_ref[region * n_req :] = jnp.broadcast_to(gain_ref[0:1, :], (rest, gain_ref.shape[1]))
    out_ref[...] = tmp_ref[...].astype(jnp.bfloat16)


def pack_images(received, gain, region, n_img):
    width = received.shape[2]
    return pl.pallas_call(
        functools.partial(pack_kernel, region),
        out_shape=jax.ShapeDtypeStruct((n_img, width), jnp.bfloat16),
        in_specs=vmem_specs(2),
        out_specs=pl.BlockSpec(memory_space=pltpu.VMEM),
        scratch_shapes=[pltpu.VMEM((n_img, width), jnp.float32)],
        compiler_params=params(24),
        cost_estimate=TINY,
    )(received, gain)


def place_kernel(n_req, half, me_ref, req_hbm, start_hbm, grid_hbm, place_ref, text_row_ref, key_ref, req_ref,
                 start_ref, grid_ref, sem_ref):
    for copy in fetch(((req_hbm, req_ref), (start_hbm, start_ref), (grid_hbm, grid_ref)), sem_ref):
        copy.wait()
    rows, n_img = place_ref.shape
    img_dev = req_ref.shape[0] // n_req
    me = me_ref[0]
    lane = lax.broadcasted_iota(jnp.int32, (1, n_img), 1)

    def one_source(s, carry):
        pos, spot = carry
        source = s

        def one_image(k, found):
            i = source * img_dev + k
            hit = req_ref[i] == me
            values = (start_ref[i], grid_ref[0, i] // 2, grid_ref[1, i] // 2)
            return tuple(jnp.where(hit, new, old) for new, old in zip(values, found))

        none = jnp.int32(-1)
        start, high, wide = lax.fori_loop(0, img_dev, one_image, (none, none, none), unroll=img_dev <= 8)
        for i in range(half):
            for j in range(half):
                cell = i * half + j
                here = lane == s * half * half + cell
                has = start >= 0
                valid = has & (i < high) & (j < wide)
                pos = jnp.where(here, jnp.where(valid, start + i * wide + j, none), pos)
                spot = jnp.where(here, jnp.where(has, start + cell, none), spot)
        return pos, spot

    empty = jnp.full((1, n_img), -1, jnp.int32)
    pos, spot = lax.fori_loop(0, n_req, one_source, (empty, empty))
    row = lax.broadcasted_iota(jnp.int32, (rows, n_img), 0)
    placed = (row == pos).astype(jnp.float32)
    region = (row == spot).astype(jnp.float32)
    place = placed.astype(jnp.bfloat16)
    place_ref[...] = place
    text_row_ref[...] = jnp.broadcast_to(1.0 - jnp.sum(placed, axis=1, keepdims=True), text_row_ref.shape)
    ones = jnp.ones((8, n_img), jnp.bfloat16)
    open_keys = (placed - region).astype(jnp.bfloat16)
    count = lax.dot_general(ones, open_keys, (((1,), (1,)), ((), ())), preferred_element_type=jnp.float32)
    key_ref[...] = 1.0 + count


def placement(me, image_request, slot_start, grids, n_req, half, rows, n_img):
    inputs = (image_request, slot_start, grids.T)
    return pl.pallas_call(
        functools.partial(place_kernel, n_req, half),
        out_shape=(
            jax.ShapeDtypeStruct((rows, n_img), jnp.bfloat16),
            jax.ShapeDtypeStruct((rows, 128), jnp.float32),
            jax.ShapeDtypeStruct((8, rows), jnp.float32),
        ),
        in_specs=[pl.BlockSpec(memory_space=pltpu.SMEM)] + [pl.BlockSpec(memory_space=pltpu.HBM)] * 3,
        out_specs=tuple(vmem_specs(3)),
        scratch_shapes=[pltpu.SMEM(x.shape, jnp.int32) for x in inputs] + [pltpu.SemaphoreType.DMA((3,))],
        compiler_params=params(8),
        cost_estimate=TINY,
    )(me, *[in_hbm(x) for x in inputs])


def cols_of(ref, owner, width):
    return ref[:, pl.ds(pl.multiple_of(owner * width, width), width)]


def scale_rows(x, gain):
    xf = x.astype(jnp.float32)
    return (xf * gain).astype(jnp.bfloat16), jnp.sum(xf * xf, axis=1, keepdims=True)


def own_kernel(me_ref, x_ref, gain_ref, w_ref, acc_ref, ss_ref, held_ref, sem_ref):
    n_ten, _, width, _ = held_ref.shape
    half = x_ref.shape[0] // 2
    copies = []
    for s in range(n_ten):
        rows = pl.ds(pl.multiple_of((me_ref[0] ^ s) * width, width), width)
        copies += [pltpu.make_async_copy(w_ref.at[j, rows], held_ref.at[s, j], sem_ref.at[s, j]) for j in range(3)]
    for copy in copies[:3]:
        copy.start()
    scaled = []
    for side in range(2):
        rows = pl.ds(side * half, half)
        x, total = scale_rows(x_ref[rows], gain_ref[me_ref[0]])
        scaled.append(x)
        ss_ref[rows] = jnp.broadcast_to(total, (half, 128))
    for j in range(3):
        copies[j].wait()
        if j == 0:
            for copy in copies[3:]:
                copy.start()
        for side in range(2):
            acc_ref[j, pl.ds(side * half, half)] = jnp.dot(
                scaled[side], held_ref[0, j], preferred_element_type=jnp.float32
            )
    for copy in copies[3:]:
        copy.wait()


def own_part(me, x, gain, w):
    rows, width = x.shape
    n_ten, cols = gain.shape[0], w.shape[2]
    return pl.pallas_call(
        own_kernel,
        out_shape=(
            jax.ShapeDtypeStruct((3, rows, cols), jnp.float32),
            jax.ShapeDtypeStruct((rows, 128), jnp.float32),
            pltpu.VMEM((n_ten, 3, width, cols), w.dtype),
        ),
        in_specs=[pl.BlockSpec(memory_space=pltpu.SMEM)] + vmem_specs(2) + [pl.BlockSpec(memory_space=pltpu.HBM)],
        out_specs=tuple(vmem_specs(3)),
        scratch_shapes=[pltpu.SemaphoreType.DMA((n_ten, 3))],
        compiler_params=params(12),
        cost_estimate=TINY,
    )(me, x, gain, in_hbm(w))


def near_kernel(near, pieces, me_ref, *refs):
    n_x = sum(pieces)
    x_refs, refs = list(refs[:n_x]), refs[n_x:]
    gain_ref, held_ref, acc_in, ss_in, acc_ref, ss_ref = refs
    half = acc_ref.shape[1] // 2
    views = []
    for n in pieces:
        mine, x_refs = x_refs[:n], x_refs[n:]
        views.append([mine[0].at[pl.ds(side * half, half)] if n == 1 else mine[side] for side in range(2)])
    scaled = {}
    for side in range(2):
        rows = pl.ds(side * half, half)
        total = ss_in[rows]
        for b, s in enumerate(near):
            scaled[side, b], part = scale_rows(views[b][side][...], gain_ref[me_ref[0] ^ s])
            total += part
        ss_ref[rows] = total
    for j in range(3):
        for side in range(2):
            rows = pl.ds(side * half, half)
            acc = acc_in[j, rows]
            for b, s in enumerate(near):
                acc += jnp.dot(scaled[side, b], held_ref[s, j], preferred_element_type=jnp.float32)
            acc_ref[j, rows] = acc


def near_part(near, me, blocks, gain, held, acc, ss):
    blocks = [b if isinstance(b, tuple) else (b,) for b in blocks]
    pieces = [len(b) for b in blocks]
    return pl.pallas_call(
        functools.partial(near_kernel, near, pieces),
        out_shape=(
            jax.ShapeDtypeStruct(acc.shape, jnp.float32),
            jax.ShapeDtypeStruct(ss.shape, jnp.float32),
        ),
        in_specs=[pl.BlockSpec(memory_space=pltpu.SMEM)]
        + vmem_specs(sum(pieces) + 4),
        out_specs=tuple(vmem_specs(2)),
        compiler_params=params(16),
        cost_estimate=TINY,
    )(me, *[h for b in blocks for h in b], gain, held, acc, ss)


def image_kernel(n_rows, n_blk, me_ref, *refs):
    x_refs, refs = refs[:n_blk], refs[n_blk:]
    gain_ref, held_ref, w_out_ref, qkv_ref, own_ref, w_out_held, sem_ref = refs
    copy = pltpu.make_async_copy(w_out_ref, w_out_held, sem_ref)
    copy.start()
    total = 0.0
    for s in range(n_blk):
        xf = x_refs[s][...].astype(jnp.float32)
        total += jnp.sum(xf * xf, axis=1, keepdims=True)
    scale = lax.rsqrt(total / D + EPS)
    total = 0.0
    scaled = []
    for s in range(n_blk):
        xf = x_refs[s][...].astype(jnp.float32)
        merged = (xf * scale * xf[n_rows : n_rows + 1]).astype(jnp.bfloat16)
        if s == 0:
            own_ref[...] = merged
        mf = merged.astype(jnp.float32)
        total += jnp.sum(mf * mf, axis=1, keepdims=True)
        scaled.append((mf * gain_ref[me_ref[0] ^ s]).astype(jnp.bfloat16))
    scale = lax.rsqrt(total / D + EPS)
    for j in range(3):
        acc = 0.0
        for s in range(n_blk):
            acc += jnp.dot(scaled[s], held_ref[s, j], preferred_element_type=jnp.float32)
        qkv_ref[j] = (acc * scale).astype(jnp.bfloat16)
    copy.wait()


def image_part(me, blocks, gain, held, w_out, n_rows):
    n_img, width = blocks[0].shape
    return pl.pallas_call(
        functools.partial(image_kernel, n_rows, len(blocks)),
        out_shape=(
            jax.ShapeDtypeStruct((3, n_img, held.shape[3]), jnp.bfloat16),
            jax.ShapeDtypeStruct((n_img, width), jnp.bfloat16),
            pltpu.VMEM(w_out.shape, w_out.dtype),
        ),
        in_specs=[pl.BlockSpec(memory_space=pltpu.SMEM)]
        + vmem_specs(len(blocks) + 2)
        + [pl.BlockSpec(memory_space=pltpu.HBM)],
        out_specs=tuple(vmem_specs(3)),
        scratch_shapes=[pltpu.SemaphoreType.DMA],
        compiler_params=params(16),
        cost_estimate=TINY,
    )(me, *blocks, gain, held, in_hbm(w_out))


def final_kernel(far, me_ref, top_ref, bottom_ref, gain_ref, held_ref, acc_ref, ss_ref, img_ref, place_ref, text_row_ref,
                 key_ref, w_out_ref, ctx_ref, far_top_ref, far_bottom_ref, qkv_ref):
    half, width = top_ref.shape
    rows, cols = 2 * half, ctx_ref.shape[1]
    owner = me_ref[0] ^ far
    scaled, scales = [], []
    for side, x_ref in enumerate((top_ref, bottom_ref)):
        part = pl.ds(side * half, half)
        x, total = scale_rows(x_ref[...], gain_ref[owner])
        scaled.append(x)
        total = ss_ref[part] + total
        scales.append((lax.rsqrt(total / D + EPS) * text_row_ref[part])[:, :1])
    for j in range(3):
        weight = held_ref[far, j]
        for side in range(2):
            part = pl.ds(side * half, half)
            prod = jnp.dot(scaled[side], weight, preferred_element_type=jnp.float32)
            put = jnp.dot(place_ref[part], img_ref[j], preferred_element_type=jnp.float32)
            qkv_ref[j, part] = ((prod + acc_ref[j, part]) * scales[side] + put).astype(jnp.bfloat16)
    step = 128
    heads = [pl.ds(h * HD, HD) for h in range(cols // HD)]
    for r in range(rows // step):
        here, last = pl.ds(r * step, step), (r + 1) * step
        row = lax.broadcasted_iota(jnp.int32, (step, last), 0) + r * step
        col = lax.broadcasted_iota(jnp.int32, (step, last), 1)
        bias = jnp.where((row >= col) & (key_ref[0:1, pl.ds(0, last)] > 0.5), 0.0, -1e30)
        scores = [
            lax.dot_general(
                qkv_ref[0, here, lanes],
                qkv_ref[1, pl.ds(0, last), lanes],
                (((1,), (1,)), ((), ())),
                preferred_element_type=jnp.float32,
            )
            for lanes in heads
        ]
        scores = [x * (LOG2E / HD**0.5) + bias for x in scores]
        tops = [jnp.max(x, axis=1, keepdims=True) for x in scores]
        expo = [jnp.exp2(x - top) for x, top in zip(scores, tops)]
        sums = [jnp.sum(x, axis=1, keepdims=True) for x in expo]
        outs = [
            jnp.dot(x.astype(jnp.bfloat16), qkv_ref[2, pl.ds(0, last), lanes], preferred_element_type=jnp.float32)
            for x, lanes in zip(expo, heads)
        ]
        for lanes, out, total in zip(heads, outs, sums):
            ctx_ref[here, lanes] = (out / total).astype(jnp.bfloat16)
    weight = cols_of(w_out_ref, owner, width)
    for side, out_ref in enumerate((far_top_ref, far_bottom_ref)):
        out_ref[...] = jnp.dot(
            ctx_ref[pl.ds(side * half, half)], weight, preferred_element_type=jnp.float32
        ).astype(jnp.bfloat16)


def final_part(far, me, block, gain, held, acc, ss, img, place, text_row, key_ok, w_out):
    half, width = block[0].shape
    rows, cols = 2 * half, held.shape[3]
    return pl.pallas_call(
        functools.partial(final_kernel, far),
        out_shape=(
            jax.ShapeDtypeStruct((rows, cols), jnp.bfloat16),
            jax.ShapeDtypeStruct((half, width), jnp.bfloat16),
            jax.ShapeDtypeStruct((half, width), jnp.bfloat16),
        ),
        in_specs=[pl.BlockSpec(memory_space=pltpu.SMEM)]
        + vmem_specs(11),
        out_specs=tuple(vmem_specs(3)),
        scratch_shapes=[pltpu.VMEM((3, rows, cols), jnp.bfloat16)],
        compiler_params=params(16),
        cost_estimate=TINY,
    )(me, *block, gain, held, acc, ss, img, place, text_row, key_ok, w_out)


def out_kernel(away, me_ref, ctx_ref, w_ref, top_ref, bottom_ref):
    half, width = top_ref.shape
    weight = cols_of(w_ref, me_ref[0] ^ away, width)
    for side, out_ref in enumerate((top_ref, bottom_ref)):
        out_ref[...] = jnp.dot(
            ctx_ref[pl.ds(side * half, half)], weight, preferred_element_type=jnp.float32
        ).astype(out_ref.dtype)


def out_part(away, me, ctx, w, width, dtype=jnp.bfloat16):
    rows, depth = ctx.shape
    return pl.pallas_call(
        functools.partial(out_kernel, away),
        out_shape=(
            jax.ShapeDtypeStruct((rows // 2, width), dtype),
            jax.ShapeDtypeStruct((rows // 2, width), dtype),
        ),
        in_specs=[pl.BlockSpec(memory_space=pltpu.SMEM)] + vmem_specs(2),
        out_specs=tuple(vmem_specs(2)),
        compiler_params=params(16),
        cost_estimate=TINY,
    )(me, ctx, w)


def add_kernel(n_top, base_ref, *refs):
    out_ref, tmp_ref, sem_ref = refs[-3:]
    refs = refs[:-3]
    half = base_ref.shape[0] // 2
    copies = []
    for side, terms in enumerate((refs[:n_top], refs[n_top:])):
        part = pl.ds(side * half, half)
        total = terms[0][...].astype(jnp.float32)
        for term in terms[1:]:
            total += term[...].astype(jnp.float32)
        tmp_ref[part] = (base_ref[part].astype(jnp.float32) + total).astype(tmp_ref.dtype)
        copy = pltpu.make_async_copy(tmp_ref.at[part], out_ref.at[part], sem_ref.at[side])
        copy.start()
        copies.append(copy)
    for copy in copies:
        copy.wait()


def add_all(base, top, bottom):
    return pl.pallas_call(
        functools.partial(add_kernel, len(top)),
        out_shape=jax.ShapeDtypeStruct(base.shape, jnp.bfloat16),
        in_specs=vmem_specs(1 + len(top) + len(bottom)),
        out_specs=pl.BlockSpec(memory_space=pl.ANY),
        scratch_shapes=[pltpu.VMEM(base.shape, jnp.bfloat16), pltpu.SemaphoreType.DMA((2,))],
        compiler_params=params(16),
        cost_estimate=TINY,
    )(base, *top, *bottom)


def scatter_terms(parts, n):
    acc = {s: [[parts[s][0]], [parts[s][1]]] for s in range(n)}
    for s in by_bits(n, reverse=True):
        for side, bit in ((0, low_bit(s)), (1, high_bit(s))):
            terms = [t.astype(jnp.float32) for t in acc[s][side]]
            out = functools.reduce(lambda a, b: a + b, terms).astype(jnp.bfloat16)
            acc[s ^ bit][side].append(swap(out, bit))
    return acc[0]


def body(text, patches, grids, image_request, slot_start, vis_gain, dec_gain, w_qkv, w_out):
    n_req = lax.axis_size("req")
    n_ten = lax.axis_size("tensor")
    me_req = lax.axis_index("req")
    me_ten = lax.axis_index("tensor")
    img_dev, side, _, width = patches.shape
    half = side // 2
    region = half * half
    length = text.shape[0]
    w3 = jnp.transpose(w_qkv, (1, 0, 2))
    req_at = me_req.astype(jnp.int32)[None]
    ten_at = me_ten.astype(jnp.int32)[None]
    order = by_bits(n_ten)
    near_at, far = order[:-1], order[-1]

    blocks = near_blocks(text, n_ten)

    outgoing, gains, vis_row = pool_images(
        req_at, image_request, jnp.transpose(patches, (1, 2, 0, 3)), dec_gain, vis_gain, n_req
    )
    received = lax.all_to_all(outgoing, "req", split_axis=0, concat_axis=0, tiled=True)

    n_rows = n_req * region
    n_img = round_up(n_rows + 1, 16)
    own, starts, outgoing = lax.optimization_barrier((text, slot_start, outgoing))
    place, text_row, key_ok = placement(req_at, image_request, starts, grids, n_req, half, length, n_img)
    acc, ss, held = own_part(ten_at, own, gains, w3)
    received, place, acc = lax.optimization_barrier((received, place, acc))

    img_own = pack_images(received, vis_row, region, n_img)
    img_blocks = [img_own] + [swap(img_own, s) for s in range(1, n_ten)]
    handed, img_blocks = lax.optimization_barrier((blocks, img_blocks))
    blocks = {**far_blocks(handed, n_ten), **blocks}

    near = [blocks[s] for s in near_at]
    acc, ss = near_part(near_at, ten_at, near, gains, held, acc, ss)
    img_qkv, merged, w_out = image_part(ten_at, img_blocks, gains, held, w_out, n_rows)
    context, far_top, far_bottom = final_part(
        far, ten_at, blocks[far], gains, held, acc, ss, img_qkv, place, text_row, key_ok, w_out
    )
    img_here = jnp.dot(place, merged, preferred_element_type=jnp.float32)
    x_in = (text.astype(jnp.float32) * text_row[:, :1] + img_here).astype(jnp.bfloat16)

    parts = {far: (far_top, far_bottom)}
    for s in reversed([0] + near_at):
        parts[s] = out_part(s, ten_at, context, w_out, width, jnp.float32 if s == 0 else jnp.bfloat16)
    top, bottom = scatter_terms(parts, n_ten)
    return add_all(x_in, top, bottom)


def solution(mesh):
    in_specs = (
        P("req", "tensor"),
        P("req", None, None, "tensor"),
        P(),
        P(),
        P(),
        P("tensor"),
        P(),
        P(None, None, "tensor"),
        P("tensor", None),
    )
    out_specs = P("req", "tensor")
    return jax.shard_map(body, mesh=mesh, in_specs=in_specs, out_specs=out_specs, check_vma=False)
```

```python
import functools

import jax
import jax.numpy as jnp
from jax import lax
from jax.experimental import pallas as pl
from jax.experimental.pallas import tpu as pltpu
from jax.sharding import PartitionSpec as P

D = 4096
HD = 128
EPS = 1e-05
LOG2E = 1.4426950408889634
TINY = pl.CostEstimate(flops=0, bytes_accessed=0, transcendentals=0)


def round_up(n, m):
    return -(-n // m) * m


def swap(x, s, axis="tensor"):
    n = lax.axis_size(axis)
    return lax.ppermute(x, axis, [(i, i ^ s) for i in range(n)])


def in_hbm(x):
    return pltpu.with_memory_space_constraint(x, pltpu.HBM)


def low_bit(s):
    return s & -s


def high_bit(s):
    return 1 << (s.bit_length() - 1)


def by_bits(n, reverse=False):
    return sorted(range(1, n), key=lambda s: (bin(s).count("1"), s), reverse=reverse)


def halves(block):
    if isinstance(block, tuple):
        return block
    half = block.shape[0] // 2
    return block[:half], block[half:]


def near_blocks(x, n):
    return {s: swap(x, s) for s in by_bits(n) if s & (s - 1) == 0}


def far_blocks(blocks, n):
    blocks = dict(blocks)
    for s in by_bits(n):
        if s not in blocks:
            low, high = low_bit(s), high_bit(s)
            blocks[s] = (swap(halves(blocks[s ^ low])[0], low), swap(halves(blocks[s ^ high])[1], high))
    return blocks


def vmem_specs(n):
    return [pl.BlockSpec(memory_space=pltpu.VMEM)] * n


def params(mib):
    return pltpu.CompilerParams(vmem_limit_bytes=mib * 1024 * 1024)


def fetch(pairs, sem_ref):
    copies = [pltpu.make_async_copy(src, dst, sem_ref.at[i]) for i, (src, dst) in enumerate(pairs)]
    for copy in copies:
        copy.start()
    return copies


def pool_kernel(n_req, me_ref, req_hbm, x_hbm, dec_hbm, vis_hbm, *refs):
    outs, refs = refs[:n_req], refs[n_req:]
    dec_out, vis_out, req_ref, x_ref, dec_ref, vis_ref, tmp_ref, sem_ref = refs
    pairs = ((req_hbm, req_ref), (x_hbm, x_ref), (dec_hbm, dec_ref), (vis_hbm, vis_ref))
    copies = fetch(pairs, sem_ref)
    side, img_dev = x_ref.shape[0], x_ref.shape[2]
    half = side // 2
    me = me_ref[0]
    rows = lax.broadcasted_iota(jnp.int32, (n_req, img_dev), 0)
    cols = lax.broadcasted_iota(jnp.int32, (n_req, img_dev), 1)
    goal = jnp.full((n_req, img_dev), -1, jnp.int32)
    tmp_ref[...] = jnp.zeros_like(tmp_ref)
    copies[0].wait()
    for k in range(img_dev):
        goal = jnp.where(cols == k, req_ref[me * img_dev + k] ^ me, goal)
    onehot = (rows == goal).astype(jnp.bfloat16)
    copies[2].wait()
    copies[3].wait()
    per = vis_ref.shape[0]
    for i in range(per):
        lanes = pl.ds(i * 128, 128)
        vis_out[:, lanes] = vis_ref[i : i + 1, :].astype(jnp.float32)
        for t in range(dec_out.shape[0]):
            at = t * per + i
            dec_out[t, :, lanes] = dec_ref[at : at + 1, :].astype(jnp.float32)
    copies[1].wait()
    for i in range(half):
        for j in range(half):
            total = x_ref[2 * i, 2 * j].astype(jnp.float32)
            for a, b in ((0, 1), (1, 0), (1, 1)):
                total += x_ref[2 * i + a, 2 * j + b].astype(jnp.float32)
            pooled = (total * 0.25).astype(jnp.bfloat16)
            tmp_ref[:, i * half + j, :] = jnp.dot(onehot, pooled, preferred_element_type=jnp.float32)
    for s in range(n_req):
        outs[s][...] = tmp_ref[s].astype(jnp.bfloat16)


def pool_images(me, image_request, patches, dec_gain, vis_gain, n_req):
    side, _, img_dev, width = patches.shape
    padded = round_up((side // 2) ** 2, 16)
    inputs = (image_request, patches, dec_gain.reshape(-1, 128), vis_gain.reshape(-1, 128))
    return pl.pallas_call(
        functools.partial(pool_kernel, n_req),
        out_shape=(jax.ShapeDtypeStruct((padded, width), jnp.bfloat16),) * n_req
        + (
            jax.ShapeDtypeStruct((dec_gain.size // width, 1, width), jnp.float32),
            jax.ShapeDtypeStruct((1, width), jnp.float32),
        ),
        in_specs=[pl.BlockSpec(memory_space=pltpu.SMEM)] + [pl.BlockSpec(memory_space=pltpu.HBM)] * 4,
        out_specs=tuple(vmem_specs(n_req + 2)),
        scratch_shapes=[pltpu.SMEM(image_request.shape, jnp.int32)]
        + [pltpu.VMEM(x.shape, x.dtype) for x in inputs[1:]]
        + [pltpu.VMEM((n_req, padded, width), jnp.float32), pltpu.SemaphoreType.DMA((4,))],
        compiler_params=params(8),
        cost_estimate=TINY,
    )(me, *[in_hbm(x) for x in inputs])


def pack_kernel(region, gain_ref, *refs):
    recs, (out_ref, tmp_ref) = refs[:-2], refs[-2:]
    for r, rec_ref in enumerate(recs):
        tmp_ref[region * r : region * (r + 1)] = rec_ref[...].astype(jnp.float32)[:region]
    done = region * len(recs)
    rest = tmp_ref.shape[0] - done
    tmp_ref[done:] = jnp.broadcast_to(gain_ref[0:1, :], (rest, gain_ref.shape[1]))
    out_ref[...] = tmp_ref[...].astype(jnp.bfloat16)


def pack_images(received, gain, region, n_img):
    width = gain.shape[1]
    return pl.pallas_call(
        functools.partial(pack_kernel, region),
        out_shape=jax.ShapeDtypeStruct((n_img, width), jnp.bfloat16),
        in_specs=vmem_specs(1 + len(received)),
        out_specs=pl.BlockSpec(memory_space=pltpu.VMEM),
        scratch_shapes=[pltpu.VMEM((n_img, width), jnp.float32)],
        compiler_params=params(4),
        cost_estimate=TINY,
    )(gain, *received)


def place_kernel(n_req, half, me_ref, req_hbm, start_hbm, grid_hbm, place_ref, text_row_ref, key_ref, req_ref,
                 start_ref, grid_ref, sem_ref):
    for copy in fetch(((req_hbm, req_ref), (start_hbm, start_ref), (grid_hbm, grid_ref)), sem_ref):
        copy.wait()
    rows, n_img = place_ref.shape
    img_dev = req_ref.shape[0] // n_req
    me = me_ref[0]
    lane = lax.broadcasted_iota(jnp.int32, (1, n_img), 1)

    def one_source(s, carry):
        pos, spot = carry
        source = me ^ s

        def one_image(k, found):
            i = source * img_dev + k
            hit = req_ref[i] == me
            values = (start_ref[i], grid_ref[0, i] // 2, grid_ref[1, i] // 2)
            return tuple(jnp.where(hit, new, old) for new, old in zip(values, found))

        none = jnp.int32(-1)
        start, high, wide = lax.fori_loop(0, img_dev, one_image, (none, none, none), unroll=img_dev <= 8)
        for i in range(half):
            for j in range(half):
                cell = i * half + j
                here = lane == s * half * half + cell
                has = start >= 0
                valid = has & (i < high) & (j < wide)
                pos = jnp.where(here, jnp.where(valid, start + i * wide + j, none), pos)
                spot = jnp.where(here, jnp.where(has, start + cell, none), spot)
        return pos, spot

    empty = jnp.full((1, n_img), -1, jnp.int32)
    pos, spot = lax.fori_loop(0, n_req, one_source, (empty, empty))
    row = lax.broadcasted_iota(jnp.int32, (rows, n_img), 0)
    placed = (row == pos).astype(jnp.float32)
    region = (row == spot).astype(jnp.float32)
    place = placed.astype(jnp.bfloat16)
    place_ref[...] = place
    text_row_ref[...] = jnp.broadcast_to(1.0 - jnp.sum(placed, axis=1, keepdims=True), text_row_ref.shape)
    ones = jnp.ones((8, n_img), jnp.bfloat16)
    open_keys = (placed - region).astype(jnp.bfloat16)
    count = lax.dot_general(ones, open_keys, (((1,), (1,)), ((), ())), preferred_element_type=jnp.float32)
    key_ref[...] = 1.0 + count


def placement(me, image_request, slot_start, grids, n_req, half, rows, n_img):
    inputs = (image_request, slot_start, grids.T)
    return pl.pallas_call(
        functools.partial(place_kernel, n_req, half),
        out_shape=(
            jax.ShapeDtypeStruct((rows, n_img), jnp.bfloat16),
            jax.ShapeDtypeStruct((rows, 128), jnp.float32),
            jax.ShapeDtypeStruct((8, rows), jnp.float32),
        ),
        in_specs=[pl.BlockSpec(memory_space=pltpu.SMEM)] + [pl.BlockSpec(memory_space=pltpu.HBM)] * 3,
        out_specs=tuple(vmem_specs(3)),
        scratch_shapes=[pltpu.SMEM(x.shape, jnp.int32) for x in inputs] + [pltpu.SemaphoreType.DMA((3,))],
        compiler_params=params(8),
        cost_estimate=TINY,
    )(me, *[in_hbm(x) for x in inputs])


def cols_of(ref, owner, width):
    return ref[:, pl.ds(pl.multiple_of(owner * width, width), width)]


def scale_rows(x, gain):
    xf = x.astype(jnp.float32)
    return (xf * gain).astype(jnp.bfloat16), jnp.sum(xf * xf, axis=1, keepdims=True)


def weight_copies(away, me_ref, w_ref, held_ref, sem_ref):
    width = held_ref.shape[2]
    copies = []
    for i, s in enumerate(away):
        rows = pl.ds(pl.multiple_of((me_ref[0] ^ s) * width, width), width)
        copies.append([pltpu.make_async_copy(w_ref.at[j, rows], held_ref.at[i, j], sem_ref.at[i, j]) for j in range(3)])
    return copies


def own_kernel(far, me_ref, x_hbm, gain_ref, w_ref, acc_ref, ss_ref, held_ref, x_ref, x_sem, sem_ref):
    half = x_ref.shape[0] // 2
    x_copy = pltpu.make_async_copy(x_hbm, x_ref, x_sem)
    x_copy.start()
    copies = weight_copies((0, far), me_ref, w_ref, held_ref, sem_ref)
    for copy in copies[0]:
        copy.start()
    x_copy.wait()
    scaled = []
    for side in range(2):
        rows = pl.ds(side * half, half)
        x, total = scale_rows(x_ref[rows], gain_ref[me_ref[0]])
        scaled.append(x)
        ss_ref[rows] = jnp.broadcast_to(total, (half, 128))
    for j in range(3):
        copies[0][j].wait()
        copies[1][j].start()
        for side in range(2):
            acc_ref[j, pl.ds(side * half, half)] = jnp.dot(
                scaled[side], held_ref[0, j], preferred_element_type=jnp.float32
            )
    for copy in copies[1]:
        copy.wait()


def own_part(far, me, x, gain, w):
    rows, width = x.shape
    cols = w.shape[2]
    return pl.pallas_call(
        functools.partial(own_kernel, far),
        out_shape=(
            jax.ShapeDtypeStruct((3, rows, cols), jnp.float32),
            jax.ShapeDtypeStruct((rows, 128), jnp.float32),
            pltpu.VMEM((2, 3, width, cols), w.dtype),
        ),
        in_specs=[
            pl.BlockSpec(memory_space=pltpu.SMEM),
            pl.BlockSpec(memory_space=pltpu.HBM),
            pl.BlockSpec(memory_space=pltpu.VMEM),
            pl.BlockSpec(memory_space=pltpu.HBM),
        ],
        out_specs=tuple(vmem_specs(3)),
        scratch_shapes=[
            pltpu.VMEM(x.shape, x.dtype),
            pltpu.SemaphoreType.DMA,
            pltpu.SemaphoreType.DMA((2, 3)),
        ],
        compiler_params=params(12),
        cost_estimate=TINY,
    )(me, in_hbm(x), gain, in_hbm(w))


def near_kernel(near, pieces, me_ref, *refs):
    n_x = sum(pieces)
    x_refs, refs = list(refs[:n_x]), refs[n_x:]
    gain_ref, acc_in, ss_in, w_ref, acc_ref, ss_ref, held_ref, sem_ref = refs
    half = acc_ref.shape[1] // 2
    copies = weight_copies(near, me_ref, w_ref, held_ref, sem_ref)
    for row in copies:
        row[0].start()
    views = []
    for n in pieces:
        mine, x_refs = x_refs[:n], x_refs[n:]
        views.append([mine[0].at[pl.ds(side * half, half)] if n == 1 else mine[side] for side in range(2)])
    scaled = {}
    for side in range(2):
        rows = pl.ds(side * half, half)
        total = ss_in[rows]
        for b, s in enumerate(near):
            scaled[side, b], part = scale_rows(views[b][side][...], gain_ref[me_ref[0] ^ s])
            total += part
        ss_ref[rows] = total
    for j in range(3):
        for row in copies:
            row[j].wait()
        if j < 2:
            for row in copies:
                row[j + 1].start()
        for side in range(2):
            rows = pl.ds(side * half, half)
            acc = acc_in[j, rows]
            for b in range(len(near)):
                acc += jnp.dot(scaled[side, b], held_ref[b, j], preferred_element_type=jnp.float32)
            acc_ref[j, rows] = acc


def near_part(near, me, blocks, gain, acc, ss, w):
    width, cols = gain.shape[2], w.shape[2]
    blocks = [b if isinstance(b, tuple) else (b,) for b in blocks]
    pieces = [len(b) for b in blocks]
    return pl.pallas_call(
        functools.partial(near_kernel, near, pieces),
        out_shape=(
            jax.ShapeDtypeStruct(acc.shape, jnp.float32),
            jax.ShapeDtypeStruct(ss.shape, jnp.float32),
            pltpu.VMEM((len(near), 3, width, cols), w.dtype),
        ),
        in_specs=[pl.BlockSpec(memory_space=pltpu.SMEM)]
        + vmem_specs(sum(pieces) + 3)
        + [pl.BlockSpec(memory_space=pltpu.HBM)],
        out_specs=tuple(vmem_specs(3)),
        scratch_shapes=[pltpu.SemaphoreType.DMA((len(near), 3))],
        compiler_params=params(12),
        cost_estimate=TINY,
    )(me, *[h for b in blocks for h in b], gain, acc, ss, in_hbm(w))


def image_kernel(n_rows, far, near, me_ref, *refs):
    n_blk = len(near) + 2
    x_refs, refs = refs[:n_blk], refs[n_blk:]
    gain_ref, held_ref, near_ref, w_out_ref, qkv_ref, own_ref, w_out_held, sem_ref = refs
    copy = pltpu.make_async_copy(w_out_ref, w_out_held, sem_ref)
    copy.start()
    total = 0.0
    for s in range(n_blk):
        xf = x_refs[s][...].astype(jnp.float32)
        total += jnp.sum(xf * xf, axis=1, keepdims=True)
    scale = lax.rsqrt(total / D + EPS)
    total = 0.0
    scaled = []
    for s in range(n_blk):
        xf = x_refs[s][...].astype(jnp.float32)
        merged = (xf * scale * xf[n_rows : n_rows + 1]).astype(jnp.bfloat16)
        if s == 0:
            own_ref[...] = merged
        mf = merged.astype(jnp.float32)
        total += jnp.sum(mf * mf, axis=1, keepdims=True)
        scaled.append((mf * gain_ref[me_ref[0] ^ s]).astype(jnp.bfloat16))
    scale = lax.rsqrt(total / D + EPS)
    for j in range(3):
        weights = [(0, held_ref[0, j]), (far, held_ref[1, j])] + [(s, near_ref[i, j]) for i, s in enumerate(near)]
        acc = 0.0
        for s, weight in weights:
            acc += jnp.dot(scaled[s], weight, preferred_element_type=jnp.float32)
        qkv_ref[j] = (acc * scale).astype(jnp.bfloat16)
    copy.wait()


def image_part(far, near, me, blocks, gain, held, near_held, w_out, n_rows):
    n_img, width = blocks[0].shape
    return pl.pallas_call(
        functools.partial(image_kernel, n_rows, far, near),
        out_shape=(
            jax.ShapeDtypeStruct((3, n_img, held.shape[3]), jnp.bfloat16),
            jax.ShapeDtypeStruct((n_img, width), jnp.bfloat16),
            pltpu.VMEM(w_out.shape, w_out.dtype),
        ),
        in_specs=[pl.BlockSpec(memory_space=pltpu.SMEM)]
        + vmem_specs(len(blocks) + 3)
        + [pl.BlockSpec(memory_space=pltpu.HBM)],
        out_specs=tuple(vmem_specs(3)),
        scratch_shapes=[pltpu.SemaphoreType.DMA],
        compiler_params=params(12),
        cost_estimate=TINY,
    )(me, *blocks, gain, held, near_held, in_hbm(w_out))


def final_kernel(far, me_ref, top_ref, bottom_ref, gain_ref, held_ref, acc_ref, ss_ref, img_ref, place_ref, text_row_ref,
                 key_ref, w_out_ref, ctx_ref, far_top_ref, far_bottom_ref, qkv_ref):
    half, width = top_ref.shape
    rows, cols = 2 * half, ctx_ref.shape[1]
    owner = me_ref[0] ^ far
    scaled, scales = [], []
    for side, x_ref in enumerate((top_ref, bottom_ref)):
        part = pl.ds(side * half, half)
        x, total = scale_rows(x_ref[...], gain_ref[owner])
        scaled.append(x)
        total = ss_ref[part] + total
        scales.append((lax.rsqrt(total / D + EPS) * text_row_ref[part])[:, :1])
    for j in range(3):
        weight = held_ref[1, j]
        for side in range(2):
            part = pl.ds(side * half, half)
            prod = jnp.dot(scaled[side], weight, preferred_element_type=jnp.float32)
            put = jnp.dot(place_ref[part], img_ref[j], preferred_element_type=jnp.float32)
            qkv_ref[j, part] = ((prod + acc_ref[j, part]) * scales[side] + put).astype(jnp.bfloat16)
    step = 128
    heads = [pl.ds(h * HD, HD) for h in range(cols // HD)]
    for r in range(rows // step):
        here, last = pl.ds(r * step, step), (r + 1) * step
        row = lax.broadcasted_iota(jnp.int32, (step, last), 0) + r * step
        col = lax.broadcasted_iota(jnp.int32, (step, last), 1)
        bias = jnp.where((row >= col) & (key_ref[0:1, pl.ds(0, last)] > 0.5), 0.0, -1e30)
        scores = [
            lax.dot_general(
                qkv_ref[0, here, lanes],
                qkv_ref[1, pl.ds(0, last), lanes],
                (((1,), (1,)), ((), ())),
                preferred_element_type=jnp.float32,
            )
            for lanes in heads
        ]
        scores = [x * (LOG2E / HD**0.5) + bias for x in scores]
        tops = [jnp.max(x, axis=1, keepdims=True) for x in scores]
        expo = [jnp.exp2(x - top) for x, top in zip(scores, tops)]
        sums = [jnp.sum(x, axis=1, keepdims=True) for x in expo]
        outs = [
            jnp.dot(x.astype(jnp.bfloat16), qkv_ref[2, pl.ds(0, last), lanes], preferred_element_type=jnp.float32)
            for x, lanes in zip(expo, heads)
        ]
        for lanes, out, total in zip(heads, outs, sums):
            ctx_ref[here, lanes] = (out / total).astype(jnp.bfloat16)
    weight = cols_of(w_out_ref, owner, width)
    for side, out_ref in enumerate((far_top_ref, far_bottom_ref)):
        out_ref[...] = jnp.dot(
            ctx_ref[pl.ds(side * half, half)], weight, preferred_element_type=jnp.float32
        ).astype(jnp.bfloat16)


def final_part(far, me, block, gain, held, acc, ss, img, place, text_row, key_ok, w_out):
    half, width = block[0].shape
    rows, cols = 2 * half, held.shape[3]
    return pl.pallas_call(
        functools.partial(final_kernel, far),
        out_shape=(
            jax.ShapeDtypeStruct((rows, cols), jnp.bfloat16),
            jax.ShapeDtypeStruct((half, width), jnp.bfloat16),
            jax.ShapeDtypeStruct((half, width), jnp.bfloat16),
        ),
        in_specs=[pl.BlockSpec(memory_space=pltpu.SMEM)]
        + vmem_specs(11),
        out_specs=tuple(vmem_specs(3)),
        scratch_shapes=[pltpu.VMEM((3, rows, cols), jnp.bfloat16)],
        compiler_params=params(12),
        cost_estimate=TINY,
    )(me, *block, gain, held, acc, ss, img, place, text_row, key_ok, w_out)


def out_kernel(away, me_ref, ctx_ref, w_ref, top_ref, bottom_ref):
    half, width = top_ref.shape
    weight = cols_of(w_ref, me_ref[0] ^ away, width)
    for side, out_ref in enumerate((top_ref, bottom_ref)):
        out_ref[...] = jnp.dot(
            ctx_ref[pl.ds(side * half, half)], weight, preferred_element_type=jnp.float32
        ).astype(out_ref.dtype)


def out_part(away, me, ctx, w, width, dtype=jnp.bfloat16):
    rows, depth = ctx.shape
    return pl.pallas_call(
        functools.partial(out_kernel, away),
        out_shape=(
            jax.ShapeDtypeStruct((rows // 2, width), dtype),
            jax.ShapeDtypeStruct((rows // 2, width), dtype),
        ),
        in_specs=[pl.BlockSpec(memory_space=pltpu.SMEM)] + vmem_specs(2),
        out_specs=tuple(vmem_specs(2)),
        compiler_params=params(12),
        cost_estimate=TINY,
    )(me, ctx, w)


def add_kernel(n_top, base_ref, *refs):
    out_ref, tmp_ref, sem_ref = refs[-3:]
    refs = refs[:-3]
    half = base_ref.shape[0] // 2
    copies = []
    for side, terms in enumerate((refs[:n_top], refs[n_top:])):
        part = pl.ds(side * half, half)
        total = terms[0][...].astype(jnp.float32)
        for term in terms[1:]:
            total += term[...].astype(jnp.float32)
        tmp_ref[part] = (base_ref[part].astype(jnp.float32) + total).astype(tmp_ref.dtype)
        copy = pltpu.make_async_copy(tmp_ref.at[part], out_ref.at[part], sem_ref.at[side])
        copy.start()
        copies.append(copy)
    for copy in copies:
        copy.wait()


def add_all(base, top, bottom):
    return pl.pallas_call(
        functools.partial(add_kernel, len(top)),
        out_shape=jax.ShapeDtypeStruct(base.shape, jnp.bfloat16),
        in_specs=vmem_specs(1 + len(top) + len(bottom)),
        out_specs=pl.BlockSpec(memory_space=pl.ANY),
        scratch_shapes=[pltpu.VMEM(base.shape, jnp.bfloat16), pltpu.SemaphoreType.DMA((2,))],
        compiler_params=params(12),
        cost_estimate=TINY,
    )(base, *top, *bottom)


def scatter_terms(parts, n):
    acc = {s: [[parts[s][0]], [parts[s][1]]] for s in range(n)}
    for s in by_bits(n, reverse=True):
        for side, bit in ((0, low_bit(s)), (1, high_bit(s))):
            terms = [t.astype(jnp.float32) for t in acc[s][side]]
            out = functools.reduce(lambda a, b: a + b, terms).astype(jnp.bfloat16)
            acc[s ^ bit][side].append(swap(out, bit))
    return acc[0]


def body(text, patches, grids, image_request, slot_start, vis_gain, dec_gain, w_qkv, w_out):
    n_req = lax.axis_size("req")
    n_ten = lax.axis_size("tensor")
    me_req = lax.axis_index("req")
    me_ten = lax.axis_index("tensor")
    img_dev, side, _, width = patches.shape
    half = side // 2
    region = half * half
    length = text.shape[0]
    w3 = jnp.transpose(w_qkv, (1, 0, 2))
    req_at = me_req.astype(jnp.int32)[None]
    ten_at = me_ten.astype(jnp.int32)[None]
    order = by_bits(n_ten)
    near_at, far = order[:-1], order[-1]

    blocks = near_blocks(text, n_ten)

    *outgoing, gains, vis_row = pool_images(
        req_at, image_request, jnp.transpose(patches, (1, 2, 0, 3)), dec_gain, vis_gain, n_req
    )
    received = [outgoing[0]] + [swap(outgoing[s], s, "req") for s in range(1, n_req)]

    n_rows = n_req * region
    n_img = round_up(n_rows + 1, 16)
    img_own = pack_images(received, vis_row, region, n_img)
    img_blocks = [img_own] + [swap(img_own, s) for s in range(1, n_ten)]
    own, img_own = lax.optimization_barrier((text, img_own))
    acc, ss, held = own_part(far, ten_at, own, gains, w3)
    handed, img_blocks, acc = lax.optimization_barrier((blocks, img_blocks, acc))
    blocks = {**far_blocks(handed, n_ten), **blocks}

    near = [blocks[s] for s in near_at]
    acc, ss, near_held = near_part(near_at, ten_at, near, gains, acc, ss, w3)
    starts, acc = lax.optimization_barrier((slot_start, acc))
    place, text_row, key_ok = placement(req_at, image_request, starts, grids, n_req, half, length, n_img)
    img_qkv, merged, w_out = image_part(far, near_at, ten_at, img_blocks, gains, held, near_held, w_out, n_rows)
    context, far_top, far_bottom = final_part(
        far, ten_at, blocks[far], gains, held, acc, ss, img_qkv, place, text_row, key_ok, w_out
    )
    img_here = jnp.dot(place, merged, preferred_element_type=jnp.float32)
    x_in = (text.astype(jnp.float32) * text_row[:, :1] + img_here).astype(jnp.bfloat16)

    parts = {far: (far_top, far_bottom)}
    for s in reversed([0] + near_at):
        parts[s] = out_part(s, ten_at, context, w_out, width, jnp.float32 if s == 0 else jnp.bfloat16)
    top, bottom = scatter_terms(parts, n_ten)
    return add_all(x_in, top, bottom)


def solution(mesh):
    in_specs = (
        P("req", "tensor"),
        P("req", None, None, "tensor"),
        P(),
        P(),
        P(),
        P("tensor"),
        P(),
        P(None, None, "tensor"),
        P("tensor", None),
    )
    out_specs = P("req", "tensor")
    return jax.shard_map(body, mesh=mesh, in_specs=in_specs, out_specs=out_specs, check_vma=False)
```

```python
import functools

import jax
import jax.numpy as jnp
from jax import lax
from jax.experimental import pallas as pl
from jax.experimental.pallas import tpu as pltpu
from jax.sharding import PartitionSpec as P

D = 4096
HD = 128
EPS = 1e-05
LOG2E = 1.4426950408889634
TINY = pl.CostEstimate(flops=0, bytes_accessed=0, transcendentals=0)


def round_up(n, m):
    return -(-n // m) * m


def swap(x, s, axis="tensor"):
    n = lax.axis_size(axis)
    return lax.ppermute(x, axis, [(i, i ^ s) for i in range(n)])


def in_hbm(x):
    return pltpu.with_memory_space_constraint(x, pltpu.HBM)


def low_bit(s):
    return s & -s


def high_bit(s):
    return 1 << (s.bit_length() - 1)


def by_bits(n, reverse=False):
    return sorted(range(1, n), key=lambda s: (bin(s).count("1"), s), reverse=reverse)


def halves(block):
    if isinstance(block, tuple):
        return block
    half = block.shape[0] // 2
    return block[:half], block[half:]


def near_blocks(x, n):
    return {s: swap(x, s) for s in by_bits(n) if s & (s - 1) == 0}


def far_blocks(blocks, n):
    blocks = dict(blocks)
    for s in by_bits(n):
        if s not in blocks:
            low, high = low_bit(s), high_bit(s)
            blocks[s] = (swap(halves(blocks[s ^ low])[0], low), swap(halves(blocks[s ^ high])[1], high))
    return blocks


def vmem_specs(n):
    return [pl.BlockSpec(memory_space=pltpu.VMEM)] * n


def params(mib):
    return pltpu.CompilerParams(vmem_limit_bytes=mib * 1024 * 1024)


def fetch(pairs, sem_ref):
    copies = [pltpu.make_async_copy(src, dst, sem_ref.at[i]) for i, (src, dst) in enumerate(pairs)]
    for copy in copies:
        copy.start()
    return copies


def pool_kernel(n_req, me_ref, req_hbm, x_hbm, dec_hbm, vis_hbm, *refs):
    outs, refs = refs[:n_req], refs[n_req:]
    dec_out, vis_out, req_ref, x_ref, dec_ref, vis_ref, tmp_ref, sem_ref = refs
    pairs = ((req_hbm, req_ref), (x_hbm, x_ref), (dec_hbm, dec_ref), (vis_hbm, vis_ref))
    copies = fetch(pairs, sem_ref)
    side, img_dev = x_ref.shape[0], x_ref.shape[2]
    half = side // 2
    me = me_ref[0]
    rows = lax.broadcasted_iota(jnp.int32, (n_req, img_dev), 0)
    cols = lax.broadcasted_iota(jnp.int32, (n_req, img_dev), 1)
    goal = jnp.full((n_req, img_dev), -1, jnp.int32)
    tmp_ref[...] = jnp.zeros_like(tmp_ref)
    copies[0].wait()
    for k in range(img_dev):
        goal = jnp.where(cols == k, req_ref[me * img_dev + k] ^ me, goal)
    onehot = (rows == goal).astype(jnp.bfloat16)
    copies[2].wait()
    copies[3].wait()
    per = vis_ref.shape[0]
    for i in range(per):
        lanes = pl.ds(i * 128, 128)
        vis_out[:, lanes] = vis_ref[i : i + 1, :].astype(jnp.float32)
        for t in range(dec_out.shape[0]):
            at = t * per + i
            dec_out[t, :, lanes] = dec_ref[at : at + 1, :].astype(jnp.float32)
    copies[1].wait()
    for i in range(half):
        for j in range(half):
            total = x_ref[2 * i, 2 * j].astype(jnp.float32)
            for a, b in ((0, 1), (1, 0), (1, 1)):
                total += x_ref[2 * i + a, 2 * j + b].astype(jnp.float32)
            pooled = (total * 0.25).astype(jnp.bfloat16)
            tmp_ref[:, i * half + j, :] = jnp.dot(onehot, pooled, preferred_element_type=jnp.float32)
    for s in range(n_req):
        outs[s][...] = tmp_ref[s].astype(jnp.bfloat16)


def pool_images(me, image_request, patches, dec_gain, vis_gain, n_req):
    side, _, img_dev, width = patches.shape
    padded = round_up((side // 2) ** 2, 16)
    inputs = (image_request, patches, dec_gain.reshape(-1, 128), vis_gain.reshape(-1, 128))
    return pl.pallas_call(
        functools.partial(pool_kernel, n_req),
        out_shape=(jax.ShapeDtypeStruct((padded, width), jnp.bfloat16),) * n_req
        + (
            jax.ShapeDtypeStruct((dec_gain.size // width, 1, width), jnp.float32),
            jax.ShapeDtypeStruct((1, width), jnp.float32),
        ),
        in_specs=[pl.BlockSpec(memory_space=pltpu.SMEM)] + [pl.BlockSpec(memory_space=pltpu.HBM)] * 4,
        out_specs=tuple(vmem_specs(n_req + 2)),
        scratch_shapes=[pltpu.SMEM(image_request.shape, jnp.int32)]
        + [pltpu.VMEM(x.shape, x.dtype) for x in inputs[1:]]
        + [pltpu.VMEM((n_req, padded, width), jnp.float32), pltpu.SemaphoreType.DMA((4,))],
        compiler_params=params(8),
        cost_estimate=TINY,
    )(me, *[in_hbm(x) for x in inputs])


def pack_kernel(region, gain_ref, *refs):
    recs, (out_ref, tmp_ref) = refs[:-2], refs[-2:]
    for r, rec_ref in enumerate(recs):
        tmp_ref[region * r : region * (r + 1)] = rec_ref[...].astype(jnp.float32)[:region]
    done = region * len(recs)
    rest = tmp_ref.shape[0] - done
    tmp_ref[done:] = jnp.broadcast_to(gain_ref[0:1, :], (rest, gain_ref.shape[1]))
    out_ref[...] = tmp_ref[...].astype(jnp.bfloat16)


def pack_images(received, gain, region, n_img):
    width = gain.shape[1]
    return pl.pallas_call(
        functools.partial(pack_kernel, region),
        out_shape=jax.ShapeDtypeStruct((n_img, width), jnp.bfloat16),
        in_specs=vmem_specs(1 + len(received)),
        out_specs=pl.BlockSpec(memory_space=pltpu.VMEM),
        scratch_shapes=[pltpu.VMEM((n_img, width), jnp.float32)],
        compiler_params=params(4),
        cost_estimate=TINY,
    )(gain, *received)


def place_kernel(n_req, half, me_ref, req_hbm, start_hbm, grid_hbm, place_ref, text_row_ref, key_ref, req_ref,
                 start_ref, grid_ref, sem_ref):
    for copy in fetch(((req_hbm, req_ref), (start_hbm, start_ref), (grid_hbm, grid_ref)), sem_ref):
        copy.wait()
    rows, n_img = place_ref.shape
    img_dev = req_ref.shape[0] // n_req
    me = me_ref[0]
    lane = lax.broadcasted_iota(jnp.int32, (1, n_img), 1)

    def one_source(s, carry):
        pos, spot = carry
        source = me ^ s

        def one_image(k, found):
            i = source * img_dev + k
            hit = req_ref[i] == me
            values = (start_ref[i], grid_ref[0, i] // 2, grid_ref[1, i] // 2)
            return tuple(jnp.where(hit, new, old) for new, old in zip(values, found))

        none = jnp.int32(-1)
        start, high, wide = lax.fori_loop(0, img_dev, one_image, (none, none, none), unroll=img_dev <= 8)
        for i in range(half):
            for j in range(half):
                cell = i * half + j
                here = lane == s * half * half + cell
                has = start >= 0
                valid = has & (i < high) & (j < wide)
                pos = jnp.where(here, jnp.where(valid, start + i * wide + j, none), pos)
                spot = jnp.where(here, jnp.where(has, start + cell, none), spot)
        return pos, spot

    empty = jnp.full((1, n_img), -1, jnp.int32)
    pos, spot = lax.fori_loop(0, n_req, one_source, (empty, empty))
    row = lax.broadcasted_iota(jnp.int32, (rows, n_img), 0)
    placed = (row == pos).astype(jnp.float32)
    region = (row == spot).astype(jnp.float32)
    place = placed.astype(jnp.bfloat16)
    place_ref[...] = place
    text_row_ref[...] = jnp.broadcast_to(1.0 - jnp.sum(placed, axis=1, keepdims=True), text_row_ref.shape)
    ones = jnp.ones((8, n_img), jnp.bfloat16)
    open_keys = (placed - region).astype(jnp.bfloat16)
    count = lax.dot_general(ones, open_keys, (((1,), (1,)), ((), ())), preferred_element_type=jnp.float32)
    key_ref[...] = 1.0 + count


def placement(me, image_request, slot_start, grids, n_req, half, rows, n_img):
    inputs = (image_request, slot_start, grids.T)
    return pl.pallas_call(
        functools.partial(place_kernel, n_req, half),
        out_shape=(
            jax.ShapeDtypeStruct((rows, n_img), jnp.bfloat16),
            jax.ShapeDtypeStruct((rows, 128), jnp.float32),
            jax.ShapeDtypeStruct((8, rows), jnp.float32),
        ),
        in_specs=[pl.BlockSpec(memory_space=pltpu.SMEM)] + [pl.BlockSpec(memory_space=pltpu.HBM)] * 3,
        out_specs=tuple(vmem_specs(3)),
        scratch_shapes=[pltpu.SMEM(x.shape, jnp.int32) for x in inputs] + [pltpu.SemaphoreType.DMA((3,))],
        compiler_params=params(8),
        cost_estimate=TINY,
    )(me, *[in_hbm(x) for x in inputs])


def cols_of(ref, owner, width):
    return ref[:, pl.ds(pl.multiple_of(owner * width, width), width)]


def scale_rows(x, gain):
    xf = x.astype(jnp.float32)
    return (xf * gain).astype(jnp.bfloat16), jnp.sum(xf * xf, axis=1, keepdims=True)


def own_kernel(me_ref, x_hbm, gain_ref, w_ref, acc_ref, ss_ref, held_ref, x_ref, x_sem, sem_ref):
    n_ten, _, width, _ = held_ref.shape
    half = x_ref.shape[0] // 2
    x_copy = pltpu.make_async_copy(x_hbm, x_ref, x_sem)
    x_copy.start()
    copies = []
    for s in range(n_ten):
        rows = pl.ds(pl.multiple_of((me_ref[0] ^ s) * width, width), width)
        copies += [pltpu.make_async_copy(w_ref.at[j, rows], held_ref.at[s, j], sem_ref.at[s, j]) for j in range(3)]
    for copy in copies:
        copy.start()
    x_copy.wait()
    scaled = []
    for side in range(2):
        rows = pl.ds(side * half, half)
        x, total = scale_rows(x_ref[rows], gain_ref[me_ref[0]])
        scaled.append(x)
        ss_ref[rows] = jnp.broadcast_to(total, (half, 128))
    for j in range(3):
        copies[j].wait()
        for side in range(2):
            acc_ref[j, pl.ds(side * half, half)] = jnp.dot(
                scaled[side], held_ref[0, j], preferred_element_type=jnp.float32
            )
    for copy in copies[3:]:
        copy.wait()


def own_part(me, x, gain, w):
    rows, width = x.shape
    n_ten, cols = gain.shape[0], w.shape[2]
    return pl.pallas_call(
        own_kernel,
        out_shape=(
            jax.ShapeDtypeStruct((3, rows, cols), jnp.float32),
            jax.ShapeDtypeStruct((rows, 128), jnp.float32),
            pltpu.VMEM((n_ten, 3, width, cols), w.dtype),
        ),
        in_specs=[
            pl.BlockSpec(memory_space=pltpu.SMEM),
            pl.BlockSpec(memory_space=pltpu.HBM),
            pl.BlockSpec(memory_space=pltpu.VMEM),
            pl.BlockSpec(memory_space=pltpu.HBM),
        ],
        out_specs=tuple(vmem_specs(3)),
        scratch_shapes=[
            pltpu.VMEM(x.shape, x.dtype),
            pltpu.SemaphoreType.DMA,
            pltpu.SemaphoreType.DMA((n_ten, 3)),
        ],
        compiler_params=params(12),
        cost_estimate=TINY,
    )(me, in_hbm(x), gain, in_hbm(w))


def near_kernel(near, pieces, me_ref, *refs):
    n_x = sum(pieces)
    x_refs, refs = list(refs[:n_x]), refs[n_x:]
    gain_ref, held_ref, acc_in, ss_in, acc_ref, ss_ref = refs
    half = acc_ref.shape[1] // 2
    views = []
    for n in pieces:
        mine, x_refs = x_refs[:n], x_refs[n:]
        views.append([mine[0].at[pl.ds(side * half, half)] if n == 1 else mine[side] for side in range(2)])
    scaled = {}
    for side in range(2):
        rows = pl.ds(side * half, half)
        total = ss_in[rows]
        for b, s in enumerate(near):
            scaled[side, b], part = scale_rows(views[b][side][...], gain_ref[me_ref[0] ^ s])
            total += part
        ss_ref[rows] = total
    for j in range(3):
        for side in range(2):
            rows = pl.ds(side * half, half)
            acc = acc_in[j, rows]
            for b, s in enumerate(near):
                acc += jnp.dot(scaled[side, b], held_ref[s, j], preferred_element_type=jnp.float32)
            acc_ref[j, rows] = acc


def near_part(near, me, blocks, gain, held, acc, ss):
    blocks = [b if isinstance(b, tuple) else (b,) for b in blocks]
    pieces = [len(b) for b in blocks]
    return pl.pallas_call(
        functools.partial(near_kernel, near, pieces),
        out_shape=(
            jax.ShapeDtypeStruct(acc.shape, jnp.float32),
            jax.ShapeDtypeStruct(ss.shape, jnp.float32),
        ),
        in_specs=[pl.BlockSpec(memory_space=pltpu.SMEM)]
        + vmem_specs(sum(pieces) + 4),
        out_specs=tuple(vmem_specs(2)),
        compiler_params=params(12),
        cost_estimate=TINY,
    )(me, *[h for b in blocks for h in b], gain, held, acc, ss)


def image_kernel(n_rows, n_blk, me_ref, *refs):
    x_refs, refs = refs[:n_blk], refs[n_blk:]
    gain_ref, held_ref, w_out_ref, qkv_ref, own_ref, w_out_held, sem_ref = refs
    copy = pltpu.make_async_copy(w_out_ref, w_out_held, sem_ref)
    copy.start()
    total = 0.0
    for s in range(n_blk):
        xf = x_refs[s][...].astype(jnp.float32)
        total += jnp.sum(xf * xf, axis=1, keepdims=True)
    scale = lax.rsqrt(total / D + EPS)
    total = 0.0
    scaled = []
    for s in range(n_blk):
        xf = x_refs[s][...].astype(jnp.float32)
        merged = (xf * scale * xf[n_rows : n_rows + 1]).astype(jnp.bfloat16)
        if s == 0:
            own_ref[...] = merged
        mf = merged.astype(jnp.float32)
        total += jnp.sum(mf * mf, axis=1, keepdims=True)
        scaled.append((mf * gain_ref[me_ref[0] ^ s]).astype(jnp.bfloat16))
    scale = lax.rsqrt(total / D + EPS)
    for j in range(3):
        acc = 0.0
        for s in range(n_blk):
            acc += jnp.dot(scaled[s], held_ref[s, j], preferred_element_type=jnp.float32)
        qkv_ref[j] = (acc * scale).astype(jnp.bfloat16)
    copy.wait()


def image_part(me, blocks, gain, held, w_out, n_rows):
    n_img, width = blocks[0].shape
    return pl.pallas_call(
        functools.partial(image_kernel, n_rows, len(blocks)),
        out_shape=(
            jax.ShapeDtypeStruct((3, n_img, held.shape[3]), jnp.bfloat16),
            jax.ShapeDtypeStruct((n_img, width), jnp.bfloat16),
            pltpu.VMEM(w_out.shape, w_out.dtype),
        ),
        in_specs=[pl.BlockSpec(memory_space=pltpu.SMEM)]
        + vmem_specs(len(blocks) + 2)
        + [pl.BlockSpec(memory_space=pltpu.HBM)],
        out_specs=tuple(vmem_specs(3)),
        scratch_shapes=[pltpu.SemaphoreType.DMA],
        compiler_params=params(12),
        cost_estimate=TINY,
    )(me, *blocks, gain, held, in_hbm(w_out))


def final_kernel(far, me_ref, top_ref, bottom_ref, gain_ref, held_ref, acc_ref, ss_ref, img_ref, place_ref, text_row_ref,
                 key_ref, w_out_ref, ctx_ref, far_top_ref, far_bottom_ref, qkv_ref):
    half, width = top_ref.shape
    rows, cols = 2 * half, ctx_ref.shape[1]
    owner = me_ref[0] ^ far
    scaled, scales = [], []
    for side, x_ref in enumerate((top_ref, bottom_ref)):
        part = pl.ds(side * half, half)
        x, total = scale_rows(x_ref[...], gain_ref[owner])
        scaled.append(x)
        total = ss_ref[part] + total
        scales.append((lax.rsqrt(total / D + EPS) * text_row_ref[part])[:, :1])
    for j in range(3):
        weight = held_ref[far, j]
        for side in range(2):
            part = pl.ds(side * half, half)
            prod = jnp.dot(scaled[side], weight, preferred_element_type=jnp.float32)
            put = jnp.dot(place_ref[part], img_ref[j], preferred_element_type=jnp.float32)
            qkv_ref[j, part] = ((prod + acc_ref[j, part]) * scales[side] + put).astype(jnp.bfloat16)
    step = 128
    heads = [pl.ds(h * HD, HD) for h in range(cols // HD)]
    for r in range(rows // step):
        here, last = pl.ds(r * step, step), (r + 1) * step
        row = lax.broadcasted_iota(jnp.int32, (step, last), 0) + r * step
        col = lax.broadcasted_iota(jnp.int32, (step, last), 1)
        bias = jnp.where((row >= col) & (key_ref[0:1, pl.ds(0, last)] > 0.5), 0.0, -1e30)
        scores = [
            lax.dot_general(
                qkv_ref[0, here, lanes],
                qkv_ref[1, pl.ds(0, last), lanes],
                (((1,), (1,)), ((), ())),
                preferred_element_type=jnp.float32,
            )
            for lanes in heads
        ]
        scores = [x * (LOG2E / HD**0.5) + bias for x in scores]
        tops = [jnp.max(x, axis=1, keepdims=True) for x in scores]
        expo = [jnp.exp2(x - top) for x, top in zip(scores, tops)]
        sums = [jnp.sum(x, axis=1, keepdims=True) for x in expo]
        outs = [
            jnp.dot(x.astype(jnp.bfloat16), qkv_ref[2, pl.ds(0, last), lanes], preferred_element_type=jnp.float32)
            for x, lanes in zip(expo, heads)
        ]
        for lanes, out, total in zip(heads, outs, sums):
            ctx_ref[here, lanes] = (out / total).astype(jnp.bfloat16)
    weight = cols_of(w_out_ref, owner, width)
    for side, out_ref in enumerate((far_top_ref, far_bottom_ref)):
        out_ref[...] = jnp.dot(
            ctx_ref[pl.ds(side * half, half)], weight, preferred_element_type=jnp.float32
        ).astype(jnp.bfloat16)


def final_part(far, me, block, gain, held, acc, ss, img, place, text_row, key_ok, w_out):
    half, width = block[0].shape
    rows, cols = 2 * half, held.shape[3]
    return pl.pallas_call(
        functools.partial(final_kernel, far),
        out_shape=(
            jax.ShapeDtypeStruct((rows, cols), jnp.bfloat16),
            jax.ShapeDtypeStruct((half, width), jnp.bfloat16),
            jax.ShapeDtypeStruct((half, width), jnp.bfloat16),
        ),
        in_specs=[pl.BlockSpec(memory_space=pltpu.SMEM)]
        + vmem_specs(11),
        out_specs=tuple(vmem_specs(3)),
        scratch_shapes=[pltpu.VMEM((3, rows, cols), jnp.bfloat16)],
        compiler_params=params(12),
        cost_estimate=TINY,
    )(me, *block, gain, held, acc, ss, img, place, text_row, key_ok, w_out)


def out_kernel(away, me_ref, ctx_ref, w_ref, top_ref, bottom_ref):
    half, width = top_ref.shape
    weight = cols_of(w_ref, me_ref[0] ^ away, width)
    for side, out_ref in enumerate((top_ref, bottom_ref)):
        out_ref[...] = jnp.dot(
            ctx_ref[pl.ds(side * half, half)], weight, preferred_element_type=jnp.float32
        ).astype(out_ref.dtype)


def out_part(away, me, ctx, w, width, dtype=jnp.bfloat16):
    rows, depth = ctx.shape
    return pl.pallas_call(
        functools.partial(out_kernel, away),
        out_shape=(
            jax.ShapeDtypeStruct((rows // 2, width), dtype),
            jax.ShapeDtypeStruct((rows // 2, width), dtype),
        ),
        in_specs=[pl.BlockSpec(memory_space=pltpu.SMEM)] + vmem_specs(2),
        out_specs=tuple(vmem_specs(2)),
        compiler_params=params(12),
        cost_estimate=TINY,
    )(me, ctx, w)


def sum_of(refs, part=slice(None)):
    return functools.reduce(lambda a, b: a + b, [ref[part].astype(jnp.float32) for ref in refs])


def first_kernel(n_top, base_ref, *refs):
    out_ref = refs[-1]
    half = base_ref.shape[0] // 2
    for side, terms in enumerate((refs[:n_top], refs[n_top:-1])):
        part = pl.ds(side * half, half)
        out_ref[part] = base_ref[part].astype(jnp.float32) + sum_of(terms)


def add_first(base, top, bottom):
    return pl.pallas_call(
        functools.partial(first_kernel, len(top)),
        out_shape=jax.ShapeDtypeStruct(base.shape, jnp.float32),
        in_specs=vmem_specs(1 + len(top) + len(bottom)),
        out_specs=pl.BlockSpec(memory_space=pltpu.VMEM),
        compiler_params=params(12),
        cost_estimate=TINY,
    )(base, *top, *bottom)


def last_kernel(n_top, base_ref, *refs):
    refs, (out_ref, tmp_ref, sem_ref) = refs[:-3], refs[-3:]
    half = base_ref.shape[0] // 2
    step = half // 2
    copies = []
    for side, terms in enumerate((refs[:n_top], refs[n_top:])):
        for i in range(2):
            part = pl.ds(side * half + i * step, step)
            total = base_ref[part] + sum_of(terms, pl.ds(i * step, step))
            tmp_ref[part] = total.astype(tmp_ref.dtype)
            copy = pltpu.make_async_copy(tmp_ref.at[part], out_ref.at[part], sem_ref.at[side, i])
            copy.start()
            copies.append(copy)
    for copy in copies:
        copy.wait()


def add_last(base, top, bottom):
    return pl.pallas_call(
        functools.partial(last_kernel, len(top)),
        out_shape=jax.ShapeDtypeStruct(base.shape, jnp.bfloat16),
        in_specs=vmem_specs(1 + len(top) + len(bottom)),
        out_specs=pl.BlockSpec(memory_space=pl.ANY),
        scratch_shapes=[pltpu.VMEM(base.shape, jnp.bfloat16), pltpu.SemaphoreType.DMA((2, 2))],
        compiler_params=params(12),
        cost_estimate=TINY,
    )(base, *top, *bottom)


def scatter_terms(parts, n):
    acc = {s: [[parts[s][0]], [parts[s][1]]] for s in range(n)}
    early, late = [[], []], [[], []]
    for s in by_bits(n, reverse=True):
        for side, bit in ((0, low_bit(s)), (1, high_bit(s))):
            terms = [t.astype(jnp.float32) for t in acc[s][side]]
            out = swap(functools.reduce(lambda a, b: a + b, terms).astype(jnp.bfloat16), bit)
            if s == bit:
                (early if len(terms) == 1 else late)[side].append(out)
            else:
                acc[s ^ bit][side].append(out)
    return early, late


def body(text, patches, grids, image_request, slot_start, vis_gain, dec_gain, w_qkv, w_out):
    n_req = lax.axis_size("req")
    n_ten = lax.axis_size("tensor")
    me_req = lax.axis_index("req")
    me_ten = lax.axis_index("tensor")
    img_dev, side, _, width = patches.shape
    half = side // 2
    region = half * half
    length = text.shape[0]
    w3 = jnp.transpose(w_qkv, (1, 0, 2))
    req_at = me_req.astype(jnp.int32)[None]
    ten_at = me_ten.astype(jnp.int32)[None]
    order = by_bits(n_ten)
    near_at, far = order[:-1], order[-1]

    blocks = near_blocks(text, n_ten)

    *outgoing, gains, vis_row = pool_images(
        req_at, image_request, jnp.transpose(patches, (1, 2, 0, 3)), dec_gain, vis_gain, n_req
    )
    received = [outgoing[0]] + [swap(outgoing[s], s, "req") for s in range(1, n_req)]

    n_rows = n_req * region
    n_img = round_up(n_rows + 1, 16)
    img_own = pack_images(received, vis_row, region, n_img)
    img_blocks = [img_own] + [swap(img_own, s) for s in range(1, n_ten)]
    own, img_own = lax.optimization_barrier((text, img_own))
    acc, ss, held = own_part(ten_at, own, gains, w3)
    starts, acc = lax.optimization_barrier((slot_start, acc))
    place, text_row, key_ok = placement(req_at, image_request, starts, grids, n_req, half, length, n_img)
    handed, img_blocks, place = lax.optimization_barrier((blocks, img_blocks, place))
    blocks = {**far_blocks(handed, n_ten), **blocks}

    near = [blocks[s] for s in near_at]
    acc, ss = near_part(near_at, ten_at, near, gains, held, acc, ss)
    img_qkv, merged, w_out = image_part(ten_at, img_blocks, gains, held, w_out, n_rows)
    context, far_top, far_bottom = final_part(
        far, ten_at, blocks[far], gains, held, acc, ss, img_qkv, place, text_row, key_ok, w_out
    )
    img_here = jnp.dot(place, merged, preferred_element_type=jnp.float32)
    x_in = (text.astype(jnp.float32) * text_row[:, :1] + img_here).astype(jnp.bfloat16)

    parts = {far: (far_top, far_bottom)}
    for s in reversed([0] + near_at):
        parts[s] = out_part(s, ten_at, context, w_out, width, jnp.float32 if s == 0 else jnp.bfloat16)
    early, late = scatter_terms(parts, n_ten)
    base = add_first(x_in, [parts[0][0]] + early[0], [parts[0][1]] + early[1])
    return add_last(base, late[0], late[1])


def solution(mesh):
    in_specs = (
        P("req", "tensor"),
        P("req", None, None, "tensor"),
        P(),
        P(),
        P(),
        P("tensor"),
        P(),
        P(None, None, "tensor"),
        P("tensor", None),
    )
    out_specs = P("req", "tensor")
    return jax.shard_map(body, mesh=mesh, in_specs=in_specs, out_specs=out_specs, check_vma=False)
```

```python
import functools

import jax
import jax.numpy as jnp
from jax import lax
from jax.experimental import pallas as pl
from jax.experimental.pallas import tpu as pltpu
from jax.sharding import PartitionSpec as P

D = 4096
HD = 128
EPS = 1e-05
LOG2E = 1.4426950408889634
TINY = pl.CostEstimate(flops=0, bytes_accessed=0, transcendentals=0)


def round_up(n, m):
    return -(-n // m) * m


def swap(x, s, axis="tensor"):
    n = lax.axis_size(axis)
    return lax.ppermute(x, axis, [(i, i ^ s) for i in range(n)])


def in_hbm(x):
    return pltpu.with_memory_space_constraint(x, pltpu.HBM)


def low_bit(s):
    return s & -s


def high_bit(s):
    return 1 << (s.bit_length() - 1)


def by_bits(n, reverse=False):
    return sorted(range(1, n), key=lambda s: (bin(s).count("1"), s), reverse=reverse)


def halves(block):
    if isinstance(block, tuple):
        return block
    half = block.shape[0] // 2
    return block[:half], block[half:]


def near_blocks(x, n):
    return {s: swap(x, s) for s in by_bits(n) if s & (s - 1) == 0}


def far_blocks(blocks, n):
    blocks = dict(blocks)
    for s in by_bits(n):
        if s not in blocks:
            low, high = low_bit(s), high_bit(s)
            blocks[s] = (swap(halves(blocks[s ^ low])[0], low), swap(halves(blocks[s ^ high])[1], high))
    return blocks


def vmem_specs(n):
    return [pl.BlockSpec(memory_space=pltpu.VMEM)] * n


def params(mib):
    return pltpu.CompilerParams(vmem_limit_bytes=mib * 1024 * 1024)


def fetch(pairs, sem_ref):
    copies = [pltpu.make_async_copy(src, dst, sem_ref.at[i]) for i, (src, dst) in enumerate(pairs)]
    for copy in copies:
        copy.start()
    return copies


NOWHERE = 1 << 20


def prep_kernel(n_req, me_ref, req_hbm, start_hbm, grid_hbm, text_hbm, x_hbm, dec_hbm, vis_hbm, *refs):
    outs, refs = refs[:n_req], refs[n_req:]
    (ctext_out, rtext_out, sel_out, table_out, key_out, dec_out, vis_out, req_ref, start_ref, grid_ref, text_ref, x_ref,
     dec_ref, vis_ref, tmp_ref, sem_ref) = refs
    pairs = (
        (req_hbm, req_ref),
        (start_hbm, start_ref),
        (grid_hbm, grid_ref),
        (text_hbm, text_ref),
        (x_hbm, x_ref),
        (dec_hbm, dec_ref),
        (vis_hbm, vis_ref),
    )
    copies = fetch(pairs, sem_ref)
    side, img_dev = x_ref.shape[0], x_ref.shape[2]
    half = side // 2
    region = half * half
    n_img, n_text, length = sel_out.shape[0], ctext_out.shape[0], text_ref.shape[0]
    me = me_ref[0]
    for copy in copies[:3]:
        copy.wait()

    found = []
    for s in range(n_req):
        source = (me ^ s) * img_dev

        def one_image(k, found, source=source):
            hit = req_ref[source + k] == me
            values = (start_ref[source + k], grid_ref[0, source + k] // 2, grid_ref[1, source + k] // 2)
            return tuple(jnp.where(hit, new, old) for new, old in zip(values, found))

        none = (jnp.int32(NOWHERE), jnp.int32(0), jnp.int32(1))
        found.append(lax.fori_loop(0, img_dev, one_image, none, unroll=img_dev <= 8))

    spot = lax.broadcasted_iota(jnp.int32, (8, length), 1)
    before = jnp.zeros((8, length), jnp.int32)
    closed = jnp.zeros((8, length), jnp.int32)
    inside = jnp.zeros((8, length), jnp.int32)
    row = lax.broadcasted_iota(jnp.int32, (n_img, 128), 0)
    pos = jnp.full((n_img, 128), -1, jnp.int32)
    target = jnp.full((n_img, 128), -1, jnp.int32)
    line = lax.broadcasted_iota(jnp.int32, (n_req, 128), 0)
    table = jnp.zeros((n_req, 128), jnp.int32)
    for s, (start, high, wide) in enumerate(found):
        count = high * wide
        c = spot - start
        here = (c >= 0) & (c < region)
        before += jnp.clip(c, 0, region)
        inside = jnp.where(here, 1, inside)
        closed = jnp.where(here & (c >= count), 1, closed)
        c = row - s * region
        here = (c >= 0) & (c < region)
        pos = jnp.where(here, start + c, pos)
        cell = c
        for w in range(1, half):
            cell = jnp.where(wide == w, c // w * half + c % w, cell)
        target = jnp.where(here & (c < count), s * region + cell, target)
        table = jnp.where(line == s, start, table)
    table_out[...] = table
    key_out[...] = 1.0 - closed.astype(jnp.float32)
    rank = jnp.where(inside == 1, -1, spot - before)[0:1]
    gather = (lax.broadcasted_iota(jnp.int32, (n_text, length), 0) == rank).astype(jnp.bfloat16)
    stays = jnp.where(target >= 0, -1, pos)[:, :1]
    keep = (lax.broadcasted_iota(jnp.int32, (n_img, length), 1) == stays).astype(jnp.bfloat16)
    sel = lax.broadcasted_iota(jnp.int32, (n_img, n_img), 1) == target[:, :1]
    sel_out[...] = sel.astype(jnp.bfloat16)
    copies[3].wait()
    text = text_ref[...]
    ctext_out[...] = jnp.dot(gather, text, preferred_element_type=jnp.float32).astype(jnp.bfloat16)
    rtext_out[...] = jnp.dot(keep, text, preferred_element_type=jnp.float32).astype(jnp.bfloat16)

    for copy in copies[4:]:
        copy.wait()
    rows = lax.broadcasted_iota(jnp.int32, (n_req, img_dev), 0)
    cols = lax.broadcasted_iota(jnp.int32, (n_req, img_dev), 1)
    goal = jnp.full((n_req, img_dev), -1, jnp.int32)
    for k in range(img_dev):
        goal = jnp.where(cols == k, req_ref[me * img_dev + k] ^ me, goal)
    onehot = (rows == goal).astype(jnp.bfloat16)
    tmp_ref[...] = jnp.zeros_like(tmp_ref)
    for i in range(half):
        for j in range(half):
            total = x_ref[2 * i, 2 * j].astype(jnp.float32)
            for a, b in ((0, 1), (1, 0), (1, 1)):
                total += x_ref[2 * i + a, 2 * j + b].astype(jnp.float32)
            pooled = (total * 0.25).astype(jnp.bfloat16)
            tmp_ref[:, i * half + j, :] = jnp.dot(onehot, pooled, preferred_element_type=jnp.float32)
    for s in range(n_req):
        outs[s][...] = tmp_ref[s].astype(jnp.bfloat16)
    per = vis_ref.shape[0]
    for i in range(per):
        lanes = pl.ds(i * 128, 128)
        vis_out[:, lanes] = vis_ref[i : i + 1, :].astype(jnp.float32)
        for t in range(dec_out.shape[0]):
            at = t * per + i
            dec_out[t, :, lanes] = dec_ref[at : at + 1, :].astype(jnp.float32)


def prepare(me, image_request, slot_start, grids, text, patches, dec_gain, vis_gain, n_req, n_text, n_img):
    side, _, img_dev, width = patches.shape
    padded = round_up((side // 2) ** 2, 16)
    inputs = (
        image_request,
        slot_start,
        grids.T,
        text,
        patches,
        dec_gain.reshape(-1, 128),
        vis_gain.reshape(-1, 128),
    )
    bf16, f32 = jnp.bfloat16, jnp.float32
    outputs = [((padded, width), bf16)] * n_req + [
        ((n_text, width), bf16),
        ((n_img, width), bf16),
        ((n_img, n_img), bf16),
        ((n_req, 128), jnp.int32),
        ((8, text.shape[0]), f32),
        ((dec_gain.size // width, 1, width), f32),
        ((1, width), f32),
    ]
    return pl.pallas_call(
        functools.partial(prep_kernel, n_req),
        out_shape=tuple(jax.ShapeDtypeStruct(shape, kind) for shape, kind in outputs),
        in_specs=[pl.BlockSpec(memory_space=pltpu.SMEM)] + [pl.BlockSpec(memory_space=pltpu.HBM)] * len(inputs),
        out_specs=tuple(vmem_specs(len(outputs))),
        scratch_shapes=[pltpu.SMEM(x.shape, jnp.int32) for x in inputs[:3]]
        + [pltpu.VMEM(x.shape, x.dtype) for x in inputs[3:]]
        + [pltpu.VMEM((n_req, padded, width), f32), pltpu.SemaphoreType.DMA((len(inputs),))],
        compiler_params=params(12),
        cost_estimate=TINY,
    )(me, *[in_hbm(x) for x in inputs])


def pack_kernel(region, gain_ref, rtext_ref, sel_ref, *refs):
    recs, (out_ref, tmp_ref) = refs[:-2], refs[-2:]
    for r, rec_ref in enumerate(recs):
        tmp_ref[region * r : region * (r + 1)] = rec_ref[...].astype(jnp.float32)[:region]
    done = region * len(recs)
    rest = tmp_ref.shape[0] - done
    tmp_ref[done:] = jnp.zeros((rest, tmp_ref.shape[1]), jnp.float32)
    picked = jnp.dot(sel_ref[...], tmp_ref[...].astype(jnp.bfloat16), preferred_element_type=jnp.float32)
    tmp_ref[...] = picked + rtext_ref[...].astype(jnp.float32)
    tmp_ref[done:] = jnp.broadcast_to(gain_ref[0:1, :], (rest, gain_ref.shape[1]))
    out_ref[...] = tmp_ref[...].astype(jnp.bfloat16)


def pack_images(received, gain, rtext, sel, region):
    n_img, width = rtext.shape
    return pl.pallas_call(
        functools.partial(pack_kernel, region),
        out_shape=jax.ShapeDtypeStruct((n_img, width), jnp.bfloat16),
        in_specs=vmem_specs(3 + len(received)),
        out_specs=pl.BlockSpec(memory_space=pltpu.VMEM),
        scratch_shapes=[pltpu.VMEM((n_img, width), jnp.float32)],
        compiler_params=params(4),
        cost_estimate=TINY,
    )(gain, rtext, sel, *received)


def place_kernel(region, n_text, table_ref, place_ref, text_row_ref):
    length, n_all = place_ref.shape
    spot = lax.broadcasted_iota(jnp.int32, (length, 128), 0)
    before = jnp.zeros((length, 128), jnp.int32)
    at = jnp.full((length, 128), -1, jnp.int32)
    for s in range(table_ref.shape[0]):
        c = spot - table_ref[s : s + 1, :]
        before += jnp.clip(c, 0, region)
        at = jnp.where((c >= 0) & (c < region), n_text + s * region + c, at)
    text_row_ref[...] = jnp.where(at < 0, 1.0, 0.0)
    at = jnp.where(at < 0, spot - before, at)[:, :1]
    place_ref[...] = (lax.broadcasted_iota(jnp.int32, (length, n_all), 1) == at).astype(jnp.bfloat16)


def placement(table, region, length, n_text, n_img):
    return pl.pallas_call(
        functools.partial(place_kernel, region, n_text),
        out_shape=(
            jax.ShapeDtypeStruct((length, n_text + n_img), jnp.bfloat16),
            jax.ShapeDtypeStruct((length, 128), jnp.float32),
        ),
        in_specs=vmem_specs(1),
        out_specs=tuple(vmem_specs(2)),
        compiler_params=params(8),
        cost_estimate=TINY,
    )(table)


def cols_of(ref, owner, width):
    return ref[:, pl.ds(pl.multiple_of(owner * width, width), width)]


def scale_rows(x, gain):
    xf = x.astype(jnp.float32)
    return (xf * gain).astype(jnp.bfloat16), jnp.sum(xf * xf, axis=1, keepdims=True)


def own_kernel(me_ref, x_ref, gain_ref, w_ref, acc_ref, ss_ref, held_ref, sem_ref):
    n_ten, _, width, _ = held_ref.shape
    half = x_ref.shape[0] // 2
    copies = []
    for s in range(n_ten):
        rows = pl.ds(pl.multiple_of((me_ref[0] ^ s) * width, width), width)
        copies += [pltpu.make_async_copy(w_ref.at[j, rows], held_ref.at[s, j], sem_ref.at[s, j]) for j in range(3)]
    for copy in copies:
        copy.start()
    scaled = []
    for side in range(2):
        rows = pl.ds(side * half, half)
        x, total = scale_rows(x_ref[rows], gain_ref[me_ref[0]])
        scaled.append(x)
        ss_ref[rows] = jnp.broadcast_to(total, (half, 128))
    for j in range(3):
        copies[j].wait()
        for side in range(2):
            acc_ref[j, pl.ds(side * half, half)] = jnp.dot(
                scaled[side], held_ref[0, j], preferred_element_type=jnp.float32
            )
    for copy in copies[3:]:
        copy.wait()


def own_part(me, x, gain, w):
    rows, width = x.shape
    n_ten, cols = gain.shape[0], w.shape[2]
    return pl.pallas_call(
        own_kernel,
        out_shape=(
            jax.ShapeDtypeStruct((3, rows, cols), jnp.float32),
            jax.ShapeDtypeStruct((rows, 128), jnp.float32),
            pltpu.VMEM((n_ten, 3, width, cols), w.dtype),
        ),
        in_specs=[pl.BlockSpec(memory_space=pltpu.SMEM)] + vmem_specs(2) + [pl.BlockSpec(memory_space=pltpu.HBM)],
        out_specs=tuple(vmem_specs(3)),
        scratch_shapes=[pltpu.SemaphoreType.DMA((n_ten, 3))],
        compiler_params=params(12),
        cost_estimate=TINY,
    )(me, x, gain, in_hbm(w))


def near_kernel(near, pieces, me_ref, *refs):
    n_x = sum(pieces)
    x_refs, refs = list(refs[:n_x]), refs[n_x:]
    gain_ref, held_ref, acc_in, ss_in, acc_ref, ss_ref = refs
    half = acc_ref.shape[1] // 2
    views = []
    for n in pieces:
        mine, x_refs = x_refs[:n], x_refs[n:]
        views.append([mine[0].at[pl.ds(side * half, half)] if n == 1 else mine[side] for side in range(2)])
    scaled = {}
    for side in range(2):
        rows = pl.ds(side * half, half)
        total = ss_in[rows]
        for b, s in enumerate(near):
            scaled[side, b], part = scale_rows(views[b][side][...], gain_ref[me_ref[0] ^ s])
            total += part
        ss_ref[rows] = total
    for j in range(3):
        for side in range(2):
            rows = pl.ds(side * half, half)
            acc = acc_in[j, rows]
            for b, s in enumerate(near):
                acc += jnp.dot(scaled[side, b], held_ref[s, j], preferred_element_type=jnp.float32)
            acc_ref[j, rows] = acc


def near_part(near, me, blocks, gain, held, acc, ss):
    blocks = [b if isinstance(b, tuple) else (b,) for b in blocks]
    pieces = [len(b) for b in blocks]
    return pl.pallas_call(
        functools.partial(near_kernel, near, pieces),
        out_shape=(
            jax.ShapeDtypeStruct(acc.shape, jnp.float32),
            jax.ShapeDtypeStruct(ss.shape, jnp.float32),
        ),
        in_specs=[pl.BlockSpec(memory_space=pltpu.SMEM)]
        + vmem_specs(sum(pieces) + 4),
        out_specs=tuple(vmem_specs(2)),
        compiler_params=params(12),
        cost_estimate=TINY,
    )(me, *[h for b in blocks for h in b], gain, held, acc, ss)


def image_kernel(n_rows, n_blk, me_ref, *refs):
    x_refs, refs = refs[:n_blk], refs[n_blk:]
    gain_ref, sel_ref, held_ref, w_out_ref, qkv_ref, own_ref, w_out_held, sem_ref = refs
    copy = pltpu.make_async_copy(w_out_ref, w_out_held, sem_ref)
    copy.start()
    is_img = jnp.sum(sel_ref[...].astype(jnp.float32), axis=1, keepdims=True) > 0.5
    total = 0.0
    for s in range(n_blk):
        xf = x_refs[s][...].astype(jnp.float32)
        total += jnp.sum(xf * xf, axis=1, keepdims=True)
    scale = lax.rsqrt(total / D + EPS)
    total = 0.0
    scaled = []
    for s in range(n_blk):
        xf = x_refs[s][...].astype(jnp.float32)
        merged = jnp.where(is_img, xf * scale * xf[n_rows : n_rows + 1], xf).astype(jnp.bfloat16)
        if s == 0:
            own_ref[...] = merged
        mf = merged.astype(jnp.float32)
        total += jnp.sum(mf * mf, axis=1, keepdims=True)
        scaled.append((mf * gain_ref[me_ref[0] ^ s]).astype(jnp.bfloat16))
    scale = lax.rsqrt(total / D + EPS)
    for j in range(3):
        acc = 0.0
        for s in range(n_blk):
            acc += jnp.dot(scaled[s], held_ref[s, j], preferred_element_type=jnp.float32)
        qkv_ref[j] = (acc * scale).astype(jnp.bfloat16)
    copy.wait()


def image_part(me, blocks, gain, sel, held, w_out, n_rows):
    n_img, width = blocks[0].shape
    return pl.pallas_call(
        functools.partial(image_kernel, n_rows, len(blocks)),
        out_shape=(
            jax.ShapeDtypeStruct((3, n_img, held.shape[3]), jnp.bfloat16),
            jax.ShapeDtypeStruct((n_img, width), jnp.bfloat16),
            pltpu.VMEM(w_out.shape, w_out.dtype),
        ),
        in_specs=[pl.BlockSpec(memory_space=pltpu.SMEM)]
        + vmem_specs(len(blocks) + 3)
        + [pl.BlockSpec(memory_space=pltpu.HBM)],
        out_specs=tuple(vmem_specs(3)),
        scratch_shapes=[pltpu.SemaphoreType.DMA],
        compiler_params=params(12),
        cost_estimate=TINY,
    )(me, *blocks, gain, sel, held, in_hbm(w_out))


def final_kernel(far, me_ref, top_ref, bottom_ref, gain_ref, held_ref, acc_ref, ss_ref, img_ref, place_ref, key_ref,
                 w_out_ref, ctx_ref, far_top_ref, far_bottom_ref, all_ref, qkv_ref):
    half, width = top_ref.shape
    n_text = 2 * half
    rows, cols = ctx_ref.shape
    owner = me_ref[0] ^ far
    scaled, scales = [], []
    for side, x_ref in enumerate((top_ref, bottom_ref)):
        part = pl.ds(side * half, half)
        x, total = scale_rows(x_ref[...], gain_ref[owner])
        scaled.append(x)
        total = ss_ref[part] + total
        scales.append(lax.rsqrt(total / D + EPS)[:, :1])
    for j in range(3):
        weight = held_ref[far, j]
        for side in range(2):
            part = pl.ds(side * half, half)
            prod = jnp.dot(scaled[side], weight, preferred_element_type=jnp.float32)
            all_ref[part] = ((prod + acc_ref[j, part]) * scales[side]).astype(jnp.bfloat16)
        all_ref[n_text:] = img_ref[j]
        qkv_ref[j] = jnp.dot(place_ref[...], all_ref[...], preferred_element_type=jnp.float32).astype(jnp.bfloat16)
    step = 128
    heads = [pl.ds(h * HD, HD) for h in range(cols // HD)]
    for r in range(rows // step):
        here, last = pl.ds(r * step, step), (r + 1) * step
        row = lax.broadcasted_iota(jnp.int32, (step, last), 0) + r * step
        col = lax.broadcasted_iota(jnp.int32, (step, last), 1)
        bias = jnp.where((row >= col) & (key_ref[0:1, pl.ds(0, last)] > 0.5), 0.0, -1e30)
        scores = [
            lax.dot_general(
                qkv_ref[0, here, lanes],
                qkv_ref[1, pl.ds(0, last), lanes],
                (((1,), (1,)), ((), ())),
                preferred_element_type=jnp.float32,
            )
            for lanes in heads
        ]
        scores = [x * (LOG2E / HD**0.5) + bias for x in scores]
        tops = [jnp.max(x, axis=1, keepdims=True) for x in scores]
        expo = [jnp.exp2(x - top) for x, top in zip(scores, tops)]
        sums = [jnp.sum(x, axis=1, keepdims=True) for x in expo]
        outs = [
            jnp.dot(x.astype(jnp.bfloat16), qkv_ref[2, pl.ds(0, last), lanes], preferred_element_type=jnp.float32)
            for x, lanes in zip(expo, heads)
        ]
        for lanes, out, total in zip(heads, outs, sums):
            ctx_ref[here, lanes] = (out / total).astype(jnp.bfloat16)
    weight = cols_of(w_out_ref, owner, width)
    half = rows // 2
    for side, out_ref in enumerate((far_top_ref, far_bottom_ref)):
        out_ref[...] = jnp.dot(
            ctx_ref[pl.ds(side * half, half)], weight, preferred_element_type=jnp.float32
        ).astype(jnp.bfloat16)


def final_part(far, me, block, gain, held, acc, ss, img, place, key_ok, w_out):
    width, cols = held.shape[2:]
    rows, n_all = place.shape
    half = rows // 2
    return pl.pallas_call(
        functools.partial(final_kernel, far),
        out_shape=(
            jax.ShapeDtypeStruct((rows, cols), jnp.bfloat16),
            jax.ShapeDtypeStruct((half, width), jnp.bfloat16),
            jax.ShapeDtypeStruct((half, width), jnp.bfloat16),
        ),
        in_specs=[pl.BlockSpec(memory_space=pltpu.SMEM)]
        + vmem_specs(10),
        out_specs=tuple(vmem_specs(3)),
        scratch_shapes=[pltpu.VMEM((n_all, cols), jnp.bfloat16), pltpu.VMEM((3, rows, cols), jnp.bfloat16)],
        compiler_params=params(12),
        cost_estimate=TINY,
    )(me, *block, gain, held, acc, ss, img, place, key_ok, w_out)


def out_kernel(away, me_ref, ctx_ref, w_ref, top_ref, bottom_ref):
    half, width = top_ref.shape
    weight = cols_of(w_ref, me_ref[0] ^ away, width)
    for side, out_ref in enumerate((top_ref, bottom_ref)):
        out_ref[...] = jnp.dot(
            ctx_ref[pl.ds(side * half, half)], weight, preferred_element_type=jnp.float32
        ).astype(out_ref.dtype)


def out_part(away, me, ctx, w, width, dtype=jnp.bfloat16):
    rows, depth = ctx.shape
    return pl.pallas_call(
        functools.partial(out_kernel, away),
        out_shape=(
            jax.ShapeDtypeStruct((rows // 2, width), dtype),
            jax.ShapeDtypeStruct((rows // 2, width), dtype),
        ),
        in_specs=[pl.BlockSpec(memory_space=pltpu.SMEM)] + vmem_specs(2),
        out_specs=tuple(vmem_specs(2)),
        compiler_params=params(12),
        cost_estimate=TINY,
    )(me, ctx, w)


def sum_of(refs, part=slice(None)):
    return functools.reduce(lambda a, b: a + b, [ref[part].astype(jnp.float32) for ref in refs])


def first_kernel(n_top, base_ref, *refs):
    out_ref = refs[-1]
    half = base_ref.shape[0] // 2
    for side, terms in enumerate((refs[:n_top], refs[n_top:-1])):
        part = pl.ds(side * half, half)
        out_ref[part] = base_ref[part].astype(jnp.float32) + sum_of(terms)


def add_first(base, top, bottom):
    return pl.pallas_call(
        functools.partial(first_kernel, len(top)),
        out_shape=jax.ShapeDtypeStruct(base.shape, jnp.float32),
        in_specs=vmem_specs(1 + len(top) + len(bottom)),
        out_specs=pl.BlockSpec(memory_space=pltpu.VMEM),
        compiler_params=params(12),
        cost_estimate=TINY,
    )(base, *top, *bottom)


def last_kernel(n_top, base_ref, *refs):
    refs, (out_ref, tmp_ref, sem_ref) = refs[:-3], refs[-3:]
    half = base_ref.shape[0] // 2
    step = half // 2
    copies = []
    for side, terms in enumerate((refs[:n_top], refs[n_top:])):
        for i in range(2):
            part = pl.ds(side * half + i * step, step)
            total = base_ref[part] + sum_of(terms, pl.ds(i * step, step))
            tmp_ref[part] = total.astype(tmp_ref.dtype)
            copy = pltpu.make_async_copy(tmp_ref.at[part], out_ref.at[part], sem_ref.at[side, i])
            copy.start()
            copies.append(copy)
    for copy in copies:
        copy.wait()


def add_last(base, top, bottom):
    return pl.pallas_call(
        functools.partial(last_kernel, len(top)),
        out_shape=jax.ShapeDtypeStruct(base.shape, jnp.bfloat16),
        in_specs=vmem_specs(1 + len(top) + len(bottom)),
        out_specs=pl.BlockSpec(memory_space=pl.ANY),
        scratch_shapes=[pltpu.VMEM(base.shape, jnp.bfloat16), pltpu.SemaphoreType.DMA((2, 2))],
        compiler_params=params(12),
        cost_estimate=TINY,
    )(base, *top, *bottom)


def scatter_terms(parts, n):
    acc = {s: [[parts[s][0]], [parts[s][1]]] for s in range(n)}
    early, late = [[], []], [[], []]
    for s in by_bits(n, reverse=True):
        for side, bit in ((0, low_bit(s)), (1, high_bit(s))):
            terms = [t.astype(jnp.float32) for t in acc[s][side]]
            out = swap(functools.reduce(lambda a, b: a + b, terms).astype(jnp.bfloat16), bit)
            if s == bit:
                (early if len(terms) == 1 else late)[side].append(out)
            else:
                acc[s ^ bit][side].append(out)
    return early, late


def body(text, patches, grids, image_request, slot_start, vis_gain, dec_gain, w_qkv, w_out):
    n_req = lax.axis_size("req")
    n_ten = lax.axis_size("tensor")
    me_req = lax.axis_index("req")
    me_ten = lax.axis_index("tensor")
    img_dev, side, _, width = patches.shape
    half = side // 2
    region = half * half
    length = text.shape[0]
    w3 = jnp.transpose(w_qkv, (1, 0, 2))
    req_at = me_req.astype(jnp.int32)[None]
    ten_at = me_ten.astype(jnp.int32)[None]
    order = by_bits(n_ten)
    near_at, far = order[:-1], order[-1]

    n_rows = n_req * region
    n_img = round_up(n_rows + 1, 16)
    n_text = round_up(length - (n_rows if img_dev == n_req else 0), 32)
    *outgoing, ctext, rtext, sel, table, key_ok, gains, vis_row = prepare(
        req_at, image_request, slot_start, grids, text, jnp.transpose(patches, (1, 2, 0, 3)), dec_gain, vis_gain, n_req,
        n_text, n_img
    )
    blocks = near_blocks(ctext, n_ten)

    received = [outgoing[0]] + [swap(outgoing[s], s, "req") for s in range(1, n_req)]
    img_own = pack_images(received, vis_row, rtext, sel, region)
    img_blocks = [img_own] + [swap(img_own, s) for s in range(1, n_ten)]
    own, img_own = lax.optimization_barrier((ctext, img_own))
    acc, ss, held = own_part(ten_at, own, gains, w3)
    handed, img_blocks, acc = lax.optimization_barrier((blocks, img_blocks, acc))
    blocks = {**far_blocks(handed, n_ten), **blocks}

    near = [blocks[s] for s in near_at]
    acc, ss = near_part(near_at, ten_at, near, gains, held, acc, ss)
    table, acc = lax.optimization_barrier((table, acc))
    place, text_row = placement(table, region, length, n_text, n_img)
    img_qkv, merged, w_out = image_part(ten_at, img_blocks, gains, sel, held, w_out, n_rows)
    context, far_top, far_bottom = final_part(
        far, ten_at, blocks[far], gains, held, acc, ss, img_qkv, place, key_ok, w_out
    )
    img_here = jnp.dot(place[:, n_text:], merged, preferred_element_type=jnp.float32)
    x_in = (text.astype(jnp.float32) * text_row[:, :1] + img_here).astype(jnp.bfloat16)

    parts = {far: (far_top, far_bottom)}
    for s in reversed([0] + near_at):
        parts[s] = out_part(s, ten_at, context, w_out, width, jnp.float32 if s == 0 else jnp.bfloat16)
    early, late = scatter_terms(parts, n_ten)
    base = add_first(x_in, [parts[0][0]] + early[0], [parts[0][1]] + early[1])
    return add_last(base, late[0], late[1])


def solution(mesh):
    in_specs = (
        P("req", "tensor"),
        P("req", None, None, "tensor"),
        P(),
        P(),
        P(),
        P("tensor"),
        P(),
        P(None, None, "tensor"),
        P("tensor", None),
    )
    out_specs = P("req", "tensor")
    return jax.shard_map(body, mesh=mesh, in_specs=in_specs, out_specs=out_specs, check_vma=False)
```

```python
import functools

import jax
import jax.numpy as jnp
from jax import lax
from jax.experimental import pallas as pl
from jax.experimental.pallas import tpu as pltpu
from jax.sharding import PartitionSpec as P

D = 4096
HD = 128
EPS = 1e-05
LOG2E = 1.4426950408889634
TINY = pl.CostEstimate(flops=0, bytes_accessed=0, transcendentals=0)


def round_up(n, m):
    return -(-n // m) * m


def swap(x, s, axis="tensor"):
    n = lax.axis_size(axis)
    return lax.ppermute(x, axis, [(i, i ^ s) for i in range(n)])


def in_hbm(x):
    return pltpu.with_memory_space_constraint(x, pltpu.HBM)


def low_bit(s):
    return s & -s


def high_bit(s):
    return 1 << (s.bit_length() - 1)


def by_bits(n, reverse=False):
    return sorted(range(1, n), key=lambda s: (bin(s).count("1"), s), reverse=reverse)


def halves(block):
    if isinstance(block, tuple):
        return block
    half = block.shape[0] // 2
    return block[:half], block[half:]


def near_blocks(x, n):
    return {s: swap(x, s) for s in by_bits(n) if s & (s - 1) == 0}


def far_blocks(blocks, n):
    blocks = dict(blocks)
    for s in by_bits(n):
        if s not in blocks:
            low, high = low_bit(s), high_bit(s)
            blocks[s] = (swap(halves(blocks[s ^ low])[0], low), swap(halves(blocks[s ^ high])[1], high))
    return blocks


def vmem_specs(n):
    return [pl.BlockSpec(memory_space=pltpu.VMEM)] * n


def params(mib):
    return pltpu.CompilerParams(vmem_limit_bytes=mib * 1024 * 1024)


def fetch(pairs, sem_ref):
    copies = [pltpu.make_async_copy(src, dst, sem_ref.at[i]) for i, (src, dst) in enumerate(pairs)]
    for copy in copies:
        copy.start()
    return copies


NOWHERE = 1 << 20


def prep_kernel(n_req, me_ref, req_hbm, start_hbm, grid_hbm, text_hbm, x_hbm, dec_hbm, vis_hbm, *refs):
    outs, refs = refs[:n_req], refs[n_req:]
    (ctext_out, rtext_out, sel_out, table_out, key_out, dec_out, vis_out, req_ref, start_ref, grid_ref, text_ref, x_ref,
     dec_ref, vis_ref, tmp_ref, sem_ref) = refs
    pairs = (
        (req_hbm, req_ref),
        (start_hbm, start_ref),
        (grid_hbm, grid_ref),
        (text_hbm, text_ref),
        (x_hbm, x_ref),
        (dec_hbm, dec_ref),
        (vis_hbm, vis_ref),
    )
    copies = fetch(pairs, sem_ref)
    side, img_dev = x_ref.shape[0], x_ref.shape[2]
    half = side // 2
    region = half * half
    n_img, n_text, length = sel_out.shape[0], ctext_out.shape[0], text_ref.shape[0]
    me = me_ref[0]
    for copy in copies[:3]:
        copy.wait()

    found = []
    for s in range(n_req):
        source = (me ^ s) * img_dev

        def one_image(k, found, source=source):
            hit = req_ref[source + k] == me
            values = (start_ref[source + k], grid_ref[0, source + k] // 2, grid_ref[1, source + k] // 2)
            return tuple(jnp.where(hit, new, old) for new, old in zip(values, found))

        none = (jnp.int32(NOWHERE), jnp.int32(0), jnp.int32(1))
        found.append(lax.fori_loop(0, img_dev, one_image, none, unroll=img_dev <= 8))

    spot = lax.broadcasted_iota(jnp.int32, (8, length), 1)
    before = jnp.zeros((8, length), jnp.int32)
    closed = jnp.zeros((8, length), jnp.int32)
    inside = jnp.zeros((8, length), jnp.int32)
    row = lax.broadcasted_iota(jnp.int32, (n_img, 128), 0)
    pos = jnp.full((n_img, 128), -1, jnp.int32)
    target = jnp.full((n_img, 128), -1, jnp.int32)
    line = lax.broadcasted_iota(jnp.int32, (n_req, 128), 0)
    table = jnp.zeros((n_req, 128), jnp.int32)
    for s, (start, high, wide) in enumerate(found):
        count = high * wide
        c = spot - start
        here = (c >= 0) & (c < region)
        before += jnp.clip(c, 0, region)
        inside = jnp.where(here, 1, inside)
        closed = jnp.where(here & (c >= count), 1, closed)
        c = row - s * region
        here = (c >= 0) & (c < region)
        pos = jnp.where(here, start + c, pos)
        cell = c
        for w in range(1, half):
            cell = jnp.where(wide == w, c // w * half + c % w, cell)
        target = jnp.where(here & (c < count), s * region + cell, target)
        table = jnp.where(line == s, start, table)
    table_out[...] = table
    key_out[...] = 1.0 - closed.astype(jnp.float32)
    rank = jnp.where(inside == 1, -1, spot - before)[0:1]
    gather = (lax.broadcasted_iota(jnp.int32, (n_text, length), 0) == rank).astype(jnp.bfloat16)
    stays = jnp.where(target >= 0, -1, pos)[:, :1]
    keep = (lax.broadcasted_iota(jnp.int32, (n_img, length), 1) == stays).astype(jnp.bfloat16)
    sel = lax.broadcasted_iota(jnp.int32, (n_img, n_img), 1) == target[:, :1]
    sel_out[...] = sel.astype(jnp.bfloat16)
    copies[3].wait()
    text = text_ref[...]
    ctext_out[...] = jnp.dot(gather, text, preferred_element_type=jnp.float32).astype(jnp.bfloat16)
    rtext_out[...] = jnp.dot(keep, text, preferred_element_type=jnp.float32).astype(jnp.bfloat16)

    for copy in copies[4:]:
        copy.wait()
    rows = lax.broadcasted_iota(jnp.int32, (n_req, img_dev), 0)
    cols = lax.broadcasted_iota(jnp.int32, (n_req, img_dev), 1)
    goal = jnp.full((n_req, img_dev), -1, jnp.int32)
    for k in range(img_dev):
        goal = jnp.where(cols == k, req_ref[me * img_dev + k] ^ me, goal)
    onehot = (rows == goal).astype(jnp.bfloat16)
    tmp_ref[...] = jnp.zeros_like(tmp_ref)
    for i in range(half):
        for j in range(half):
            total = x_ref[2 * i, 2 * j].astype(jnp.float32)
            for a, b in ((0, 1), (1, 0), (1, 1)):
                total += x_ref[2 * i + a, 2 * j + b].astype(jnp.float32)
            pooled = (total * 0.25).astype(jnp.bfloat16)
            tmp_ref[:, i * half + j, :] = jnp.dot(onehot, pooled, preferred_element_type=jnp.float32)
    for s in range(n_req):
        outs[s][...] = tmp_ref[s].astype(jnp.bfloat16)
    per = vis_ref.shape[0]
    for i in range(per):
        lanes = pl.ds(i * 128, 128)
        vis_out[:, lanes] = vis_ref[i : i + 1, :].astype(jnp.float32)
        for t in range(dec_out.shape[0]):
            at = t * per + i
            dec_out[t, :, lanes] = dec_ref[at : at + 1, :].astype(jnp.float32)


def prepare(me, image_request, slot_start, grids, text, patches, dec_gain, vis_gain, n_req, n_text, n_img):
    side, _, img_dev, width = patches.shape
    padded = round_up((side // 2) ** 2, 16)
    inputs = (
        image_request,
        slot_start,
        grids.T,
        text,
        patches,
        dec_gain.reshape(-1, 128),
        vis_gain.reshape(-1, 128),
    )
    bf16, f32 = jnp.bfloat16, jnp.float32
    outputs = [((padded, width), bf16)] * n_req + [
        ((n_text, width), bf16),
        ((n_img, width), bf16),
        ((n_img, n_img), bf16),
        ((n_req, 128), jnp.int32),
        ((8, text.shape[0]), f32),
        ((dec_gain.size // width, 1, width), f32),
        ((1, width), f32),
    ]
    return pl.pallas_call(
        functools.partial(prep_kernel, n_req),
        out_shape=tuple(jax.ShapeDtypeStruct(shape, kind) for shape, kind in outputs),
        in_specs=[pl.BlockSpec(memory_space=pltpu.SMEM)] + [pl.BlockSpec(memory_space=pltpu.HBM)] * len(inputs),
        out_specs=tuple(vmem_specs(len(outputs))),
        scratch_shapes=[pltpu.SMEM(x.shape, jnp.int32) for x in inputs[:3]]
        + [pltpu.VMEM(x.shape, x.dtype) for x in inputs[3:]]
        + [pltpu.VMEM((n_req, padded, width), f32), pltpu.SemaphoreType.DMA((len(inputs),))],
        compiler_params=params(12),
        cost_estimate=TINY,
    )(me, *[in_hbm(x) for x in inputs])


def pack_kernel(region, gain_ref, rtext_ref, sel_ref, *refs):
    recs, (out_ref, tmp_ref) = refs[:-2], refs[-2:]
    for r, rec_ref in enumerate(recs):
        tmp_ref[region * r : region * (r + 1)] = rec_ref[...].astype(jnp.float32)[:region]
    done = region * len(recs)
    rest = tmp_ref.shape[0] - done
    tmp_ref[done:] = jnp.zeros((rest, tmp_ref.shape[1]), jnp.float32)
    picked = jnp.dot(sel_ref[...], tmp_ref[...].astype(jnp.bfloat16), preferred_element_type=jnp.float32)
    tmp_ref[...] = picked + rtext_ref[...].astype(jnp.float32)
    tmp_ref[done:] = jnp.broadcast_to(gain_ref[0:1, :], (rest, gain_ref.shape[1]))
    out_ref[...] = tmp_ref[...].astype(jnp.bfloat16)


def pack_images(received, gain, rtext, sel, region):
    n_img, width = rtext.shape
    return pl.pallas_call(
        functools.partial(pack_kernel, region),
        out_shape=jax.ShapeDtypeStruct((n_img, width), jnp.bfloat16),
        in_specs=vmem_specs(3 + len(received)),
        out_specs=pl.BlockSpec(memory_space=pltpu.VMEM),
        scratch_shapes=[pltpu.VMEM((n_img, width), jnp.float32)],
        compiler_params=params(4),
        cost_estimate=TINY,
    )(gain, rtext, sel, *received)


def place_kernel(region, n_text, table_ref, place_ref, text_row_ref):
    length, n_all = place_ref.shape
    spot = lax.broadcasted_iota(jnp.int32, (length, 128), 0)
    before = jnp.zeros((length, 128), jnp.int32)
    at = jnp.full((length, 128), -1, jnp.int32)
    for s in range(table_ref.shape[0]):
        c = spot - table_ref[s : s + 1, :]
        before += jnp.clip(c, 0, region)
        at = jnp.where((c >= 0) & (c < region), n_text + s * region + c, at)
    text_row_ref[...] = jnp.where(at < 0, 1.0, 0.0)
    at = jnp.where(at < 0, spot - before, at)[:, :1]
    place_ref[...] = (lax.broadcasted_iota(jnp.int32, (length, n_all), 1) == at).astype(jnp.bfloat16)


def placement(table, region, length, n_text, n_img):
    return pl.pallas_call(
        functools.partial(place_kernel, region, n_text),
        out_shape=(
            jax.ShapeDtypeStruct((length, n_text + n_img), jnp.bfloat16),
            jax.ShapeDtypeStruct((length, 128), jnp.float32),
        ),
        in_specs=vmem_specs(1),
        out_specs=tuple(vmem_specs(2)),
        compiler_params=params(8),
        cost_estimate=TINY,
    )(table)


def cols_of(ref, owner, width):
    return ref[:, pl.ds(pl.multiple_of(owner * width, width), width)]


def scale_rows(x, gain):
    xf = x.astype(jnp.float32)
    return (xf * gain).astype(jnp.bfloat16), jnp.sum(xf * xf, axis=1, keepdims=True)


def own_kernel(me_ref, x_ref, gain_ref, w_ref, acc_ref, ss_ref, held_ref, sem_ref):
    n_ten, _, width, _ = held_ref.shape
    half = x_ref.shape[0] // 2
    copies = []
    for s in range(n_ten):
        rows = pl.ds(pl.multiple_of((me_ref[0] ^ s) * width, width), width)
        copies += [pltpu.make_async_copy(w_ref.at[j, rows], held_ref.at[s, j], sem_ref.at[s, j]) for j in range(3)]
    for copy in copies:
        copy.start()
    scaled = []
    for side in range(2):
        rows = pl.ds(side * half, half)
        x, total = scale_rows(x_ref[rows], gain_ref[me_ref[0]])
        scaled.append(x)
        ss_ref[rows] = jnp.broadcast_to(total, (half, 128))
    for j in range(3):
        copies[j].wait()
        for side in range(2):
            acc_ref[j, pl.ds(side * half, half)] = jnp.dot(
                scaled[side], held_ref[0, j], preferred_element_type=jnp.float32
            )
    for copy in copies[3:]:
        copy.wait()


def own_part(me, x, gain, w):
    rows, width = x.shape
    n_ten, cols = gain.shape[0], w.shape[2]
    return pl.pallas_call(
        own_kernel,
        out_shape=(
            jax.ShapeDtypeStruct((3, rows, cols), jnp.float32),
            jax.ShapeDtypeStruct((rows, 128), jnp.float32),
            pltpu.VMEM((n_ten, 3, width, cols), w.dtype),
        ),
        in_specs=[pl.BlockSpec(memory_space=pltpu.SMEM)] + vmem_specs(2) + [pl.BlockSpec(memory_space=pltpu.HBM)],
        out_specs=tuple(vmem_specs(3)),
        scratch_shapes=[pltpu.SemaphoreType.DMA((n_ten, 3))],
        compiler_params=params(12),
        cost_estimate=TINY,
    )(me, x, gain, in_hbm(w))


def near_kernel(near, pieces, me_ref, *refs):
    n_x = sum(pieces)
    x_refs, refs = list(refs[:n_x]), refs[n_x:]
    gain_ref, held_ref, acc_in, ss_in, acc_ref, ss_ref = refs
    half = acc_ref.shape[1] // 2
    views = []
    for n in pieces:
        mine, x_refs = x_refs[:n], x_refs[n:]
        views.append([mine[0].at[pl.ds(side * half, half)] if n == 1 else mine[side] for side in range(2)])
    scaled = {}
    for side in range(2):
        rows = pl.ds(side * half, half)
        total = ss_in[rows]
        for b, s in enumerate(near):
            scaled[side, b], part = scale_rows(views[b][side][...], gain_ref[me_ref[0] ^ s])
            total += part
        ss_ref[rows] = total
    for j in range(3):
        for side in range(2):
            rows = pl.ds(side * half, half)
            acc = acc_in[j, rows]
            for b, s in enumerate(near):
                acc += jnp.dot(scaled[side, b], held_ref[s, j], preferred_element_type=jnp.float32)
            acc_ref[j, rows] = acc


def near_part(near, me, blocks, gain, held, acc, ss):
    blocks = [b if isinstance(b, tuple) else (b,) for b in blocks]
    pieces = [len(b) for b in blocks]
    return pl.pallas_call(
        functools.partial(near_kernel, near, pieces),
        out_shape=(
            jax.ShapeDtypeStruct(acc.shape, jnp.float32),
            jax.ShapeDtypeStruct(ss.shape, jnp.float32),
        ),
        in_specs=[pl.BlockSpec(memory_space=pltpu.SMEM)]
        + vmem_specs(sum(pieces) + 4),
        out_specs=tuple(vmem_specs(2)),
        compiler_params=params(12),
        cost_estimate=TINY,
    )(me, *[h for b in blocks for h in b], gain, held, acc, ss)


def image_kernel(n_rows, n_blk, me_ref, *refs):
    x_refs, refs = refs[:n_blk], refs[n_blk:]
    gain_ref, sel_ref, held_ref, w_out_ref, qkv_ref, own_ref, w_out_held, sem_ref = refs
    copy = pltpu.make_async_copy(w_out_ref, w_out_held, sem_ref)
    copy.start()
    is_img = jnp.sum(sel_ref[...].astype(jnp.float32), axis=1, keepdims=True) > 0.5
    total = 0.0
    for s in range(n_blk):
        xf = x_refs[s][...].astype(jnp.float32)
        total += jnp.sum(xf * xf, axis=1, keepdims=True)
    scale = lax.rsqrt(total / D + EPS)
    total = 0.0
    scaled = []
    for s in range(n_blk):
        xf = x_refs[s][...].astype(jnp.float32)
        merged = jnp.where(is_img, xf * scale * xf[n_rows : n_rows + 1], xf).astype(jnp.bfloat16)
        if s == 0:
            own_ref[...] = merged
        mf = merged.astype(jnp.float32)
        total += jnp.sum(mf * mf, axis=1, keepdims=True)
        scaled.append((mf * gain_ref[me_ref[0] ^ s]).astype(jnp.bfloat16))
    scale = lax.rsqrt(total / D + EPS)
    for j in range(3):
        acc = 0.0
        for s in range(n_blk):
            acc += jnp.dot(scaled[s], held_ref[s, j], preferred_element_type=jnp.float32)
        qkv_ref[j] = (acc * scale).astype(jnp.bfloat16)
    copy.wait()


def image_part(me, blocks, gain, sel, held, w_out, n_rows):
    n_img, width = blocks[0].shape
    return pl.pallas_call(
        functools.partial(image_kernel, n_rows, len(blocks)),
        out_shape=(
            jax.ShapeDtypeStruct((3, n_img, held.shape[3]), jnp.bfloat16),
            jax.ShapeDtypeStruct((n_img, width), jnp.bfloat16),
            pltpu.VMEM(w_out.shape, w_out.dtype),
        ),
        in_specs=[pl.BlockSpec(memory_space=pltpu.SMEM)]
        + vmem_specs(len(blocks) + 3)
        + [pl.BlockSpec(memory_space=pltpu.HBM)],
        out_specs=tuple(vmem_specs(3)),
        scratch_shapes=[pltpu.SemaphoreType.DMA],
        compiler_params=params(12),
        cost_estimate=pl.CostEstimate(flops=10**11, bytes_accessed=0, transcendentals=0),
    )(me, *blocks, gain, sel, held, in_hbm(w_out))


def final_kernel(far, me_ref, top_ref, bottom_ref, gain_ref, held_ref, acc_ref, ss_ref, img_ref, place_ref, key_ref,
                 w_out_ref, ctx_ref, far_top_ref, far_bottom_ref, all_ref, qkv_ref):
    half, width = top_ref.shape
    n_text = 2 * half
    rows, cols = ctx_ref.shape
    owner = me_ref[0] ^ far
    scaled, scales = [], []
    for side, x_ref in enumerate((top_ref, bottom_ref)):
        part = pl.ds(side * half, half)
        x, total = scale_rows(x_ref[...], gain_ref[owner])
        scaled.append(x)
        total = ss_ref[part] + total
        scales.append(lax.rsqrt(total / D + EPS)[:, :1])
    for j in range(3):
        weight = held_ref[far, j]
        for side in range(2):
            part = pl.ds(side * half, half)
            prod = jnp.dot(scaled[side], weight, preferred_element_type=jnp.float32)
            all_ref[part] = ((prod + acc_ref[j, part]) * scales[side]).astype(jnp.bfloat16)
        all_ref[n_text:] = img_ref[j]
        qkv_ref[j] = jnp.dot(place_ref[...], all_ref[...], preferred_element_type=jnp.float32).astype(jnp.bfloat16)
    step = 128
    heads = [pl.ds(h * HD, HD) for h in range(cols // HD)]
    for r in range(rows // step):
        here, last = pl.ds(r * step, step), (r + 1) * step
        row = lax.broadcasted_iota(jnp.int32, (step, last), 0) + r * step
        col = lax.broadcasted_iota(jnp.int32, (step, last), 1)
        bias = jnp.where((row >= col) & (key_ref[0:1, pl.ds(0, last)] > 0.5), 0.0, -1e30)
        scores = [
            lax.dot_general(
                qkv_ref[0, here, lanes],
                qkv_ref[1, pl.ds(0, last), lanes],
                (((1,), (1,)), ((), ())),
                preferred_element_type=jnp.float32,
            )
            for lanes in heads
        ]
        scores = [x * (LOG2E / HD**0.5) + bias for x in scores]
        tops = [jnp.max(x, axis=1, keepdims=True) for x in scores]
        expo = [jnp.exp2(x - top) for x, top in zip(scores, tops)]
        sums = [jnp.sum(x, axis=1, keepdims=True) for x in expo]
        outs = [
            jnp.dot(x.astype(jnp.bfloat16), qkv_ref[2, pl.ds(0, last), lanes], preferred_element_type=jnp.float32)
            for x, lanes in zip(expo, heads)
        ]
        for lanes, out, total in zip(heads, outs, sums):
            ctx_ref[here, lanes] = (out / total).astype(jnp.bfloat16)
    weight = cols_of(w_out_ref, owner, width)
    half = rows // 2
    for side, out_ref in enumerate((far_top_ref, far_bottom_ref)):
        out_ref[...] = jnp.dot(
            ctx_ref[pl.ds(side * half, half)], weight, preferred_element_type=jnp.float32
        ).astype(jnp.bfloat16)


def final_part(far, me, block, gain, held, acc, ss, img, place, key_ok, w_out):
    width, cols = held.shape[2:]
    rows, n_all = place.shape
    half = rows // 2
    return pl.pallas_call(
        functools.partial(final_kernel, far),
        out_shape=(
            jax.ShapeDtypeStruct((rows, cols), jnp.bfloat16),
            jax.ShapeDtypeStruct((half, width), jnp.bfloat16),
            jax.ShapeDtypeStruct((half, width), jnp.bfloat16),
        ),
        in_specs=[pl.BlockSpec(memory_space=pltpu.SMEM)]
        + vmem_specs(10),
        out_specs=tuple(vmem_specs(3)),
        scratch_shapes=[pltpu.VMEM((n_all, cols), jnp.bfloat16), pltpu.VMEM((3, rows, cols), jnp.bfloat16)],
        compiler_params=params(12),
        cost_estimate=TINY,
    )(me, *block, gain, held, acc, ss, img, place, key_ok, w_out)


def out_kernel(away, me_ref, ctx_ref, w_ref, top_ref, bottom_ref):
    half, width = top_ref.shape
    weight = cols_of(w_ref, me_ref[0] ^ away, width)
    for side, out_ref in enumerate((top_ref, bottom_ref)):
        out_ref[...] = jnp.dot(
            ctx_ref[pl.ds(side * half, half)], weight, preferred_element_type=jnp.float32
        ).astype(out_ref.dtype)


def out_part(away, me, ctx, w, width, dtype=jnp.bfloat16):
    rows, depth = ctx.shape
    return pl.pallas_call(
        functools.partial(out_kernel, away),
        out_shape=(
            jax.ShapeDtypeStruct((rows // 2, width), dtype),
            jax.ShapeDtypeStruct((rows // 2, width), dtype),
        ),
        in_specs=[pl.BlockSpec(memory_space=pltpu.SMEM)] + vmem_specs(2),
        out_specs=tuple(vmem_specs(2)),
        compiler_params=params(12),
        cost_estimate=TINY,
    )(me, ctx, w)


def sum_of(refs, part=slice(None)):
    return functools.reduce(lambda a, b: a + b, [ref[part].astype(jnp.float32) for ref in refs])


def first_kernel(n_top, base_ref, *refs):
    out_ref = refs[-1]
    half = base_ref.shape[0] // 2
    for side, terms in enumerate((refs[:n_top], refs[n_top:-1])):
        part = pl.ds(side * half, half)
        out_ref[part] = base_ref[part].astype(jnp.float32) + sum_of(terms)


def add_first(base, top, bottom):
    return pl.pallas_call(
        functools.partial(first_kernel, len(top)),
        out_shape=jax.ShapeDtypeStruct(base.shape, jnp.float32),
        in_specs=vmem_specs(1 + len(top) + len(bottom)),
        out_specs=pl.BlockSpec(memory_space=pltpu.VMEM),
        compiler_params=params(12),
        cost_estimate=TINY,
    )(base, *top, *bottom)


def last_kernel(n_top, base_ref, *refs):
    refs, (out_ref, tmp_ref, sem_ref) = refs[:-3], refs[-3:]
    half = base_ref.shape[0] // 2
    step = half // 2
    copies = []
    for side, terms in enumerate((refs[:n_top], refs[n_top:])):
        for i in range(2):
            part = pl.ds(side * half + i * step, step)
            total = base_ref[part] + sum_of(terms, pl.ds(i * step, step))
            tmp_ref[part] = total.astype(tmp_ref.dtype)
            copy = pltpu.make_async_copy(tmp_ref.at[part], out_ref.at[part], sem_ref.at[side, i])
            copy.start()
            copies.append(copy)
    for copy in copies:
        copy.wait()


def add_last(base, top, bottom):
    return pl.pallas_call(
        functools.partial(last_kernel, len(top)),
        out_shape=jax.ShapeDtypeStruct(base.shape, jnp.bfloat16),
        in_specs=vmem_specs(1 + len(top) + len(bottom)),
        out_specs=pl.BlockSpec(memory_space=pl.ANY),
        scratch_shapes=[pltpu.VMEM(base.shape, jnp.bfloat16), pltpu.SemaphoreType.DMA((2, 2))],
        compiler_params=params(12),
        cost_estimate=TINY,
    )(base, *top, *bottom)


def scatter_terms(parts, n):
    acc = {s: [[parts[s][0]], [parts[s][1]]] for s in range(n)}
    early, late = [[], []], [[], []]
    for s in by_bits(n, reverse=True):
        for side, bit in ((0, low_bit(s)), (1, high_bit(s))):
            terms = [t.astype(jnp.float32) for t in acc[s][side]]
            out = swap(functools.reduce(lambda a, b: a + b, terms).astype(jnp.bfloat16), bit)
            if s == bit:
                (early if len(terms) == 1 else late)[side].append(out)
            else:
                acc[s ^ bit][side].append(out)
    return early, late


def body(text, patches, grids, image_request, slot_start, vis_gain, dec_gain, w_qkv, w_out):
    n_req = lax.axis_size("req")
    n_ten = lax.axis_size("tensor")
    me_req = lax.axis_index("req")
    me_ten = lax.axis_index("tensor")
    img_dev, side, _, width = patches.shape
    half = side // 2
    region = half * half
    length = text.shape[0]
    w3 = jnp.transpose(w_qkv, (1, 0, 2))
    req_at = me_req.astype(jnp.int32)[None]
    ten_at = me_ten.astype(jnp.int32)[None]
    order = by_bits(n_ten)
    near_at, far = order[:-1], order[-1]

    n_rows = n_req * region
    n_img = round_up(n_rows + 1, 16)
    n_text = round_up(length - (n_rows if img_dev == n_req else 0), 32)
    *outgoing, ctext, rtext, sel, table, key_ok, gains, vis_row = prepare(
        req_at, image_request, slot_start, grids, text, jnp.transpose(patches, (1, 2, 0, 3)), dec_gain, vis_gain, n_req,
        n_text, n_img
    )
    blocks = near_blocks(ctext, n_ten)

    received = [outgoing[0]] + [swap(outgoing[s], s, "req") for s in range(1, n_req)]
    img_own = pack_images(received, vis_row, rtext, sel, region)
    img_blocks = [img_own] + [swap(img_own, s) for s in range(1, n_ten)]
    own, img_own = lax.optimization_barrier((ctext, img_own))
    acc, ss, held = own_part(ten_at, own, gains, w3)
    handed, img_own = lax.optimization_barrier((blocks, img_own))
    blocks = {**far_blocks(handed, n_ten), **blocks}

    near = [blocks[s] for s in near_at]
    acc, ss = near_part(near_at, ten_at, near, gains, held, acc, ss)
    table, acc = lax.optimization_barrier((table, acc))
    place, text_row = placement(table, region, length, n_text, n_img)
    img_qkv, merged, w_out = image_part(ten_at, img_blocks, gains, sel, held, w_out, n_rows)
    context, far_top, far_bottom = final_part(
        far, ten_at, blocks[far], gains, held, acc, ss, img_qkv, place, key_ok, w_out
    )
    img_here = jnp.dot(place[:, n_text:], merged, preferred_element_type=jnp.float32)
    x_in = (text.astype(jnp.float32) * text_row[:, :1] + img_here).astype(jnp.bfloat16)

    parts = {far: (far_top, far_bottom)}
    for s in reversed([0] + near_at):
        parts[s] = out_part(s, ten_at, context, w_out, width, jnp.float32 if s == 0 else jnp.bfloat16)
    early, late = scatter_terms(parts, n_ten)
    base = add_first(x_in, [parts[0][0]] + early[0], [parts[0][1]] + early[1])
    return add_last(base, late[0], late[1])


def solution(mesh):
    in_specs = (
        P("req", "tensor"),
        P("req", None, None, "tensor"),
        P(),
        P(),
        P(),
        P("tensor"),
        P(),
        P(None, None, "tensor"),
        P("tensor", None),
    )
    out_specs = P("req", "tensor")
    return jax.shard_map(body, mesh=mesh, in_specs=in_specs, out_specs=out_specs, check_vma=False)
```

```python
import functools

import jax
import jax.numpy as jnp
from jax import lax
from jax.experimental import pallas as pl
from jax.experimental.pallas import tpu as pltpu
from jax.sharding import PartitionSpec as P

D = 4096
HD = 128
EPS = 1e-05
LOG2E = 1.4426950408889634
TINY = pl.CostEstimate(flops=0, bytes_accessed=0, transcendentals=0)


def round_up(n, m):
    return -(-n // m) * m


def swap(x, s, axis="tensor"):
    n = lax.axis_size(axis)
    return lax.ppermute(x, axis, [(i, i ^ s) for i in range(n)])


def in_hbm(x):
    return pltpu.with_memory_space_constraint(x, pltpu.HBM)


def low_bit(s):
    return s & -s


def high_bit(s):
    return 1 << (s.bit_length() - 1)


def by_bits(n, reverse=False):
    return sorted(range(1, n), key=lambda s: (bin(s).count("1"), s), reverse=reverse)


def halves(block):
    if isinstance(block, tuple):
        return block
    half = block.shape[0] // 2
    return block[:half], block[half:]


def near_blocks(x, n):
    return {s: swap(x, s) for s in by_bits(n) if s & (s - 1) == 0}


def far_blocks(blocks, n):
    blocks = dict(blocks)
    for s in by_bits(n):
        if s not in blocks:
            low, high = low_bit(s), high_bit(s)
            blocks[s] = (swap(halves(blocks[s ^ low])[0], low), swap(halves(blocks[s ^ high])[1], high))
    return blocks


def vmem_specs(n):
    return [pl.BlockSpec(memory_space=pltpu.VMEM)] * n


def params(mib):
    return pltpu.CompilerParams(vmem_limit_bytes=mib * 1024 * 1024)


def fetch(pairs, sem_ref):
    copies = [pltpu.make_async_copy(src, dst, sem_ref.at[i]) for i, (src, dst) in enumerate(pairs)]
    for copy in copies:
        copy.start()
    return copies


NOWHERE = 1 << 20


def prep_kernel(n_req, me_ref, req_hbm, start_hbm, grid_hbm, text_hbm, x_hbm, dec_hbm, vis_hbm, *refs):
    (even_out, odd_out, ctext_out, rtext_out, sel_out, table_out, key_out, dec_out, vis_out, req_ref, start_ref, grid_ref,
     text_ref, x_ref, dec_ref, vis_ref, tmp_ref, sem_ref) = refs
    pairs = (
        (req_hbm, req_ref),
        (start_hbm, start_ref),
        (grid_hbm, grid_ref),
        (text_hbm, text_ref),
        (x_hbm, x_ref),
        (dec_hbm, dec_ref),
        (vis_hbm, vis_ref),
    )
    copies = fetch(pairs, sem_ref)
    side, img_dev = x_ref.shape[0], x_ref.shape[2]
    half = side // 2
    region = half * half
    n_img, n_text, length = sel_out.shape[0], ctext_out.shape[0], text_ref.shape[0]
    me = me_ref[0]
    for copy in copies[:3]:
        copy.wait()

    found = []
    for s in range(n_req):
        source = (me ^ s) * img_dev

        def one_image(k, found, source=source):
            hit = req_ref[source + k] == me
            values = (start_ref[source + k], grid_ref[0, source + k] // 2, grid_ref[1, source + k] // 2)
            return tuple(jnp.where(hit, new, old) for new, old in zip(values, found))

        none = (jnp.int32(NOWHERE), jnp.int32(0), jnp.int32(1))
        found.append(lax.fori_loop(0, img_dev, one_image, none, unroll=img_dev <= 8))

    spot = lax.broadcasted_iota(jnp.int32, (8, length), 1)
    before = jnp.zeros((8, length), jnp.int32)
    closed = jnp.zeros((8, length), jnp.int32)
    inside = jnp.zeros((8, length), jnp.int32)
    row = lax.broadcasted_iota(jnp.int32, (n_img, 128), 0)
    pos = jnp.full((n_img, 128), -1, jnp.int32)
    target = jnp.full((n_img, 128), -1, jnp.int32)
    line = lax.broadcasted_iota(jnp.int32, (n_req, 128), 0)
    table = jnp.zeros((n_req, 128), jnp.int32)
    for s, (start, high, wide) in enumerate(found):
        count = high * wide
        c = spot - start
        here = (c >= 0) & (c < region)
        before += jnp.clip(c, 0, region)
        inside = jnp.where(here, 1, inside)
        closed = jnp.where(here & (c >= count), 1, closed)
        c = row - s * region
        here = (c >= 0) & (c < region)
        pos = jnp.where(here, start + c, pos)
        cell = c
        for w in range(1, half):
            cell = jnp.where(wide == w, c // w * half + c % w, cell)
        target = jnp.where(here & (c < count), s * region + cell, target)
        table = jnp.where(line == s, start, table)
    table_out[...] = table
    key_out[...] = 1.0 - closed.astype(jnp.float32)
    rank = jnp.where(inside == 1, -1, spot - before)[0:1]
    gather = (lax.broadcasted_iota(jnp.int32, (n_text, length), 0) == rank).astype(jnp.bfloat16)
    stays = jnp.where(target >= 0, -1, pos)[:, :1]
    keep = (lax.broadcasted_iota(jnp.int32, (n_img, length), 1) == stays).astype(jnp.bfloat16)
    sel = lax.broadcasted_iota(jnp.int32, (n_img, n_img), 1) == target[:, :1]
    sel_out[...] = sel.astype(jnp.bfloat16)
    copies[3].wait()
    text = text_ref[...]
    ctext_out[...] = jnp.dot(gather, text, preferred_element_type=jnp.float32).astype(jnp.bfloat16)
    rtext_out[...] = jnp.dot(keep, text, preferred_element_type=jnp.float32).astype(jnp.bfloat16)

    for copy in copies[4:]:
        copy.wait()
    rows = lax.broadcasted_iota(jnp.int32, (n_req, img_dev), 0)
    cols = lax.broadcasted_iota(jnp.int32, (n_req, img_dev), 1)
    goal = jnp.full((n_req, img_dev), -1, jnp.int32)
    for k in range(img_dev):
        goal = jnp.where(cols == k, req_ref[me * img_dev + k] ^ me, goal)
    onehot = (rows == goal).astype(jnp.bfloat16)
    tmp_ref[...] = jnp.zeros_like(tmp_ref)
    for i in range(half):
        for j in range(half):
            total = x_ref[2 * i, 2 * j].astype(jnp.float32)
            for a, b in ((0, 1), (1, 0), (1, 1)):
                total += x_ref[2 * i + a, 2 * j + b].astype(jnp.float32)
            pooled = (total * 0.25).astype(jnp.bfloat16)
            tmp_ref[:, i * half + j, :] = jnp.dot(onehot, pooled, preferred_element_type=jnp.float32)
    for s in range(n_req):
        (even_out, odd_out)[s % 2][s // 2] = tmp_ref[s].astype(jnp.bfloat16)
    per = vis_ref.shape[0]
    for i in range(per):
        lanes = pl.ds(i * 128, 128)
        vis_out[:, lanes] = vis_ref[i : i + 1, :].astype(jnp.float32)
        for t in range(dec_out.shape[0]):
            at = t * per + i
            dec_out[t, :, lanes] = dec_ref[at : at + 1, :].astype(jnp.float32)


def prepare(me, image_request, slot_start, grids, text, patches, dec_gain, vis_gain, n_req, n_text, n_img):
    side, _, img_dev, width = patches.shape
    padded = round_up((side // 2) ** 2, 16)
    inputs = (
        image_request,
        slot_start,
        grids.T,
        text,
        patches,
        dec_gain.reshape(-1, 128),
        vis_gain.reshape(-1, 128),
    )
    bf16, f32 = jnp.bfloat16, jnp.float32
    outputs = [((n_req // 2, padded, width), bf16)] * 2 + [
        ((n_text, width), bf16),
        ((n_img, width), bf16),
        ((n_img, n_img), bf16),
        ((n_req, 128), jnp.int32),
        ((8, text.shape[0]), f32),
        ((dec_gain.size // width, 1, width), f32),
        ((1, width), f32),
    ]
    return pl.pallas_call(
        functools.partial(prep_kernel, n_req),
        out_shape=tuple(jax.ShapeDtypeStruct(shape, kind) for shape, kind in outputs),
        in_specs=[pl.BlockSpec(memory_space=pltpu.SMEM)] + [pl.BlockSpec(memory_space=pltpu.HBM)] * len(inputs),
        out_specs=tuple(vmem_specs(len(outputs))),
        scratch_shapes=[pltpu.SMEM(x.shape, jnp.int32) for x in inputs[:3]]
        + [pltpu.VMEM(x.shape, x.dtype) for x in inputs[3:]]
        + [pltpu.VMEM((n_req, padded, width), f32), pltpu.SemaphoreType.DMA((len(inputs),))],
        compiler_params=params(12),
        cost_estimate=TINY,
    )(me, *[in_hbm(x) for x in inputs])


def mix_kernel(even_ref, odd_ref, *outs):
    rows = even_ref.shape[1]
    for i, out_ref in enumerate(outs):
        out_ref[:rows] = even_ref[i]
        out_ref[rows:] = odd_ref[i]


def mix_pairs(even, odd):
    n, rows, width = even.shape
    return pl.pallas_call(
        mix_kernel,
        out_shape=(jax.ShapeDtypeStruct((2 * rows, width), jnp.bfloat16),) * n,
        in_specs=vmem_specs(2),
        out_specs=tuple(vmem_specs(n)),
        compiler_params=params(4),
        cost_estimate=TINY,
    )(even, odd)


def pack_kernel(region, gain_ref, rtext_ref, sel_ref, *refs):
    recs, (out_ref, tmp_ref) = refs[:-2], refs[-2:]
    done = 0
    for rec_ref in recs:
        rows = rec_ref.shape[0] // 2
        pair = rec_ref[...].astype(jnp.float32)
        for first in (0, rows):
            tmp_ref[done : done + region] = pair[first : first + region]
            done += region
    rest = tmp_ref.shape[0] - done
    tmp_ref[done:] = jnp.zeros((rest, tmp_ref.shape[1]), jnp.float32)
    picked = jnp.dot(sel_ref[...], tmp_ref[...].astype(jnp.bfloat16), preferred_element_type=jnp.float32)
    tmp_ref[...] = picked + rtext_ref[...].astype(jnp.float32)
    tmp_ref[done:] = jnp.broadcast_to(gain_ref[0:1, :], (rest, gain_ref.shape[1]))
    out_ref[...] = tmp_ref[...].astype(jnp.bfloat16)


def pack_images(received, gain, rtext, sel, region):
    n_img, width = rtext.shape
    return pl.pallas_call(
        functools.partial(pack_kernel, region),
        out_shape=jax.ShapeDtypeStruct((n_img, width), jnp.bfloat16),
        in_specs=vmem_specs(3 + len(received)),
        out_specs=pl.BlockSpec(memory_space=pltpu.VMEM),
        scratch_shapes=[pltpu.VMEM((n_img, width), jnp.float32)],
        compiler_params=params(4),
        cost_estimate=TINY,
    )(gain, rtext, sel, *received)


def place_kernel(region, n_text, table_ref, place_ref, text_row_ref):
    length, n_all = place_ref.shape
    spot = lax.broadcasted_iota(jnp.int32, (length, 128), 0)
    before = jnp.zeros((length, 128), jnp.int32)
    at = jnp.full((length, 128), -1, jnp.int32)
    for s in range(table_ref.shape[0]):
        c = spot - table_ref[s : s + 1, :]
        before += jnp.clip(c, 0, region)
        at = jnp.where((c >= 0) & (c < region), n_text + s * region + c, at)
    text_row_ref[...] = jnp.where(at < 0, 1.0, 0.0)
    at = jnp.where(at < 0, spot - before, at)[:, :1]
    place_ref[...] = (lax.broadcasted_iota(jnp.int32, (length, n_all), 1) == at).astype(jnp.bfloat16)


def placement(table, region, length, n_text, n_img):
    return pl.pallas_call(
        functools.partial(place_kernel, region, n_text),
        out_shape=(
            jax.ShapeDtypeStruct((length, n_text + n_img), jnp.bfloat16),
            jax.ShapeDtypeStruct((length, 128), jnp.float32),
        ),
        in_specs=vmem_specs(1),
        out_specs=tuple(vmem_specs(2)),
        compiler_params=params(8),
        cost_estimate=TINY,
    )(table)


def cols_of(ref, owner, width):
    return ref[:, pl.ds(pl.multiple_of(owner * width, width), width)]


def scale_rows(x, gain):
    xf = x.astype(jnp.float32)
    return (xf * gain).astype(jnp.bfloat16), jnp.sum(xf * xf, axis=1, keepdims=True)


def own_kernel(me_ref, x_ref, gain_ref, w_ref, acc_ref, ss_ref, held_ref, sem_ref):
    n_ten, _, width, _ = held_ref.shape
    half = x_ref.shape[0] // 2
    copies = []
    for s in range(n_ten):
        rows = pl.ds(pl.multiple_of((me_ref[0] ^ s) * width, width), width)
        copies += [pltpu.make_async_copy(w_ref.at[j, rows], held_ref.at[s, j], sem_ref.at[s, j]) for j in range(3)]
    for copy in copies:
        copy.start()
    scaled = []
    for side in range(2):
        rows = pl.ds(side * half, half)
        x, total = scale_rows(x_ref[rows], gain_ref[me_ref[0]])
        scaled.append(x)
        ss_ref[rows] = jnp.broadcast_to(total, (half, 128))
    for j in range(3):
        copies[j].wait()
        for side in range(2):
            acc_ref[j, pl.ds(side * half, half)] = jnp.dot(
                scaled[side], held_ref[0, j], preferred_element_type=jnp.float32
            )
    for copy in copies[3:]:
        copy.wait()


def own_part(me, x, gain, w):
    rows, width = x.shape
    n_ten, cols = gain.shape[0], w.shape[2]
    return pl.pallas_call(
        own_kernel,
        out_shape=(
            jax.ShapeDtypeStruct((3, rows, cols), jnp.float32),
            jax.ShapeDtypeStruct((rows, 128), jnp.float32),
            pltpu.VMEM((n_ten, 3, width, cols), w.dtype),
        ),
        in_specs=[pl.BlockSpec(memory_space=pltpu.SMEM)] + vmem_specs(2) + [pl.BlockSpec(memory_space=pltpu.HBM)],
        out_specs=tuple(vmem_specs(3)),
        scratch_shapes=[pltpu.SemaphoreType.DMA((n_ten, 3))],
        compiler_params=params(12),
        cost_estimate=TINY,
    )(me, x, gain, in_hbm(w))


def near_kernel(near, pieces, me_ref, *refs):
    n_x = sum(pieces)
    x_refs, refs = list(refs[:n_x]), refs[n_x:]
    gain_ref, held_ref, acc_in, ss_in, acc_ref, ss_ref = refs
    half = acc_ref.shape[1] // 2
    views = []
    for n in pieces:
        mine, x_refs = x_refs[:n], x_refs[n:]
        views.append([mine[0].at[pl.ds(side * half, half)] if n == 1 else mine[side] for side in range(2)])
    scaled = {}
    for side in range(2):
        rows = pl.ds(side * half, half)
        total = ss_in[rows]
        for b, s in enumerate(near):
            scaled[side, b], part = scale_rows(views[b][side][...], gain_ref[me_ref[0] ^ s])
            total += part
        ss_ref[rows] = total
    for j in range(3):
        for side in range(2):
            rows = pl.ds(side * half, half)
            acc = acc_in[j, rows]
            for b, s in enumerate(near):
                acc += jnp.dot(scaled[side, b], held_ref[s, j], preferred_element_type=jnp.float32)
            acc_ref[j, rows] = acc


def near_part(near, me, blocks, gain, held, acc, ss):
    blocks = [b if isinstance(b, tuple) else (b,) for b in blocks]
    pieces = [len(b) for b in blocks]
    return pl.pallas_call(
        functools.partial(near_kernel, near, pieces),
        out_shape=(
            jax.ShapeDtypeStruct(acc.shape, jnp.float32),
            jax.ShapeDtypeStruct(ss.shape, jnp.float32),
        ),
        in_specs=[pl.BlockSpec(memory_space=pltpu.SMEM)]
        + vmem_specs(sum(pieces) + 4),
        out_specs=tuple(vmem_specs(2)),
        compiler_params=params(12),
        cost_estimate=TINY,
    )(me, *[h for b in blocks for h in b], gain, held, acc, ss)


def image_kernel(n_rows, n_blk, me_ref, *refs):
    x_refs, refs = refs[:n_blk], refs[n_blk:]
    gain_ref, sel_ref, held_ref, w_out_ref, qkv_ref, own_ref, w_out_held, sem_ref = refs
    copy = pltpu.make_async_copy(w_out_ref, w_out_held, sem_ref)
    copy.start()
    is_img = jnp.sum(sel_ref[...].astype(jnp.float32), axis=1, keepdims=True) > 0.5
    total = 0.0
    for s in range(n_blk):
        xf = x_refs[s][...].astype(jnp.float32)
        total += jnp.sum(xf * xf, axis=1, keepdims=True)
    scale = lax.rsqrt(total / D + EPS)
    total = 0.0
    scaled = []
    for s in range(n_blk):
        xf = x_refs[s][...].astype(jnp.float32)
        merged = jnp.where(is_img, xf * scale * xf[n_rows : n_rows + 1], xf).astype(jnp.bfloat16)
        if s == 0:
            own_ref[...] = merged
        mf = merged.astype(jnp.float32)
        total += jnp.sum(mf * mf, axis=1, keepdims=True)
        scaled.append((mf * gain_ref[me_ref[0] ^ s]).astype(jnp.bfloat16))
    scale = lax.rsqrt(total / D + EPS)
    for j in range(3):
        acc = 0.0
        for s in range(n_blk):
            acc += jnp.dot(scaled[s], held_ref[s, j], preferred_element_type=jnp.float32)
        qkv_ref[j] = (acc * scale).astype(jnp.bfloat16)
    copy.wait()


def image_part(me, blocks, gain, sel, held, w_out, n_rows):
    n_img, width = blocks[0].shape
    return pl.pallas_call(
        functools.partial(image_kernel, n_rows, len(blocks)),
        out_shape=(
            jax.ShapeDtypeStruct((3, n_img, held.shape[3]), jnp.bfloat16),
            jax.ShapeDtypeStruct((n_img, width), jnp.bfloat16),
            pltpu.VMEM(w_out.shape, w_out.dtype),
        ),
        in_specs=[pl.BlockSpec(memory_space=pltpu.SMEM)]
        + vmem_specs(len(blocks) + 3)
        + [pl.BlockSpec(memory_space=pltpu.HBM)],
        out_specs=tuple(vmem_specs(3)),
        scratch_shapes=[pltpu.SemaphoreType.DMA],
        compiler_params=params(12),
        cost_estimate=pl.CostEstimate(flops=10**11, bytes_accessed=0, transcendentals=0),
    )(me, *blocks, gain, sel, held, in_hbm(w_out))


def final_kernel(far, me_ref, top_ref, bottom_ref, gain_ref, held_ref, acc_ref, ss_ref, img_ref, place_ref, key_ref,
                 w_out_ref, ctx_ref, far_top_ref, far_bottom_ref, all_ref, qkv_ref):
    half, width = top_ref.shape
    n_text = 2 * half
    rows, cols = ctx_ref.shape
    owner = me_ref[0] ^ far
    scaled, scales = [], []
    for side, x_ref in enumerate((top_ref, bottom_ref)):
        part = pl.ds(side * half, half)
        x, total = scale_rows(x_ref[...], gain_ref[owner])
        scaled.append(x)
        total = ss_ref[part] + total
        scales.append(lax.rsqrt(total / D + EPS)[:, :1])
    for j in range(3):
        weight = held_ref[far, j]
        for side in range(2):
            part = pl.ds(side * half, half)
            prod = jnp.dot(scaled[side], weight, preferred_element_type=jnp.float32)
            all_ref[part] = ((prod + acc_ref[j, part]) * scales[side]).astype(jnp.bfloat16)
        all_ref[n_text:] = img_ref[j]
        qkv_ref[j] = jnp.dot(place_ref[...], all_ref[...], preferred_element_type=jnp.float32).astype(jnp.bfloat16)
    step = 128
    heads = [pl.ds(h * HD, HD) for h in range(cols // HD)]
    for r in range(rows // step):
        here, last = pl.ds(r * step, step), (r + 1) * step
        row = lax.broadcasted_iota(jnp.int32, (step, last), 0) + r * step
        col = lax.broadcasted_iota(jnp.int32, (step, last), 1)
        bias = jnp.where((row >= col) & (key_ref[0:1, pl.ds(0, last)] > 0.5), 0.0, -1e30)
        scores = [
            lax.dot_general(
                qkv_ref[0, here, lanes],
                qkv_ref[1, pl.ds(0, last), lanes],
                (((1,), (1,)), ((), ())),
                preferred_element_type=jnp.float32,
            )
            for lanes in heads
        ]
        scores = [x * (LOG2E / HD**0.5) + bias for x in scores]
        tops = [jnp.max(x, axis=1, keepdims=True) for x in scores]
        expo = [jnp.exp2(x - top) for x, top in zip(scores, tops)]
        sums = [jnp.sum(x, axis=1, keepdims=True) for x in expo]
        outs = [
            jnp.dot(x.astype(jnp.bfloat16), qkv_ref[2, pl.ds(0, last), lanes], preferred_element_type=jnp.float32)
            for x, lanes in zip(expo, heads)
        ]
        for lanes, out, total in zip(heads, outs, sums):
            ctx_ref[here, lanes] = (out / total).astype(jnp.bfloat16)
    weight = cols_of(w_out_ref, owner, width)
    half = rows // 2
    for side, out_ref in enumerate((far_top_ref, far_bottom_ref)):
        out_ref[...] = jnp.dot(
            ctx_ref[pl.ds(side * half, half)], weight, preferred_element_type=jnp.float32
        ).astype(jnp.bfloat16)


def final_part(far, me, block, gain, held, acc, ss, img, place, key_ok, w_out):
    width, cols = held.shape[2:]
    rows, n_all = place.shape
    half = rows // 2
    return pl.pallas_call(
        functools.partial(final_kernel, far),
        out_shape=(
            jax.ShapeDtypeStruct((rows, cols), jnp.bfloat16),
            jax.ShapeDtypeStruct((half, width), jnp.bfloat16),
            jax.ShapeDtypeStruct((half, width), jnp.bfloat16),
        ),
        in_specs=[pl.BlockSpec(memory_space=pltpu.SMEM)]
        + vmem_specs(10),
        out_specs=tuple(vmem_specs(3)),
        scratch_shapes=[pltpu.VMEM((n_all, cols), jnp.bfloat16), pltpu.VMEM((3, rows, cols), jnp.bfloat16)],
        compiler_params=params(12),
        cost_estimate=TINY,
    )(me, *block, gain, held, acc, ss, img, place, key_ok, w_out)


def out_kernel(away, me_ref, ctx_ref, w_ref, top_ref, bottom_ref):
    half, width = top_ref.shape
    weight = cols_of(w_ref, me_ref[0] ^ away, width)
    for side, out_ref in enumerate((top_ref, bottom_ref)):
        out_ref[...] = jnp.dot(
            ctx_ref[pl.ds(side * half, half)], weight, preferred_element_type=jnp.float32
        ).astype(out_ref.dtype)


def out_part(away, me, ctx, w, width, dtype=jnp.bfloat16):
    rows, depth = ctx.shape
    return pl.pallas_call(
        functools.partial(out_kernel, away),
        out_shape=(
            jax.ShapeDtypeStruct((rows // 2, width), dtype),
            jax.ShapeDtypeStruct((rows // 2, width), dtype),
        ),
        in_specs=[pl.BlockSpec(memory_space=pltpu.SMEM)] + vmem_specs(2),
        out_specs=tuple(vmem_specs(2)),
        compiler_params=params(12),
        cost_estimate=TINY,
    )(me, ctx, w)


def sum_of(refs, part=slice(None)):
    return functools.reduce(lambda a, b: a + b, [ref[part].astype(jnp.float32) for ref in refs])


def first_kernel(n_top, base_ref, *refs):
    out_ref = refs[-1]
    half = base_ref.shape[0] // 2
    for side, terms in enumerate((refs[:n_top], refs[n_top:-1])):
        part = pl.ds(side * half, half)
        out_ref[part] = base_ref[part].astype(jnp.float32) + sum_of(terms)


def add_first(base, top, bottom):
    return pl.pallas_call(
        functools.partial(first_kernel, len(top)),
        out_shape=jax.ShapeDtypeStruct(base.shape, jnp.float32),
        in_specs=vmem_specs(1 + len(top) + len(bottom)),
        out_specs=pl.BlockSpec(memory_space=pltpu.VMEM),
        compiler_params=params(12),
        cost_estimate=TINY,
    )(base, *top, *bottom)


def last_kernel(n_top, base_ref, *refs):
    refs, (out_ref, tmp_ref, sem_ref) = refs[:-3], refs[-3:]
    half = base_ref.shape[0] // 2
    step = half // 2
    copies = []
    for side, terms in enumerate((refs[:n_top], refs[n_top:])):
        for i in range(2):
            part = pl.ds(side * half + i * step, step)
            total = base_ref[part] + sum_of(terms, pl.ds(i * step, step))
            tmp_ref[part] = total.astype(tmp_ref.dtype)
            copy = pltpu.make_async_copy(tmp_ref.at[part], out_ref.at[part], sem_ref.at[side, i])
            copy.start()
            copies.append(copy)
    for copy in copies:
        copy.wait()


def add_last(base, top, bottom):
    return pl.pallas_call(
        functools.partial(last_kernel, len(top)),
        out_shape=jax.ShapeDtypeStruct(base.shape, jnp.bfloat16),
        in_specs=vmem_specs(1 + len(top) + len(bottom)),
        out_specs=pl.BlockSpec(memory_space=pl.ANY),
        scratch_shapes=[pltpu.VMEM(base.shape, jnp.bfloat16), pltpu.SemaphoreType.DMA((2, 2))],
        compiler_params=params(12),
        cost_estimate=TINY,
    )(base, *top, *bottom)


def scatter_terms(parts, n):
    acc = {s: [[parts[s][0]], [parts[s][1]]] for s in range(n)}
    early, late = [[], []], [[], []]
    for s in by_bits(n, reverse=True):
        for side, bit in ((0, low_bit(s)), (1, high_bit(s))):
            terms = [t.astype(jnp.float32) for t in acc[s][side]]
            out = swap(functools.reduce(lambda a, b: a + b, terms).astype(jnp.bfloat16), bit)
            if s == bit:
                (early if len(terms) == 1 else late)[side].append(out)
            else:
                acc[s ^ bit][side].append(out)
    return early, late


def body(text, patches, grids, image_request, slot_start, vis_gain, dec_gain, w_qkv, w_out):
    n_req = lax.axis_size("req")
    n_ten = lax.axis_size("tensor")
    me_req = lax.axis_index("req")
    me_ten = lax.axis_index("tensor")
    img_dev, side, _, width = patches.shape
    half = side // 2
    region = half * half
    length = text.shape[0]
    w3 = jnp.transpose(w_qkv, (1, 0, 2))
    req_at = me_req.astype(jnp.int32)[None]
    ten_at = me_ten.astype(jnp.int32)[None]
    order = by_bits(n_ten)
    near_at, far = order[:-1], order[-1]

    n_rows = n_req * region
    n_img = round_up(n_rows + 1, 16)
    n_text = round_up(length - (n_rows if img_dev == n_req else 0), 32)
    even, odd, ctext, rtext, sel, table, key_ok, gains, vis_row = prepare(
        req_at, image_request, slot_start, grids, text, jnp.transpose(patches, (1, 2, 0, 3)), dec_gain, vis_gain, n_req,
        n_text, n_img
    )
    blocks = near_blocks(ctext, n_ten)

    pairs = mix_pairs(even, swap(odd, 1, "req"))
    received = [pairs[0]] + [swap(pairs[i], 2 * i, "req") for i in range(1, n_req // 2)]
    img_own = pack_images(received, vis_row, rtext, sel, region)
    img_blocks = [img_own] + [swap(img_own, s) for s in range(1, n_ten)]
    own, img_own = lax.optimization_barrier((ctext, img_own))
    acc, ss, held = own_part(ten_at, own, gains, w3)
    handed, img_own = lax.optimization_barrier((blocks, img_own))
    blocks = {**far_blocks(handed, n_ten), **blocks}

    near = [blocks[s] for s in near_at]
    acc, ss = near_part(near_at, ten_at, near, gains, held, acc, ss)
    table, acc = lax.optimization_barrier((table, acc))
    place, text_row = placement(table, region, length, n_text, n_img)
    img_qkv, merged, w_out = image_part(ten_at, img_blocks, gains, sel, held, w_out, n_rows)
    context, far_top, far_bottom = final_part(
        far, ten_at, blocks[far], gains, held, acc, ss, img_qkv, place, key_ok, w_out
    )
    img_here = jnp.dot(place[:, n_text:], merged, preferred_element_type=jnp.float32)
    x_in = (text.astype(jnp.float32) * text_row[:, :1] + img_here).astype(jnp.bfloat16)

    parts = {far: (far_top, far_bottom)}
    for s in reversed([0] + near_at):
        parts[s] = out_part(s, ten_at, context, w_out, width, jnp.float32 if s == 0 else jnp.bfloat16)
    early, late = scatter_terms(parts, n_ten)
    base = add_first(x_in, [parts[0][0]] + early[0], [parts[0][1]] + early[1])
    return add_last(base, late[0], late[1])


def solution(mesh):
    in_specs = (
        P("req", "tensor"),
        P("req", None, None, "tensor"),
        P(),
        P(),
        P(),
        P("tensor"),
        P(),
        P(None, None, "tensor"),
        P("tensor", None),
    )
    out_specs = P("req", "tensor")
    return jax.shard_map(body, mesh=mesh, in_specs=in_specs, out_specs=out_specs, check_vma=False)
```

```python
import functools

import jax
import jax.numpy as jnp
from jax import lax
from jax.experimental import pallas as pl
from jax.experimental.pallas import tpu as pltpu
from jax.sharding import PartitionSpec as P

D = 4096
HD = 128
EPS = 1e-05
LOG2E = 1.4426950408889634
TINY = pl.CostEstimate(flops=0, bytes_accessed=0, transcendentals=0)


def round_up(n, m):
    return -(-n // m) * m


def swap(x, s, axis="tensor"):
    n = lax.axis_size(axis)
    return lax.ppermute(x, axis, [(i, i ^ s) for i in range(n)])


def in_hbm(x):
    return pltpu.with_memory_space_constraint(x, pltpu.HBM)


def low_bit(s):
    return s & -s


def high_bit(s):
    return 1 << (s.bit_length() - 1)


def by_bits(n, reverse=False):
    return sorted(range(1, n), key=lambda s: (bin(s).count("1"), s), reverse=reverse)


def halves(block):
    if isinstance(block, tuple):
        return block
    half = block.shape[0] // 2
    return block[:half], block[half:]


def near_blocks(x, n):
    return {s: swap(x, s) for s in by_bits(n) if s & (s - 1) == 0}


def far_blocks(blocks, n):
    blocks = dict(blocks)
    for s in by_bits(n):
        if s not in blocks:
            low, high = low_bit(s), high_bit(s)
            blocks[s] = (swap(halves(blocks[s ^ low])[0], low), swap(halves(blocks[s ^ high])[1], high))
    return blocks


def vmem_specs(n):
    return [pl.BlockSpec(memory_space=pltpu.VMEM)] * n


def params(mib):
    return pltpu.CompilerParams(vmem_limit_bytes=mib * 1024 * 1024)


def fetch(pairs, sem_ref):
    copies = [pltpu.make_async_copy(src, dst, sem_ref.at[i]) for i, (src, dst) in enumerate(pairs)]
    for copy in copies:
        copy.start()
    return copies


NOWHERE = 1 << 20


def prep_kernel(n_req, me_ref, req_hbm, start_hbm, grid_hbm, text_hbm, x_hbm, dec_hbm, vis_hbm, *refs):
    (even_out, odd_out, ctext_out, rtext_out, sel_out, table_out, key_out, dec_out, vis_out, req_ref, start_ref, grid_ref,
     text_ref, x_ref, dec_ref, vis_ref, tmp_ref, sem_ref) = refs
    pairs = (
        (req_hbm, req_ref),
        (start_hbm, start_ref),
        (grid_hbm, grid_ref),
        (text_hbm, text_ref),
        (x_hbm, x_ref),
        (dec_hbm, dec_ref),
        (vis_hbm, vis_ref),
    )
    copies = fetch(pairs, sem_ref)
    side, img_dev = x_ref.shape[0], x_ref.shape[2]
    half = side // 2
    region = half * half
    n_img, n_text, length = sel_out.shape[0], ctext_out.shape[0], text_ref.shape[0]
    me = me_ref[0]
    for copy in copies[:3]:
        copy.wait()

    found = []
    for s in range(n_req):
        source = (me ^ s) * img_dev

        def one_image(k, found, source=source):
            hit = req_ref[source + k] == me
            values = (start_ref[source + k], grid_ref[0, source + k] // 2, grid_ref[1, source + k] // 2)
            return tuple(jnp.where(hit, new, old) for new, old in zip(values, found))

        none = (jnp.int32(NOWHERE), jnp.int32(0), jnp.int32(1))
        found.append(lax.fori_loop(0, img_dev, one_image, none, unroll=img_dev <= 8))

    spot = lax.broadcasted_iota(jnp.int32, (8, length), 1)
    before = jnp.zeros((8, length), jnp.int32)
    closed = jnp.zeros((8, length), jnp.int32)
    inside = jnp.zeros((8, length), jnp.int32)
    row = lax.broadcasted_iota(jnp.int32, (n_img, 128), 0)
    pos = jnp.full((n_img, 128), -1, jnp.int32)
    target = jnp.full((n_img, 128), -1, jnp.int32)
    line = lax.broadcasted_iota(jnp.int32, (n_req, 128), 0)
    table = jnp.zeros((n_req, 128), jnp.int32)
    for s, (start, high, wide) in enumerate(found):
        count = high * wide
        c = spot - start
        here = (c >= 0) & (c < region)
        before += jnp.clip(c, 0, region)
        inside = jnp.where(here, 1, inside)
        closed = jnp.where(here & (c >= count), 1, closed)
        c = row - s * region
        here = (c >= 0) & (c < region)
        pos = jnp.where(here, start + c, pos)
        cell = c
        for w in range(1, half):
            cell = jnp.where(wide == w, c // w * half + c % w, cell)
        target = jnp.where(here & (c < count), s * region + cell, target)
        table = jnp.where(line == s, start, table)
    table_out[...] = table
    key_out[...] = 1.0 - closed.astype(jnp.float32)
    rank = jnp.where(inside == 1, -1, spot - before)[0:1]
    gather = (lax.broadcasted_iota(jnp.int32, (n_text, length), 0) == rank).astype(jnp.bfloat16)
    stays = jnp.where(target >= 0, -1, pos)[:, :1]
    keep = (lax.broadcasted_iota(jnp.int32, (n_img, length), 1) == stays).astype(jnp.bfloat16)
    sel = lax.broadcasted_iota(jnp.int32, (n_img, n_img), 1) == target[:, :1]
    sel_out[...] = sel.astype(jnp.bfloat16)
    copies[3].wait()
    text = text_ref[...]
    ctext_out[...] = jnp.dot(gather, text, preferred_element_type=jnp.float32).astype(jnp.bfloat16)
    rtext_out[...] = jnp.dot(keep, text, preferred_element_type=jnp.float32).astype(jnp.bfloat16)

    for copy in copies[4:]:
        copy.wait()
    rows = lax.broadcasted_iota(jnp.int32, (n_req, img_dev), 0)
    cols = lax.broadcasted_iota(jnp.int32, (n_req, img_dev), 1)
    goal = jnp.full((n_req, img_dev), -1, jnp.int32)
    for k in range(img_dev):
        goal = jnp.where(cols == k, req_ref[me * img_dev + k] ^ me, goal)
    onehot = (rows == goal).astype(jnp.bfloat16)
    tmp_ref[...] = jnp.zeros_like(tmp_ref)
    for i in range(half):
        for j in range(half):
            total = x_ref[2 * i, 2 * j].astype(jnp.float32)
            for a, b in ((0, 1), (1, 0), (1, 1)):
                total += x_ref[2 * i + a, 2 * j + b].astype(jnp.float32)
            pooled = (total * 0.25).astype(jnp.bfloat16)
            tmp_ref[:, i * half + j, :] = jnp.dot(onehot, pooled, preferred_element_type=jnp.float32)
    for s in range(n_req):
        (even_out, odd_out)[s % 2][s // 2] = tmp_ref[s].astype(jnp.bfloat16)
    per = vis_ref.shape[0]
    for i in range(per):
        lanes = pl.ds(i * 128, 128)
        vis_out[:, lanes] = vis_ref[i : i + 1, :].astype(jnp.float32)
        for t in range(dec_out.shape[0]):
            at = t * per + i
            dec_out[t, :, lanes] = dec_ref[at : at + 1, :].astype(jnp.float32)


def prepare(me, image_request, slot_start, grids, text, patches, dec_gain, vis_gain, n_req, n_text, n_img):
    side, _, img_dev, width = patches.shape
    padded = round_up((side // 2) ** 2, 16)
    inputs = (
        image_request,
        slot_start,
        grids.T,
        text,
        patches,
        dec_gain.reshape(-1, 128),
        vis_gain.reshape(-1, 128),
    )
    bf16, f32 = jnp.bfloat16, jnp.float32
    outputs = [((n_req // 2, padded, width), bf16)] * 2 + [
        ((n_text, width), bf16),
        ((n_img, width), bf16),
        ((n_img, n_img), bf16),
        ((n_req, 128), jnp.int32),
        ((8, text.shape[0]), f32),
        ((dec_gain.size // width, 1, width), f32),
        ((1, width), f32),
    ]
    return pl.pallas_call(
        functools.partial(prep_kernel, n_req),
        out_shape=tuple(jax.ShapeDtypeStruct(shape, kind) for shape, kind in outputs),
        in_specs=[pl.BlockSpec(memory_space=pltpu.SMEM)] + [pl.BlockSpec(memory_space=pltpu.HBM)] * len(inputs),
        out_specs=tuple(vmem_specs(len(outputs))),
        scratch_shapes=[pltpu.SMEM(x.shape, jnp.int32) for x in inputs[:3]]
        + [pltpu.VMEM(x.shape, x.dtype) for x in inputs[3:]]
        + [pltpu.VMEM((n_req, padded, width), f32), pltpu.SemaphoreType.DMA((len(inputs),))],
        compiler_params=params(12),
        cost_estimate=TINY,
    )(me, *[in_hbm(x) for x in inputs])


def mix_kernel(even_ref, odd_ref, *outs):
    rows = even_ref.shape[1]
    for i, out_ref in enumerate(outs):
        out_ref[:rows] = even_ref[i]
        out_ref[rows:] = odd_ref[i]


def mix_pairs(even, odd):
    n, rows, width = even.shape
    return pl.pallas_call(
        mix_kernel,
        out_shape=(jax.ShapeDtypeStruct((2 * rows, width), jnp.bfloat16),) * n,
        in_specs=vmem_specs(2),
        out_specs=tuple(vmem_specs(n)),
        compiler_params=params(4),
        cost_estimate=TINY,
    )(even, odd)


def pack_kernel(region, gain_ref, rtext_ref, sel_ref, *refs):
    recs, (out_ref, tmp_ref) = refs[:-2], refs[-2:]
    done = 0
    for rec_ref in recs:
        rows = rec_ref.shape[0] // 2
        pair = rec_ref[...].astype(jnp.float32)
        for first in (0, rows):
            tmp_ref[done : done + region] = pair[first : first + region]
            done += region
    rest = tmp_ref.shape[0] - done
    tmp_ref[done:] = jnp.zeros((rest, tmp_ref.shape[1]), jnp.float32)
    picked = jnp.dot(sel_ref[...], tmp_ref[...].astype(jnp.bfloat16), preferred_element_type=jnp.float32)
    tmp_ref[...] = picked + rtext_ref[...].astype(jnp.float32)
    tmp_ref[done:] = jnp.broadcast_to(gain_ref[0:1, :], (rest, gain_ref.shape[1]))
    out_ref[...] = tmp_ref[...].astype(jnp.bfloat16)


def pack_images(received, gain, rtext, sel, region):
    n_img, width = rtext.shape
    return pl.pallas_call(
        functools.partial(pack_kernel, region),
        out_shape=jax.ShapeDtypeStruct((n_img, width), jnp.bfloat16),
        in_specs=vmem_specs(3 + len(received)),
        out_specs=pl.BlockSpec(memory_space=pltpu.VMEM),
        scratch_shapes=[pltpu.VMEM((n_img, width), jnp.float32)],
        compiler_params=params(4),
        cost_estimate=TINY,
    )(gain, rtext, sel, *received)


def place_kernel(region, table_ref, text_at_ref, img_at_ref, text_row_ref):
    length, n_text = text_at_ref.shape
    spot = lax.broadcasted_iota(jnp.int32, (length, 128), 0)
    before = jnp.zeros((length, 128), jnp.int32)
    at = jnp.full((length, 128), -1, jnp.int32)
    for s in range(table_ref.shape[0]):
        c = spot - table_ref[s : s + 1, :]
        before += jnp.clip(c, 0, region)
        at = jnp.where((c >= 0) & (c < region), s * region + c, at)
    text_row_ref[...] = jnp.where(at < 0, 1.0, 0.0)
    rank = jnp.where(at < 0, spot - before, -1)[:, :1]
    text_at_ref[...] = (lax.broadcasted_iota(jnp.int32, (length, n_text), 1) == rank).astype(jnp.bfloat16)
    lane = lax.broadcasted_iota(jnp.int32, img_at_ref.shape, 1)
    img_at_ref[...] = (lane == at[:, :1]).astype(jnp.bfloat16)


def placement(table, region, length, n_text, n_img):
    return pl.pallas_call(
        functools.partial(place_kernel, region),
        out_shape=(
            jax.ShapeDtypeStruct((length, n_text), jnp.bfloat16),
            jax.ShapeDtypeStruct((length, n_img), jnp.bfloat16),
            jax.ShapeDtypeStruct((length, 128), jnp.float32),
        ),
        in_specs=vmem_specs(1),
        out_specs=tuple(vmem_specs(3)),
        compiler_params=params(8),
        cost_estimate=TINY,
    )(table)


def cols_of(ref, owner, width):
    return ref[:, pl.ds(pl.multiple_of(owner * width, width), width)]


def scale_rows(x, gain):
    xf = x.astype(jnp.float32)
    return (xf * gain).astype(jnp.bfloat16), jnp.sum(xf * xf, axis=1, keepdims=True)


def own_kernel(me_ref, x_ref, gain_ref, w_ref, acc_ref, ss_ref, held_ref, sem_ref):
    n_ten, _, width, _ = held_ref.shape
    half = x_ref.shape[0] // 2
    copies = []
    for s in range(n_ten):
        rows = pl.ds(pl.multiple_of((me_ref[0] ^ s) * width, width), width)
        copies += [pltpu.make_async_copy(w_ref.at[j, rows], held_ref.at[s, j], sem_ref.at[s, j]) for j in range(3)]
    for copy in copies:
        copy.start()
    scaled = []
    for side in range(2):
        rows = pl.ds(side * half, half)
        x, total = scale_rows(x_ref[rows], gain_ref[me_ref[0]])
        scaled.append(x)
        ss_ref[rows] = jnp.broadcast_to(total, (half, 128))
    for j in range(3):
        copies[j].wait()
        for side in range(2):
            acc_ref[j, pl.ds(side * half, half)] = jnp.dot(
                scaled[side], held_ref[0, j], preferred_element_type=jnp.float32
            )
    for copy in copies[3:]:
        copy.wait()


def own_part(me, x, gain, w):
    rows, width = x.shape
    n_ten, cols = gain.shape[0], w.shape[2]
    return pl.pallas_call(
        own_kernel,
        out_shape=(
            jax.ShapeDtypeStruct((3, rows, cols), jnp.float32),
            jax.ShapeDtypeStruct((rows, 128), jnp.float32),
            pltpu.VMEM((n_ten, 3, width, cols), w.dtype),
        ),
        in_specs=[pl.BlockSpec(memory_space=pltpu.SMEM)] + vmem_specs(2) + [pl.BlockSpec(memory_space=pltpu.HBM)],
        out_specs=tuple(vmem_specs(3)),
        scratch_shapes=[pltpu.SemaphoreType.DMA((n_ten, 3))],
        compiler_params=params(12),
        cost_estimate=TINY,
    )(me, x, gain, in_hbm(w))


def near_kernel(near, pieces, me_ref, *refs):
    n_x = sum(pieces)
    x_refs, refs = list(refs[:n_x]), refs[n_x:]
    gain_ref, held_ref, acc_in, ss_in, acc_ref, ss_ref = refs
    half = acc_ref.shape[1] // 2
    views = []
    for n in pieces:
        mine, x_refs = x_refs[:n], x_refs[n:]
        views.append([mine[0].at[pl.ds(side * half, half)] if n == 1 else mine[side] for side in range(2)])
    scaled = {}
    for side in range(2):
        rows = pl.ds(side * half, half)
        total = ss_in[rows]
        for b, s in enumerate(near):
            scaled[side, b], part = scale_rows(views[b][side][...], gain_ref[me_ref[0] ^ s])
            total += part
        ss_ref[rows] = total
    for j in range(3):
        for side in range(2):
            rows = pl.ds(side * half, half)
            acc = acc_in[j, rows]
            for b, s in enumerate(near):
                acc += jnp.dot(scaled[side, b], held_ref[s, j], preferred_element_type=jnp.float32)
            acc_ref[j, rows] = acc


def near_part(near, me, blocks, gain, held, acc, ss):
    blocks = [b if isinstance(b, tuple) else (b,) for b in blocks]
    pieces = [len(b) for b in blocks]
    return pl.pallas_call(
        functools.partial(near_kernel, near, pieces),
        out_shape=(
            jax.ShapeDtypeStruct(acc.shape, jnp.float32),
            jax.ShapeDtypeStruct(ss.shape, jnp.float32),
        ),
        in_specs=[pl.BlockSpec(memory_space=pltpu.SMEM)]
        + vmem_specs(sum(pieces) + 4),
        out_specs=tuple(vmem_specs(2)),
        compiler_params=params(12),
        cost_estimate=TINY,
    )(me, *[h for b in blocks for h in b], gain, held, acc, ss)


def image_kernel(n_rows, n_blk, me_ref, *refs):
    x_refs, refs = refs[:n_blk], refs[n_blk:]
    gain_ref, sel_ref, held_ref, w_out_ref, qkv_ref, own_ref, w_out_held, sem_ref = refs
    copy = pltpu.make_async_copy(w_out_ref, w_out_held, sem_ref)
    copy.start()
    is_img = jnp.sum(sel_ref[...].astype(jnp.float32), axis=1, keepdims=True) > 0.5
    total = 0.0
    for s in range(n_blk):
        xf = x_refs[s][...].astype(jnp.float32)
        total += jnp.sum(xf * xf, axis=1, keepdims=True)
    scale = lax.rsqrt(total / D + EPS)
    total = 0.0
    scaled = []
    for s in range(n_blk):
        xf = x_refs[s][...].astype(jnp.float32)
        merged = jnp.where(is_img, xf * scale * xf[n_rows : n_rows + 1], xf).astype(jnp.bfloat16)
        if s == 0:
            own_ref[...] = merged
        mf = merged.astype(jnp.float32)
        total += jnp.sum(mf * mf, axis=1, keepdims=True)
        scaled.append((mf * gain_ref[me_ref[0] ^ s]).astype(jnp.bfloat16))
    scale = lax.rsqrt(total / D + EPS)
    for j in range(3):
        acc = 0.0
        for s in range(n_blk):
            acc += jnp.dot(scaled[s], held_ref[s, j], preferred_element_type=jnp.float32)
        qkv_ref[j] = (acc * scale).astype(jnp.bfloat16)
    copy.wait()


def image_part(me, blocks, gain, sel, held, w_out, n_rows):
    n_img, width = blocks[0].shape
    return pl.pallas_call(
        functools.partial(image_kernel, n_rows, len(blocks)),
        out_shape=(
            jax.ShapeDtypeStruct((3, n_img, held.shape[3]), jnp.bfloat16),
            jax.ShapeDtypeStruct((n_img, width), jnp.bfloat16),
            pltpu.VMEM(w_out.shape, w_out.dtype),
        ),
        in_specs=[pl.BlockSpec(memory_space=pltpu.SMEM)]
        + vmem_specs(len(blocks) + 3)
        + [pl.BlockSpec(memory_space=pltpu.HBM)],
        out_specs=tuple(vmem_specs(3)),
        scratch_shapes=[pltpu.SemaphoreType.DMA],
        compiler_params=params(12),
        cost_estimate=pl.CostEstimate(flops=10**11, bytes_accessed=0, transcendentals=0),
    )(me, *blocks, gain, sel, held, in_hbm(w_out))


def project_side(side, far, me_ref, x_ref, gain_ref, held_ref, acc_ref, ss_ref, out_ref):
    half = x_ref.shape[0]
    part = pl.ds(side * half, half)
    x, total = scale_rows(x_ref[...], gain_ref[me_ref[0] ^ far])
    scale = lax.rsqrt((ss_ref[part] + total) / D + EPS)[:, :1]
    for j in range(3):
        prod = jnp.dot(x, held_ref[far, j], preferred_element_type=jnp.float32)
        out_ref[j, part] = ((prod + acc_ref[j, part]) * scale).astype(jnp.bfloat16)


def attend(edges, first, qkv_ref, key_ref, ctx_ref):
    heads = [pl.ds(h * HD, HD) for h in range(ctx_ref.shape[1] // HD)]
    for low, last in zip(edges, edges[1:]):
        here, step = pl.ds(low, last - low), last - low
        row = lax.broadcasted_iota(jnp.int32, (step, last), 0) + low
        col = lax.broadcasted_iota(jnp.int32, (step, last), 1)
        bias = jnp.where((row >= col) & (key_ref[0:1, pl.ds(0, last)] > 0.5), 0.0, -1e30)
        scores = [
            lax.dot_general(
                qkv_ref[0, here, lanes],
                qkv_ref[1, pl.ds(0, last), lanes],
                (((1,), (1,)), ((), ())),
                preferred_element_type=jnp.float32,
            )
            for lanes in heads
        ]
        scores = [x * (LOG2E / HD**0.5) + bias for x in scores]
        tops = [jnp.max(x, axis=1, keepdims=True) for x in scores]
        expo = [jnp.exp2(x - top) for x, top in zip(scores, tops)]
        sums = [jnp.sum(x, axis=1, keepdims=True) for x in expo]
        outs = [
            jnp.dot(x.astype(jnp.bfloat16), qkv_ref[2, pl.ds(0, last), lanes], preferred_element_type=jnp.float32)
            for x, lanes in zip(expo, heads)
        ]
        for lanes, out, total in zip(heads, outs, sums):
            ctx_ref[pl.ds(low - first, step), lanes] = (out / total).astype(jnp.bfloat16)


def put_columns(product, outs):
    half = outs[0].shape[1]
    for i, out_ref in enumerate(outs):
        out_ref[...] = product[:, i * half : (i + 1) * half].astype(out_ref.dtype)


def head_kernel(far, me_ref, top_ref, gain_ref, held_ref, acc_ref, ss_ref, img_ref, text_at_ref, img_at_ref, key_ref,
                w_out_ref, text_qkv_ref, qkv_ref, ctx_ref, left_ref, right_ref):
    rows = ctx_ref.shape[0]
    width = 2 * left_ref.shape[1]
    project_side(0, far, me_ref, top_ref, gain_ref, held_ref, acc_ref, ss_ref, text_qkv_ref)
    for j in range(3):
        qkv = jnp.dot(text_at_ref[:rows, :rows], text_qkv_ref[j], preferred_element_type=jnp.float32)
        qkv += jnp.dot(img_at_ref[:rows], img_ref[j], preferred_element_type=jnp.float32)
        qkv_ref[j] = qkv.astype(jnp.bfloat16)
    attend([0, rows], 0, qkv_ref, key_ref, ctx_ref)
    weight = cols_of(w_out_ref, me_ref[0] ^ far, width)
    put_columns(jnp.dot(ctx_ref[...], weight, preferred_element_type=jnp.float32), (left_ref, right_ref))


def head_part(far, me, top, gain, held, acc, ss, img, text_at, img_at, key_ok, w_out):
    width, cols = held.shape[2:]
    rows = top.shape[0]
    bf16 = jnp.bfloat16
    return pl.pallas_call(
        functools.partial(head_kernel, far),
        out_shape=(
            jax.ShapeDtypeStruct((3, rows, cols), bf16),
            jax.ShapeDtypeStruct((3, rows, cols), bf16),
            jax.ShapeDtypeStruct((rows, cols), bf16),
            jax.ShapeDtypeStruct((rows, width // 2), bf16),
            jax.ShapeDtypeStruct((rows, width // 2), bf16),
        ),
        in_specs=[pl.BlockSpec(memory_space=pltpu.SMEM)] + vmem_specs(10),
        out_specs=tuple(vmem_specs(5)),
        compiler_params=params(12),
        cost_estimate=TINY,
    )(me, top, gain, held, acc, ss, img, text_at, img_at, key_ok, w_out)


def tail_kernel(far, me_ref, bottom_ref, gain_ref, held_ref, acc_ref, ss_ref, img_ref, text_at_ref, img_at_ref,
                key_ref, w_out_ref, top_qkv_ref, head_qkv_ref, ctx_ref, left_ref, right_ref, text_qkv_ref, qkv_ref):
    first = top_qkv_ref.shape[1]
    length = text_at_ref.shape[0]
    width = 2 * left_ref.shape[1]
    project_side(1, far, me_ref, bottom_ref, gain_ref, held_ref, acc_ref, ss_ref, text_qkv_ref)
    for j in range(3):
        text_qkv_ref[j, :first] = top_qkv_ref[j]
        qkv_ref[j, :first] = head_qkv_ref[j]
        qkv = jnp.dot(text_at_ref[first:], text_qkv_ref[j], preferred_element_type=jnp.float32)
        qkv += jnp.dot(img_at_ref[first:], img_ref[j], preferred_element_type=jnp.float32)
        qkv_ref[j, first:] = qkv.astype(jnp.bfloat16)
    edges = [first] + [at for at in range(128, length, 128) if at > first] + [length]
    attend(edges, first, qkv_ref, key_ref, ctx_ref)
    weight = cols_of(w_out_ref, me_ref[0] ^ far, width)
    put_columns(jnp.dot(ctx_ref[...], weight, preferred_element_type=jnp.float32), (left_ref, right_ref))


def tail_part(far, me, bottom, gain, held, acc, ss, img, text_at, img_at, key_ok, w_out, top_qkv, head_qkv):
    width, cols = held.shape[2:]
    length, n_text = text_at.shape
    rows = length - top_qkv.shape[1]
    bf16 = jnp.bfloat16
    return pl.pallas_call(
        functools.partial(tail_kernel, far),
        out_shape=(
            jax.ShapeDtypeStruct((rows, cols), bf16),
            jax.ShapeDtypeStruct((rows, width // 2), bf16),
            jax.ShapeDtypeStruct((rows, width // 2), bf16),
        ),
        in_specs=[pl.BlockSpec(memory_space=pltpu.SMEM)] + vmem_specs(12),
        out_specs=tuple(vmem_specs(3)),
        scratch_shapes=[pltpu.VMEM((3, n_text, cols), bf16), pltpu.VMEM((3, length, cols), bf16)],
        compiler_params=params(12),
        cost_estimate=pl.CostEstimate(flops=10**10, bytes_accessed=0, transcendentals=0),
    )(me, bottom, gain, held, acc, ss, img, text_at, img_at, key_ok, w_out, top_qkv, head_qkv)


def out_kernel(away, me_ref, head_ref, tail_ref, w_ref, left_ref, right_ref):
    first = head_ref.shape[0]
    weight = cols_of(w_ref, me_ref[0] ^ away, 2 * left_ref.shape[1])
    for ctx_ref, rows in ((head_ref, slice(None, first)), (tail_ref, slice(first, None))):
        product = jnp.dot(ctx_ref[...], weight, preferred_element_type=jnp.float32)
        put_columns(product, (left_ref.at[rows], right_ref.at[rows]))


def out_part(away, me, head, tail, w, width, dtype=jnp.bfloat16):
    rows = head.shape[0] + tail.shape[0]
    return pl.pallas_call(
        functools.partial(out_kernel, away),
        out_shape=(jax.ShapeDtypeStruct((rows, width // 2), dtype),) * 2,
        in_specs=[pl.BlockSpec(memory_space=pltpu.SMEM)] + vmem_specs(3),
        out_specs=tuple(vmem_specs(2)),
        compiler_params=params(12),
        cost_estimate=pl.CostEstimate(flops=10**9, bytes_accessed=0, transcendentals=0),
    )(me, head, tail, w)


def sum_of(refs):
    return functools.reduce(lambda a, b: a + b, [ref[...].astype(jnp.float32) for ref in refs])


def first_kernel(n_left, base_ref, *refs):
    out_ref = refs[-1]
    half = base_ref.shape[1] // 2
    for side, terms in enumerate((refs[:n_left], refs[n_left:-1])):
        part = pl.ds(side * half, half)
        out_ref[:, part] = base_ref[:, part].astype(jnp.float32) + sum_of(terms)


def add_first(base, left, right):
    return pl.pallas_call(
        functools.partial(first_kernel, len(left)),
        out_shape=jax.ShapeDtypeStruct(base.shape, jnp.float32),
        in_specs=vmem_specs(1 + len(left) + len(right)),
        out_specs=pl.BlockSpec(memory_space=pltpu.VMEM),
        compiler_params=params(12),
        cost_estimate=TINY,
    )(base, *left, *right)


def last_kernel(n_left, base_ref, *refs):
    refs, (out_ref, tmp_ref, sem_ref) = refs[:-3], refs[-3:]
    half = base_ref.shape[1] // 2
    copies = []
    for side, terms in enumerate((refs[:n_left], refs[n_left:])):
        part = pl.ds(side * half, half)
        tmp_ref[:, part] = (base_ref[:, part] + sum_of(terms)).astype(tmp_ref.dtype)
        copy = pltpu.make_async_copy(tmp_ref.at[:, part], out_ref.at[:, part], sem_ref.at[side])
        copy.start()
        copies.append(copy)
    for copy in copies:
        copy.wait()


def add_last(base, left, right):
    return pl.pallas_call(
        functools.partial(last_kernel, len(left)),
        out_shape=jax.ShapeDtypeStruct(base.shape, jnp.bfloat16),
        in_specs=vmem_specs(1 + len(left) + len(right)),
        out_specs=pl.BlockSpec(memory_space=pl.ANY),
        scratch_shapes=[pltpu.VMEM(base.shape, jnp.bfloat16), pltpu.SemaphoreType.DMA((2,))],
        compiler_params=params(12),
        cost_estimate=TINY,
    )(base, *left, *right)


def scatter_terms(parts, got, n):
    acc = {s: [[parts[s][0]], [parts[s][1]]] for s in parts}
    far = n - 1
    acc[far ^ low_bit(far)][0].append(got[0])
    acc[far ^ high_bit(far)][1].append(got[1])
    early, late = [[], []], [[], []]
    for s in by_bits(n, reverse=True)[1:]:
        for side, bit in ((0, low_bit(s)), (1, high_bit(s))):
            terms = [t.astype(jnp.float32) for t in acc[s][side]]
            out = swap(functools.reduce(lambda a, b: a + b, terms).astype(jnp.bfloat16), bit)
            if s == bit:
                (early if len(terms) == 1 else late)[side].append(out)
            else:
                acc[s ^ bit][side].append(out)
    return early, late


def body(text, patches, grids, image_request, slot_start, vis_gain, dec_gain, w_qkv, w_out):
    n_req = lax.axis_size("req")
    n_ten = lax.axis_size("tensor")
    me_req = lax.axis_index("req")
    me_ten = lax.axis_index("tensor")
    img_dev, side, _, width = patches.shape
    half = side // 2
    region = half * half
    length = text.shape[0]
    w3 = jnp.transpose(w_qkv, (1, 0, 2))
    req_at = me_req.astype(jnp.int32)[None]
    ten_at = me_ten.astype(jnp.int32)[None]
    order = by_bits(n_ten)
    near_at, far = order[:-1], order[-1]

    n_rows = n_req * region
    n_img = round_up(n_rows + 1, 16)
    n_text = round_up(length - (n_rows if img_dev == n_req else 0), 32)
    even, odd, ctext, rtext, sel, table, key_ok, gains, vis_row = prepare(
        req_at, image_request, slot_start, grids, text, jnp.transpose(patches, (1, 2, 0, 3)), dec_gain, vis_gain, n_req,
        n_text, n_img
    )
    blocks = near_blocks(ctext, n_ten)

    pairs = mix_pairs(even, swap(odd, 1, "req"))
    received = [pairs[0]] + [swap(pairs[i], 2 * i, "req") for i in range(1, n_req // 2)]
    img_own = pack_images(received, vis_row, rtext, sel, region)
    img_blocks = [img_own] + [swap(img_own, s) for s in range(1, n_ten)]
    own, img_own = lax.optimization_barrier((ctext, img_own))
    acc, ss, held = own_part(ten_at, own, gains, w3)
    handed, img_own = lax.optimization_barrier((blocks, img_own))
    blocks = {**far_blocks(handed, n_ten), **blocks}

    near = [blocks[s] for s in near_at]
    acc, ss = near_part(near_at, ten_at, near, gains, held, acc, ss)
    table, acc = lax.optimization_barrier((table, acc))
    text_at, img_at, text_row = placement(table, region, length, n_text, n_img)
    img_blocks, text_at = lax.optimization_barrier((img_blocks, text_at))
    img_qkv, merged, w_out = image_part(ten_at, img_blocks, gains, sel, held, w_out, n_rows)

    shared = (gains, held, acc, ss, img_qkv, text_at, img_at, key_ok, w_out)
    top_qkv, head_qkv, head_ctx, *head_far = head_part(far, ten_at, blocks[far][0], *shared)
    tail_ctx, *tail_far = tail_part(far, ten_at, blocks[far][1], *shared, top_qkv, head_qkv)

    img_here = jnp.dot(img_at, merged, preferred_element_type=jnp.float32)
    x_in = (text.astype(jnp.float32) * text_row[:, :1] + img_here).astype(jnp.bfloat16)

    bits = (low_bit(far), high_bit(far))
    head_got = [swap(t, bit) for t, bit in zip(head_far, bits)]
    tail_got = [swap(t, bit) for t, bit in zip(tail_far, bits)]
    head_got, head_ctx, tail_ctx = lax.optimization_barrier((head_got, head_ctx, tail_ctx))
    parts = {}
    for s in reversed([0] + near_at):
        parts[s] = out_part(s, ten_at, head_ctx, tail_ctx, w_out, width, jnp.float32 if s == 0 else jnp.bfloat16)
    got = [jnp.concatenate(pair, axis=0) for pair in zip(head_got, tail_got)]
    early, late = scatter_terms(parts, got, n_ten)
    base = add_first(x_in, [parts[0][0]] + early[0], [parts[0][1]] + early[1])
    return add_last(base, late[0], late[1])


def solution(mesh):
    in_specs = (
        P("req", "tensor"),
        P("req", None, None, "tensor"),
        P(),
        P(),
        P(),
        P("tensor"),
        P(),
        P(None, None, "tensor"),
        P("tensor", None),
    )
    out_specs = P("req", "tensor")
    return jax.shard_map(body, mesh=mesh, in_specs=in_specs, out_specs=out_specs, check_vma=False)
```

```python
import functools

import jax
import jax.numpy as jnp
from jax import lax
from jax.experimental import pallas as pl
from jax.experimental.pallas import tpu as pltpu
from jax.sharding import PartitionSpec as P

D = 4096
HD = 128
EPS = 1e-05
LOG2E = 1.4426950408889634
TINY = pl.CostEstimate(flops=0, bytes_accessed=0, transcendentals=0)


def round_up(n, m):
    return -(-n // m) * m


def swap(x, s, axis="tensor"):
    n = lax.axis_size(axis)
    return lax.ppermute(x, axis, [(i, i ^ s) for i in range(n)])


def in_hbm(x):
    return pltpu.with_memory_space_constraint(x, pltpu.HBM)


def low_bit(s):
    return s & -s


def high_bit(s):
    return 1 << (s.bit_length() - 1)


def by_bits(n, reverse=False):
    return sorted(range(1, n), key=lambda s: (bin(s).count("1"), s), reverse=reverse)


def halves(block):
    if isinstance(block, tuple):
        return block
    half = block.shape[0] // 2
    return block[:half], block[half:]


def near_blocks(x, n):
    return {s: swap(x, s) for s in by_bits(n) if s & (s - 1) == 0}


def far_blocks(blocks, n):
    blocks = dict(blocks)
    for s in by_bits(n):
        if s not in blocks:
            low, high = low_bit(s), high_bit(s)
            blocks[s] = (swap(halves(blocks[s ^ low])[0], low), swap(halves(blocks[s ^ high])[1], high))
    return blocks


def vmem_specs(n):
    return [pl.BlockSpec(memory_space=pltpu.VMEM)] * n


def params(mib):
    return pltpu.CompilerParams(vmem_limit_bytes=mib * 1024 * 1024)


def fetch(pairs, sem_ref):
    copies = [pltpu.make_async_copy(src, dst, sem_ref.at[i]) for i, (src, dst) in enumerate(pairs)]
    for copy in copies:
        copy.start()
    return copies


NOWHERE = 1 << 20


def prep_kernel(n_req, me_ref, req_hbm, start_hbm, grid_hbm, text_hbm, x_hbm, dec_hbm, vis_hbm, *refs):
    (even_out, odd_out, ctext_out, rtext_out, sel_out, table_out, key_out, dec_out, vis_out, req_ref, start_ref, grid_ref,
     text_ref, x_ref, dec_ref, vis_ref, tmp_ref, sem_ref) = refs
    pairs = (
        (req_hbm, req_ref),
        (start_hbm, start_ref),
        (grid_hbm, grid_ref),
        (text_hbm, text_ref),
        (x_hbm, x_ref),
        (dec_hbm, dec_ref),
        (vis_hbm, vis_ref),
    )
    copies = fetch(pairs, sem_ref)
    side, img_dev = x_ref.shape[0], x_ref.shape[2]
    half = side // 2
    region = half * half
    n_img, n_text, length = sel_out.shape[0], ctext_out.shape[0], text_ref.shape[0]
    me = me_ref[0]
    for copy in copies[:3]:
        copy.wait()

    found = []
    for s in range(n_req):
        source = (me ^ s) * img_dev

        def one_image(k, found, source=source):
            hit = req_ref[source + k] == me
            values = (start_ref[source + k], grid_ref[0, source + k] // 2, grid_ref[1, source + k] // 2)
            return tuple(jnp.where(hit, new, old) for new, old in zip(values, found))

        none = (jnp.int32(NOWHERE), jnp.int32(0), jnp.int32(1))
        found.append(lax.fori_loop(0, img_dev, one_image, none, unroll=img_dev <= 8))

    spot = lax.broadcasted_iota(jnp.int32, (8, length), 1)
    before = jnp.zeros((8, length), jnp.int32)
    closed = jnp.zeros((8, length), jnp.int32)
    inside = jnp.zeros((8, length), jnp.int32)
    row = lax.broadcasted_iota(jnp.int32, (n_img, 128), 0)
    pos = jnp.full((n_img, 128), -1, jnp.int32)
    target = jnp.full((n_img, 128), -1, jnp.int32)
    line = lax.broadcasted_iota(jnp.int32, (n_req, 128), 0)
    table = jnp.zeros((n_req, 128), jnp.int32)
    for s, (start, high, wide) in enumerate(found):
        count = high * wide
        c = spot - start
        here = (c >= 0) & (c < region)
        before += jnp.clip(c, 0, region)
        inside = jnp.where(here, 1, inside)
        closed = jnp.where(here & (c >= count), 1, closed)
        c = row - s * region
        here = (c >= 0) & (c < region)
        pos = jnp.where(here, start + c, pos)
        cell = c
        for w in range(1, half):
            cell = jnp.where(wide == w, c // w * half + c % w, cell)
        target = jnp.where(here & (c < count), s * region + cell, target)
        table = jnp.where(line == s, start, table)
    table_out[...] = table
    key_out[...] = 1.0 - closed.astype(jnp.float32)
    rank = jnp.where(inside == 1, -1, spot - before)[0:1]
    gather = (lax.broadcasted_iota(jnp.int32, (n_text, length), 0) == rank).astype(jnp.bfloat16)
    stays = jnp.where(target >= 0, -1, pos)[:, :1]
    keep = (lax.broadcasted_iota(jnp.int32, (n_img, length), 1) == stays).astype(jnp.bfloat16)
    sel = lax.broadcasted_iota(jnp.int32, (n_img, n_img), 1) == target[:, :1]
    sel_out[...] = sel.astype(jnp.bfloat16)
    copies[3].wait()
    text = text_ref[...]
    ctext_out[...] = jnp.dot(gather, text, preferred_element_type=jnp.float32).astype(jnp.bfloat16)
    rtext_out[...] = jnp.dot(keep, text, preferred_element_type=jnp.float32).astype(jnp.bfloat16)

    for copy in copies[4:]:
        copy.wait()
    rows = lax.broadcasted_iota(jnp.int32, (n_req, img_dev), 0)
    cols = lax.broadcasted_iota(jnp.int32, (n_req, img_dev), 1)
    goal = jnp.full((n_req, img_dev), -1, jnp.int32)
    for k in range(img_dev):
        goal = jnp.where(cols == k, req_ref[me * img_dev + k] ^ me, goal)
    onehot = (rows == goal).astype(jnp.bfloat16)
    tmp_ref[...] = jnp.zeros_like(tmp_ref)
    for i in range(half):
        for j in range(half):
            total = x_ref[2 * i, 2 * j].astype(jnp.float32)
            for a, b in ((0, 1), (1, 0), (1, 1)):
                total += x_ref[2 * i + a, 2 * j + b].astype(jnp.float32)
            pooled = (total * 0.25).astype(jnp.bfloat16)
            tmp_ref[:, i * half + j, :] = jnp.dot(onehot, pooled, preferred_element_type=jnp.float32)
    for s in range(n_req):
        (even_out, odd_out)[s % 2][s // 2] = tmp_ref[s].astype(jnp.bfloat16)
    per = vis_ref.shape[0]
    for i in range(per):
        lanes = pl.ds(i * 128, 128)
        vis_out[:, lanes] = vis_ref[i : i + 1, :].astype(jnp.float32)
        for t in range(dec_out.shape[0]):
            at = t * per + i
            dec_out[t, :, lanes] = dec_ref[at : at + 1, :].astype(jnp.float32)


def prepare(me, image_request, slot_start, grids, text, patches, dec_gain, vis_gain, n_req, n_text, n_img):
    side, _, img_dev, width = patches.shape
    padded = round_up((side // 2) ** 2, 16)
    inputs = (
        image_request,
        slot_start,
        grids.T,
        text,
        patches,
        dec_gain.reshape(-1, 128),
        vis_gain.reshape(-1, 128),
    )
    bf16, f32 = jnp.bfloat16, jnp.float32
    outputs = [((n_req // 2, padded, width), bf16)] * 2 + [
        ((n_text, width), bf16),
        ((n_img, width), bf16),
        ((n_img, n_img), bf16),
        ((n_req, 128), jnp.int32),
        ((8, text.shape[0]), f32),
        ((dec_gain.size // width, 1, width), f32),
        ((1, width), f32),
    ]
    return pl.pallas_call(
        functools.partial(prep_kernel, n_req),
        out_shape=tuple(jax.ShapeDtypeStruct(shape, kind) for shape, kind in outputs),
        in_specs=[pl.BlockSpec(memory_space=pltpu.SMEM)] + [pl.BlockSpec(memory_space=pltpu.HBM)] * len(inputs),
        out_specs=tuple(vmem_specs(len(outputs))),
        scratch_shapes=[pltpu.SMEM(x.shape, jnp.int32) for x in inputs[:3]]
        + [pltpu.VMEM(x.shape, x.dtype) for x in inputs[3:]]
        + [pltpu.VMEM((n_req, padded, width), f32), pltpu.SemaphoreType.DMA((len(inputs),))],
        compiler_params=params(12),
        cost_estimate=TINY,
    )(me, *[in_hbm(x) for x in inputs])


def mix_kernel(even_ref, odd_ref, *outs):
    rows = even_ref.shape[1]
    for i, out_ref in enumerate(outs):
        out_ref[:rows] = even_ref[i]
        out_ref[rows:] = odd_ref[i]


def mix_pairs(even, odd):
    n, rows, width = even.shape
    return pl.pallas_call(
        mix_kernel,
        out_shape=(jax.ShapeDtypeStruct((2 * rows, width), jnp.bfloat16),) * n,
        in_specs=vmem_specs(2),
        out_specs=tuple(vmem_specs(n)),
        compiler_params=params(4),
        cost_estimate=TINY,
    )(even, odd)


def pack_kernel(region, gain_ref, rtext_ref, sel_ref, *refs):
    recs, (out_ref, tmp_ref) = refs[:-2], refs[-2:]
    done = 0
    for rec_ref in recs:
        rows = rec_ref.shape[0] // 2
        pair = rec_ref[...].astype(jnp.float32)
        for first in (0, rows):
            tmp_ref[done : done + region] = pair[first : first + region]
            done += region
    rest = tmp_ref.shape[0] - done
    tmp_ref[done:] = jnp.zeros((rest, tmp_ref.shape[1]), jnp.float32)
    picked = jnp.dot(sel_ref[...], tmp_ref[...].astype(jnp.bfloat16), preferred_element_type=jnp.float32)
    tmp_ref[...] = picked + rtext_ref[...].astype(jnp.float32)
    tmp_ref[done:] = jnp.broadcast_to(gain_ref[0:1, :], (rest, gain_ref.shape[1]))
    out_ref[...] = tmp_ref[...].astype(jnp.bfloat16)


def pack_images(received, gain, rtext, sel, region):
    n_img, width = rtext.shape
    return pl.pallas_call(
        functools.partial(pack_kernel, region),
        out_shape=jax.ShapeDtypeStruct((n_img, width), jnp.bfloat16),
        in_specs=vmem_specs(3 + len(received)),
        out_specs=pl.BlockSpec(memory_space=pltpu.VMEM),
        scratch_shapes=[pltpu.VMEM((n_img, width), jnp.float32)],
        compiler_params=params(4),
        cost_estimate=TINY,
    )(gain, rtext, sel, *received)


def place_kernel(region, table_ref, text_at_ref, img_at_ref, text_row_ref):
    length, n_text = text_at_ref.shape
    spot = lax.broadcasted_iota(jnp.int32, (length, 128), 0)
    before = jnp.zeros((length, 128), jnp.int32)
    at = jnp.full((length, 128), -1, jnp.int32)
    for s in range(table_ref.shape[0]):
        c = spot - table_ref[s : s + 1, :]
        before += jnp.clip(c, 0, region)
        at = jnp.where((c >= 0) & (c < region), s * region + c, at)
    text_row_ref[...] = jnp.where(at < 0, 1.0, 0.0)
    rank = jnp.where(at < 0, spot - before, -1)[:, :1]
    text_at_ref[...] = (lax.broadcasted_iota(jnp.int32, (length, n_text), 1) == rank).astype(jnp.bfloat16)
    lane = lax.broadcasted_iota(jnp.int32, img_at_ref.shape, 1)
    img_at_ref[...] = (lane == at[:, :1]).astype(jnp.bfloat16)


def placement(table, region, length, n_text, n_img):
    return pl.pallas_call(
        functools.partial(place_kernel, region),
        out_shape=(
            jax.ShapeDtypeStruct((length, n_text), jnp.bfloat16),
            jax.ShapeDtypeStruct((length, n_img), jnp.bfloat16),
            jax.ShapeDtypeStruct((length, 128), jnp.float32),
        ),
        in_specs=vmem_specs(1),
        out_specs=tuple(vmem_specs(3)),
        compiler_params=params(8),
        cost_estimate=TINY,
    )(table)


def cols_of(ref, owner, width):
    return ref[:, pl.ds(pl.multiple_of(owner * width, width), width)]


def scale_rows(x, gain):
    xf = x.astype(jnp.float32)
    return (xf * gain).astype(jnp.bfloat16), jnp.sum(xf * xf, axis=1, keepdims=True)


def own_kernel(me_ref, x_ref, gain_ref, w_ref, acc_ref, ss_ref, held_ref, sem_ref):
    n_ten, _, width, _ = held_ref.shape
    half = x_ref.shape[0] // 2
    copies = []
    for s in range(n_ten):
        rows = pl.ds(pl.multiple_of((me_ref[0] ^ s) * width, width), width)
        copies += [pltpu.make_async_copy(w_ref.at[j, rows], held_ref.at[s, j], sem_ref.at[s, j]) for j in range(3)]
    for copy in copies:
        copy.start()
    scaled = []
    for side in range(2):
        rows = pl.ds(side * half, half)
        x, total = scale_rows(x_ref[rows], gain_ref[me_ref[0]])
        scaled.append(x)
        ss_ref[rows] = jnp.broadcast_to(total, (half, 128))
    for j in range(3):
        copies[j].wait()
        for side in range(2):
            acc_ref[j, pl.ds(side * half, half)] = jnp.dot(
                scaled[side], held_ref[0, j], preferred_element_type=jnp.float32
            )
    for copy in copies[3:]:
        copy.wait()


def own_part(me, x, gain, w):
    rows, width = x.shape
    n_ten, cols = gain.shape[0], w.shape[2]
    return pl.pallas_call(
        own_kernel,
        out_shape=(
            jax.ShapeDtypeStruct((3, rows, cols), jnp.float32),
            jax.ShapeDtypeStruct((rows, 128), jnp.float32),
            pltpu.VMEM((n_ten, 3, width, cols), w.dtype),
        ),
        in_specs=[pl.BlockSpec(memory_space=pltpu.SMEM)] + vmem_specs(2) + [pl.BlockSpec(memory_space=pltpu.HBM)],
        out_specs=tuple(vmem_specs(3)),
        scratch_shapes=[pltpu.SemaphoreType.DMA((n_ten, 3))],
        compiler_params=params(12),
        cost_estimate=TINY,
    )(me, x, gain, in_hbm(w))


def near_kernel(near, pieces, me_ref, *refs):
    n_x = sum(pieces)
    x_refs, refs = list(refs[:n_x]), refs[n_x:]
    gain_ref, held_ref, acc_in, ss_in, acc_ref, ss_ref = refs
    half = acc_ref.shape[1] // 2
    views = []
    for n in pieces:
        mine, x_refs = x_refs[:n], x_refs[n:]
        views.append([mine[0].at[pl.ds(side * half, half)] if n == 1 else mine[side] for side in range(2)])
    scaled = {}
    for side in range(2):
        rows = pl.ds(side * half, half)
        total = ss_in[rows]
        for b, s in enumerate(near):
            scaled[side, b], part = scale_rows(views[b][side][...], gain_ref[me_ref[0] ^ s])
            total += part
        ss_ref[rows] = total
    for j in range(3):
        for side in range(2):
            rows = pl.ds(side * half, half)
            acc = acc_in[j, rows]
            for b, s in enumerate(near):
                acc += jnp.dot(scaled[side, b], held_ref[s, j], preferred_element_type=jnp.float32)
            acc_ref[j, rows] = acc


def near_part(near, me, blocks, gain, held, acc, ss):
    blocks = [b if isinstance(b, tuple) else (b,) for b in blocks]
    pieces = [len(b) for b in blocks]
    return pl.pallas_call(
        functools.partial(near_kernel, near, pieces),
        out_shape=(
            jax.ShapeDtypeStruct(acc.shape, jnp.float32),
            jax.ShapeDtypeStruct(ss.shape, jnp.float32),
        ),
        in_specs=[pl.BlockSpec(memory_space=pltpu.SMEM)]
        + vmem_specs(sum(pieces) + 4),
        out_specs=tuple(vmem_specs(2)),
        compiler_params=params(12),
        cost_estimate=pl.CostEstimate(flops=10**11, bytes_accessed=0, transcendentals=0),
    )(me, *[h for b in blocks for h in b], gain, held, acc, ss)


def image_kernel(n_rows, n_blk, me_ref, *refs):
    x_refs, refs = refs[:n_blk], refs[n_blk:]
    gain_ref, sel_ref, held_ref, w_out_ref, qkv_ref, own_ref, w_out_held, sem_ref = refs
    copy = pltpu.make_async_copy(w_out_ref, w_out_held, sem_ref)
    copy.start()
    is_img = jnp.sum(sel_ref[...].astype(jnp.float32), axis=1, keepdims=True) > 0.5
    total = 0.0
    for s in range(n_blk):
        xf = x_refs[s][...].astype(jnp.float32)
        total += jnp.sum(xf * xf, axis=1, keepdims=True)
    scale = lax.rsqrt(total / D + EPS)
    total = 0.0
    scaled = []
    for s in range(n_blk):
        xf = x_refs[s][...].astype(jnp.float32)
        merged = jnp.where(is_img, xf * scale * xf[n_rows : n_rows + 1], xf).astype(jnp.bfloat16)
        if s == 0:
            own_ref[...] = merged
        mf = merged.astype(jnp.float32)
        total += jnp.sum(mf * mf, axis=1, keepdims=True)
        scaled.append((mf * gain_ref[me_ref[0] ^ s]).astype(jnp.bfloat16))
    scale = lax.rsqrt(total / D + EPS)
    for j in range(3):
        acc = 0.0
        for s in range(n_blk):
            acc += jnp.dot(scaled[s], held_ref[s, j], preferred_element_type=jnp.float32)
        qkv_ref[j] = (acc * scale).astype(jnp.bfloat16)
    copy.wait()


def image_part(me, blocks, gain, sel, held, w_out, n_rows):
    n_img, width = blocks[0].shape
    return pl.pallas_call(
        functools.partial(image_kernel, n_rows, len(blocks)),
        out_shape=(
            jax.ShapeDtypeStruct((3, n_img, held.shape[3]), jnp.bfloat16),
            jax.ShapeDtypeStruct((n_img, width), jnp.bfloat16),
            pltpu.VMEM(w_out.shape, w_out.dtype),
        ),
        in_specs=[pl.BlockSpec(memory_space=pltpu.SMEM)]
        + vmem_specs(len(blocks) + 3)
        + [pl.BlockSpec(memory_space=pltpu.HBM)],
        out_specs=tuple(vmem_specs(3)),
        scratch_shapes=[pltpu.SemaphoreType.DMA],
        compiler_params=params(12),
        cost_estimate=pl.CostEstimate(flops=0, bytes_accessed=0, transcendentals=0),
    )(me, *blocks, gain, sel, held, in_hbm(w_out))


def project_side(side, far, me_ref, x_ref, gain_ref, held_ref, acc_ref, ss_ref, out_ref):
    half = x_ref.shape[0]
    part = pl.ds(side * half, half)
    x, total = scale_rows(x_ref[...], gain_ref[me_ref[0] ^ far])
    scale = lax.rsqrt((ss_ref[part] + total) / D + EPS)[:, :1]
    for j in range(3):
        prod = jnp.dot(x, held_ref[far, j], preferred_element_type=jnp.float32)
        out_ref[j, part] = ((prod + acc_ref[j, part]) * scale).astype(jnp.bfloat16)


def attend(edges, first, qkv_ref, key_ref, ctx_ref):
    heads = [pl.ds(h * HD, HD) for h in range(ctx_ref.shape[1] // HD)]
    for low, last in zip(edges, edges[1:]):
        here, step = pl.ds(low, last - low), last - low
        row = lax.broadcasted_iota(jnp.int32, (step, last), 0) + low
        col = lax.broadcasted_iota(jnp.int32, (step, last), 1)
        bias = jnp.where((row >= col) & (key_ref[0:1, pl.ds(0, last)] > 0.5), 0.0, -1e30)
        scores = [
            lax.dot_general(
                qkv_ref[0, here, lanes],
                qkv_ref[1, pl.ds(0, last), lanes],
                (((1,), (1,)), ((), ())),
                preferred_element_type=jnp.float32,
            )
            for lanes in heads
        ]
        scores = [x * (LOG2E / HD**0.5) + bias for x in scores]
        tops = [jnp.max(x, axis=1, keepdims=True) for x in scores]
        expo = [jnp.exp2(x - top) for x, top in zip(scores, tops)]
        sums = [jnp.sum(x, axis=1, keepdims=True) for x in expo]
        outs = [
            jnp.dot(x.astype(jnp.bfloat16), qkv_ref[2, pl.ds(0, last), lanes], preferred_element_type=jnp.float32)
            for x, lanes in zip(expo, heads)
        ]
        for lanes, out, total in zip(heads, outs, sums):
            ctx_ref[pl.ds(low - first, step), lanes] = (out / total).astype(jnp.bfloat16)


def put_columns(product, outs):
    half = outs[0].shape[1]
    for i, out_ref in enumerate(outs):
        out_ref[...] = product[:, i * half : (i + 1) * half].astype(out_ref.dtype)


def head_kernel(far, me_ref, top_ref, gain_ref, held_ref, acc_ref, ss_ref, img_ref, text_at_ref, img_at_ref, key_ref,
                w_out_ref, text_qkv_ref, qkv_ref, ctx_ref, left_ref, right_ref):
    rows = ctx_ref.shape[0]
    width = 2 * left_ref.shape[1]
    project_side(0, far, me_ref, top_ref, gain_ref, held_ref, acc_ref, ss_ref, text_qkv_ref)
    for j in range(3):
        qkv = jnp.dot(text_at_ref[:rows, :rows], text_qkv_ref[j], preferred_element_type=jnp.float32)
        qkv += jnp.dot(img_at_ref[:rows], img_ref[j], preferred_element_type=jnp.float32)
        qkv_ref[j] = qkv.astype(jnp.bfloat16)
    attend([0, rows], 0, qkv_ref, key_ref, ctx_ref)
    weight = cols_of(w_out_ref, me_ref[0] ^ far, width)
    put_columns(jnp.dot(ctx_ref[...], weight, preferred_element_type=jnp.float32), (left_ref, right_ref))


def head_part(far, me, top, gain, held, acc, ss, img, text_at, img_at, key_ok, w_out):
    width, cols = held.shape[2:]
    rows = top.shape[0]
    bf16 = jnp.bfloat16
    return pl.pallas_call(
        functools.partial(head_kernel, far),
        out_shape=(
            jax.ShapeDtypeStruct((3, rows, cols), bf16),
            jax.ShapeDtypeStruct((3, rows, cols), bf16),
            jax.ShapeDtypeStruct((rows, cols), bf16),
            jax.ShapeDtypeStruct((rows, width // 2), bf16),
            jax.ShapeDtypeStruct((rows, width // 2), bf16),
        ),
        in_specs=[pl.BlockSpec(memory_space=pltpu.SMEM)] + vmem_specs(10),
        out_specs=tuple(vmem_specs(5)),
        compiler_params=params(12),
        cost_estimate=TINY,
    )(me, top, gain, held, acc, ss, img, text_at, img_at, key_ok, w_out)


def tail_kernel(far, me_ref, bottom_ref, gain_ref, held_ref, acc_ref, ss_ref, img_ref, text_at_ref, img_at_ref,
                key_ref, w_out_ref, top_qkv_ref, head_qkv_ref, ctx_ref, left_ref, right_ref, text_qkv_ref, qkv_ref):
    first = top_qkv_ref.shape[1]
    length = text_at_ref.shape[0]
    width = 2 * left_ref.shape[1]
    project_side(1, far, me_ref, bottom_ref, gain_ref, held_ref, acc_ref, ss_ref, text_qkv_ref)
    for j in range(3):
        text_qkv_ref[j, :first] = top_qkv_ref[j]
        qkv_ref[j, :first] = head_qkv_ref[j]
        qkv = jnp.dot(text_at_ref[first:], text_qkv_ref[j], preferred_element_type=jnp.float32)
        qkv += jnp.dot(img_at_ref[first:], img_ref[j], preferred_element_type=jnp.float32)
        qkv_ref[j, first:] = qkv.astype(jnp.bfloat16)
    edges = [first] + [at for at in range(128, length, 128) if at > first] + [length]
    attend(edges, first, qkv_ref, key_ref, ctx_ref)
    weight = cols_of(w_out_ref, me_ref[0] ^ far, width)
    put_columns(jnp.dot(ctx_ref[...], weight, preferred_element_type=jnp.float32), (left_ref, right_ref))


def tail_part(far, me, bottom, gain, held, acc, ss, img, text_at, img_at, key_ok, w_out, top_qkv, head_qkv):
    width, cols = held.shape[2:]
    length, n_text = text_at.shape
    rows = length - top_qkv.shape[1]
    bf16 = jnp.bfloat16
    return pl.pallas_call(
        functools.partial(tail_kernel, far),
        out_shape=(
            jax.ShapeDtypeStruct((rows, cols), bf16),
            jax.ShapeDtypeStruct((rows, width // 2), bf16),
            jax.ShapeDtypeStruct((rows, width // 2), bf16),
        ),
        in_specs=[pl.BlockSpec(memory_space=pltpu.SMEM)] + vmem_specs(12),
        out_specs=tuple(vmem_specs(3)),
        scratch_shapes=[pltpu.VMEM((3, n_text, cols), bf16), pltpu.VMEM((3, length, cols), bf16)],
        compiler_params=params(12),
        cost_estimate=pl.CostEstimate(flops=10**10, bytes_accessed=0, transcendentals=0),
    )(me, bottom, gain, held, acc, ss, img, text_at, img_at, key_ok, w_out, top_qkv, head_qkv)


def out_kernel(away, me_ref, head_ref, tail_ref, w_ref, left_ref, right_ref):
    first = head_ref.shape[0]
    weight = cols_of(w_ref, me_ref[0] ^ away, 2 * left_ref.shape[1])
    for ctx_ref, rows in ((head_ref, slice(None, first)), (tail_ref, slice(first, None))):
        product = jnp.dot(ctx_ref[...], weight, preferred_element_type=jnp.float32)
        put_columns(product, (left_ref.at[rows], right_ref.at[rows]))


def out_part(away, me, head, tail, w, width, dtype=jnp.bfloat16):
    rows = head.shape[0] + tail.shape[0]
    return pl.pallas_call(
        functools.partial(out_kernel, away),
        out_shape=(jax.ShapeDtypeStruct((rows, width // 2), dtype),) * 2,
        in_specs=[pl.BlockSpec(memory_space=pltpu.SMEM)] + vmem_specs(3),
        out_specs=tuple(vmem_specs(2)),
        compiler_params=params(12),
        cost_estimate=pl.CostEstimate(flops=10**9, bytes_accessed=0, transcendentals=0),
    )(me, head, tail, w)


def sum_of(refs):
    return functools.reduce(lambda a, b: a + b, [ref[...].astype(jnp.float32) for ref in refs])


def first_kernel(n_left, base_ref, *refs):
    out_ref = refs[-1]
    half = base_ref.shape[1] // 2
    for side, terms in enumerate((refs[:n_left], refs[n_left:-1])):
        part = pl.ds(side * half, half)
        out_ref[:, part] = base_ref[:, part].astype(jnp.float32) + sum_of(terms)


def add_first(base, left, right):
    return pl.pallas_call(
        functools.partial(first_kernel, len(left)),
        out_shape=jax.ShapeDtypeStruct(base.shape, jnp.float32),
        in_specs=vmem_specs(1 + len(left) + len(right)),
        out_specs=pl.BlockSpec(memory_space=pltpu.VMEM),
        compiler_params=params(12),
        cost_estimate=TINY,
    )(base, *left, *right)


def last_kernel(n_left, base_ref, *refs):
    refs, (out_ref, tmp_ref, sem_ref) = refs[:-3], refs[-3:]
    half = base_ref.shape[1] // 2
    copies = []
    for side, terms in enumerate((refs[:n_left], refs[n_left:])):
        part = pl.ds(side * half, half)
        tmp_ref[:, part] = (base_ref[:, part] + sum_of(terms)).astype(tmp_ref.dtype)
        copy = pltpu.make_async_copy(tmp_ref.at[:, part], out_ref.at[:, part], sem_ref.at[side])
        copy.start()
        copies.append(copy)
    for copy in copies:
        copy.wait()


def add_last(base, left, right):
    return pl.pallas_call(
        functools.partial(last_kernel, len(left)),
        out_shape=jax.ShapeDtypeStruct(base.shape, jnp.bfloat16),
        in_specs=vmem_specs(1 + len(left) + len(right)),
        out_specs=pl.BlockSpec(memory_space=pl.ANY),
        scratch_shapes=[pltpu.VMEM(base.shape, jnp.bfloat16), pltpu.SemaphoreType.DMA((2,))],
        compiler_params=params(12),
        cost_estimate=TINY,
    )(base, *left, *right)


def scatter_terms(parts, got, n):
    acc = {s: [[parts[s][0]], [parts[s][1]]] for s in parts}
    far = n - 1
    acc[far ^ low_bit(far)][0].append(got[0])
    acc[far ^ high_bit(far)][1].append(got[1])
    early, late = [[], []], [[], []]
    for s in by_bits(n, reverse=True)[1:]:
        for side, bit in ((0, low_bit(s)), (1, high_bit(s))):
            terms = [t.astype(jnp.float32) for t in acc[s][side]]
            out = swap(functools.reduce(lambda a, b: a + b, terms).astype(jnp.bfloat16), bit)
            if s == bit:
                (early if len(terms) == 1 else late)[side].append(out)
            else:
                acc[s ^ bit][side].append(out)
    return early, late


def body(text, patches, grids, image_request, slot_start, vis_gain, dec_gain, w_qkv, w_out):
    n_req = lax.axis_size("req")
    n_ten = lax.axis_size("tensor")
    me_req = lax.axis_index("req")
    me_ten = lax.axis_index("tensor")
    img_dev, side, _, width = patches.shape
    half = side // 2
    region = half * half
    length = text.shape[0]
    w3 = jnp.transpose(w_qkv, (1, 0, 2))
    req_at = me_req.astype(jnp.int32)[None]
    ten_at = me_ten.astype(jnp.int32)[None]
    order = by_bits(n_ten)
    near_at, far = order[:-1], order[-1]

    n_rows = n_req * region
    n_img = round_up(n_rows + 1, 16)
    n_text = round_up(length - (n_rows if img_dev == n_req else 0), 32)
    even, odd, ctext, rtext, sel, table, key_ok, gains, vis_row = prepare(
        req_at, image_request, slot_start, grids, text, jnp.transpose(patches, (1, 2, 0, 3)), dec_gain, vis_gain, n_req,
        n_text, n_img
    )
    blocks = near_blocks(ctext, n_ten)

    pairs = mix_pairs(even, swap(odd, 1, "req"))
    received = [pairs[0]] + [swap(pairs[i], 2 * i, "req") for i in range(1, n_req // 2)]
    img_own = pack_images(received, vis_row, rtext, sel, region)
    img_blocks = [img_own] + [swap(img_own, s) for s in range(1, n_ten)]
    own, img_own = lax.optimization_barrier((ctext, img_own))
    acc, ss, held = own_part(ten_at, own, gains, w3)
    handed, img_own = lax.optimization_barrier((blocks, img_own))
    blocks = {**far_blocks(handed, n_ten), **blocks}

    near = [blocks[s] for s in near_at]
    acc, ss = near_part(near_at, ten_at, near, gains, held, acc, ss)
    table, acc = lax.optimization_barrier((table, acc))
    text_at, img_at, text_row = placement(table, region, length, n_text, n_img)
    img_blocks, text_at = lax.optimization_barrier((img_blocks, text_at))
    img_qkv, merged, w_out = image_part(ten_at, img_blocks, gains, sel, held, w_out, n_rows)

    shared = (gains, held, acc, ss, img_qkv, text_at, img_at, key_ok, w_out)
    top_qkv, head_qkv, head_ctx, *head_far = head_part(far, ten_at, blocks[far][0], *shared)
    tail_ctx, *tail_far = tail_part(far, ten_at, blocks[far][1], *shared, top_qkv, head_qkv)

    img_here = jnp.dot(img_at, merged, preferred_element_type=jnp.float32)
    x_in = (text.astype(jnp.float32) * text_row[:, :1] + img_here).astype(jnp.bfloat16)

    bits = (low_bit(far), high_bit(far))
    head_got = [swap(t, bit) for t, bit in zip(head_far, bits)]
    tail_got = [swap(t, bit) for t, bit in zip(tail_far, bits)]
    head_got, head_ctx, tail_ctx = lax.optimization_barrier((head_got, head_ctx, tail_ctx))
    parts = {}
    for s in reversed([0] + near_at):
        parts[s] = out_part(s, ten_at, head_ctx, tail_ctx, w_out, width, jnp.float32 if s == 0 else jnp.bfloat16)
    got = [jnp.concatenate(pair, axis=0) for pair in zip(head_got, tail_got)]
    early, late = scatter_terms(parts, got, n_ten)
    base = add_first(x_in, [parts[0][0]] + early[0], [parts[0][1]] + early[1])
    return add_last(base, late[0], late[1])


def solution(mesh):
    in_specs = (
        P("req", "tensor"),
        P("req", None, None, "tensor"),
        P(),
        P(),
        P(),
        P("tensor"),
        P(),
        P(None, None, "tensor"),
        P("tensor", None),
    )
    out_specs = P("req", "tensor")
    return jax.shard_map(body, mesh=mesh, in_specs=in_specs, out_specs=out_specs, check_vma=False)
```

```python
import functools

import jax
import jax.numpy as jnp
from jax import lax
from jax.experimental import pallas as pl
from jax.experimental.pallas import tpu as pltpu
from jax.sharding import PartitionSpec as P

D = 4096
HD = 128
EPS = 1e-05
LOG2E = 1.4426950408889634
TINY = pl.CostEstimate(flops=0, bytes_accessed=0, transcendentals=0)


def round_up(n, m):
    return -(-n // m) * m


def swap(x, s, axis="tensor"):
    n = lax.axis_size(axis)
    return lax.ppermute(x, axis, [(i, i ^ s) for i in range(n)])


def in_hbm(x):
    return pltpu.with_memory_space_constraint(x, pltpu.HBM)


def low_bit(s):
    return s & -s


def high_bit(s):
    return 1 << (s.bit_length() - 1)


def by_bits(n, reverse=False):
    return sorted(range(1, n), key=lambda s: (bin(s).count("1"), s), reverse=reverse)


def halves(block):
    if isinstance(block, tuple):
        return block
    half = block.shape[0] // 2
    return block[:half], block[half:]


def near_blocks(x, n):
    return {s: swap(x, s) for s in by_bits(n) if s & (s - 1) == 0}


def far_blocks(blocks, n):
    blocks = dict(blocks)
    for s in by_bits(n):
        if s not in blocks:
            low, high = low_bit(s), high_bit(s)
            blocks[s] = (swap(halves(blocks[s ^ low])[0], low), swap(halves(blocks[s ^ high])[1], high))
    return blocks


def vmem_specs(n):
    return [pl.BlockSpec(memory_space=pltpu.VMEM)] * n


def params(mib):
    return pltpu.CompilerParams(vmem_limit_bytes=mib * 1024 * 1024)


def fetch(pairs, sem_ref):
    copies = [pltpu.make_async_copy(src, dst, sem_ref.at[i]) for i, (src, dst) in enumerate(pairs)]
    for copy in copies:
        copy.start()
    return copies


NOWHERE = 1 << 20


def find_images(n_req, img_dev, me, req_ref, start_ref, grid_ref=None):
    found = []
    for s in range(n_req):
        source = (me ^ s) * img_dev

        def one_image(k, found, source=source):
            hit = req_ref[source + k] == me
            values = (start_ref[source + k],)
            if grid_ref is not None:
                values += (grid_ref[0, source + k] // 2, grid_ref[1, source + k] // 2)
            return tuple(jnp.where(hit, new, old) for new, old in zip(values, found))

        none = (jnp.int32(NOWHERE), jnp.int32(0), jnp.int32(1))[: 1 if grid_ref is None else 3]
        found.append(lax.fori_loop(0, img_dev, one_image, none, unroll=img_dev <= 8))
    return found


def text_kernel(n_req, region, me_ref, req_hbm, start_hbm, text_hbm, ctext_out, req_ref, start_ref, text_ref, sem_ref):
    copies = fetch(((req_hbm, req_ref), (start_hbm, start_ref), (text_hbm, text_ref)), sem_ref)
    n_text, length = ctext_out.shape[0], text_ref.shape[0]
    spot = lax.broadcasted_iota(jnp.int32, (8, length), 1)
    before = jnp.zeros((8, length), jnp.int32)
    inside = jnp.zeros((8, length), jnp.int32)
    copies[0].wait()
    copies[1].wait()
    for (start,) in find_images(n_req, req_ref.shape[0] // n_req, me_ref[0], req_ref, start_ref):
        c = spot - start
        before += jnp.clip(c, 0, region)
        inside = jnp.where((c >= 0) & (c < region), 1, inside)
    rank = jnp.where(inside == 1, -1, spot - before)[0:1]
    gather = (lax.broadcasted_iota(jnp.int32, (n_text, length), 0) == rank).astype(jnp.bfloat16)
    copies[2].wait()
    ctext_out[...] = jnp.dot(gather, text_ref[...], preferred_element_type=jnp.float32).astype(jnp.bfloat16)


def gather_text(me, image_request, slot_start, text, n_req, region, n_text):
    inputs = (image_request, slot_start, text)
    return pl.pallas_call(
        functools.partial(text_kernel, n_req, region),
        out_shape=jax.ShapeDtypeStruct((n_text, text.shape[1]), text.dtype),
        in_specs=[pl.BlockSpec(memory_space=pltpu.SMEM)] + [pl.BlockSpec(memory_space=pltpu.HBM)] * 3,
        out_specs=pl.BlockSpec(memory_space=pltpu.VMEM),
        scratch_shapes=[pltpu.SMEM(x.shape, jnp.int32) for x in inputs[:2]]
        + [pltpu.VMEM(text.shape, text.dtype), pltpu.SemaphoreType.DMA((3,))],
        compiler_params=params(8),
        cost_estimate=TINY,
    )(me, *[in_hbm(x) for x in inputs])


def prep_kernel(n_req, me_ref, req_hbm, start_hbm, grid_hbm, text_hbm, x_hbm, dec_hbm, vis_hbm, *refs):
    (even_out, odd_out, rtext_out, sel_out, table_out, key_out, dec_out, vis_out, req_ref, start_ref, grid_ref,
     text_ref, x_ref, dec_ref, vis_ref, tmp_ref, sem_ref) = refs
    pairs = (
        (req_hbm, req_ref),
        (start_hbm, start_ref),
        (grid_hbm, grid_ref),
        (x_hbm, x_ref),
        (text_hbm, text_ref),
        (dec_hbm, dec_ref),
        (vis_hbm, vis_ref),
    )
    copies = fetch(pairs, sem_ref)
    side, img_dev = x_ref.shape[0], x_ref.shape[2]
    half = side // 2
    region = half * half
    n_img, length = sel_out.shape[0], text_ref.shape[0]
    me = me_ref[0]
    tmp_ref[...] = jnp.zeros_like(tmp_ref)
    for copy in copies[:3]:
        copy.wait()

    spot = lax.broadcasted_iota(jnp.int32, (8, length), 1)
    closed = jnp.zeros((8, length), jnp.int32)
    row = lax.broadcasted_iota(jnp.int32, (n_img, 128), 0)
    pos = jnp.full((n_img, 128), -1, jnp.int32)
    target = jnp.full((n_img, 128), -1, jnp.int32)
    line = lax.broadcasted_iota(jnp.int32, (n_req, 128), 0)
    table = jnp.zeros((n_req, 128), jnp.int32)
    for s, (start, high, wide) in enumerate(find_images(n_req, img_dev, me, req_ref, start_ref, grid_ref)):
        count = high * wide
        c = spot - start
        closed = jnp.where((c >= count) & (c < region) & (c >= 0), 1, closed)
        c = row - s * region
        here = (c >= 0) & (c < region)
        pos = jnp.where(here, start + c, pos)
        cell = c
        for w in range(1, half):
            cell = jnp.where(wide == w, c // w * half + c % w, cell)
        target = jnp.where(here & (c < count), s * region + cell, target)
        table = jnp.where(line == s, start, table)
    table_out[...] = table
    key_out[...] = 1.0 - closed.astype(jnp.float32)
    stays = jnp.where(target >= 0, -1, pos)[:, :1]
    keep = (lax.broadcasted_iota(jnp.int32, (n_img, length), 1) == stays).astype(jnp.bfloat16)
    sel = lax.broadcasted_iota(jnp.int32, (n_img, n_img), 1) == target[:, :1]
    sel_out[...] = sel.astype(jnp.bfloat16)
    rows = lax.broadcasted_iota(jnp.int32, (n_req, img_dev), 0)
    cols = lax.broadcasted_iota(jnp.int32, (n_req, img_dev), 1)
    goal = jnp.full((n_req, img_dev), -1, jnp.int32)
    for k in range(img_dev):
        goal = jnp.where(cols == k, req_ref[me * img_dev + k] ^ me, goal)
    onehot = (rows == goal).astype(jnp.bfloat16)

    for copy in copies[3:]:
        copy.wait()
    rtext_out[...] = jnp.dot(keep, text_ref[...], preferred_element_type=jnp.float32).astype(jnp.bfloat16)
    for i in range(half):
        for j in range(half):
            total = x_ref[2 * i, 2 * j].astype(jnp.float32)
            for a, b in ((0, 1), (1, 0), (1, 1)):
                total += x_ref[2 * i + a, 2 * j + b].astype(jnp.float32)
            pooled = (total * 0.25).astype(jnp.bfloat16)
            tmp_ref[:, i * half + j, :] = jnp.dot(onehot, pooled, preferred_element_type=jnp.float32)
    for s in range(n_req):
        (even_out, odd_out)[s % 2][s // 2] = tmp_ref[s].astype(jnp.bfloat16)
    per = vis_ref.shape[0]
    for i in range(per):
        lanes = pl.ds(i * 128, 128)
        vis_out[:, lanes] = vis_ref[i : i + 1, :].astype(jnp.float32)
        for t in range(dec_out.shape[0]):
            at = t * per + i
            dec_out[t, :, lanes] = dec_ref[at : at + 1, :].astype(jnp.float32)


def prepare(me, image_request, slot_start, grids, text, patches, dec_gain, vis_gain, n_req, n_img):
    side, _, img_dev, width = patches.shape
    padded = round_up((side // 2) ** 2, 16)
    inputs = (
        image_request,
        slot_start,
        grids.T,
        text,
        patches,
        dec_gain.reshape(-1, 128),
        vis_gain.reshape(-1, 128),
    )
    bf16, f32 = jnp.bfloat16, jnp.float32
    outputs = [((n_req // 2, padded, width), bf16)] * 2 + [
        ((n_img, width), bf16),
        ((n_img, n_img), bf16),
        ((n_req, 128), jnp.int32),
        ((8, text.shape[0]), f32),
        ((dec_gain.size // width, 1, width), f32),
        ((1, width), f32),
    ]
    return pl.pallas_call(
        functools.partial(prep_kernel, n_req),
        out_shape=tuple(jax.ShapeDtypeStruct(shape, kind) for shape, kind in outputs),
        in_specs=[pl.BlockSpec(memory_space=pltpu.SMEM)] + [pl.BlockSpec(memory_space=pltpu.HBM)] * len(inputs),
        out_specs=tuple(vmem_specs(len(outputs))),
        scratch_shapes=[pltpu.SMEM(x.shape, jnp.int32) for x in inputs[:3]]
        + [pltpu.VMEM(x.shape, x.dtype) for x in inputs[3:]]
        + [pltpu.VMEM((n_req, padded, width), f32), pltpu.SemaphoreType.DMA((len(inputs),))],
        compiler_params=params(12),
        cost_estimate=TINY,
    )(me, *[in_hbm(x) for x in inputs])


def mix_kernel(region, even_ref, odd_ref, *refs):
    outs, tmp_ref = refs[:-1], refs[-1]
    for i, out_ref in enumerate(outs):
        tmp_ref[:region] = even_ref[i].astype(jnp.float32)[:region]
        tmp_ref[region : 2 * region] = odd_ref[i].astype(jnp.float32)[:region]
        tmp_ref[2 * region :] = jnp.zeros((tmp_ref.shape[0] - 2 * region, tmp_ref.shape[1]), jnp.float32)
        out_ref[...] = tmp_ref[...].astype(jnp.bfloat16)


def mix_pairs(even, odd, region):
    n, _, width = even.shape
    rows = round_up(2 * region, 8)
    return pl.pallas_call(
        functools.partial(mix_kernel, region),
        out_shape=(jax.ShapeDtypeStruct((rows, width), jnp.bfloat16),) * n,
        in_specs=vmem_specs(2),
        out_specs=tuple(vmem_specs(n)),
        scratch_shapes=[pltpu.VMEM((rows, width), jnp.float32)],
        compiler_params=params(4),
        cost_estimate=TINY,
    )(even, odd)


def pack_kernel(region, gain_ref, rtext_ref, sel_ref, *refs):
    recs, (out_ref, tmp_ref) = refs[:-2], refs[-2:]
    done = 0
    for rec_ref in recs:
        tmp_ref[done : done + 2 * region] = rec_ref[...].astype(jnp.float32)[: 2 * region]
        done += 2 * region
    rest = tmp_ref.shape[0] - done
    tmp_ref[done:] = jnp.zeros((rest, tmp_ref.shape[1]), jnp.float32)
    picked = jnp.dot(sel_ref[...], tmp_ref[...].astype(jnp.bfloat16), preferred_element_type=jnp.float32)
    tmp_ref[...] = picked + rtext_ref[...].astype(jnp.float32)
    tmp_ref[done:] = jnp.broadcast_to(gain_ref[0:1, :], (rest, gain_ref.shape[1]))
    out_ref[...] = tmp_ref[...].astype(jnp.bfloat16)


def pack_images(received, gain, rtext, sel, region):
    n_img, width = rtext.shape
    return pl.pallas_call(
        functools.partial(pack_kernel, region),
        out_shape=jax.ShapeDtypeStruct((n_img, width), jnp.bfloat16),
        in_specs=vmem_specs(3 + len(received)),
        out_specs=pl.BlockSpec(memory_space=pltpu.VMEM),
        scratch_shapes=[pltpu.VMEM((n_img, width), jnp.float32)],
        compiler_params=params(4),
        cost_estimate=TINY,
    )(gain, rtext, sel, *received)


def place_kernel(region, table_ref, text_at_ref, img_at_ref, text_row_ref):
    length, n_text = text_at_ref.shape
    spot = lax.broadcasted_iota(jnp.int32, (length, 128), 0)
    before = jnp.zeros((length, 128), jnp.int32)
    at = jnp.full((length, 128), -1, jnp.int32)
    for s in range(table_ref.shape[0]):
        c = spot - table_ref[s : s + 1, :]
        before += jnp.clip(c, 0, region)
        at = jnp.where((c >= 0) & (c < region), s * region + c, at)
    text_row_ref[...] = jnp.where(at < 0, 1.0, 0.0)
    rank = jnp.where(at < 0, spot - before, -1)[:, :1]
    text_at_ref[...] = (lax.broadcasted_iota(jnp.int32, (length, n_text), 1) == rank).astype(jnp.bfloat16)
    lane = lax.broadcasted_iota(jnp.int32, img_at_ref.shape, 1)
    img_at_ref[...] = (lane == at[:, :1]).astype(jnp.bfloat16)


def placement(table, region, length, n_text, n_img):
    return pl.pallas_call(
        functools.partial(place_kernel, region),
        out_shape=(
            jax.ShapeDtypeStruct((length, n_text), jnp.bfloat16),
            jax.ShapeDtypeStruct((length, n_img), jnp.bfloat16),
            jax.ShapeDtypeStruct((length, 128), jnp.float32),
        ),
        in_specs=vmem_specs(1),
        out_specs=tuple(vmem_specs(3)),
        compiler_params=params(8),
        cost_estimate=TINY,
    )(table)


def cols_of(ref, owner, width):
    return ref[:, pl.ds(pl.multiple_of(owner * width, width), width)]


def scale_rows(x, gain):
    xf = x.astype(jnp.float32)
    return (xf * gain).astype(jnp.bfloat16), jnp.sum(xf * xf, axis=1, keepdims=True)


def own_kernel(me_ref, x_ref, gain_ref, w_ref, acc_ref, ss_ref, held_ref, sem_ref):
    n_ten, _, width, _ = held_ref.shape
    half = x_ref.shape[0] // 2
    copies = []
    for s in range(n_ten):
        rows = pl.ds(pl.multiple_of((me_ref[0] ^ s) * width, width), width)
        copies += [pltpu.make_async_copy(w_ref.at[j, rows], held_ref.at[s, j], sem_ref.at[s, j]) for j in range(3)]
    for copy in copies:
        copy.start()
    scaled = []
    for side in range(2):
        rows = pl.ds(side * half, half)
        x, total = scale_rows(x_ref[rows], gain_ref[me_ref[0]])
        scaled.append(x)
        ss_ref[rows] = jnp.broadcast_to(total, (half, 128))
    for j in range(3):
        copies[j].wait()
        for side in range(2):
            acc_ref[j, pl.ds(side * half, half)] = jnp.dot(
                scaled[side], held_ref[0, j], preferred_element_type=jnp.float32
            )
    for copy in copies[3:]:
        copy.wait()


def own_part(me, x, gain, w):
    rows, width = x.shape
    n_ten, cols = gain.shape[0], w.shape[2]
    return pl.pallas_call(
        own_kernel,
        out_shape=(
            jax.ShapeDtypeStruct((3, rows, cols), jnp.float32),
            jax.ShapeDtypeStruct((rows, 128), jnp.float32),
            pltpu.VMEM((n_ten, 3, width, cols), w.dtype),
        ),
        in_specs=[pl.BlockSpec(memory_space=pltpu.SMEM)] + vmem_specs(2) + [pl.BlockSpec(memory_space=pltpu.HBM)],
        out_specs=tuple(vmem_specs(3)),
        scratch_shapes=[pltpu.SemaphoreType.DMA((n_ten, 3))],
        compiler_params=params(12),
        cost_estimate=TINY,
    )(me, x, gain, in_hbm(w))


def near_kernel(near, pieces, me_ref, *refs):
    n_x = sum(pieces)
    x_refs, refs = list(refs[:n_x]), refs[n_x:]
    gain_ref, held_ref, acc_in, ss_in, acc_ref, ss_ref = refs
    half = acc_ref.shape[1] // 2
    views = []
    for n in pieces:
        mine, x_refs = x_refs[:n], x_refs[n:]
        views.append([mine[0].at[pl.ds(side * half, half)] if n == 1 else mine[side] for side in range(2)])
    scaled = {}
    for side in range(2):
        rows = pl.ds(side * half, half)
        total = ss_in[rows]
        for b, s in enumerate(near):
            scaled[side, b], part = scale_rows(views[b][side][...], gain_ref[me_ref[0] ^ s])
            total += part
        ss_ref[rows] = total
    for j in range(3):
        for side in range(2):
            rows = pl.ds(side * half, half)
            acc = acc_in[j, rows]
            for b, s in enumerate(near):
                acc += jnp.dot(scaled[side, b], held_ref[s, j], preferred_element_type=jnp.float32)
            acc_ref[j, rows] = acc


def near_part(near, me, blocks, gain, held, acc, ss):
    blocks = [b if isinstance(b, tuple) else (b,) for b in blocks]
    pieces = [len(b) for b in blocks]
    return pl.pallas_call(
        functools.partial(near_kernel, near, pieces),
        out_shape=(
            jax.ShapeDtypeStruct(acc.shape, jnp.float32),
            jax.ShapeDtypeStruct(ss.shape, jnp.float32),
        ),
        in_specs=[pl.BlockSpec(memory_space=pltpu.SMEM)]
        + vmem_specs(sum(pieces) + 4),
        out_specs=tuple(vmem_specs(2)),
        compiler_params=params(12),
        cost_estimate=pl.CostEstimate(flops=10**11, bytes_accessed=0, transcendentals=0),
    )(me, *[h for b in blocks for h in b], gain, held, acc, ss)


def image_kernel(n_rows, n_blk, me_ref, *refs):
    x_refs, refs = refs[:n_blk], refs[n_blk:]
    gain_ref, sel_ref, held_ref, w_out_ref, qkv_ref, own_ref, w_out_held, sem_ref = refs
    copy = pltpu.make_async_copy(w_out_ref, w_out_held, sem_ref)
    copy.start()
    is_img = jnp.sum(sel_ref[...].astype(jnp.float32), axis=1, keepdims=True) > 0.5
    total = 0.0
    for s in range(n_blk):
        xf = x_refs[s][...].astype(jnp.float32)
        total += jnp.sum(xf * xf, axis=1, keepdims=True)
    scale = lax.rsqrt(total / D + EPS)
    total = 0.0
    scaled = []
    for s in range(n_blk):
        xf = x_refs[s][...].astype(jnp.float32)
        merged = jnp.where(is_img, xf * scale * xf[n_rows : n_rows + 1], xf).astype(jnp.bfloat16)
        if s == 0:
            own_ref[...] = merged
        mf = merged.astype(jnp.float32)
        total += jnp.sum(mf * mf, axis=1, keepdims=True)
        scaled.append((mf * gain_ref[me_ref[0] ^ s]).astype(jnp.bfloat16))
    scale = lax.rsqrt(total / D + EPS)
    for j in range(3):
        acc = 0.0
        for s in range(n_blk):
            acc += jnp.dot(scaled[s], held_ref[s, j], preferred_element_type=jnp.float32)
        qkv_ref[j] = (acc * scale).astype(jnp.bfloat16)
    copy.wait()


def image_part(me, blocks, gain, sel, held, w_out, n_rows):
    n_img, width = blocks[0].shape
    return pl.pallas_call(
        functools.partial(image_kernel, n_rows, len(blocks)),
        out_shape=(
            jax.ShapeDtypeStruct((3, n_img, held.shape[3]), jnp.bfloat16),
            jax.ShapeDtypeStruct((n_img, width), jnp.bfloat16),
            pltpu.VMEM(w_out.shape, w_out.dtype),
        ),
        in_specs=[pl.BlockSpec(memory_space=pltpu.SMEM)]
        + vmem_specs(len(blocks) + 3)
        + [pl.BlockSpec(memory_space=pltpu.HBM)],
        out_specs=tuple(vmem_specs(3)),
        scratch_shapes=[pltpu.SemaphoreType.DMA],
        compiler_params=params(12),
        cost_estimate=pl.CostEstimate(flops=0, bytes_accessed=0, transcendentals=0),
    )(me, *blocks, gain, sel, held, in_hbm(w_out))


def project_side(side, far, me_ref, x_ref, gain_ref, held_ref, acc_ref, ss_ref, out_ref):
    half = x_ref.shape[0]
    part = pl.ds(side * half, half)
    x, total = scale_rows(x_ref[...], gain_ref[me_ref[0] ^ far])
    scale = lax.rsqrt((ss_ref[part] + total) / D + EPS)[:, :1]
    for j in range(3):
        prod = jnp.dot(x, held_ref[far, j], preferred_element_type=jnp.float32)
        out_ref[j, part] = ((prod + acc_ref[j, part]) * scale).astype(jnp.bfloat16)


def attend(edges, first, qkv_ref, key_ref, ctx_ref):
    heads = [pl.ds(h * HD, HD) for h in range(ctx_ref.shape[1] // HD)]
    for low, last in zip(edges, edges[1:]):
        here, step = pl.ds(low, last - low), last - low
        row = lax.broadcasted_iota(jnp.int32, (step, last), 0) + low
        col = lax.broadcasted_iota(jnp.int32, (step, last), 1)
        bias = jnp.where((row >= col) & (key_ref[0:1, pl.ds(0, last)] > 0.5), 0.0, -1e30)
        scores = [
            lax.dot_general(
                qkv_ref[0, here, lanes],
                qkv_ref[1, pl.ds(0, last), lanes],
                (((1,), (1,)), ((), ())),
                preferred_element_type=jnp.float32,
            )
            for lanes in heads
        ]
        scores = [x * (LOG2E / HD**0.5) + bias for x in scores]
        tops = [jnp.max(x, axis=1, keepdims=True) for x in scores]
        expo = [jnp.exp2(x - top) for x, top in zip(scores, tops)]
        sums = [jnp.sum(x, axis=1, keepdims=True) for x in expo]
        outs = [
            jnp.dot(x.astype(jnp.bfloat16), qkv_ref[2, pl.ds(0, last), lanes], preferred_element_type=jnp.float32)
            for x, lanes in zip(expo, heads)
        ]
        for lanes, out, total in zip(heads, outs, sums):
            ctx_ref[pl.ds(low - first, step), lanes] = (out / total).astype(jnp.bfloat16)


def put_columns(product, outs):
    half = outs[0].shape[1]
    for i, out_ref in enumerate(outs):
        out_ref[...] = product[:, i * half : (i + 1) * half].astype(out_ref.dtype)


def head_kernel(far, me_ref, top_ref, gain_ref, held_ref, acc_ref, ss_ref, img_ref, text_at_ref, img_at_ref, key_ref,
                w_out_ref, text_qkv_ref, qkv_ref, ctx_ref, left_ref, right_ref):
    rows = ctx_ref.shape[0]
    width = 2 * left_ref.shape[1]
    project_side(0, far, me_ref, top_ref, gain_ref, held_ref, acc_ref, ss_ref, text_qkv_ref)
    for j in range(3):
        qkv = jnp.dot(text_at_ref[:rows, :rows], text_qkv_ref[j], preferred_element_type=jnp.float32)
        qkv += jnp.dot(img_at_ref[:rows], img_ref[j], preferred_element_type=jnp.float32)
        qkv_ref[j] = qkv.astype(jnp.bfloat16)
    attend([0, rows], 0, qkv_ref, key_ref, ctx_ref)
    weight = cols_of(w_out_ref, me_ref[0] ^ far, width)
    put_columns(jnp.dot(ctx_ref[...], weight, preferred_element_type=jnp.float32), (left_ref, right_ref))


def head_part(far, me, top, gain, held, acc, ss, img, text_at, img_at, key_ok, w_out):
    width, cols = held.shape[2:]
    rows = top.shape[0]
    bf16 = jnp.bfloat16
    return pl.pallas_call(
        functools.partial(head_kernel, far),
        out_shape=(
            jax.ShapeDtypeStruct((3, rows, cols), bf16),
            jax.ShapeDtypeStruct((3, rows, cols), bf16),
            jax.ShapeDtypeStruct((rows, cols), bf16),
            jax.ShapeDtypeStruct((rows, width // 2), bf16),
            jax.ShapeDtypeStruct((rows, width // 2), bf16),
        ),
        in_specs=[pl.BlockSpec(memory_space=pltpu.SMEM)] + vmem_specs(10),
        out_specs=tuple(vmem_specs(5)),
        compiler_params=params(12),
        cost_estimate=TINY,
    )(me, top, gain, held, acc, ss, img, text_at, img_at, key_ok, w_out)


def tail_kernel(far, me_ref, bottom_ref, gain_ref, held_ref, acc_ref, ss_ref, img_ref, text_at_ref, img_at_ref,
                key_ref, w_out_ref, top_qkv_ref, head_qkv_ref, ctx_ref, left_ref, right_ref, text_qkv_ref, qkv_ref):
    first = top_qkv_ref.shape[1]
    length = text_at_ref.shape[0]
    width = 2 * left_ref.shape[1]
    project_side(1, far, me_ref, bottom_ref, gain_ref, held_ref, acc_ref, ss_ref, text_qkv_ref)
    for j in range(3):
        text_qkv_ref[j, :first] = top_qkv_ref[j]
        qkv_ref[j, :first] = head_qkv_ref[j]
        qkv = jnp.dot(text_at_ref[first:], text_qkv_ref[j], preferred_element_type=jnp.float32)
        qkv += jnp.dot(img_at_ref[first:], img_ref[j], preferred_element_type=jnp.float32)
        qkv_ref[j, first:] = qkv.astype(jnp.bfloat16)
    edges = [first] + [at for at in range(128, length, 128) if at > first] + [length]
    attend(edges, first, qkv_ref, key_ref, ctx_ref)
    weight = cols_of(w_out_ref, me_ref[0] ^ far, width)
    put_columns(jnp.dot(ctx_ref[...], weight, preferred_element_type=jnp.float32), (left_ref, right_ref))


def tail_part(far, me, bottom, gain, held, acc, ss, img, text_at, img_at, key_ok, w_out, top_qkv, head_qkv):
    width, cols = held.shape[2:]
    length, n_text = text_at.shape
    rows = length - top_qkv.shape[1]
    bf16 = jnp.bfloat16
    return pl.pallas_call(
        functools.partial(tail_kernel, far),
        out_shape=(
            jax.ShapeDtypeStruct((rows, cols), bf16),
            jax.ShapeDtypeStruct((rows, width // 2), bf16),
            jax.ShapeDtypeStruct((rows, width // 2), bf16),
        ),
        in_specs=[pl.BlockSpec(memory_space=pltpu.SMEM)] + vmem_specs(12),
        out_specs=tuple(vmem_specs(3)),
        scratch_shapes=[pltpu.VMEM((3, n_text, cols), bf16), pltpu.VMEM((3, length, cols), bf16)],
        compiler_params=params(12),
        cost_estimate=pl.CostEstimate(flops=10**10, bytes_accessed=0, transcendentals=0),
    )(me, bottom, gain, held, acc, ss, img, text_at, img_at, key_ok, w_out, top_qkv, head_qkv)


def out_kernel(away, me_ref, head_ref, tail_ref, w_ref, left_ref, right_ref):
    first = head_ref.shape[0]
    weight = cols_of(w_ref, me_ref[0] ^ away, 2 * left_ref.shape[1])
    for ctx_ref, rows in ((head_ref, slice(None, first)), (tail_ref, slice(first, None))):
        product = jnp.dot(ctx_ref[...], weight, preferred_element_type=jnp.float32)
        put_columns(product, (left_ref.at[rows], right_ref.at[rows]))


def out_part(away, me, head, tail, w, width, dtype=jnp.bfloat16):
    rows = head.shape[0] + tail.shape[0]
    return pl.pallas_call(
        functools.partial(out_kernel, away),
        out_shape=(jax.ShapeDtypeStruct((rows, width // 2), dtype),) * 2,
        in_specs=[pl.BlockSpec(memory_space=pltpu.SMEM)] + vmem_specs(3),
        out_specs=tuple(vmem_specs(2)),
        compiler_params=params(12),
        cost_estimate=pl.CostEstimate(flops=10**9, bytes_accessed=0, transcendentals=0),
    )(me, head, tail, w)


def sum_of(refs):
    return functools.reduce(lambda a, b: a + b, [ref[...].astype(jnp.float32) for ref in refs])


def first_kernel(n_left, base_ref, *refs):
    out_ref = refs[-1]
    half = base_ref.shape[1] // 2
    for side, terms in enumerate((refs[:n_left], refs[n_left:-1])):
        part = pl.ds(side * half, half)
        out_ref[:, part] = base_ref[:, part].astype(jnp.float32) + sum_of(terms)


def add_first(base, left, right):
    return pl.pallas_call(
        functools.partial(first_kernel, len(left)),
        out_shape=jax.ShapeDtypeStruct(base.shape, jnp.float32),
        in_specs=vmem_specs(1 + len(left) + len(right)),
        out_specs=pl.BlockSpec(memory_space=pltpu.VMEM),
        compiler_params=params(12),
        cost_estimate=TINY,
    )(base, *left, *right)


def last_kernel(n_left, base_ref, *refs):
    refs, (out_ref, tmp_ref, sem_ref) = refs[:-3], refs[-3:]
    half = base_ref.shape[1] // 2
    copies = []
    for side, terms in enumerate((refs[:n_left], refs[n_left:])):
        part = pl.ds(side * half, half)
        tmp_ref[:, part] = (base_ref[:, part] + sum_of(terms)).astype(tmp_ref.dtype)
        copy = pltpu.make_async_copy(tmp_ref.at[:, part], out_ref.at[:, part], sem_ref.at[side])
        copy.start()
        copies.append(copy)
    for copy in copies:
        copy.wait()


def add_last(base, left, right):
    return pl.pallas_call(
        functools.partial(last_kernel, len(left)),
        out_shape=jax.ShapeDtypeStruct(base.shape, jnp.bfloat16),
        in_specs=vmem_specs(1 + len(left) + len(right)),
        out_specs=pl.BlockSpec(memory_space=pl.ANY),
        scratch_shapes=[pltpu.VMEM(base.shape, jnp.bfloat16), pltpu.SemaphoreType.DMA((2,))],
        compiler_params=params(12),
        cost_estimate=TINY,
    )(base, *left, *right)


def scatter_terms(parts, got, n):
    acc = {s: [[parts[s][0]], [parts[s][1]]] for s in parts}
    far = n - 1
    acc[far ^ low_bit(far)][0].append(got[0])
    acc[far ^ high_bit(far)][1].append(got[1])
    early, late = [[], []], [[], []]
    for s in by_bits(n, reverse=True)[1:]:
        for side, bit in ((0, low_bit(s)), (1, high_bit(s))):
            terms = [t.astype(jnp.float32) for t in acc[s][side]]
            out = swap(functools.reduce(lambda a, b: a + b, terms).astype(jnp.bfloat16), bit)
            if s == bit:
                (early if len(terms) == 1 else late)[side].append(out)
            else:
                acc[s ^ bit][side].append(out)
    return early, late


def body(text, patches, grids, image_request, slot_start, vis_gain, dec_gain, w_qkv, w_out):
    n_req = lax.axis_size("req")
    n_ten = lax.axis_size("tensor")
    me_req = lax.axis_index("req")
    me_ten = lax.axis_index("tensor")
    img_dev, side, _, width = patches.shape
    half = side // 2
    region = half * half
    length = text.shape[0]
    w3 = jnp.transpose(w_qkv, (1, 0, 2))
    req_at = me_req.astype(jnp.int32)[None]
    ten_at = me_ten.astype(jnp.int32)[None]
    order = by_bits(n_ten)
    near_at, far = order[:-1], order[-1]

    n_rows = n_req * region
    n_img = round_up(n_rows + 1, 16)
    n_text = round_up(length - (n_rows if img_dev == n_req else 0), 32)
    ctext = gather_text(req_at, image_request, slot_start, text, n_req, region, n_text)
    blocks = near_blocks(ctext, n_ten)

    late_text, ctext = lax.optimization_barrier((text, ctext))
    even, odd, rtext, sel, table, key_ok, gains, vis_row = prepare(
        req_at, image_request, slot_start, grids, late_text, jnp.transpose(patches, (1, 2, 0, 3)), dec_gain, vis_gain,
        n_req, n_img
    )
    pairs = mix_pairs(even, swap(odd, 1, "req"), region)
    received = [pairs[0]] + [swap(pairs[i], 2 * i, "req") for i in range(1, n_req // 2)]
    img_own = pack_images(received, vis_row, rtext, sel, region)
    img_blocks = [img_own] + [swap(img_own, s) for s in range(1, n_ten)]
    own, img_own = lax.optimization_barrier((ctext, img_own))
    acc, ss, held = own_part(ten_at, own, gains, w3)
    handed, img_own = lax.optimization_barrier((blocks, img_own))
    blocks = {**far_blocks(handed, n_ten), **blocks}

    near = [blocks[s] for s in near_at]
    acc, ss = near_part(near_at, ten_at, near, gains, held, acc, ss)
    table, acc = lax.optimization_barrier((table, acc))
    text_at, img_at, text_row = placement(table, region, length, n_text, n_img)
    img_blocks, text_at = lax.optimization_barrier((img_blocks, text_at))
    img_qkv, merged, w_out = image_part(ten_at, img_blocks, gains, sel, held, w_out, n_rows)

    shared = (gains, held, acc, ss, img_qkv, text_at, img_at, key_ok, w_out)
    top_qkv, head_qkv, head_ctx, *head_far = head_part(far, ten_at, blocks[far][0], *shared)
    tail_ctx, *tail_far = tail_part(far, ten_at, blocks[far][1], *shared, top_qkv, head_qkv)

    img_here = jnp.dot(img_at, merged, preferred_element_type=jnp.float32)
    x_in = (text.astype(jnp.float32) * text_row[:, :1] + img_here).astype(jnp.bfloat16)

    bits = (low_bit(far), high_bit(far))
    head_got = [swap(t, bit) for t, bit in zip(head_far, bits)]
    tail_got = [swap(t, bit) for t, bit in zip(tail_far, bits)]
    head_got, head_ctx, tail_ctx = lax.optimization_barrier((head_got, head_ctx, tail_ctx))
    parts = {}
    for s in reversed([0] + near_at):
        parts[s] = out_part(s, ten_at, head_ctx, tail_ctx, w_out, width, jnp.float32 if s == 0 else jnp.bfloat16)
    got = [jnp.concatenate(pair, axis=0) for pair in zip(head_got, tail_got)]
    early, late = scatter_terms(parts, got, n_ten)
    base = add_first(x_in, [parts[0][0]] + early[0], [parts[0][1]] + early[1])
    return add_last(base, late[0], late[1])


def solution(mesh):
    in_specs = (
        P("req", "tensor"),
        P("req", None, None, "tensor"),
        P(),
        P(),
        P(),
        P("tensor"),
        P(),
        P(None, None, "tensor"),
        P("tensor", None),
    )
    out_specs = P("req", "tensor")
    return jax.shard_map(body, mesh=mesh, in_specs=in_specs, out_specs=out_specs, check_vma=False)
```

```python
import functools

import jax
import jax.numpy as jnp
from jax import lax
from jax.experimental import pallas as pl
from jax.experimental.pallas import tpu as pltpu
from jax.sharding import PartitionSpec as P

D = 4096
HD = 128
EPS = 1e-05
LOG2E = 1.4426950408889634
TINY = pl.CostEstimate(flops=0, bytes_accessed=0, transcendentals=0)


def round_up(n, m):
    return -(-n // m) * m


def swap(x, s, axis="tensor"):
    n = lax.axis_size(axis)
    return lax.ppermute(x, axis, [(i, i ^ s) for i in range(n)])


def in_hbm(x):
    return pltpu.with_memory_space_constraint(x, pltpu.HBM)


def low_bit(s):
    return s & -s


def high_bit(s):
    return 1 << (s.bit_length() - 1)


def by_bits(n, reverse=False):
    return sorted(range(1, n), key=lambda s: (bin(s).count("1"), s), reverse=reverse)


def halves(block):
    if isinstance(block, tuple):
        return block
    half = round_up(block.shape[0] // 2, 16)
    return block[:half], block[half:]


def near_blocks(x, n):
    return {s: swap(x, s) for s in by_bits(n) if s & (s - 1) == 0}


def far_blocks(blocks, n):
    blocks = dict(blocks)
    for s in by_bits(n):
        if s not in blocks:
            low, high = low_bit(s), high_bit(s)
            blocks[s] = (swap(halves(blocks[s ^ low])[0], low), swap(halves(blocks[s ^ high])[1], high))
    return blocks


def vmem_specs(n):
    return [pl.BlockSpec(memory_space=pltpu.VMEM)] * n


def params(mib):
    return pltpu.CompilerParams(vmem_limit_bytes=mib * 1024 * 1024)


def fetch(pairs, sem_ref):
    copies = [pltpu.make_async_copy(src, dst, sem_ref.at[i]) for i, (src, dst) in enumerate(pairs)]
    for copy in copies:
        copy.start()
    return copies


NOWHERE = 1 << 20


def find_images(n_req, img_dev, me, req_ref, start_ref, grid_ref=None):
    found = []
    for s in range(n_req):
        source = (me ^ s) * img_dev

        def one_image(k, found, source=source):
            hit = req_ref[source + k] == me
            values = (start_ref[source + k],)
            if grid_ref is not None:
                values += (grid_ref[0, source + k] // 2, grid_ref[1, source + k] // 2)
            return tuple(jnp.where(hit, new, old) for new, old in zip(values, found))

        none = (jnp.int32(NOWHERE), jnp.int32(0), jnp.int32(1))[: 1 if grid_ref is None else 3]
        found.append(lax.fori_loop(0, img_dev, one_image, none, unroll=img_dev <= 8))
    return found


def text_kernel(n_req, region, me_ref, req_hbm, start_hbm, text_hbm, ctext_out, req_ref, start_ref, text_ref, sem_ref):
    copies = fetch(((req_hbm, req_ref), (start_hbm, start_ref), (text_hbm, text_ref)), sem_ref)
    n_text, length = ctext_out.shape[0], text_ref.shape[0]
    spot = lax.broadcasted_iota(jnp.int32, (8, length), 1)
    before = jnp.zeros((8, length), jnp.int32)
    inside = jnp.zeros((8, length), jnp.int32)
    copies[0].wait()
    copies[1].wait()
    for (start,) in find_images(n_req, req_ref.shape[0] // n_req, me_ref[0], req_ref, start_ref):
        c = spot - start
        before += jnp.clip(c, 0, region)
        inside = jnp.where((c >= 0) & (c < region), 1, inside)
    rank = jnp.where(inside == 1, -1, spot - before)[0:1]
    gather = (lax.broadcasted_iota(jnp.int32, (n_text, length), 0) == rank).astype(jnp.bfloat16)
    copies[2].wait()
    ctext_out[...] = jnp.dot(gather, text_ref[...], preferred_element_type=jnp.float32).astype(jnp.bfloat16)


def gather_text(me, image_request, slot_start, text, n_req, region, n_text):
    inputs = (image_request, slot_start, text)
    return pl.pallas_call(
        functools.partial(text_kernel, n_req, region),
        out_shape=jax.ShapeDtypeStruct((n_text, text.shape[1]), text.dtype),
        in_specs=[pl.BlockSpec(memory_space=pltpu.SMEM)] + [pl.BlockSpec(memory_space=pltpu.HBM)] * 3,
        out_specs=pl.BlockSpec(memory_space=pltpu.VMEM),
        scratch_shapes=[pltpu.SMEM(x.shape, jnp.int32) for x in inputs[:2]]
        + [pltpu.VMEM(text.shape, text.dtype), pltpu.SemaphoreType.DMA((3,))],
        compiler_params=params(8),
        cost_estimate=TINY,
    )(me, *[in_hbm(x) for x in inputs])


def prep_kernel(n_req, me_ref, req_hbm, start_hbm, grid_hbm, text_hbm, x_hbm, dec_hbm, vis_hbm, *refs):
    (even_out, odd_out, rtext_out, sel_out, table_out, key_out, dec_out, vis_out, req_ref, start_ref, grid_ref,
     text_ref, x_ref, dec_ref, vis_ref, tmp_ref, sem_ref) = refs
    pairs = (
        (req_hbm, req_ref),
        (start_hbm, start_ref),
        (grid_hbm, grid_ref),
        (x_hbm, x_ref),
        (text_hbm, text_ref),
        (dec_hbm, dec_ref),
        (vis_hbm, vis_ref),
    )
    copies = fetch(pairs, sem_ref)
    side, img_dev = x_ref.shape[0], x_ref.shape[2]
    half = side // 2
    region = half * half
    n_img, length = sel_out.shape[0], text_ref.shape[0]
    me = me_ref[0]
    tmp_ref[...] = jnp.zeros_like(tmp_ref)
    for copy in copies[:3]:
        copy.wait()

    spot = lax.broadcasted_iota(jnp.int32, (8, length), 1)
    closed = jnp.zeros((8, length), jnp.int32)
    row = lax.broadcasted_iota(jnp.int32, (n_img, 128), 0)
    pos = jnp.full((n_img, 128), -1, jnp.int32)
    target = jnp.full((n_img, 128), -1, jnp.int32)
    line = lax.broadcasted_iota(jnp.int32, (n_req, 128), 0)
    table = jnp.zeros((n_req, 128), jnp.int32)
    for s, (start, high, wide) in enumerate(find_images(n_req, img_dev, me, req_ref, start_ref, grid_ref)):
        count = high * wide
        c = spot - start
        closed = jnp.where((c >= count) & (c < region) & (c >= 0), 1, closed)
        c = row - s * region
        here = (c >= 0) & (c < region)
        pos = jnp.where(here, start + c, pos)
        cell = c
        for w in range(1, half):
            cell = jnp.where(wide == w, c // w * half + c % w, cell)
        target = jnp.where(here & (c < count), s * region + cell, target)
        table = jnp.where(line == s, start, table)
    table_out[...] = table
    key_out[...] = 1.0 - closed.astype(jnp.float32)
    stays = jnp.where(target >= 0, -1, pos)[:, :1]
    keep = (lax.broadcasted_iota(jnp.int32, (n_img, length), 1) == stays).astype(jnp.bfloat16)
    sel = lax.broadcasted_iota(jnp.int32, (n_img, n_img), 1) == target[:, :1]
    sel_out[...] = sel.astype(jnp.bfloat16)
    rows = lax.broadcasted_iota(jnp.int32, (n_req, img_dev), 0)
    cols = lax.broadcasted_iota(jnp.int32, (n_req, img_dev), 1)
    goal = jnp.full((n_req, img_dev), -1, jnp.int32)
    for k in range(img_dev):
        goal = jnp.where(cols == k, req_ref[me * img_dev + k] ^ me, goal)
    onehot = (rows == goal).astype(jnp.bfloat16)

    for copy in copies[3:]:
        copy.wait()
    rtext_out[...] = jnp.dot(keep, text_ref[...], preferred_element_type=jnp.float32).astype(jnp.bfloat16)
    for i in range(half):
        for j in range(half):
            total = x_ref[2 * i, 2 * j].astype(jnp.float32)
            for a, b in ((0, 1), (1, 0), (1, 1)):
                total += x_ref[2 * i + a, 2 * j + b].astype(jnp.float32)
            pooled = (total * 0.25).astype(jnp.bfloat16)
            tmp_ref[:, i * half + j, :] = jnp.dot(onehot, pooled, preferred_element_type=jnp.float32)
    for s in range(n_req):
        (even_out, odd_out)[s % 2][s // 2] = tmp_ref[s].astype(jnp.bfloat16)
    per = vis_ref.shape[0]
    for i in range(per):
        lanes = pl.ds(i * 128, 128)
        vis_out[:, lanes] = vis_ref[i : i + 1, :].astype(jnp.float32)
        for t in range(dec_out.shape[0]):
            at = t * per + i
            dec_out[t, :, lanes] = dec_ref[at : at + 1, :].astype(jnp.float32)


def prepare(me, image_request, slot_start, grids, text, patches, dec_gain, vis_gain, n_req, n_img):
    side, _, img_dev, width = patches.shape
    padded = round_up((side // 2) ** 2, 16)
    inputs = (
        image_request,
        slot_start,
        grids.T,
        text,
        patches,
        dec_gain.reshape(-1, 128),
        vis_gain.reshape(-1, 128),
    )
    bf16, f32 = jnp.bfloat16, jnp.float32
    outputs = [((n_req // 2, padded, width), bf16)] * 2 + [
        ((n_img, width), bf16),
        ((n_img, n_img), bf16),
        ((n_req, 128), jnp.int32),
        ((8, text.shape[0]), f32),
        ((dec_gain.size // width, 1, width), f32),
        ((1, width), f32),
    ]
    return pl.pallas_call(
        functools.partial(prep_kernel, n_req),
        out_shape=tuple(jax.ShapeDtypeStruct(shape, kind) for shape, kind in outputs),
        in_specs=[pl.BlockSpec(memory_space=pltpu.SMEM)] + [pl.BlockSpec(memory_space=pltpu.HBM)] * len(inputs),
        out_specs=tuple(vmem_specs(len(outputs))),
        scratch_shapes=[pltpu.SMEM(x.shape, jnp.int32) for x in inputs[:3]]
        + [pltpu.VMEM(x.shape, x.dtype) for x in inputs[3:]]
        + [pltpu.VMEM((n_req, padded, width), f32), pltpu.SemaphoreType.DMA((len(inputs),))],
        compiler_params=params(12),
        cost_estimate=TINY,
    )(me, *[in_hbm(x) for x in inputs])


def mix_kernel(region, even_ref, odd_ref, *refs):
    outs, tmp_ref = refs[:-1], refs[-1]
    for i, out_ref in enumerate(outs):
        tmp_ref[:region] = even_ref[i].astype(jnp.float32)[:region]
        tmp_ref[region : 2 * region] = odd_ref[i].astype(jnp.float32)[:region]
        tmp_ref[2 * region :] = jnp.zeros((tmp_ref.shape[0] - 2 * region, tmp_ref.shape[1]), jnp.float32)
        out_ref[...] = tmp_ref[...].astype(jnp.bfloat16)


def mix_pairs(even, odd, region):
    n, _, width = even.shape
    rows = round_up(2 * region, 8)
    return pl.pallas_call(
        functools.partial(mix_kernel, region),
        out_shape=(jax.ShapeDtypeStruct((rows, width), jnp.bfloat16),) * n,
        in_specs=vmem_specs(2),
        out_specs=tuple(vmem_specs(n)),
        scratch_shapes=[pltpu.VMEM((rows, width), jnp.float32)],
        compiler_params=params(4),
        cost_estimate=TINY,
    )(even, odd)


def pack_kernel(region, gain_ref, rtext_ref, sel_ref, *refs):
    recs, (out_ref, tmp_ref) = refs[:-2], refs[-2:]
    done = 0
    for rec_ref in recs:
        tmp_ref[done : done + 2 * region] = rec_ref[...].astype(jnp.float32)[: 2 * region]
        done += 2 * region
    rest = tmp_ref.shape[0] - done
    tmp_ref[done:] = jnp.zeros((rest, tmp_ref.shape[1]), jnp.float32)
    picked = jnp.dot(sel_ref[...], tmp_ref[...].astype(jnp.bfloat16), preferred_element_type=jnp.float32)
    tmp_ref[...] = picked + rtext_ref[...].astype(jnp.float32)
    tmp_ref[done:] = jnp.broadcast_to(gain_ref[0:1, :], (rest, gain_ref.shape[1]))
    out_ref[...] = tmp_ref[...].astype(jnp.bfloat16)


def pack_images(received, gain, rtext, sel, region):
    n_img, width = rtext.shape
    return pl.pallas_call(
        functools.partial(pack_kernel, region),
        out_shape=jax.ShapeDtypeStruct((n_img, width), jnp.bfloat16),
        in_specs=vmem_specs(3 + len(received)),
        out_specs=pl.BlockSpec(memory_space=pltpu.VMEM),
        scratch_shapes=[pltpu.VMEM((n_img, width), jnp.float32)],
        compiler_params=params(4),
        cost_estimate=TINY,
    )(gain, rtext, sel, *received)


def place_kernel(region, table_ref, text_at_ref, img_at_ref, text_row_ref):
    length, n_text = text_at_ref.shape
    spot = lax.broadcasted_iota(jnp.int32, (length, 128), 0)
    before = jnp.zeros((length, 128), jnp.int32)
    at = jnp.full((length, 128), -1, jnp.int32)
    for s in range(table_ref.shape[0]):
        c = spot - table_ref[s : s + 1, :]
        before += jnp.clip(c, 0, region)
        at = jnp.where((c >= 0) & (c < region), s * region + c, at)
    text_row_ref[...] = jnp.where(at < 0, 1.0, 0.0)
    rank = jnp.where(at < 0, spot - before, -1)[:, :1]
    text_at_ref[...] = (lax.broadcasted_iota(jnp.int32, (length, n_text), 1) == rank).astype(jnp.bfloat16)
    lane = lax.broadcasted_iota(jnp.int32, img_at_ref.shape, 1)
    img_at_ref[...] = (lane == at[:, :1]).astype(jnp.bfloat16)


def placement(table, region, length, n_text, n_img):
    return pl.pallas_call(
        functools.partial(place_kernel, region),
        out_shape=(
            jax.ShapeDtypeStruct((length, n_text), jnp.bfloat16),
            jax.ShapeDtypeStruct((length, n_img), jnp.bfloat16),
            jax.ShapeDtypeStruct((length, 128), jnp.float32),
        ),
        in_specs=vmem_specs(1),
        out_specs=tuple(vmem_specs(3)),
        compiler_params=params(8),
        cost_estimate=TINY,
    )(table)


def cols_of(ref, owner, width):
    return ref[:, pl.ds(pl.multiple_of(owner * width, width), width)]


def scale_rows(x, gain):
    xf = x.astype(jnp.float32)
    return (xf * gain).astype(jnp.bfloat16), jnp.sum(xf * xf, axis=1, keepdims=True)


def own_kernel(me_ref, x_ref, gain_ref, w_ref, acc_ref, ss_ref, held_ref, sem_ref):
    n_ten, _, width, _ = held_ref.shape
    half = x_ref.shape[0] // 2
    copies = []
    for s in range(n_ten):
        rows = pl.ds(pl.multiple_of((me_ref[0] ^ s) * width, width), width)
        copies += [pltpu.make_async_copy(w_ref.at[j, rows], held_ref.at[s, j], sem_ref.at[s, j]) for j in range(3)]
    for copy in copies:
        copy.start()
    scaled = []
    for side in range(2):
        rows = pl.ds(side * half, half)
        x, total = scale_rows(x_ref[rows], gain_ref[me_ref[0]])
        scaled.append(x)
        ss_ref[rows] = jnp.broadcast_to(total, (half, 128))
    for j in range(3):
        copies[j].wait()
        for side in range(2):
            acc_ref[j, pl.ds(side * half, half)] = jnp.dot(
                scaled[side], held_ref[0, j], preferred_element_type=jnp.float32
            )
    for copy in copies[3:]:
        copy.wait()


def own_part(me, x, gain, w):
    rows, width = x.shape
    n_ten, cols = gain.shape[0], w.shape[2]
    return pl.pallas_call(
        own_kernel,
        out_shape=(
            jax.ShapeDtypeStruct((3, rows, cols), jnp.float32),
            jax.ShapeDtypeStruct((rows, 128), jnp.float32),
            pltpu.VMEM((n_ten, 3, width, cols), w.dtype),
        ),
        in_specs=[pl.BlockSpec(memory_space=pltpu.SMEM)] + vmem_specs(2) + [pl.BlockSpec(memory_space=pltpu.HBM)],
        out_specs=tuple(vmem_specs(3)),
        scratch_shapes=[pltpu.SemaphoreType.DMA((n_ten, 3))],
        compiler_params=params(12),
        cost_estimate=TINY,
    )(me, x, gain, in_hbm(w))


def near_kernel(near, pieces, me_ref, *refs):
    n_x = sum(pieces)
    x_refs, refs = list(refs[:n_x]), refs[n_x:]
    gain_ref, held_ref, acc_in, ss_in, acc_ref, ss_ref = refs
    half = acc_ref.shape[1] // 2
    views = []
    for n in pieces:
        mine, x_refs = x_refs[:n], x_refs[n:]
        views.append([mine[0].at[pl.ds(side * half, half)] if n == 1 else mine[side] for side in range(2)])
    scaled = {}
    for side in range(2):
        rows = pl.ds(side * half, half)
        total = ss_in[rows]
        for b, s in enumerate(near):
            scaled[side, b], part = scale_rows(views[b][side][...], gain_ref[me_ref[0] ^ s])
            total += part
        ss_ref[rows] = total
    for j in range(3):
        for side in range(2):
            rows = pl.ds(side * half, half)
            acc = acc_in[j, rows]
            for b, s in enumerate(near):
                acc += jnp.dot(scaled[side, b], held_ref[s, j], preferred_element_type=jnp.float32)
            acc_ref[j, rows] = acc


def near_part(near, me, blocks, gain, held, acc, ss):
    blocks = [b if isinstance(b, tuple) else (b,) for b in blocks]
    pieces = [len(b) for b in blocks]
    return pl.pallas_call(
        functools.partial(near_kernel, near, pieces),
        out_shape=(
            jax.ShapeDtypeStruct(acc.shape, jnp.float32),
            jax.ShapeDtypeStruct(ss.shape, jnp.float32),
        ),
        in_specs=[pl.BlockSpec(memory_space=pltpu.SMEM)]
        + vmem_specs(sum(pieces) + 4),
        out_specs=tuple(vmem_specs(2)),
        compiler_params=params(12),
        cost_estimate=pl.CostEstimate(flops=10**11, bytes_accessed=0, transcendentals=0),
    )(me, *[h for b in blocks for h in b], gain, held, acc, ss)


def image_rows(x, vis_row, is_img, gain):
    xf = x.astype(jnp.float32)
    y = jnp.where(is_img, xf * vis_row, xf)
    sums = [jnp.sum(t * t, axis=1, keepdims=True) for t in (xf, y)]
    return (y * gain).astype(jnp.bfloat16), *sums


def image_flags(sel_ref):
    return jnp.sum(sel_ref[...].astype(jnp.float32), axis=1, keepdims=True) > 0.5


def image_kernel(n_rows, away, me_ref, *refs):
    x_refs, refs = refs[: len(away)], refs[len(away) :]
    gain_ref, sel_ref, held_ref, w_out_ref, acc_ref, sums_ref, w_out_held, sem_ref = refs
    copy = pltpu.make_async_copy(w_out_ref, w_out_held, sem_ref)
    copy.start()
    is_img = image_flags(sel_ref)
    before, after = 0.0, 0.0
    scaled = []
    for s, x_ref in zip(away, x_refs):
        x = x_ref[...]
        vis_row = x.astype(jnp.float32)[n_rows : n_rows + 1]
        rows, one, two = image_rows(x, vis_row, is_img, gain_ref[me_ref[0] ^ s])
        scaled.append(rows)
        before += one
        after += two
    sums_ref[0] = jnp.broadcast_to(before, sums_ref.shape[1:])
    sums_ref[1] = jnp.broadcast_to(after, sums_ref.shape[1:])
    for j in range(3):
        acc = 0.0
        for s, rows in zip(away, scaled):
            acc += jnp.dot(rows, held_ref[s, j], preferred_element_type=jnp.float32)
        acc_ref[j] = acc
    copy.wait()


def image_part(away, me, blocks, gain, sel, held, w_out, n_rows):
    n_img = sel.shape[0]
    return pl.pallas_call(
        functools.partial(image_kernel, n_rows, away),
        out_shape=(
            jax.ShapeDtypeStruct((3, n_img, held.shape[3]), jnp.float32),
            jax.ShapeDtypeStruct((2, n_img, 128), jnp.float32),
            pltpu.VMEM(w_out.shape, w_out.dtype),
        ),
        in_specs=[pl.BlockSpec(memory_space=pltpu.SMEM)]
        + vmem_specs(len(blocks) + 3)
        + [pl.BlockSpec(memory_space=pltpu.HBM)],
        out_specs=tuple(vmem_specs(3)),
        scratch_shapes=[pltpu.SemaphoreType.DMA],
        compiler_params=params(12),
        cost_estimate=TINY,
    )(me, *blocks, gain, sel, held, in_hbm(w_out))


def image_end_kernel(n_rows, away, me_ref, *refs):
    x_refs, refs = refs[: 2 * len(away)], refs[2 * len(away) :]
    own_ref, gain_ref, sel_ref, held_ref, acc_ref, sums_ref, qkv_ref, merged_ref = refs
    is_img = image_flags(sel_ref)
    half = x_refs[0].shape[0]
    before, after = sums_ref[0], sums_ref[1]
    parts = ((0, half), (half, sel_ref.shape[0]))
    scaled, one, two = [], [[], []], [[], []]
    for i, s in enumerate(away):
        vis_row = x_refs[2 * i + 1][...].astype(jnp.float32)[n_rows - half : n_rows - half + 1]
        for side, (low, high) in enumerate(parts):
            x = x_refs[2 * i + side][...]
            rows, a, b = image_rows(x, vis_row, is_img[low:high], gain_ref[me_ref[0] ^ s])
            scaled.append(rows)
            one[side].append(a)
            two[side].append(b)
    norms, scales = [], []
    for side, (low, high) in enumerate(parts):
        merge = lax.rsqrt((before[low:high] + sum(one[side])) / D + EPS)[:, :1]
        merge = jnp.where(is_img[low:high], merge, 1.0)
        mean = (after[low:high] + sum(two[side]))[:, :1] * merge * merge / D
        norms.append(lax.rsqrt(mean + EPS) * merge)
        scales.append(merge)
    for j in range(3):
        for side, (low, high) in enumerate(parts):
            acc = acc_ref[j, low:high]
            for i, s in enumerate(away):
                acc += jnp.dot(scaled[2 * i + side], held_ref[s, j], preferred_element_type=jnp.float32)
            qkv_ref[j, low:high] = (acc * norms[side]).astype(jnp.bfloat16)
    own = own_ref[...].astype(jnp.float32)
    own = jnp.where(is_img, own * own[n_rows : n_rows + 1], own)
    for side, (low, high) in enumerate(parts):
        merged_ref[low:high] = (own[low:high] * scales[side]).astype(jnp.bfloat16)


def image_end(away, me, blocks, own, gain, sel, held, acc, sums, n_rows):
    n_img, width = own.shape
    return pl.pallas_call(
        functools.partial(image_end_kernel, n_rows, away),
        out_shape=(
            jax.ShapeDtypeStruct((3, n_img, held.shape[3]), jnp.bfloat16),
            jax.ShapeDtypeStruct((n_img, width), jnp.bfloat16),
        ),
        in_specs=[pl.BlockSpec(memory_space=pltpu.SMEM)] + vmem_specs(2 * len(blocks) + 6),
        out_specs=tuple(vmem_specs(2)),
        compiler_params=params(12),
        cost_estimate=TINY,
    )(me, *[h for b in blocks for h in b], own, gain, sel, held, acc, sums)


def project_side(side, far, me_ref, x_ref, gain_ref, held_ref, acc_ref, ss_ref, out_ref):
    half = x_ref.shape[0]
    part = pl.ds(side * half, half)
    x, total = scale_rows(x_ref[...], gain_ref[me_ref[0] ^ far])
    scale = lax.rsqrt((ss_ref[part] + total) / D + EPS)[:, :1]
    for j in range(3):
        prod = jnp.dot(x, held_ref[far, j], preferred_element_type=jnp.float32)
        out_ref[j, part] = ((prod + acc_ref[j, part]) * scale).astype(jnp.bfloat16)


def attend(edges, first, qkv_ref, key_ref, ctx_ref):
    heads = [pl.ds(h * HD, HD) for h in range(ctx_ref.shape[1] // HD)]
    for low, last in zip(edges, edges[1:]):
        here, step = pl.ds(low, last - low), last - low
        row = lax.broadcasted_iota(jnp.int32, (step, last), 0) + low
        col = lax.broadcasted_iota(jnp.int32, (step, last), 1)
        bias = jnp.where((row >= col) & (key_ref[0:1, pl.ds(0, last)] > 0.5), 0.0, -1e30)
        scores = [
            lax.dot_general(
                qkv_ref[0, here, lanes],
                qkv_ref[1, pl.ds(0, last), lanes],
                (((1,), (1,)), ((), ())),
                preferred_element_type=jnp.float32,
            )
            for lanes in heads
        ]
        scores = [x * (LOG2E / HD**0.5) + bias for x in scores]
        tops = [jnp.max(x, axis=1, keepdims=True) for x in scores]
        expo = [jnp.exp2(x - top) for x, top in zip(scores, tops)]
        sums = [jnp.sum(x, axis=1, keepdims=True) for x in expo]
        outs = [
            jnp.dot(x.astype(jnp.bfloat16), qkv_ref[2, pl.ds(0, last), lanes], preferred_element_type=jnp.float32)
            for x, lanes in zip(expo, heads)
        ]
        for lanes, out, total in zip(heads, outs, sums):
            ctx_ref[pl.ds(low - first, step), lanes] = (out / total).astype(jnp.bfloat16)


def put_columns(product, outs):
    half = outs[0].shape[1]
    for i, out_ref in enumerate(outs):
        out_ref[...] = product[:, i * half : (i + 1) * half].astype(out_ref.dtype)


def head_kernel(far, me_ref, top_ref, gain_ref, held_ref, acc_ref, ss_ref, img_ref, text_at_ref, img_at_ref, key_ref,
                w_out_ref, text_qkv_ref, qkv_ref, ctx_ref, left_ref, right_ref):
    rows = ctx_ref.shape[0]
    width = 2 * left_ref.shape[1]
    project_side(0, far, me_ref, top_ref, gain_ref, held_ref, acc_ref, ss_ref, text_qkv_ref)
    for j in range(3):
        qkv = jnp.dot(text_at_ref[:rows, :rows], text_qkv_ref[j], preferred_element_type=jnp.float32)
        qkv += jnp.dot(img_at_ref[:rows], img_ref[j], preferred_element_type=jnp.float32)
        qkv_ref[j] = qkv.astype(jnp.bfloat16)
    attend([0, rows], 0, qkv_ref, key_ref, ctx_ref)
    weight = cols_of(w_out_ref, me_ref[0] ^ far, width)
    put_columns(jnp.dot(ctx_ref[...], weight, preferred_element_type=jnp.float32), (left_ref, right_ref))


def head_part(far, me, top, gain, held, acc, ss, img, text_at, img_at, key_ok, w_out):
    width, cols = held.shape[2:]
    rows = top.shape[0]
    bf16 = jnp.bfloat16
    return pl.pallas_call(
        functools.partial(head_kernel, far),
        out_shape=(
            jax.ShapeDtypeStruct((3, rows, cols), bf16),
            jax.ShapeDtypeStruct((3, rows, cols), bf16),
            jax.ShapeDtypeStruct((rows, cols), bf16),
            jax.ShapeDtypeStruct((rows, width // 2), bf16),
            jax.ShapeDtypeStruct((rows, width // 2), bf16),
        ),
        in_specs=[pl.BlockSpec(memory_space=pltpu.SMEM)] + vmem_specs(10),
        out_specs=tuple(vmem_specs(5)),
        compiler_params=params(12),
        cost_estimate=TINY,
    )(me, top, gain, held, acc, ss, img, text_at, img_at, key_ok, w_out)


def tail_kernel(far, me_ref, bottom_ref, gain_ref, held_ref, acc_ref, ss_ref, img_ref, text_at_ref, img_at_ref,
                key_ref, w_out_ref, top_qkv_ref, head_qkv_ref, ctx_ref, left_ref, right_ref, text_qkv_ref, qkv_ref):
    first = top_qkv_ref.shape[1]
    length = text_at_ref.shape[0]
    width = 2 * left_ref.shape[1]
    project_side(1, far, me_ref, bottom_ref, gain_ref, held_ref, acc_ref, ss_ref, text_qkv_ref)
    for j in range(3):
        text_qkv_ref[j, :first] = top_qkv_ref[j]
        qkv_ref[j, :first] = head_qkv_ref[j]
        qkv = jnp.dot(text_at_ref[first:], text_qkv_ref[j], preferred_element_type=jnp.float32)
        qkv += jnp.dot(img_at_ref[first:], img_ref[j], preferred_element_type=jnp.float32)
        qkv_ref[j, first:] = qkv.astype(jnp.bfloat16)
    edges = [first] + [at for at in range(128, length, 128) if at > first] + [length]
    attend(edges, first, qkv_ref, key_ref, ctx_ref)
    weight = cols_of(w_out_ref, me_ref[0] ^ far, width)
    put_columns(jnp.dot(ctx_ref[...], weight, preferred_element_type=jnp.float32), (left_ref, right_ref))


def tail_part(far, me, bottom, gain, held, acc, ss, img, text_at, img_at, key_ok, w_out, top_qkv, head_qkv):
    width, cols = held.shape[2:]
    length, n_text = text_at.shape
    rows = length - top_qkv.shape[1]
    bf16 = jnp.bfloat16
    return pl.pallas_call(
        functools.partial(tail_kernel, far),
        out_shape=(
            jax.ShapeDtypeStruct((rows, cols), bf16),
            jax.ShapeDtypeStruct((rows, width // 2), bf16),
            jax.ShapeDtypeStruct((rows, width // 2), bf16),
        ),
        in_specs=[pl.BlockSpec(memory_space=pltpu.SMEM)] + vmem_specs(12),
        out_specs=tuple(vmem_specs(3)),
        scratch_shapes=[pltpu.VMEM((3, n_text, cols), bf16), pltpu.VMEM((3, length, cols), bf16)],
        compiler_params=params(12),
        cost_estimate=pl.CostEstimate(flops=10**10, bytes_accessed=0, transcendentals=0),
    )(me, bottom, gain, held, acc, ss, img, text_at, img_at, key_ok, w_out, top_qkv, head_qkv)


def out_kernel(away, me_ref, head_ref, tail_ref, w_ref, left_ref, right_ref):
    first = head_ref.shape[0]
    weight = cols_of(w_ref, me_ref[0] ^ away, 2 * left_ref.shape[1])
    for ctx_ref, rows in ((head_ref, slice(None, first)), (tail_ref, slice(first, None))):
        product = jnp.dot(ctx_ref[...], weight, preferred_element_type=jnp.float32)
        put_columns(product, (left_ref.at[rows], right_ref.at[rows]))


def out_part(away, me, head, tail, w, width, dtype=jnp.bfloat16):
    rows = head.shape[0] + tail.shape[0]
    return pl.pallas_call(
        functools.partial(out_kernel, away),
        out_shape=(jax.ShapeDtypeStruct((rows, width // 2), dtype),) * 2,
        in_specs=[pl.BlockSpec(memory_space=pltpu.SMEM)] + vmem_specs(3),
        out_specs=tuple(vmem_specs(2)),
        compiler_params=params(12),
        cost_estimate=pl.CostEstimate(flops=10**9, bytes_accessed=0, transcendentals=0),
    )(me, head, tail, w)


def sum_of(refs):
    return functools.reduce(lambda a, b: a + b, [ref[...].astype(jnp.float32) for ref in refs])


def first_kernel(n_left, base_ref, *refs):
    out_ref = refs[-1]
    half = base_ref.shape[1] // 2
    for side, terms in enumerate((refs[:n_left], refs[n_left:-1])):
        part = pl.ds(side * half, half)
        out_ref[:, part] = base_ref[:, part].astype(jnp.float32) + sum_of(terms)


def add_first(base, left, right):
    return pl.pallas_call(
        functools.partial(first_kernel, len(left)),
        out_shape=jax.ShapeDtypeStruct(base.shape, jnp.float32),
        in_specs=vmem_specs(1 + len(left) + len(right)),
        out_specs=pl.BlockSpec(memory_space=pltpu.VMEM),
        compiler_params=params(12),
        cost_estimate=TINY,
    )(base, *left, *right)


def last_kernel(n_left, base_ref, *refs):
    refs, (out_ref, tmp_ref, sem_ref) = refs[:-3], refs[-3:]
    half = base_ref.shape[1] // 2
    copies = []
    for side, terms in enumerate((refs[:n_left], refs[n_left:])):
        part = pl.ds(side * half, half)
        tmp_ref[:, part] = (base_ref[:, part] + sum_of(terms)).astype(tmp_ref.dtype)
        copy = pltpu.make_async_copy(tmp_ref.at[:, part], out_ref.at[:, part], sem_ref.at[side])
        copy.start()
        copies.append(copy)
    for copy in copies:
        copy.wait()


def add_last(base, left, right):
    return pl.pallas_call(
        functools.partial(last_kernel, len(left)),
        out_shape=jax.ShapeDtypeStruct(base.shape, jnp.bfloat16),
        in_specs=vmem_specs(1 + len(left) + len(right)),
        out_specs=pl.BlockSpec(memory_space=pl.ANY),
        scratch_shapes=[pltpu.VMEM(base.shape, jnp.bfloat16), pltpu.SemaphoreType.DMA((2,))],
        compiler_params=params(12),
        cost_estimate=TINY,
    )(base, *left, *right)


def scatter_terms(parts, got, n):
    acc = {s: [[parts[s][0]], [parts[s][1]]] for s in parts}
    far = n - 1
    acc[far ^ low_bit(far)][0].append(got[0])
    acc[far ^ high_bit(far)][1].append(got[1])
    early, late = [[], []], [[], []]
    for s in by_bits(n, reverse=True)[1:]:
        for side, bit in ((0, low_bit(s)), (1, high_bit(s))):
            terms = [t.astype(jnp.float32) for t in acc[s][side]]
            out = swap(functools.reduce(lambda a, b: a + b, terms).astype(jnp.bfloat16), bit)
            if s == bit:
                (early if len(terms) == 1 else late)[side].append(out)
            else:
                acc[s ^ bit][side].append(out)
    return early, late


def body(text, patches, grids, image_request, slot_start, vis_gain, dec_gain, w_qkv, w_out):
    n_req = lax.axis_size("req")
    n_ten = lax.axis_size("tensor")
    me_req = lax.axis_index("req")
    me_ten = lax.axis_index("tensor")
    img_dev, side, _, width = patches.shape
    half = side // 2
    region = half * half
    length = text.shape[0]
    w3 = jnp.transpose(w_qkv, (1, 0, 2))
    req_at = me_req.astype(jnp.int32)[None]
    ten_at = me_ten.astype(jnp.int32)[None]
    order = by_bits(n_ten)
    near_at, far = order[:-1], order[-1]

    n_rows = n_req * region
    n_img = round_up(n_rows + 1, 16)
    n_text = round_up(length - (n_rows if img_dev == n_req else 0), 32)
    ctext = gather_text(req_at, image_request, slot_start, text, n_req, region, n_text)
    blocks = near_blocks(ctext, n_ten)

    late_text, ctext = lax.optimization_barrier((text, ctext))
    even, odd, rtext, sel, table, key_ok, gains, vis_row = prepare(
        req_at, image_request, slot_start, grids, late_text, jnp.transpose(patches, (1, 2, 0, 3)), dec_gain, vis_gain,
        n_req, n_img
    )
    pairs = mix_pairs(even, swap(odd, 1, "req"), region)
    received = [pairs[0]] + [swap(pairs[i], 2 * i, "req") for i in range(1, n_req // 2)]
    ctext, pairs = lax.optimization_barrier((ctext, pairs))
    acc, ss, held = own_part(ten_at, ctext, gains, w3)
    received, acc = lax.optimization_barrier((received, acc))
    img_own = pack_images(received, vis_row, rtext, sel, region)
    img_near = near_blocks(img_own, n_ten)
    handed, img_own = lax.optimization_barrier((blocks, img_own))
    blocks = {**far_blocks(handed, n_ten), **blocks}

    near = [blocks[s] for s in near_at]
    acc, ss = near_part(near_at, ten_at, near, gains, held, acc, ss)
    table, img_near, acc = lax.optimization_barrier((table, img_near, acc))
    text_at, img_at, text_row = placement(table, region, length, n_text, n_img)
    img_blocks = far_blocks(img_near, n_ten)
    img_near, text_at = lax.optimization_barrier((img_near, text_at))
    one_bit = [0] + sorted(img_near)
    img_acc, img_sums, w_out = image_part(
        one_bit, ten_at, [img_own] + [img_near[s] for s in one_bit[1:]], gains, sel, held, w_out, n_rows
    )
    more_bits = [s for s in order if s not in img_near]
    img_qkv, merged = image_end(
        more_bits, ten_at, [img_blocks[s] for s in more_bits], img_own, gains, sel, held, img_acc, img_sums, n_rows
    )

    shared = (gains, held, acc, ss, img_qkv, text_at, img_at, key_ok, w_out)
    top_qkv, head_qkv, head_ctx, *head_far = head_part(far, ten_at, blocks[far][0], *shared)
    tail_ctx, *tail_far = tail_part(far, ten_at, blocks[far][1], *shared, top_qkv, head_qkv)

    img_here = jnp.dot(img_at, merged, preferred_element_type=jnp.float32)
    x_in = (text.astype(jnp.float32) * text_row[:, :1] + img_here).astype(jnp.bfloat16)

    bits = (low_bit(far), high_bit(far))
    head_got = [swap(t, bit) for t, bit in zip(head_far, bits)]
    tail_got = [swap(t, bit) for t, bit in zip(tail_far, bits)]
    head_got, head_ctx, tail_ctx = lax.optimization_barrier((head_got, head_ctx, tail_ctx))
    parts = {}
    for s in reversed([0] + near_at):
        parts[s] = out_part(s, ten_at, head_ctx, tail_ctx, w_out, width, jnp.float32 if s == 0 else jnp.bfloat16)
    got = [jnp.concatenate(pair, axis=0) for pair in zip(head_got, tail_got)]
    early, late = scatter_terms(parts, got, n_ten)
    base = add_first(x_in, [parts[0][0]] + early[0], [parts[0][1]] + early[1])
    return add_last(base, late[0], late[1])


def solution(mesh):
    in_specs = (
        P("req", "tensor"),
        P("req", None, None, "tensor"),
        P(),
        P(),
        P(),
        P("tensor"),
        P(),
        P(None, None, "tensor"),
        P("tensor", None),
    )
    out_specs = P("req", "tensor")
    return jax.shard_map(body, mesh=mesh, in_specs=in_specs, out_specs=out_specs, check_vma=False)
```

```python
import functools

import jax
import jax.numpy as jnp
from jax import lax
from jax.experimental import pallas as pl
from jax.experimental.pallas import tpu as pltpu
from jax.sharding import PartitionSpec as P

D = 4096
HD = 128
EPS = 1e-05
LOG2E = 1.4426950408889634
TINY = pl.CostEstimate(flops=0, bytes_accessed=0, transcendentals=0)


def round_up(n, m):
    return -(-n // m) * m


def swap(x, s, axis="tensor"):
    n = lax.axis_size(axis)
    return lax.ppermute(x, axis, [(i, i ^ s) for i in range(n)])


def in_hbm(x):
    return pltpu.with_memory_space_constraint(x, pltpu.HBM)


def low_bit(s):
    return s & -s


def high_bit(s):
    return 1 << (s.bit_length() - 1)


def by_bits(n, reverse=False):
    return sorted(range(1, n), key=lambda s: (bin(s).count("1"), s), reverse=reverse)


def halves(block):
    if isinstance(block, tuple):
        return block
    half = block.shape[0] // 2
    return block[:half], block[half:]


def near_blocks(x, n):
    return {s: swap(x, s) for s in by_bits(n) if s & (s - 1) == 0}


def far_blocks(blocks, n):
    blocks = dict(blocks)
    for s in by_bits(n):
        if s not in blocks:
            low, high = low_bit(s), high_bit(s)
            blocks[s] = (swap(halves(blocks[s ^ low])[0], low), swap(halves(blocks[s ^ high])[1], high))
    return blocks


def vmem_specs(n):
    return [pl.BlockSpec(memory_space=pltpu.VMEM)] * n


def params(mib):
    return pltpu.CompilerParams(vmem_limit_bytes=mib * 1024 * 1024)


def fetch(pairs, sem_ref):
    copies = [pltpu.make_async_copy(src, dst, sem_ref.at[i]) for i, (src, dst) in enumerate(pairs)]
    for copy in copies:
        copy.start()
    return copies


NOWHERE = 1 << 20


def find_images(n_req, img_dev, me, req_ref, start_ref, grid_ref=None):
    found = []
    for s in range(n_req):
        source = (me ^ s) * img_dev

        def one_image(k, found, source=source):
            hit = req_ref[source + k] == me
            values = (start_ref[source + k],)
            if grid_ref is not None:
                values += (grid_ref[0, source + k] // 2, grid_ref[1, source + k] // 2)
            return tuple(jnp.where(hit, new, old) for new, old in zip(values, found))

        none = (jnp.int32(NOWHERE), jnp.int32(0), jnp.int32(1))[: 1 if grid_ref is None else 3]
        found.append(lax.fori_loop(0, img_dev, one_image, none, unroll=img_dev <= 8))
    return found


def text_kernel(n_req, region, me_ref, req_hbm, start_hbm, text_hbm, ctext_out, req_ref, start_ref, text_ref, sem_ref):
    copies = fetch(((req_hbm, req_ref), (start_hbm, start_ref), (text_hbm, text_ref)), sem_ref)
    n_text, length = ctext_out.shape[0], text_ref.shape[0]
    spot = lax.broadcasted_iota(jnp.int32, (8, length), 1)
    before = jnp.zeros((8, length), jnp.int32)
    inside = jnp.zeros((8, length), jnp.int32)
    copies[0].wait()
    copies[1].wait()
    for (start,) in find_images(n_req, req_ref.shape[0] // n_req, me_ref[0], req_ref, start_ref):
        c = spot - start
        before += jnp.clip(c, 0, region)
        inside = jnp.where((c >= 0) & (c < region), 1, inside)
    rank = jnp.where(inside == 1, -1, spot - before)[0:1]
    gather = (lax.broadcasted_iota(jnp.int32, (n_text, length), 0) == rank).astype(jnp.bfloat16)
    copies[2].wait()
    ctext_out[...] = jnp.dot(gather, text_ref[...], preferred_element_type=jnp.float32).astype(jnp.bfloat16)


def gather_text(me, image_request, slot_start, text, n_req, region, n_text):
    inputs = (image_request, slot_start, text)
    return pl.pallas_call(
        functools.partial(text_kernel, n_req, region),
        out_shape=jax.ShapeDtypeStruct((n_text, text.shape[1]), text.dtype),
        in_specs=[pl.BlockSpec(memory_space=pltpu.SMEM)] + [pl.BlockSpec(memory_space=pltpu.HBM)] * 3,
        out_specs=pl.BlockSpec(memory_space=pltpu.VMEM),
        scratch_shapes=[pltpu.SMEM(x.shape, jnp.int32) for x in inputs[:2]]
        + [pltpu.VMEM(text.shape, text.dtype), pltpu.SemaphoreType.DMA((3,))],
        compiler_params=params(8),
        cost_estimate=TINY,
    )(me, *[in_hbm(x) for x in inputs])


def prep_kernel(n_req, me_ref, req_hbm, start_hbm, grid_hbm, text_hbm, x_hbm, dec_hbm, vis_hbm, *refs):
    (even_out, odd_out, rtext_out, sel_out, table_out, key_out, dec_out, vis_out, req_ref, start_ref, grid_ref,
     text_ref, x_ref, dec_ref, vis_ref, tmp_ref, sem_ref) = refs
    pairs = (
        (req_hbm, req_ref),
        (start_hbm, start_ref),
        (grid_hbm, grid_ref),
        (x_hbm, x_ref),
        (text_hbm, text_ref),
        (dec_hbm, dec_ref),
        (vis_hbm, vis_ref),
    )
    copies = fetch(pairs, sem_ref)
    side, img_dev = x_ref.shape[0], x_ref.shape[2]
    half = side // 2
    region = half * half
    n_img, length = sel_out.shape[0], text_ref.shape[0]
    me = me_ref[0]
    tmp_ref[...] = jnp.zeros_like(tmp_ref)
    for copy in copies[:3]:
        copy.wait()

    spot = lax.broadcasted_iota(jnp.int32, (8, length), 1)
    closed = jnp.zeros((8, length), jnp.int32)
    row = lax.broadcasted_iota(jnp.int32, (n_img, 128), 0)
    pos = jnp.full((n_img, 128), -1, jnp.int32)
    target = jnp.full((n_img, 128), -1, jnp.int32)
    line = lax.broadcasted_iota(jnp.int32, (n_req, 128), 0)
    table = jnp.zeros((n_req, 128), jnp.int32)
    for s, (start, high, wide) in enumerate(find_images(n_req, img_dev, me, req_ref, start_ref, grid_ref)):
        count = high * wide
        c = spot - start
        closed = jnp.where((c >= count) & (c < region) & (c >= 0), 1, closed)
        c = row - s * region
        here = (c >= 0) & (c < region)
        pos = jnp.where(here, start + c, pos)
        cell = c
        for w in range(1, half):
            cell = jnp.where(wide == w, c // w * half + c % w, cell)
        target = jnp.where(here & (c < count), s * region + cell, target)
        table = jnp.where(line == s, start, table)
    table_out[...] = table
    key_out[...] = 1.0 - closed.astype(jnp.float32)
    stays = jnp.where(target >= 0, -1, pos)[:, :1]
    keep = (lax.broadcasted_iota(jnp.int32, (n_img, length), 1) == stays).astype(jnp.bfloat16)
    sel = lax.broadcasted_iota(jnp.int32, (n_img, n_img), 1) == target[:, :1]
    sel_out[...] = sel.astype(jnp.bfloat16)
    rows = lax.broadcasted_iota(jnp.int32, (n_req, img_dev), 0)
    cols = lax.broadcasted_iota(jnp.int32, (n_req, img_dev), 1)
    goal = jnp.full((n_req, img_dev), -1, jnp.int32)
    for k in range(img_dev):
        goal = jnp.where(cols == k, req_ref[me * img_dev + k] ^ me, goal)
    onehot = (rows == goal).astype(jnp.bfloat16)

    for copy in copies[3:]:
        copy.wait()
    rtext_out[...] = jnp.dot(keep, text_ref[...], preferred_element_type=jnp.float32).astype(jnp.bfloat16)
    for i in range(half):
        for j in range(half):
            total = x_ref[2 * i, 2 * j].astype(jnp.float32)
            for a, b in ((0, 1), (1, 0), (1, 1)):
                total += x_ref[2 * i + a, 2 * j + b].astype(jnp.float32)
            pooled = (total * 0.25).astype(jnp.bfloat16)
            tmp_ref[:, i * half + j, :] = jnp.dot(onehot, pooled, preferred_element_type=jnp.float32)
    for s in range(n_req):
        (even_out, odd_out)[s % 2][s // 2] = tmp_ref[s].astype(jnp.bfloat16)
    per = vis_ref.shape[0]
    for i in range(per):
        lanes = pl.ds(i * 128, 128)
        vis_out[:, lanes] = vis_ref[i : i + 1, :].astype(jnp.float32)
        for t in range(dec_out.shape[0]):
            at = t * per + i
            dec_out[t, :, lanes] = dec_ref[at : at + 1, :].astype(jnp.float32)


def prepare(me, image_request, slot_start, grids, text, patches, dec_gain, vis_gain, n_req, n_img):
    side, _, img_dev, width = patches.shape
    padded = round_up((side // 2) ** 2, 16)
    inputs = (
        image_request,
        slot_start,
        grids.T,
        text,
        patches,
        dec_gain.reshape(-1, 128),
        vis_gain.reshape(-1, 128),
    )
    bf16, f32 = jnp.bfloat16, jnp.float32
    outputs = [((n_req // 2, padded, width), bf16)] * 2 + [
        ((n_img, width), bf16),
        ((n_img, n_img), bf16),
        ((n_req, 128), jnp.int32),
        ((8, text.shape[0]), f32),
        ((dec_gain.size // width, 1, width), f32),
        ((1, width), f32),
    ]
    return pl.pallas_call(
        functools.partial(prep_kernel, n_req),
        out_shape=tuple(jax.ShapeDtypeStruct(shape, kind) for shape, kind in outputs),
        in_specs=[pl.BlockSpec(memory_space=pltpu.SMEM)] + [pl.BlockSpec(memory_space=pltpu.HBM)] * len(inputs),
        out_specs=tuple(vmem_specs(len(outputs))),
        scratch_shapes=[pltpu.SMEM(x.shape, jnp.int32) for x in inputs[:3]]
        + [pltpu.VMEM(x.shape, x.dtype) for x in inputs[3:]]
        + [pltpu.VMEM((n_req, padded, width), f32), pltpu.SemaphoreType.DMA((len(inputs),))],
        compiler_params=params(12),
        cost_estimate=TINY,
    )(me, *[in_hbm(x) for x in inputs])


def mix_kernel(region, even_ref, odd_ref, *refs):
    outs, tmp_ref = refs[:-1], refs[-1]
    for i, out_ref in enumerate(outs):
        tmp_ref[:region] = even_ref[i].astype(jnp.float32)[:region]
        tmp_ref[region : 2 * region] = odd_ref[i].astype(jnp.float32)[:region]
        tmp_ref[2 * region :] = jnp.zeros((tmp_ref.shape[0] - 2 * region, tmp_ref.shape[1]), jnp.float32)
        out_ref[...] = tmp_ref[...].astype(jnp.bfloat16)


def mix_pairs(even, odd, region):
    n, _, width = even.shape
    rows = round_up(2 * region, 8)
    return pl.pallas_call(
        functools.partial(mix_kernel, region),
        out_shape=(jax.ShapeDtypeStruct((rows, width), jnp.bfloat16),) * n,
        in_specs=vmem_specs(2),
        out_specs=tuple(vmem_specs(n)),
        scratch_shapes=[pltpu.VMEM((rows, width), jnp.float32)],
        compiler_params=params(4),
        cost_estimate=TINY,
    )(even, odd)


def pack_kernel(region, gain_ref, rtext_ref, sel_ref, *refs):
    recs, (out_ref, tmp_ref) = refs[:-2], refs[-2:]
    done = 0
    for rec_ref in recs:
        tmp_ref[done : done + 2 * region] = rec_ref[...].astype(jnp.float32)[: 2 * region]
        done += 2 * region
    rest = tmp_ref.shape[0] - done
    tmp_ref[done:] = jnp.zeros((rest, tmp_ref.shape[1]), jnp.float32)
    picked = jnp.dot(sel_ref[...], tmp_ref[...].astype(jnp.bfloat16), preferred_element_type=jnp.float32)
    tmp_ref[...] = picked + rtext_ref[...].astype(jnp.float32)
    tmp_ref[done:] = jnp.broadcast_to(gain_ref[0:1, :], (rest, gain_ref.shape[1]))
    out_ref[...] = tmp_ref[...].astype(jnp.bfloat16)


def pack_images(received, gain, rtext, sel, region):
    n_img, width = rtext.shape
    return pl.pallas_call(
        functools.partial(pack_kernel, region),
        out_shape=jax.ShapeDtypeStruct((n_img, width), jnp.bfloat16),
        in_specs=vmem_specs(3 + len(received)),
        out_specs=pl.BlockSpec(memory_space=pltpu.VMEM),
        scratch_shapes=[pltpu.VMEM((n_img, width), jnp.float32)],
        compiler_params=params(4),
        cost_estimate=TINY,
    )(gain, rtext, sel, *received)


def place_kernel(region, table_ref, text_at_ref, img_at_ref, text_row_ref):
    length, n_text = text_at_ref.shape
    spot = lax.broadcasted_iota(jnp.int32, (length, 128), 0)
    before = jnp.zeros((length, 128), jnp.int32)
    at = jnp.full((length, 128), -1, jnp.int32)
    for s in range(table_ref.shape[0]):
        c = spot - table_ref[s : s + 1, :]
        before += jnp.clip(c, 0, region)
        at = jnp.where((c >= 0) & (c < region), s * region + c, at)
    text_row_ref[...] = jnp.where(at < 0, 1.0, 0.0)
    rank = jnp.where(at < 0, spot - before, -1)[:, :1]
    text_at_ref[...] = (lax.broadcasted_iota(jnp.int32, (length, n_text), 1) == rank).astype(jnp.bfloat16)
    lane = lax.broadcasted_iota(jnp.int32, img_at_ref.shape, 1)
    img_at_ref[...] = (lane == at[:, :1]).astype(jnp.bfloat16)


def placement(table, region, length, n_text, n_img):
    return pl.pallas_call(
        functools.partial(place_kernel, region),
        out_shape=(
            jax.ShapeDtypeStruct((length, n_text), jnp.bfloat16),
            jax.ShapeDtypeStruct((length, n_img), jnp.bfloat16),
            jax.ShapeDtypeStruct((length, 128), jnp.float32),
        ),
        in_specs=vmem_specs(1),
        out_specs=tuple(vmem_specs(3)),
        compiler_params=params(8),
        cost_estimate=TINY,
    )(table)


def cols_of(ref, owner, width):
    return ref[:, pl.ds(pl.multiple_of(owner * width, width), width)]


def scale_rows(x, gain):
    xf = x.astype(jnp.float32)
    return (xf * gain).astype(jnp.bfloat16), jnp.sum(xf * xf, axis=1, keepdims=True)


def own_kernel(me_ref, x_ref, gain_ref, w_ref, acc_ref, ss_ref, held_ref, sem_ref):
    n_ten, _, width, _ = held_ref.shape
    half = x_ref.shape[0] // 2
    copies = []
    for s in range(n_ten):
        rows = pl.ds(pl.multiple_of((me_ref[0] ^ s) * width, width), width)
        copies += [pltpu.make_async_copy(w_ref.at[j, rows], held_ref.at[s, j], sem_ref.at[s, j]) for j in range(3)]
    for copy in copies:
        copy.start()
    scaled = []
    for side in range(2):
        rows = pl.ds(side * half, half)
        x, total = scale_rows(x_ref[rows], gain_ref[me_ref[0]])
        scaled.append(x)
        ss_ref[rows] = jnp.broadcast_to(total, (half, 128))
    for j in range(3):
        copies[j].wait()
        for side in range(2):
            acc_ref[j, pl.ds(side * half, half)] = jnp.dot(
                scaled[side], held_ref[0, j], preferred_element_type=jnp.float32
            )
    for copy in copies[3:]:
        copy.wait()


def own_part(me, x, gain, w):
    rows, width = x.shape
    n_ten, cols = gain.shape[0], w.shape[2]
    return pl.pallas_call(
        own_kernel,
        out_shape=(
            jax.ShapeDtypeStruct((3, rows, cols), jnp.float32),
            jax.ShapeDtypeStruct((rows, 128), jnp.float32),
            pltpu.VMEM((n_ten, 3, width, cols), w.dtype),
        ),
        in_specs=[pl.BlockSpec(memory_space=pltpu.SMEM)] + vmem_specs(2) + [pl.BlockSpec(memory_space=pltpu.HBM)],
        out_specs=tuple(vmem_specs(3)),
        scratch_shapes=[pltpu.SemaphoreType.DMA((n_ten, 3))],
        compiler_params=params(12),
        cost_estimate=TINY,
    )(me, x, gain, in_hbm(w))


def near_kernel(near, pieces, me_ref, *refs):
    n_x = sum(pieces)
    x_refs, refs = list(refs[:n_x]), refs[n_x:]
    gain_ref, held_ref, acc_in, ss_in, acc_ref, ss_ref = refs
    half = acc_ref.shape[1] // 2
    views = []
    for n in pieces:
        mine, x_refs = x_refs[:n], x_refs[n:]
        views.append([mine[0].at[pl.ds(side * half, half)] if n == 1 else mine[side] for side in range(2)])
    scaled = {}
    for side in range(2):
        rows = pl.ds(side * half, half)
        total = ss_in[rows]
        for b, s in enumerate(near):
            scaled[side, b], part = scale_rows(views[b][side][...], gain_ref[me_ref[0] ^ s])
            total += part
        ss_ref[rows] = total
    for j in range(3):
        for side in range(2):
            rows = pl.ds(side * half, half)
            acc = acc_in[j, rows]
            for b, s in enumerate(near):
                acc += jnp.dot(scaled[side, b], held_ref[s, j], preferred_element_type=jnp.float32)
            acc_ref[j, rows] = acc


def near_part(near, me, blocks, gain, held, acc, ss):
    blocks = [b if isinstance(b, tuple) else (b,) for b in blocks]
    pieces = [len(b) for b in blocks]
    return pl.pallas_call(
        functools.partial(near_kernel, near, pieces),
        out_shape=(
            jax.ShapeDtypeStruct(acc.shape, jnp.float32),
            jax.ShapeDtypeStruct(ss.shape, jnp.float32),
        ),
        in_specs=[pl.BlockSpec(memory_space=pltpu.SMEM)]
        + vmem_specs(sum(pieces) + 4),
        out_specs=tuple(vmem_specs(2)),
        compiler_params=params(12),
        cost_estimate=pl.CostEstimate(flops=10**11, bytes_accessed=0, transcendentals=0),
    )(me, *[h for b in blocks for h in b], gain, held, acc, ss)


def image_kernel(n_rows, n_blk, me_ref, *refs):
    x_refs, refs = refs[:n_blk], refs[n_blk:]
    gain_ref, sel_ref, held_ref, w_out_ref, qkv_ref, own_ref, w_out_held, sem_ref = refs
    copy = pltpu.make_async_copy(w_out_ref, w_out_held, sem_ref)
    copy.start()
    is_img = jnp.sum(sel_ref[...].astype(jnp.float32), axis=1, keepdims=True) > 0.5
    total = 0.0
    for s in range(n_blk):
        xf = x_refs[s][...].astype(jnp.float32)
        total += jnp.sum(xf * xf, axis=1, keepdims=True)
    scale = lax.rsqrt(total / D + EPS)
    total = 0.0
    scaled = []
    for s in range(n_blk):
        xf = x_refs[s][...].astype(jnp.float32)
        merged = jnp.where(is_img, xf * scale * xf[n_rows : n_rows + 1], xf).astype(jnp.bfloat16)
        if s == 0:
            own_ref[...] = merged
        mf = merged.astype(jnp.float32)
        total += jnp.sum(mf * mf, axis=1, keepdims=True)
        scaled.append((mf * gain_ref[me_ref[0] ^ s]).astype(jnp.bfloat16))
    scale = lax.rsqrt(total / D + EPS)
    for j in range(3):
        acc = 0.0
        for s in range(n_blk):
            acc += jnp.dot(scaled[s], held_ref[s, j], preferred_element_type=jnp.float32)
        qkv_ref[j] = (acc * scale).astype(jnp.bfloat16)
    copy.wait()


def image_part(me, blocks, gain, sel, held, w_out, n_rows):
    n_img, width = blocks[0].shape
    return pl.pallas_call(
        functools.partial(image_kernel, n_rows, len(blocks)),
        out_shape=(
            jax.ShapeDtypeStruct((3, n_img, held.shape[3]), jnp.bfloat16),
            jax.ShapeDtypeStruct((n_img, width), jnp.bfloat16),
            pltpu.VMEM(w_out.shape, w_out.dtype),
        ),
        in_specs=[pl.BlockSpec(memory_space=pltpu.SMEM)]
        + vmem_specs(len(blocks) + 3)
        + [pl.BlockSpec(memory_space=pltpu.HBM)],
        out_specs=tuple(vmem_specs(3)),
        scratch_shapes=[pltpu.SemaphoreType.DMA],
        compiler_params=params(12),
        cost_estimate=pl.CostEstimate(flops=0, bytes_accessed=0, transcendentals=0),
    )(me, *blocks, gain, sel, held, in_hbm(w_out))


def project_side(side, far, me_ref, x_ref, gain_ref, held_ref, acc_ref, ss_ref, out_ref):
    half = x_ref.shape[0]
    part = pl.ds(side * half, half)
    x, total = scale_rows(x_ref[...], gain_ref[me_ref[0] ^ far])
    scale = lax.rsqrt((ss_ref[part] + total) / D + EPS)[:, :1]
    for j in range(3):
        prod = jnp.dot(x, held_ref[far, j], preferred_element_type=jnp.float32)
        out_ref[j, part] = ((prod + acc_ref[j, part]) * scale).astype(jnp.bfloat16)


def attend(edges, first, qkv_ref, key_ref, ctx_ref):
    heads = [pl.ds(h * HD, HD) for h in range(ctx_ref.shape[1] // HD)]
    for low, last in zip(edges, edges[1:]):
        here, step = pl.ds(low, last - low), last - low
        row = lax.broadcasted_iota(jnp.int32, (step, last), 0) + low
        col = lax.broadcasted_iota(jnp.int32, (step, last), 1)
        bias = jnp.where((row >= col) & (key_ref[0:1, pl.ds(0, last)] > 0.5), 0.0, -1e30)
        scores = [
            lax.dot_general(
                qkv_ref[0, here, lanes],
                qkv_ref[1, pl.ds(0, last), lanes],
                (((1,), (1,)), ((), ())),
                preferred_element_type=jnp.float32,
            )
            for lanes in heads
        ]
        scores = [x * (LOG2E / HD**0.5) + bias for x in scores]
        tops = [jnp.max(x, axis=1, keepdims=True) for x in scores]
        expo = [jnp.exp2(x - top) for x, top in zip(scores, tops)]
        sums = [jnp.sum(x, axis=1, keepdims=True) for x in expo]
        outs = [
            jnp.dot(x.astype(jnp.bfloat16), qkv_ref[2, pl.ds(0, last), lanes], preferred_element_type=jnp.float32)
            for x, lanes in zip(expo, heads)
        ]
        for lanes, out, total in zip(heads, outs, sums):
            ctx_ref[pl.ds(low - first, step), lanes] = (out / total).astype(jnp.bfloat16)


def put_columns(product, outs):
    half = outs[0].shape[1]
    for i, out_ref in enumerate(outs):
        out_ref[...] = product[:, i * half : (i + 1) * half].astype(out_ref.dtype)


def head_kernel(far, me_ref, top_ref, gain_ref, held_ref, acc_ref, ss_ref, img_ref, text_at_ref, img_at_ref, key_ref,
                w_out_ref, text_qkv_ref, qkv_ref, ctx_ref, left_ref, right_ref):
    rows = ctx_ref.shape[0]
    width = 2 * left_ref.shape[1]
    project_side(0, far, me_ref, top_ref, gain_ref, held_ref, acc_ref, ss_ref, text_qkv_ref)
    for j in range(3):
        qkv = jnp.dot(text_at_ref[:rows, :rows], text_qkv_ref[j], preferred_element_type=jnp.float32)
        qkv += jnp.dot(img_at_ref[:rows], img_ref[j], preferred_element_type=jnp.float32)
        qkv_ref[j] = qkv.astype(jnp.bfloat16)
    attend([0, rows], 0, qkv_ref, key_ref, ctx_ref)
    weight = cols_of(w_out_ref, me_ref[0] ^ far, width)
    put_columns(jnp.dot(ctx_ref[...], weight, preferred_element_type=jnp.float32), (left_ref, right_ref))


def head_part(far, me, top, gain, held, acc, ss, img, text_at, img_at, key_ok, w_out):
    width, cols = held.shape[2:]
    rows = top.shape[0]
    bf16 = jnp.bfloat16
    return pl.pallas_call(
        functools.partial(head_kernel, far),
        out_shape=(
            jax.ShapeDtypeStruct((3, rows, cols), bf16),
            jax.ShapeDtypeStruct((3, rows, cols), bf16),
            jax.ShapeDtypeStruct((rows, cols), bf16),
            jax.ShapeDtypeStruct((rows, width // 2), bf16),
            jax.ShapeDtypeStruct((rows, width // 2), bf16),
        ),
        in_specs=[pl.BlockSpec(memory_space=pltpu.SMEM)] + vmem_specs(10),
        out_specs=tuple(vmem_specs(5)),
        compiler_params=params(12),
        cost_estimate=TINY,
    )(me, top, gain, held, acc, ss, img, text_at, img_at, key_ok, w_out)


def tail_kernel(far, me_ref, bottom_ref, gain_ref, held_ref, acc_ref, ss_ref, img_ref, text_at_ref, img_at_ref,
                key_ref, w_out_ref, top_qkv_ref, head_qkv_ref, ctx_ref, left_ref, right_ref, text_qkv_ref, qkv_ref):
    first = top_qkv_ref.shape[1]
    length = text_at_ref.shape[0]
    width = 2 * left_ref.shape[1]
    project_side(1, far, me_ref, bottom_ref, gain_ref, held_ref, acc_ref, ss_ref, text_qkv_ref)
    for j in range(3):
        text_qkv_ref[j, :first] = top_qkv_ref[j]
        qkv_ref[j, :first] = head_qkv_ref[j]
        qkv = jnp.dot(text_at_ref[first:], text_qkv_ref[j], preferred_element_type=jnp.float32)
        qkv += jnp.dot(img_at_ref[first:], img_ref[j], preferred_element_type=jnp.float32)
        qkv_ref[j, first:] = qkv.astype(jnp.bfloat16)
    edges = [first] + [at for at in range(128, length, 128) if at > first] + [length]
    attend(edges, first, qkv_ref, key_ref, ctx_ref)
    weight = cols_of(w_out_ref, me_ref[0] ^ far, width)
    put_columns(jnp.dot(ctx_ref[...], weight, preferred_element_type=jnp.float32), (left_ref, right_ref))


def tail_part(far, me, bottom, gain, held, acc, ss, img, text_at, img_at, key_ok, w_out, top_qkv, head_qkv):
    width, cols = held.shape[2:]
    length, n_text = text_at.shape
    rows = length - top_qkv.shape[1]
    bf16 = jnp.bfloat16
    return pl.pallas_call(
        functools.partial(tail_kernel, far),
        out_shape=(
            jax.ShapeDtypeStruct((rows, cols), bf16),
            jax.ShapeDtypeStruct((rows, width // 2), bf16),
            jax.ShapeDtypeStruct((rows, width // 2), bf16),
        ),
        in_specs=[pl.BlockSpec(memory_space=pltpu.SMEM)] + vmem_specs(12),
        out_specs=tuple(vmem_specs(3)),
        scratch_shapes=[pltpu.VMEM((3, n_text, cols), bf16), pltpu.VMEM((3, length, cols), bf16)],
        compiler_params=params(12),
        cost_estimate=pl.CostEstimate(flops=10**10, bytes_accessed=0, transcendentals=0),
    )(me, bottom, gain, held, acc, ss, img, text_at, img_at, key_ok, w_out, top_qkv, head_qkv)


def out_kernel(away, me_ref, head_ref, tail_ref, w_ref, left_ref, right_ref):
    first = head_ref.shape[0]
    weight = cols_of(w_ref, me_ref[0] ^ away, 2 * left_ref.shape[1])
    for ctx_ref, rows in ((head_ref, slice(None, first)), (tail_ref, slice(first, None))):
        product = jnp.dot(ctx_ref[...], weight, preferred_element_type=jnp.float32)
        put_columns(product, (left_ref.at[rows], right_ref.at[rows]))


def out_part(away, me, head, tail, w, width, dtype=jnp.bfloat16):
    rows = head.shape[0] + tail.shape[0]
    return pl.pallas_call(
        functools.partial(out_kernel, away),
        out_shape=(jax.ShapeDtypeStruct((rows, width // 2), dtype),) * 2,
        in_specs=[pl.BlockSpec(memory_space=pltpu.SMEM)] + vmem_specs(3),
        out_specs=tuple(vmem_specs(2)),
        compiler_params=params(12),
        cost_estimate=pl.CostEstimate(flops=10**9, bytes_accessed=0, transcendentals=0),
    )(me, head, tail, w)


def sum_of(refs):
    return functools.reduce(lambda a, b: a + b, [ref[...].astype(jnp.float32) for ref in refs])


def first_kernel(n_left, base_ref, *refs):
    out_ref = refs[-1]
    half = base_ref.shape[1] // 2
    for side, terms in enumerate((refs[:n_left], refs[n_left:-1])):
        part = pl.ds(side * half, half)
        out_ref[:, part] = base_ref[:, part].astype(jnp.float32) + sum_of(terms)


def add_first(base, left, right):
    return pl.pallas_call(
        functools.partial(first_kernel, len(left)),
        out_shape=jax.ShapeDtypeStruct(base.shape, jnp.float32),
        in_specs=vmem_specs(1 + len(left) + len(right)),
        out_specs=pl.BlockSpec(memory_space=pltpu.VMEM),
        compiler_params=params(12),
        cost_estimate=TINY,
    )(base, *left, *right)


def last_kernel(n_left, base_ref, *refs):
    refs, (out_ref, tmp_ref, sem_ref) = refs[:-3], refs[-3:]
    half = base_ref.shape[1] // 2
    copies = []
    for side, terms in enumerate((refs[:n_left], refs[n_left:])):
        part = pl.ds(side * half, half)
        tmp_ref[:, part] = (base_ref[:, part] + sum_of(terms)).astype(tmp_ref.dtype)
        copy = pltpu.make_async_copy(tmp_ref.at[:, part], out_ref.at[:, part], sem_ref.at[side])
        copy.start()
        copies.append(copy)
    for copy in copies:
        copy.wait()


def add_last(base, left, right):
    return pl.pallas_call(
        functools.partial(last_kernel, len(left)),
        out_shape=jax.ShapeDtypeStruct(base.shape, jnp.bfloat16),
        in_specs=vmem_specs(1 + len(left) + len(right)),
        out_specs=pl.BlockSpec(memory_space=pl.ANY),
        scratch_shapes=[pltpu.VMEM(base.shape, jnp.bfloat16), pltpu.SemaphoreType.DMA((2,))],
        compiler_params=params(12),
        cost_estimate=TINY,
    )(base, *left, *right)


def scatter_terms(parts, got, n):
    acc = {s: [[parts[s][0]], [parts[s][1]]] for s in parts}
    far = n - 1
    acc[far ^ low_bit(far)][0].append(got[0])
    acc[far ^ high_bit(far)][1].append(got[1])
    early, late = [[], []], [[], []]
    for s in by_bits(n, reverse=True)[1:]:
        for side, bit in ((0, low_bit(s)), (1, high_bit(s))):
            terms = [t.astype(jnp.float32) for t in acc[s][side]]
            out = swap(functools.reduce(lambda a, b: a + b, terms).astype(jnp.bfloat16), bit)
            if s == bit:
                (early if len(terms) == 1 else late)[side].append(out)
            else:
                acc[s ^ bit][side].append(out)
    return early, late


def body(text, patches, grids, image_request, slot_start, vis_gain, dec_gain, w_qkv, w_out):
    n_req = lax.axis_size("req")
    n_ten = lax.axis_size("tensor")
    me_req = lax.axis_index("req")
    me_ten = lax.axis_index("tensor")
    img_dev, side, _, width = patches.shape
    half = side // 2
    region = half * half
    length = text.shape[0]
    w3 = jnp.transpose(w_qkv, (1, 0, 2))
    req_at = me_req.astype(jnp.int32)[None]
    ten_at = me_ten.astype(jnp.int32)[None]
    order = by_bits(n_ten)
    near_at, far = order[:-1], order[-1]

    n_rows = n_req * region
    n_img = round_up(n_rows + 1, 16)
    n_text = round_up(length - (n_rows if img_dev == n_req else 0), 32)
    ctext = gather_text(req_at, image_request, slot_start, text, n_req, region, n_text)
    blocks = near_blocks(ctext, n_ten)

    late_text, ctext = lax.optimization_barrier((text, ctext))
    even, odd, rtext, sel, table, key_ok, gains, vis_row = prepare(
        req_at, image_request, slot_start, grids, late_text, jnp.transpose(patches, (1, 2, 0, 3)), dec_gain, vis_gain,
        n_req, n_img
    )
    pairs = mix_pairs(even, swap(odd, 1, "req"), region)
    received = [pairs[0]] + [swap(pairs[i], 2 * i, "req") for i in range(1, n_req // 2)]
    ctext, table, pairs = lax.optimization_barrier((ctext, table, pairs))
    acc, ss, held = own_part(ten_at, ctext, gains, w3)
    text_at, img_at, text_row = placement(table, region, length, n_text, n_img)
    received, acc, text_at = lax.optimization_barrier((received, acc, text_at))
    img_own = pack_images(received, vis_row, rtext, sel, region)
    img_blocks = [img_own] + [swap(img_own, s) for s in range(1, n_ten)]
    handed, img_own = lax.optimization_barrier((blocks, img_own))
    blocks = {**far_blocks(handed, n_ten), **blocks}

    near = [blocks[s] for s in near_at]
    acc, ss = near_part(near_at, ten_at, near, gains, held, acc, ss)
    img_blocks, acc = lax.optimization_barrier((img_blocks, acc))
    img_qkv, merged, w_out = image_part(ten_at, img_blocks, gains, sel, held, w_out, n_rows)

    shared = (gains, held, acc, ss, img_qkv, text_at, img_at, key_ok, w_out)
    top_qkv, head_qkv, head_ctx, *head_far = head_part(far, ten_at, blocks[far][0], *shared)
    tail_ctx, *tail_far = tail_part(far, ten_at, blocks[far][1], *shared, top_qkv, head_qkv)

    img_here = jnp.dot(img_at, merged, preferred_element_type=jnp.float32)
    x_in = (text.astype(jnp.float32) * text_row[:, :1] + img_here).astype(jnp.bfloat16)

    bits = (low_bit(far), high_bit(far))
    head_got = [swap(t, bit) for t, bit in zip(head_far, bits)]
    tail_got = [swap(t, bit) for t, bit in zip(tail_far, bits)]
    head_got, head_ctx, tail_ctx = lax.optimization_barrier((head_got, head_ctx, tail_ctx))
    parts = {}
    for s in reversed([0] + near_at):
        parts[s] = out_part(s, ten_at, head_ctx, tail_ctx, w_out, width, jnp.float32 if s == 0 else jnp.bfloat16)
    got = [jnp.concatenate(pair, axis=0) for pair in zip(head_got, tail_got)]
    early, late = scatter_terms(parts, got, n_ten)
    base = add_first(x_in, [parts[0][0]] + early[0], [parts[0][1]] + early[1])
    return add_last(base, late[0], late[1])


def solution(mesh):
    in_specs = (
        P("req", "tensor"),
        P("req", None, None, "tensor"),
        P(),
        P(),
        P(),
        P("tensor"),
        P(),
        P(None, None, "tensor"),
        P("tensor", None),
    )
    out_specs = P("req", "tensor")
    return jax.shard_map(body, mesh=mesh, in_specs=in_specs, out_specs=out_specs, check_vma=False)
```

```python
import functools

import jax
import jax.numpy as jnp
from jax import lax
from jax.experimental import pallas as pl
from jax.experimental.pallas import tpu as pltpu
from jax.sharding import PartitionSpec as P

D = 4096
HD = 128
EPS = 1e-05
LOG2E = 1.4426950408889634
TINY = pl.CostEstimate(flops=0, bytes_accessed=0, transcendentals=0)


def round_up(n, m):
    return -(-n // m) * m


def swap(x, s, axis="tensor"):
    n = lax.axis_size(axis)
    return lax.ppermute(x, axis, [(i, i ^ s) for i in range(n)])


def in_hbm(x):
    return pltpu.with_memory_space_constraint(x, pltpu.HBM)


def low_bit(s):
    return s & -s


def high_bit(s):
    return 1 << (s.bit_length() - 1)


def by_bits(n, reverse=False):
    return sorted(range(1, n), key=lambda s: (bin(s).count("1"), s), reverse=reverse)


def halves(block):
    if isinstance(block, tuple):
        return block
    half = round_up(block.shape[0] // 2, 16)
    return block[:half], block[half:]


def near_blocks(x, n):
    return {s: swap(x, s) for s in by_bits(n) if s & (s - 1) == 0}


def far_blocks(blocks, n):
    blocks = dict(blocks)
    for s in by_bits(n):
        if s not in blocks:
            low, high = low_bit(s), high_bit(s)
            blocks[s] = (swap(halves(blocks[s ^ low])[0], low), swap(halves(blocks[s ^ high])[1], high))
    return blocks


def vmem_specs(n):
    return [pl.BlockSpec(memory_space=pltpu.VMEM)] * n


def params(mib):
    return pltpu.CompilerParams(vmem_limit_bytes=mib * 1024 * 1024)


def fetch(pairs, sem_ref):
    copies = [pltpu.make_async_copy(src, dst, sem_ref.at[i]) for i, (src, dst) in enumerate(pairs)]
    for copy in copies:
        copy.start()
    return copies


NOWHERE = 1 << 20


def find_images(n_req, img_dev, me, req_ref, start_ref, grid_ref=None):
    found = []
    for s in range(n_req):
        source = (me ^ s) * img_dev

        def one_image(k, found, source=source):
            hit = req_ref[source + k] == me
            values = (start_ref[source + k],)
            if grid_ref is not None:
                values += (grid_ref[0, source + k] // 2, grid_ref[1, source + k] // 2)
            return tuple(jnp.where(hit, new, old) for new, old in zip(values, found))

        none = (jnp.int32(NOWHERE), jnp.int32(0), jnp.int32(1))[: 1 if grid_ref is None else 3]
        found.append(lax.fori_loop(0, img_dev, one_image, none, unroll=img_dev <= 8))
    return found


def text_kernel(n_req, region, me_ref, req_hbm, start_hbm, text_hbm, ctext_out, req_ref, start_ref, text_ref, sem_ref):
    copies = fetch(((req_hbm, req_ref), (start_hbm, start_ref), (text_hbm, text_ref)), sem_ref)
    n_text, length = ctext_out.shape[0], text_ref.shape[0]
    spot = lax.broadcasted_iota(jnp.int32, (8, length), 1)
    before = jnp.zeros((8, length), jnp.int32)
    inside = jnp.zeros((8, length), jnp.int32)
    copies[0].wait()
    copies[1].wait()
    for (start,) in find_images(n_req, req_ref.shape[0] // n_req, me_ref[0], req_ref, start_ref):
        c = spot - start
        before += jnp.clip(c, 0, region)
        inside = jnp.where((c >= 0) & (c < region), 1, inside)
    rank = jnp.where(inside == 1, -1, spot - before)[0:1]
    gather = (lax.broadcasted_iota(jnp.int32, (n_text, length), 0) == rank).astype(jnp.bfloat16)
    copies[2].wait()
    ctext_out[...] = jnp.dot(gather, text_ref[...], preferred_element_type=jnp.float32).astype(jnp.bfloat16)


def gather_text(me, image_request, slot_start, text, n_req, region, n_text):
    inputs = (image_request, slot_start, text)
    return pl.pallas_call(
        functools.partial(text_kernel, n_req, region),
        out_shape=jax.ShapeDtypeStruct((n_text, text.shape[1]), text.dtype),
        in_specs=[pl.BlockSpec(memory_space=pltpu.SMEM)] + [pl.BlockSpec(memory_space=pltpu.HBM)] * 3,
        out_specs=pl.BlockSpec(memory_space=pltpu.VMEM),
        scratch_shapes=[pltpu.SMEM(x.shape, jnp.int32) for x in inputs[:2]]
        + [pltpu.VMEM(text.shape, text.dtype), pltpu.SemaphoreType.DMA((3,))],
        compiler_params=params(8),
        cost_estimate=TINY,
    )(me, *[in_hbm(x) for x in inputs])


def prep_kernel(n_req, me_ref, req_hbm, start_hbm, grid_hbm, text_hbm, x_hbm, dec_hbm, vis_hbm, *refs):
    (even_out, odd_out, rtext_out, sel_out, table_out, key_out, dec_out, vis_out, req_ref, start_ref, grid_ref,
     text_ref, x_ref, dec_ref, vis_ref, tmp_ref, sem_ref) = refs
    pairs = (
        (req_hbm, req_ref),
        (start_hbm, start_ref),
        (grid_hbm, grid_ref),
        (x_hbm, x_ref),
        (text_hbm, text_ref),
        (dec_hbm, dec_ref),
        (vis_hbm, vis_ref),
    )
    copies = fetch(pairs, sem_ref)
    side, img_dev = x_ref.shape[0], x_ref.shape[2]
    half = side // 2
    region = half * half
    n_img, length = sel_out.shape[0], text_ref.shape[0]
    me = me_ref[0]
    tmp_ref[...] = jnp.zeros_like(tmp_ref)
    for copy in copies[:3]:
        copy.wait()

    spot = lax.broadcasted_iota(jnp.int32, (8, length), 1)
    closed = jnp.zeros((8, length), jnp.int32)
    row = lax.broadcasted_iota(jnp.int32, (n_img, 128), 0)
    pos = jnp.full((n_img, 128), -1, jnp.int32)
    target = jnp.full((n_img, 128), -1, jnp.int32)
    line = lax.broadcasted_iota(jnp.int32, (n_req, 128), 0)
    table = jnp.zeros((n_req, 128), jnp.int32)
    for s, (start, high, wide) in enumerate(find_images(n_req, img_dev, me, req_ref, start_ref, grid_ref)):
        count = high * wide
        c = spot - start
        closed = jnp.where((c >= count) & (c < region) & (c >= 0), 1, closed)
        c = row - s * region
        here = (c >= 0) & (c < region)
        pos = jnp.where(here, start + c, pos)
        cell = c
        for w in range(1, half):
            cell = jnp.where(wide == w, c // w * half + c % w, cell)
        target = jnp.where(here & (c < count), s * region + cell, target)
        table = jnp.where(line == s, start, table)
    table_out[...] = table
    key_out[...] = 1.0 - closed.astype(jnp.float32)
    stays = jnp.where(target >= 0, -1, pos)[:, :1]
    keep = (lax.broadcasted_iota(jnp.int32, (n_img, length), 1) == stays).astype(jnp.bfloat16)
    sel = lax.broadcasted_iota(jnp.int32, (n_img, n_img), 1) == target[:, :1]
    sel_out[...] = sel.astype(jnp.bfloat16)
    rows = lax.broadcasted_iota(jnp.int32, (n_req, img_dev), 0)
    cols = lax.broadcasted_iota(jnp.int32, (n_req, img_dev), 1)
    goal = jnp.full((n_req, img_dev), -1, jnp.int32)
    for k in range(img_dev):
        goal = jnp.where(cols == k, req_ref[me * img_dev + k] ^ me, goal)
    onehot = (rows == goal).astype(jnp.bfloat16)

    for copy in copies[3:]:
        copy.wait()
    rtext_out[...] = jnp.dot(keep, text_ref[...], preferred_element_type=jnp.float32).astype(jnp.bfloat16)
    for i in range(half):
        for j in range(half):
            total = x_ref[2 * i, 2 * j].astype(jnp.float32)
            for a, b in ((0, 1), (1, 0), (1, 1)):
                total += x_ref[2 * i + a, 2 * j + b].astype(jnp.float32)
            pooled = (total * 0.25).astype(jnp.bfloat16)
            tmp_ref[:, i * half + j, :] = jnp.dot(onehot, pooled, preferred_element_type=jnp.float32)
    for s in range(n_req):
        (even_out, odd_out)[s % 2][s // 2] = tmp_ref[s].astype(jnp.bfloat16)
    per = vis_ref.shape[0]
    for i in range(per):
        lanes = pl.ds(i * 128, 128)
        vis_out[:, lanes] = vis_ref[i : i + 1, :].astype(jnp.float32)
        for t in range(dec_out.shape[0]):
            at = t * per + i
            dec_out[t, :, lanes] = dec_ref[at : at + 1, :].astype(jnp.float32)


def prepare(me, image_request, slot_start, grids, text, patches, dec_gain, vis_gain, n_req, n_img):
    side, _, img_dev, width = patches.shape
    padded = round_up((side // 2) ** 2, 16)
    inputs = (
        image_request,
        slot_start,
        grids.T,
        text,
        patches,
        dec_gain.reshape(-1, 128),
        vis_gain.reshape(-1, 128),
    )
    bf16, f32 = jnp.bfloat16, jnp.float32
    outputs = [((n_req // 2, padded, width), bf16)] * 2 + [
        ((n_img, width), bf16),
        ((n_img, n_img), bf16),
        ((n_req, 128), jnp.int32),
        ((8, text.shape[0]), f32),
        ((dec_gain.size // width, 1, width), f32),
        ((1, width), f32),
    ]
    return pl.pallas_call(
        functools.partial(prep_kernel, n_req),
        out_shape=tuple(jax.ShapeDtypeStruct(shape, kind) for shape, kind in outputs),
        in_specs=[pl.BlockSpec(memory_space=pltpu.SMEM)] + [pl.BlockSpec(memory_space=pltpu.HBM)] * len(inputs),
        out_specs=tuple(vmem_specs(len(outputs))),
        scratch_shapes=[pltpu.SMEM(x.shape, jnp.int32) for x in inputs[:3]]
        + [pltpu.VMEM(x.shape, x.dtype) for x in inputs[3:]]
        + [pltpu.VMEM((n_req, padded, width), f32), pltpu.SemaphoreType.DMA((len(inputs),))],
        compiler_params=params(12),
        cost_estimate=TINY,
    )(me, *[in_hbm(x) for x in inputs])


def mix_kernel(region, even_ref, odd_ref, *refs):
    outs, tmp_ref = refs[:-1], refs[-1]
    for i, out_ref in enumerate(outs):
        tmp_ref[:region] = even_ref[i].astype(jnp.float32)[:region]
        tmp_ref[region : 2 * region] = odd_ref[i].astype(jnp.float32)[:region]
        tmp_ref[2 * region :] = jnp.zeros((tmp_ref.shape[0] - 2 * region, tmp_ref.shape[1]), jnp.float32)
        out_ref[...] = tmp_ref[...].astype(jnp.bfloat16)


def mix_pairs(even, odd, region):
    n, _, width = even.shape
    rows = round_up(2 * region, 8)
    return pl.pallas_call(
        functools.partial(mix_kernel, region),
        out_shape=(jax.ShapeDtypeStruct((rows, width), jnp.bfloat16),) * n,
        in_specs=vmem_specs(2),
        out_specs=tuple(vmem_specs(n)),
        scratch_shapes=[pltpu.VMEM((rows, width), jnp.float32)],
        compiler_params=params(4),
        cost_estimate=TINY,
    )(even, odd)


def pack_kernel(region, gain_ref, rtext_ref, sel_ref, *refs):
    recs, (out_ref, tmp_ref) = refs[:-2], refs[-2:]
    done = 0
    for rec_ref in recs:
        tmp_ref[done : done + 2 * region] = rec_ref[...].astype(jnp.float32)[: 2 * region]
        done += 2 * region
    rest = tmp_ref.shape[0] - done
    tmp_ref[done:] = jnp.zeros((rest, tmp_ref.shape[1]), jnp.float32)
    picked = jnp.dot(sel_ref[...], tmp_ref[...].astype(jnp.bfloat16), preferred_element_type=jnp.float32)
    tmp_ref[...] = picked + rtext_ref[...].astype(jnp.float32)
    tmp_ref[done:] = jnp.broadcast_to(gain_ref[0:1, :], (rest, gain_ref.shape[1]))
    out_ref[...] = tmp_ref[...].astype(jnp.bfloat16)


def pack_images(received, gain, rtext, sel, region):
    n_img, width = rtext.shape
    return pl.pallas_call(
        functools.partial(pack_kernel, region),
        out_shape=jax.ShapeDtypeStruct((n_img, width), jnp.bfloat16),
        in_specs=vmem_specs(3 + len(received)),
        out_specs=pl.BlockSpec(memory_space=pltpu.VMEM),
        scratch_shapes=[pltpu.VMEM((n_img, width), jnp.float32)],
        compiler_params=params(4),
        cost_estimate=TINY,
    )(gain, rtext, sel, *received)


def place_kernel(region, table_ref, text_at_ref, img_at_ref, text_row_ref):
    length, n_text = text_at_ref.shape
    spot = lax.broadcasted_iota(jnp.int32, (length, 128), 0)
    before = jnp.zeros((length, 128), jnp.int32)
    at = jnp.full((length, 128), -1, jnp.int32)
    for s in range(table_ref.shape[0]):
        c = spot - table_ref[s : s + 1, :]
        before += jnp.clip(c, 0, region)
        at = jnp.where((c >= 0) & (c < region), s * region + c, at)
    text_row_ref[...] = jnp.where(at < 0, 1.0, 0.0)
    rank = jnp.where(at < 0, spot - before, -1)[:, :1]
    text_at_ref[...] = (lax.broadcasted_iota(jnp.int32, (length, n_text), 1) == rank).astype(jnp.bfloat16)
    lane = lax.broadcasted_iota(jnp.int32, img_at_ref.shape, 1)
    img_at_ref[...] = (lane == at[:, :1]).astype(jnp.bfloat16)


def placement(table, region, length, n_text, n_img):
    return pl.pallas_call(
        functools.partial(place_kernel, region),
        out_shape=(
            jax.ShapeDtypeStruct((length, n_text), jnp.bfloat16),
            jax.ShapeDtypeStruct((length, n_img), jnp.bfloat16),
            jax.ShapeDtypeStruct((length, 128), jnp.float32),
        ),
        in_specs=vmem_specs(1),
        out_specs=tuple(vmem_specs(3)),
        compiler_params=params(8),
        cost_estimate=TINY,
    )(table)


def cols_of(ref, owner, width):
    return ref[:, pl.ds(pl.multiple_of(owner * width, width), width)]


def scale_rows(x, gain):
    xf = x.astype(jnp.float32)
    return (xf * gain).astype(jnp.bfloat16), jnp.sum(xf * xf, axis=1, keepdims=True)


def own_kernel(me_ref, x_ref, gain_ref, w_ref, acc_ref, ss_ref, held_ref, sem_ref):
    n_ten, _, width, _ = held_ref.shape
    half = x_ref.shape[0] // 2
    copies = []
    for s in range(n_ten):
        rows = pl.ds(pl.multiple_of((me_ref[0] ^ s) * width, width), width)
        copies += [pltpu.make_async_copy(w_ref.at[j, rows], held_ref.at[s, j], sem_ref.at[s, j]) for j in range(3)]
    for copy in copies:
        copy.start()
    scaled = []
    for side in range(2):
        rows = pl.ds(side * half, half)
        x, total = scale_rows(x_ref[rows], gain_ref[me_ref[0]])
        scaled.append(x)
        ss_ref[rows] = jnp.broadcast_to(total, (half, 128))
    for j in range(3):
        copies[j].wait()
        for side in range(2):
            acc_ref[j, pl.ds(side * half, half)] = jnp.dot(
                scaled[side], held_ref[0, j], preferred_element_type=jnp.float32
            )
    for copy in copies[3:]:
        copy.wait()


def own_part(me, x, gain, w):
    rows, width = x.shape
    n_ten, cols = gain.shape[0], w.shape[2]
    return pl.pallas_call(
        own_kernel,
        out_shape=(
            jax.ShapeDtypeStruct((3, rows, cols), jnp.float32),
            jax.ShapeDtypeStruct((rows, 128), jnp.float32),
            pltpu.VMEM((n_ten, 3, width, cols), w.dtype),
        ),
        in_specs=[pl.BlockSpec(memory_space=pltpu.SMEM)] + vmem_specs(2) + [pl.BlockSpec(memory_space=pltpu.HBM)],
        out_specs=tuple(vmem_specs(3)),
        scratch_shapes=[pltpu.SemaphoreType.DMA((n_ten, 3))],
        compiler_params=params(12),
        cost_estimate=TINY,
    )(me, x, gain, in_hbm(w))


def near_kernel(near, pieces, me_ref, *refs):
    n_x = sum(pieces)
    x_refs, refs = list(refs[:n_x]), refs[n_x:]
    gain_ref, held_ref, acc_in, ss_in, acc_ref, ss_ref = refs
    half = acc_ref.shape[1] // 2
    views = []
    for n in pieces:
        mine, x_refs = x_refs[:n], x_refs[n:]
        views.append([mine[0].at[pl.ds(side * half, half)] if n == 1 else mine[side] for side in range(2)])
    scaled = {}
    for side in range(2):
        rows = pl.ds(side * half, half)
        total = ss_in[rows]
        for b, s in enumerate(near):
            scaled[side, b], part = scale_rows(views[b][side][...], gain_ref[me_ref[0] ^ s])
            total += part
        ss_ref[rows] = total
    for j in range(3):
        for side in range(2):
            rows = pl.ds(side * half, half)
            acc = acc_in[j, rows]
            for b, s in enumerate(near):
                acc += jnp.dot(scaled[side, b], held_ref[s, j], preferred_element_type=jnp.float32)
            acc_ref[j, rows] = acc


def near_part(near, me, blocks, gain, held, acc, ss):
    blocks = [b if isinstance(b, tuple) else (b,) for b in blocks]
    pieces = [len(b) for b in blocks]
    return pl.pallas_call(
        functools.partial(near_kernel, near, pieces),
        out_shape=(
            jax.ShapeDtypeStruct(acc.shape, jnp.float32),
            jax.ShapeDtypeStruct(ss.shape, jnp.float32),
        ),
        in_specs=[pl.BlockSpec(memory_space=pltpu.SMEM)]
        + vmem_specs(sum(pieces) + 4),
        out_specs=tuple(vmem_specs(2)),
        compiler_params=params(12),
        cost_estimate=pl.CostEstimate(flops=10**11, bytes_accessed=0, transcendentals=0),
    )(me, *[h for b in blocks for h in b], gain, held, acc, ss)


def image_rows(x, vis_row, is_img, gain):
    xf = x.astype(jnp.float32)
    y = jnp.where(is_img, xf * vis_row, xf)
    sums = [jnp.sum(t * t, axis=1, keepdims=True) for t in (xf, y)]
    return (y * gain).astype(jnp.bfloat16), *sums


def image_flags(sel_ref):
    return jnp.sum(sel_ref[...].astype(jnp.float32), axis=1, keepdims=True) > 0.5


def image_kernel(n_rows, away, me_ref, *refs):
    x_refs, refs = refs[: len(away)], refs[len(away) :]
    gain_ref, sel_ref, held_ref, w_out_ref, acc_ref, sums_ref, w_out_held, sem_ref = refs
    copy = pltpu.make_async_copy(w_out_ref, w_out_held, sem_ref)
    copy.start()
    is_img = image_flags(sel_ref)
    before, after = 0.0, 0.0
    scaled = []
    for s, x_ref in zip(away, x_refs):
        x = x_ref[...]
        vis_row = x.astype(jnp.float32)[n_rows : n_rows + 1]
        rows, one, two = image_rows(x, vis_row, is_img, gain_ref[me_ref[0] ^ s])
        scaled.append(rows)
        before += one
        after += two
    sums_ref[0] = jnp.broadcast_to(before, sums_ref.shape[1:])
    sums_ref[1] = jnp.broadcast_to(after, sums_ref.shape[1:])
    for j in range(3):
        acc = 0.0
        for s, rows in zip(away, scaled):
            acc += jnp.dot(rows, held_ref[s, j], preferred_element_type=jnp.float32)
        acc_ref[j] = acc
    copy.wait()


def image_part(away, me, blocks, gain, sel, held, w_out, n_rows):
    n_img = sel.shape[0]
    return pl.pallas_call(
        functools.partial(image_kernel, n_rows, away),
        out_shape=(
            jax.ShapeDtypeStruct((3, n_img, held.shape[3]), jnp.float32),
            jax.ShapeDtypeStruct((2, n_img, 128), jnp.float32),
            pltpu.VMEM(w_out.shape, w_out.dtype),
        ),
        in_specs=[pl.BlockSpec(memory_space=pltpu.SMEM)]
        + vmem_specs(len(blocks) + 3)
        + [pl.BlockSpec(memory_space=pltpu.HBM)],
        out_specs=tuple(vmem_specs(3)),
        scratch_shapes=[pltpu.SemaphoreType.DMA],
        compiler_params=params(12),
        cost_estimate=pl.CostEstimate(flops=3*10**9, bytes_accessed=0, transcendentals=0),
    )(me, *blocks, gain, sel, held, in_hbm(w_out))


def image_end_kernel(n_rows, away, me_ref, *refs):
    x_refs, refs = refs[: 2 * len(away)], refs[2 * len(away) :]
    own_ref, gain_ref, sel_ref, held_ref, acc_ref, sums_ref, qkv_ref, merged_ref = refs
    is_img = image_flags(sel_ref)
    half = x_refs[0].shape[0]
    before, after = sums_ref[0], sums_ref[1]
    parts = ((0, half), (half, sel_ref.shape[0]))
    scaled, one, two = [], [[], []], [[], []]
    for i, s in enumerate(away):
        vis_row = x_refs[2 * i + 1][...].astype(jnp.float32)[n_rows - half : n_rows - half + 1]
        for side, (low, high) in enumerate(parts):
            x = x_refs[2 * i + side][...]
            rows, a, b = image_rows(x, vis_row, is_img[low:high], gain_ref[me_ref[0] ^ s])
            scaled.append(rows)
            one[side].append(a)
            two[side].append(b)
    norms, scales = [], []
    for side, (low, high) in enumerate(parts):
        merge = lax.rsqrt((before[low:high] + sum(one[side])) / D + EPS)[:, :1]
        merge = jnp.where(is_img[low:high], merge, 1.0)
        mean = (after[low:high] + sum(two[side]))[:, :1] * merge * merge / D
        norms.append(lax.rsqrt(mean + EPS) * merge)
        scales.append(merge)
    for j in range(3):
        for side, (low, high) in enumerate(parts):
            acc = acc_ref[j, low:high]
            for i, s in enumerate(away):
                acc += jnp.dot(scaled[2 * i + side], held_ref[s, j], preferred_element_type=jnp.float32)
            qkv_ref[j, low:high] = (acc * norms[side]).astype(jnp.bfloat16)
    own = own_ref[...].astype(jnp.float32)
    own = jnp.where(is_img, own * own[n_rows : n_rows + 1], own)
    for side, (low, high) in enumerate(parts):
        merged_ref[low:high] = (own[low:high] * scales[side]).astype(jnp.bfloat16)


def image_end(away, me, blocks, own, gain, sel, held, acc, sums, n_rows):
    n_img, width = own.shape
    return pl.pallas_call(
        functools.partial(image_end_kernel, n_rows, away),
        out_shape=(
            jax.ShapeDtypeStruct((3, n_img, held.shape[3]), jnp.bfloat16),
            jax.ShapeDtypeStruct((n_img, width), jnp.bfloat16),
        ),
        in_specs=[pl.BlockSpec(memory_space=pltpu.SMEM)] + vmem_specs(2 * len(blocks) + 6),
        out_specs=tuple(vmem_specs(2)),
        compiler_params=params(12),
        cost_estimate=TINY,
    )(me, *[h for b in blocks for h in b], own, gain, sel, held, acc, sums)


def project_side(side, far, me_ref, x_ref, gain_ref, held_ref, acc_ref, ss_ref, out_ref):
    half = x_ref.shape[0]
    part = pl.ds(side * half, half)
    x, total = scale_rows(x_ref[...], gain_ref[me_ref[0] ^ far])
    scale = lax.rsqrt((ss_ref[part] + total) / D + EPS)[:, :1]
    for j in range(3):
        prod = jnp.dot(x, held_ref[far, j], preferred_element_type=jnp.float32)
        out_ref[j, part] = ((prod + acc_ref[j, part]) * scale).astype(jnp.bfloat16)


def attend(edges, first, qkv_ref, key_ref, ctx_ref):
    heads = [pl.ds(h * HD, HD) for h in range(ctx_ref.shape[1] // HD)]
    for low, last in zip(edges, edges[1:]):
        here, step = pl.ds(low, last - low), last - low
        row = lax.broadcasted_iota(jnp.int32, (step, last), 0) + low
        col = lax.broadcasted_iota(jnp.int32, (step, last), 1)
        bias = jnp.where((row >= col) & (key_ref[0:1, pl.ds(0, last)] > 0.5), 0.0, -1e30)
        scores = [
            lax.dot_general(
                qkv_ref[0, here, lanes],
                qkv_ref[1, pl.ds(0, last), lanes],
                (((1,), (1,)), ((), ())),
                preferred_element_type=jnp.float32,
            )
            for lanes in heads
        ]
        scores = [x * (LOG2E / HD**0.5) + bias for x in scores]
        tops = [jnp.max(x, axis=1, keepdims=True) for x in scores]
        expo = [jnp.exp2(x - top) for x, top in zip(scores, tops)]
        sums = [jnp.sum(x, axis=1, keepdims=True) for x in expo]
        outs = [
            jnp.dot(x.astype(jnp.bfloat16), qkv_ref[2, pl.ds(0, last), lanes], preferred_element_type=jnp.float32)
            for x, lanes in zip(expo, heads)
        ]
        for lanes, out, total in zip(heads, outs, sums):
            ctx_ref[pl.ds(low - first, step), lanes] = (out / total).astype(jnp.bfloat16)


def put_columns(product, outs):
    half = outs[0].shape[1]
    for i, out_ref in enumerate(outs):
        out_ref[...] = product[:, i * half : (i + 1) * half].astype(out_ref.dtype)


def head_kernel(far, me_ref, top_ref, gain_ref, held_ref, acc_ref, ss_ref, img_ref, text_at_ref, img_at_ref, key_ref,
                w_out_ref, text_qkv_ref, qkv_ref, ctx_ref, left_ref, right_ref):
    rows = ctx_ref.shape[0]
    width = 2 * left_ref.shape[1]
    project_side(0, far, me_ref, top_ref, gain_ref, held_ref, acc_ref, ss_ref, text_qkv_ref)
    for j in range(3):
        qkv = jnp.dot(text_at_ref[:rows, :rows], text_qkv_ref[j], preferred_element_type=jnp.float32)
        qkv += jnp.dot(img_at_ref[:rows], img_ref[j], preferred_element_type=jnp.float32)
        qkv_ref[j] = qkv.astype(jnp.bfloat16)
    attend([0, rows], 0, qkv_ref, key_ref, ctx_ref)
    weight = cols_of(w_out_ref, me_ref[0] ^ far, width)
    put_columns(jnp.dot(ctx_ref[...], weight, preferred_element_type=jnp.float32), (left_ref, right_ref))


def head_part(far, me, top, gain, held, acc, ss, img, text_at, img_at, key_ok, w_out):
    width, cols = held.shape[2:]
    rows = top.shape[0]
    bf16 = jnp.bfloat16
    return pl.pallas_call(
        functools.partial(head_kernel, far),
        out_shape=(
            jax.ShapeDtypeStruct((3, rows, cols), bf16),
            jax.ShapeDtypeStruct((3, rows, cols), bf16),
            jax.ShapeDtypeStruct((rows, cols), bf16),
            jax.ShapeDtypeStruct((rows, width // 2), bf16),
            jax.ShapeDtypeStruct((rows, width // 2), bf16),
        ),
        in_specs=[pl.BlockSpec(memory_space=pltpu.SMEM)] + vmem_specs(10),
        out_specs=tuple(vmem_specs(5)),
        compiler_params=params(12),
        cost_estimate=TINY,
    )(me, top, gain, held, acc, ss, img, text_at, img_at, key_ok, w_out)


def tail_kernel(far, me_ref, bottom_ref, gain_ref, held_ref, acc_ref, ss_ref, img_ref, text_at_ref, img_at_ref,
                key_ref, w_out_ref, top_qkv_ref, head_qkv_ref, ctx_ref, left_ref, right_ref, text_qkv_ref, qkv_ref):
    first = top_qkv_ref.shape[1]
    length = text_at_ref.shape[0]
    width = 2 * left_ref.shape[1]
    project_side(1, far, me_ref, bottom_ref, gain_ref, held_ref, acc_ref, ss_ref, text_qkv_ref)
    for j in range(3):
        text_qkv_ref[j, :first] = top_qkv_ref[j]
        qkv_ref[j, :first] = head_qkv_ref[j]
        qkv = jnp.dot(text_at_ref[first:], text_qkv_ref[j], preferred_element_type=jnp.float32)
        qkv += jnp.dot(img_at_ref[first:], img_ref[j], preferred_element_type=jnp.float32)
        qkv_ref[j, first:] = qkv.astype(jnp.bfloat16)
    edges = [first] + [at for at in range(128, length, 128) if at > first] + [length]
    attend(edges, first, qkv_ref, key_ref, ctx_ref)
    weight = cols_of(w_out_ref, me_ref[0] ^ far, width)
    put_columns(jnp.dot(ctx_ref[...], weight, preferred_element_type=jnp.float32), (left_ref, right_ref))


def tail_part(far, me, bottom, gain, held, acc, ss, img, text_at, img_at, key_ok, w_out, top_qkv, head_qkv):
    width, cols = held.shape[2:]
    length, n_text = text_at.shape
    rows = length - top_qkv.shape[1]
    bf16 = jnp.bfloat16
    return pl.pallas_call(
        functools.partial(tail_kernel, far),
        out_shape=(
            jax.ShapeDtypeStruct((rows, cols), bf16),
            jax.ShapeDtypeStruct((rows, width // 2), bf16),
            jax.ShapeDtypeStruct((rows, width // 2), bf16),
        ),
        in_specs=[pl.BlockSpec(memory_space=pltpu.SMEM)] + vmem_specs(12),
        out_specs=tuple(vmem_specs(3)),
        scratch_shapes=[pltpu.VMEM((3, n_text, cols), bf16), pltpu.VMEM((3, length, cols), bf16)],
        compiler_params=params(12),
        cost_estimate=pl.CostEstimate(flops=10**10, bytes_accessed=0, transcendentals=0),
    )(me, bottom, gain, held, acc, ss, img, text_at, img_at, key_ok, w_out, top_qkv, head_qkv)


def out_kernel(away, me_ref, head_ref, tail_ref, w_ref, left_ref, right_ref):
    first = head_ref.shape[0]
    weight = cols_of(w_ref, me_ref[0] ^ away, 2 * left_ref.shape[1])
    for ctx_ref, rows in ((head_ref, slice(None, first)), (tail_ref, slice(first, None))):
        product = jnp.dot(ctx_ref[...], weight, preferred_element_type=jnp.float32)
        put_columns(product, (left_ref.at[rows], right_ref.at[rows]))


def out_part(away, me, head, tail, w, width, dtype=jnp.bfloat16):
    rows = head.shape[0] + tail.shape[0]
    return pl.pallas_call(
        functools.partial(out_kernel, away),
        out_shape=(jax.ShapeDtypeStruct((rows, width // 2), dtype),) * 2,
        in_specs=[pl.BlockSpec(memory_space=pltpu.SMEM)] + vmem_specs(3),
        out_specs=tuple(vmem_specs(2)),
        compiler_params=params(12),
        cost_estimate=pl.CostEstimate(flops=10**9, bytes_accessed=0, transcendentals=0),
    )(me, head, tail, w)


def sum_of(refs):
    return functools.reduce(lambda a, b: a + b, [ref[...].astype(jnp.float32) for ref in refs])


def first_kernel(n_left, base_ref, *refs):
    out_ref = refs[-1]
    half = base_ref.shape[1] // 2
    for side, terms in enumerate((refs[:n_left], refs[n_left:-1])):
        part = pl.ds(side * half, half)
        out_ref[:, part] = base_ref[:, part].astype(jnp.float32) + sum_of(terms)


def add_first(base, left, right):
    return pl.pallas_call(
        functools.partial(first_kernel, len(left)),
        out_shape=jax.ShapeDtypeStruct(base.shape, jnp.float32),
        in_specs=vmem_specs(1 + len(left) + len(right)),
        out_specs=pl.BlockSpec(memory_space=pltpu.VMEM),
        compiler_params=params(12),
        cost_estimate=TINY,
    )(base, *left, *right)


def last_kernel(n_left, base_ref, *refs):
    refs, (out_ref, tmp_ref, sem_ref) = refs[:-3], refs[-3:]
    half = base_ref.shape[1] // 2
    copies = []
    for side, terms in enumerate((refs[:n_left], refs[n_left:])):
        part = pl.ds(side * half, half)
        tmp_ref[:, part] = (base_ref[:, part] + sum_of(terms)).astype(tmp_ref.dtype)
        copy = pltpu.make_async_copy(tmp_ref.at[:, part], out_ref.at[:, part], sem_ref.at[side])
        copy.start()
        copies.append(copy)
    for copy in copies:
        copy.wait()


def add_last(base, left, right):
    return pl.pallas_call(
        functools.partial(last_kernel, len(left)),
        out_shape=jax.ShapeDtypeStruct(base.shape, jnp.bfloat16),
        in_specs=vmem_specs(1 + len(left) + len(right)),
        out_specs=pl.BlockSpec(memory_space=pl.ANY),
        scratch_shapes=[pltpu.VMEM(base.shape, jnp.bfloat16), pltpu.SemaphoreType.DMA((2,))],
        compiler_params=params(12),
        cost_estimate=TINY,
    )(base, *left, *right)


def scatter_terms(parts, got, n):
    acc = {s: [[parts[s][0]], [parts[s][1]]] for s in parts}
    far = n - 1
    acc[far ^ low_bit(far)][0].append(got[0])
    acc[far ^ high_bit(far)][1].append(got[1])
    early, late = [[], []], [[], []]
    for s in by_bits(n, reverse=True)[1:]:
        for side, bit in ((0, low_bit(s)), (1, high_bit(s))):
            terms = [t.astype(jnp.float32) for t in acc[s][side]]
            out = swap(functools.reduce(lambda a, b: a + b, terms).astype(jnp.bfloat16), bit)
            if s == bit:
                (early if len(terms) == 1 else late)[side].append(out)
            else:
                acc[s ^ bit][side].append(out)
    return early, late


def body(text, patches, grids, image_request, slot_start, vis_gain, dec_gain, w_qkv, w_out):
    n_req = lax.axis_size("req")
    n_ten = lax.axis_size("tensor")
    me_req = lax.axis_index("req")
    me_ten = lax.axis_index("tensor")
    img_dev, side, _, width = patches.shape
    half = side // 2
    region = half * half
    length = text.shape[0]
    w3 = jnp.transpose(w_qkv, (1, 0, 2))
    req_at = me_req.astype(jnp.int32)[None]
    ten_at = me_ten.astype(jnp.int32)[None]
    order = by_bits(n_ten)
    near_at, far = order[:-1], order[-1]

    n_rows = n_req * region
    n_img = round_up(n_rows + 1, 16)
    n_text = round_up(length - (n_rows if img_dev == n_req else 0), 32)
    ctext = gather_text(req_at, image_request, slot_start, text, n_req, region, n_text)
    blocks = near_blocks(ctext, n_ten)

    late_text, ctext = lax.optimization_barrier((text, ctext))
    even, odd, rtext, sel, table, key_ok, gains, vis_row = prepare(
        req_at, image_request, slot_start, grids, late_text, jnp.transpose(patches, (1, 2, 0, 3)), dec_gain, vis_gain,
        n_req, n_img
    )
    pairs = mix_pairs(even, swap(odd, 1, "req"), region)
    received = [pairs[0]] + [swap(pairs[i], 2 * i, "req") for i in range(1, n_req // 2)]
    ctext, table, pairs = lax.optimization_barrier((ctext, table, pairs))
    acc, ss, held = own_part(ten_at, ctext, gains, w3)
    text_at, img_at, text_row = placement(table, region, length, n_text, n_img)
    received, acc, text_at = lax.optimization_barrier((received, acc, text_at))
    img_own = pack_images(received, vis_row, rtext, sel, region)
    img_near = near_blocks(img_own, n_ten)
    one_bit = sorted(img_near)
    more_bits = [s for s in order if s not in img_near]

    blocks, img_own = lax.optimization_barrier((blocks, img_own))
    acc, ss = near_part(one_bit, ten_at, [blocks[s] for s in one_bit], gains, held, acc, ss)
    blocks, acc = lax.optimization_barrier((blocks, acc))
    blocks = far_blocks(blocks, n_ten)
    between = more_bits[:-1]
    if between:
        acc, ss = near_part(between, ten_at, [blocks[s] for s in between], gains, held, acc, ss)
    img_blocks = far_blocks(img_near, n_ten)
    img_acc, img_sums, w_out = image_part(
        [0] + one_bit, ten_at, [img_own] + [img_near[s] for s in one_bit], gains, sel, held, w_out, n_rows
    )
    img_qkv, merged = image_end(
        more_bits, ten_at, [img_blocks[s] for s in more_bits], img_own, gains, sel, held, img_acc, img_sums, n_rows
    )

    shared = (gains, held, acc, ss, img_qkv, text_at, img_at, key_ok, w_out)
    top_qkv, head_qkv, head_ctx, *head_far = head_part(far, ten_at, blocks[far][0], *shared)
    tail_ctx, *tail_far = tail_part(far, ten_at, blocks[far][1], *shared, top_qkv, head_qkv)

    img_here = jnp.dot(img_at, merged, preferred_element_type=jnp.float32)
    x_in = (text.astype(jnp.float32) * text_row[:, :1] + img_here).astype(jnp.bfloat16)

    bits = (low_bit(far), high_bit(far))
    head_got = [swap(t, bit) for t, bit in zip(head_far, bits)]
    tail_got = [swap(t, bit) for t, bit in zip(tail_far, bits)]
    head_got, head_ctx, tail_ctx = lax.optimization_barrier((head_got, head_ctx, tail_ctx))
    parts = {}
    for s in reversed([0] + near_at):
        parts[s] = out_part(s, ten_at, head_ctx, tail_ctx, w_out, width, jnp.float32 if s == 0 else jnp.bfloat16)
    got = [jnp.concatenate(pair, axis=0) for pair in zip(head_got, tail_got)]
    early, late = scatter_terms(parts, got, n_ten)
    base = add_first(x_in, [parts[0][0]] + early[0], [parts[0][1]] + early[1])
    return add_last(base, late[0], late[1])


def solution(mesh):
    in_specs = (
        P("req", "tensor"),
        P("req", None, None, "tensor"),
        P(),
        P(),
        P(),
        P("tensor"),
        P(),
        P(None, None, "tensor"),
        P("tensor", None),
    )
    out_specs = P("req", "tensor")
    return jax.shard_map(body, mesh=mesh, in_specs=in_specs, out_specs=out_specs, check_vma=False)
```

```python
import functools

import jax
import jax.numpy as jnp
from jax import lax
from jax.experimental import pallas as pl
from jax.experimental.pallas import tpu as pltpu
from jax.sharding import PartitionSpec as P

D = 4096
HD = 128
EPS = 1e-05
LOG2E = 1.4426950408889634
TINY = pl.CostEstimate(flops=0, bytes_accessed=0, transcendentals=0)


def round_up(n, m):
    return -(-n // m) * m


def swap(x, s, axis="tensor"):
    n = lax.axis_size(axis)
    return lax.ppermute(x, axis, [(i, i ^ s) for i in range(n)])


def in_hbm(x):
    return pltpu.with_memory_space_constraint(x, pltpu.HBM)


def low_bit(s):
    return s & -s


def high_bit(s):
    return 1 << (s.bit_length() - 1)


def by_bits(n, reverse=False):
    return sorted(range(1, n), key=lambda s: (bin(s).count("1"), s), reverse=reverse)


def halves(block):
    if isinstance(block, tuple):
        return block
    half = block.shape[0] // 2
    return block[:half], block[half:]


def near_blocks(x, n):
    return {s: swap(x, s) for s in by_bits(n) if s & (s - 1) == 0}


def far_blocks(blocks, n):
    blocks = dict(blocks)
    for s in by_bits(n):
        if s not in blocks:
            low, high = low_bit(s), high_bit(s)
            blocks[s] = (swap(halves(blocks[s ^ low])[0], low), swap(halves(blocks[s ^ high])[1], high))
    return blocks


def vmem_specs(n):
    return [pl.BlockSpec(memory_space=pltpu.VMEM)] * n


def params(mib):
    return pltpu.CompilerParams(vmem_limit_bytes=mib * 1024 * 1024)


def fetch(pairs, sem_ref):
    copies = [pltpu.make_async_copy(src, dst, sem_ref.at[i]) for i, (src, dst) in enumerate(pairs)]
    for copy in copies:
        copy.start()
    return copies


NOWHERE = 1 << 20


def find_images(n_req, img_dev, me, req_ref, start_ref, grid_ref=None):
    found = []
    for s in range(n_req):
        source = (me ^ s) * img_dev

        def one_image(k, found, source=source):
            hit = req_ref[source + k] == me
            values = (start_ref[source + k],)
            if grid_ref is not None:
                values += (grid_ref[0, source + k] // 2, grid_ref[1, source + k] // 2)
            return tuple(jnp.where(hit, new, old) for new, old in zip(values, found))

        none = (jnp.int32(NOWHERE), jnp.int32(0), jnp.int32(1))[: 1 if grid_ref is None else 3]
        found.append(lax.fori_loop(0, img_dev, one_image, none, unroll=img_dev <= 8))
    return found


def text_kernel(n_req, region, me_ref, req_hbm, start_hbm, text_hbm, *refs):
    others, (ctext_out, text_ref, *kept), (req_ref, start_ref, sem_ref) = refs[:3], refs[3:8], refs[8:]
    pairs = ((req_hbm, req_ref), (start_hbm, start_ref), (text_hbm, text_ref)) + tuple(zip(others, kept))
    copies = fetch(pairs, sem_ref)
    n_text, length = ctext_out.shape[0], text_ref.shape[0]
    spot = lax.broadcasted_iota(jnp.int32, (8, length), 1)
    before = jnp.zeros((8, length), jnp.int32)
    inside = jnp.zeros((8, length), jnp.int32)
    copies[0].wait()
    copies[1].wait()
    for (start,) in find_images(n_req, req_ref.shape[0] // n_req, me_ref[0], req_ref, start_ref):
        c = spot - start
        before += jnp.clip(c, 0, region)
        inside = jnp.where((c >= 0) & (c < region), 1, inside)
    rank = jnp.where(inside == 1, -1, spot - before)[0:1]
    gather = (lax.broadcasted_iota(jnp.int32, (n_text, length), 0) == rank).astype(jnp.bfloat16)
    copies[2].wait()
    ctext_out[...] = jnp.dot(gather, text_ref[...], preferred_element_type=jnp.float32).astype(jnp.bfloat16)
    for copy in copies[3:]:
        copy.wait()


def gather_text(me, image_request, slot_start, text, patches, dec_gain, vis_gain, n_req, region, n_text):
    inputs = (image_request, slot_start, text, patches, dec_gain.reshape(-1, 128), vis_gain.reshape(-1, 128))
    return pl.pallas_call(
        functools.partial(text_kernel, n_req, region),
        out_shape=(jax.ShapeDtypeStruct((n_text, text.shape[1]), text.dtype),)
        + tuple(pltpu.VMEM(x.shape, x.dtype) for x in inputs[2:]),
        in_specs=[pl.BlockSpec(memory_space=pltpu.SMEM)] + [pl.BlockSpec(memory_space=pltpu.HBM)] * len(inputs),
        out_specs=tuple(vmem_specs(len(inputs) - 1)),
        scratch_shapes=[pltpu.SMEM(x.shape, jnp.int32) for x in inputs[:2]] + [pltpu.SemaphoreType.DMA((len(inputs),))],
        compiler_params=params(8),
        cost_estimate=TINY,
    )(me, *[in_hbm(x) for x in inputs])


def prep_kernel(n_req, me_ref, req_hbm, start_hbm, grid_hbm, text_ref, x_ref, dec_ref, vis_ref, *refs):
    (even_out, odd_out, rtext_out, sel_out, table_out, key_out, dec_out, vis_out, req_ref, start_ref, grid_ref,
     pool_ref, tmp_ref, sem_ref) = refs
    copies = fetch(((req_hbm, req_ref), (start_hbm, start_ref), (grid_hbm, grid_ref)), sem_ref)
    side, img_dev = x_ref.shape[0], x_ref.shape[2]
    half = side // 2
    region = half * half
    n_img, length = sel_out.shape[0], text_ref.shape[0]
    me = me_ref[0]
    for i in range(half):
        for j in range(half):
            total = x_ref[2 * i, 2 * j].astype(jnp.float32)
            for a, b in ((0, 1), (1, 0), (1, 1)):
                total += x_ref[2 * i + a, 2 * j + b].astype(jnp.float32)
            pool_ref[i * half + j] = total * 0.25
    tmp_ref[...] = jnp.zeros_like(tmp_ref)
    for copy in copies:
        copy.wait()

    spot = lax.broadcasted_iota(jnp.int32, (8, length), 1)
    closed = jnp.zeros((8, length), jnp.int32)
    row = lax.broadcasted_iota(jnp.int32, (n_img, 128), 0)
    pos = jnp.full((n_img, 128), -1, jnp.int32)
    target = jnp.full((n_img, 128), -1, jnp.int32)
    line = lax.broadcasted_iota(jnp.int32, (n_req, 128), 0)
    table = jnp.zeros((n_req, 128), jnp.int32)
    for s, (start, high, wide) in enumerate(find_images(n_req, img_dev, me, req_ref, start_ref, grid_ref)):
        count = high * wide
        c = spot - start
        closed = jnp.where((c >= count) & (c < region) & (c >= 0), 1, closed)
        c = row - s * region
        here = (c >= 0) & (c < region)
        pos = jnp.where(here, start + c, pos)
        cell = c
        for w in range(1, half):
            cell = jnp.where(wide == w, c // w * half + c % w, cell)
        target = jnp.where(here & (c < count), s * region + cell, target)
        table = jnp.where(line == s, start, table)
    table_out[...] = table
    key_out[...] = 1.0 - closed.astype(jnp.float32)
    stays = jnp.where(target >= 0, -1, pos)[:, :1]
    keep = (lax.broadcasted_iota(jnp.int32, (n_img, length), 1) == stays).astype(jnp.bfloat16)
    sel = lax.broadcasted_iota(jnp.int32, (n_img, n_img), 1) == target[:, :1]
    sel_out[...] = sel.astype(jnp.bfloat16)
    rows = lax.broadcasted_iota(jnp.int32, (n_req, img_dev), 0)
    cols = lax.broadcasted_iota(jnp.int32, (n_req, img_dev), 1)
    goal = jnp.full((n_req, img_dev), -1, jnp.int32)
    for k in range(img_dev):
        goal = jnp.where(cols == k, req_ref[me * img_dev + k] ^ me, goal)
    onehot = (rows == goal).astype(jnp.bfloat16)

    rtext_out[...] = jnp.dot(keep, text_ref[...], preferred_element_type=jnp.float32).astype(jnp.bfloat16)
    for cell in range(region):
        pooled = pool_ref[cell].astype(jnp.bfloat16)
        tmp_ref[:, cell, :] = jnp.dot(onehot, pooled, preferred_element_type=jnp.float32)
    for s in range(n_req):
        (even_out, odd_out)[s % 2][s // 2] = tmp_ref[s].astype(jnp.bfloat16)
    per = vis_ref.shape[0]
    for i in range(per):
        lanes = pl.ds(i * 128, 128)
        vis_out[:, lanes] = vis_ref[i : i + 1, :].astype(jnp.float32)
        for t in range(dec_out.shape[0]):
            at = t * per + i
            dec_out[t, :, lanes] = dec_ref[at : at + 1, :].astype(jnp.float32)


def prepare(me, image_request, slot_start, grids, text, patches, dec_rows, vis_rows, n_req, n_img):
    side, _, img_dev, width = patches.shape
    padded = round_up((side // 2) ** 2, 16)
    inputs = (image_request, slot_start, grids.T)
    bf16, f32 = jnp.bfloat16, jnp.float32
    outputs = [((n_req // 2, padded, width), bf16)] * 2 + [
        ((n_img, width), bf16),
        ((n_img, n_img), bf16),
        ((n_req, 128), jnp.int32),
        ((8, text.shape[0]), f32),
        ((dec_rows.size // width, 1, width), f32),
        ((1, width), f32),
    ]
    return pl.pallas_call(
        functools.partial(prep_kernel, n_req),
        out_shape=tuple(jax.ShapeDtypeStruct(shape, kind) for shape, kind in outputs),
        in_specs=[pl.BlockSpec(memory_space=pltpu.SMEM)]
        + [pl.BlockSpec(memory_space=pltpu.HBM)] * 3
        + vmem_specs(4),
        out_specs=tuple(vmem_specs(len(outputs))),
        scratch_shapes=[pltpu.SMEM(x.shape, jnp.int32) for x in inputs]
        + [
            pltpu.VMEM(((side // 2) ** 2, img_dev, width), f32),
            pltpu.VMEM((n_req, padded, width), f32),
            pltpu.SemaphoreType.DMA((3,)),
        ],
        compiler_params=params(12),
        cost_estimate=TINY,
    )(me, *[in_hbm(x) for x in inputs], text, patches, dec_rows, vis_rows)


def mix_kernel(region, even_ref, odd_ref, *refs):
    outs, tmp_ref = refs[:-1], refs[-1]
    for i, out_ref in enumerate(outs):
        tmp_ref[:region] = even_ref[i].astype(jnp.float32)[:region]
        tmp_ref[region : 2 * region] = odd_ref[i].astype(jnp.float32)[:region]
        tmp_ref[2 * region :] = jnp.zeros((tmp_ref.shape[0] - 2 * region, tmp_ref.shape[1]), jnp.float32)
        out_ref[...] = tmp_ref[...].astype(jnp.bfloat16)


def mix_pairs(even, odd, region):
    n, _, width = even.shape
    rows = round_up(2 * region, 8)
    return pl.pallas_call(
        functools.partial(mix_kernel, region),
        out_shape=(jax.ShapeDtypeStruct((rows, width), jnp.bfloat16),) * n,
        in_specs=vmem_specs(2),
        out_specs=tuple(vmem_specs(n)),
        scratch_shapes=[pltpu.VMEM((rows, width), jnp.float32)],
        compiler_params=params(4),
        cost_estimate=TINY,
    )(even, odd)


def pack_kernel(region, gain_ref, rtext_ref, sel_ref, *refs):
    recs, (out_ref, tmp_ref) = refs[:-2], refs[-2:]
    done = 0
    for rec_ref in recs:
        tmp_ref[done : done + 2 * region] = rec_ref[...].astype(jnp.float32)[: 2 * region]
        done += 2 * region
    rest = tmp_ref.shape[0] - done
    tmp_ref[done:] = jnp.zeros((rest, tmp_ref.shape[1]), jnp.float32)
    picked = jnp.dot(sel_ref[...], tmp_ref[...].astype(jnp.bfloat16), preferred_element_type=jnp.float32)
    tmp_ref[...] = picked + rtext_ref[...].astype(jnp.float32)
    tmp_ref[done:] = jnp.broadcast_to(gain_ref[0:1, :], (rest, gain_ref.shape[1]))
    out_ref[...] = tmp_ref[...].astype(jnp.bfloat16)


def pack_images(received, gain, rtext, sel, region):
    n_img, width = rtext.shape
    return pl.pallas_call(
        functools.partial(pack_kernel, region),
        out_shape=jax.ShapeDtypeStruct((n_img, width), jnp.bfloat16),
        in_specs=vmem_specs(3 + len(received)),
        out_specs=pl.BlockSpec(memory_space=pltpu.VMEM),
        scratch_shapes=[pltpu.VMEM((n_img, width), jnp.float32)],
        compiler_params=params(4),
        cost_estimate=TINY,
    )(gain, rtext, sel, *received)


def place_kernel(region, table_ref, text_at_ref, img_at_ref, text_row_ref):
    length, n_text = text_at_ref.shape
    spot = lax.broadcasted_iota(jnp.int32, (length, 128), 0)
    before = jnp.zeros((length, 128), jnp.int32)
    at = jnp.full((length, 128), -1, jnp.int32)
    for s in range(table_ref.shape[0]):
        c = spot - table_ref[s : s + 1, :]
        before += jnp.clip(c, 0, region)
        at = jnp.where((c >= 0) & (c < region), s * region + c, at)
    text_row_ref[...] = jnp.where(at < 0, 1.0, 0.0)
    rank = jnp.where(at < 0, spot - before, -1)[:, :1]
    text_at_ref[...] = (lax.broadcasted_iota(jnp.int32, (length, n_text), 1) == rank).astype(jnp.bfloat16)
    lane = lax.broadcasted_iota(jnp.int32, img_at_ref.shape, 1)
    img_at_ref[...] = (lane == at[:, :1]).astype(jnp.bfloat16)


def placement(table, region, length, n_text, n_img):
    return pl.pallas_call(
        functools.partial(place_kernel, region),
        out_shape=(
            jax.ShapeDtypeStruct((length, n_text), jnp.bfloat16),
            jax.ShapeDtypeStruct((length, n_img), jnp.bfloat16),
            jax.ShapeDtypeStruct((length, 128), jnp.float32),
        ),
        in_specs=vmem_specs(1),
        out_specs=tuple(vmem_specs(3)),
        compiler_params=params(8),
        cost_estimate=TINY,
    )(table)


def cols_of(ref, owner, width):
    return ref[:, pl.ds(pl.multiple_of(owner * width, width), width)]


def scale_rows(x, gain):
    xf = x.astype(jnp.float32)
    return (xf * gain).astype(jnp.bfloat16), jnp.sum(xf * xf, axis=1, keepdims=True)


def own_kernel(me_ref, x_ref, gain_ref, w_ref, acc_ref, ss_ref, held_ref, sem_ref):
    n_ten, _, width, _ = held_ref.shape
    half = x_ref.shape[0] // 2
    copies = []
    for s in range(n_ten):
        rows = pl.ds(pl.multiple_of((me_ref[0] ^ s) * width, width), width)
        copies += [pltpu.make_async_copy(w_ref.at[j, rows], held_ref.at[s, j], sem_ref.at[s, j]) for j in range(3)]
    for copy in copies:
        copy.start()
    scaled = []
    for side in range(2):
        rows = pl.ds(side * half, half)
        x, total = scale_rows(x_ref[rows], gain_ref[me_ref[0]])
        scaled.append(x)
        ss_ref[rows] = jnp.broadcast_to(total, (half, 128))
    for j in range(3):
        copies[j].wait()
        for side in range(2):
            acc_ref[j, pl.ds(side * half, half)] = jnp.dot(
                scaled[side], held_ref[0, j], preferred_element_type=jnp.float32
            )
    for copy in copies[3:]:
        copy.wait()


def own_part(me, x, gain, w):
    rows, width = x.shape
    n_ten, cols = gain.shape[0], w.shape[2]
    return pl.pallas_call(
        own_kernel,
        out_shape=(
            jax.ShapeDtypeStruct((3, rows, cols), jnp.float32),
            jax.ShapeDtypeStruct((rows, 128), jnp.float32),
            pltpu.VMEM((n_ten, 3, width, cols), w.dtype),
        ),
        in_specs=[pl.BlockSpec(memory_space=pltpu.SMEM)] + vmem_specs(2) + [pl.BlockSpec(memory_space=pltpu.HBM)],
        out_specs=tuple(vmem_specs(3)),
        scratch_shapes=[pltpu.SemaphoreType.DMA((n_ten, 3))],
        compiler_params=params(12),
        cost_estimate=TINY,
    )(me, x, gain, in_hbm(w))


def near_kernel(near, pieces, me_ref, *refs):
    n_x = sum(pieces)
    x_refs, refs = list(refs[:n_x]), refs[n_x:]
    gain_ref, held_ref, acc_in, ss_in, acc_ref, ss_ref = refs
    half = acc_ref.shape[1] // 2
    views = []
    for n in pieces:
        mine, x_refs = x_refs[:n], x_refs[n:]
        views.append([mine[0].at[pl.ds(side * half, half)] if n == 1 else mine[side] for side in range(2)])
    scaled = {}
    for side in range(2):
        rows = pl.ds(side * half, half)
        total = ss_in[rows]
        for b, s in enumerate(near):
            scaled[side, b], part = scale_rows(views[b][side][...], gain_ref[me_ref[0] ^ s])
            total += part
        ss_ref[rows] = total
    for j in range(3):
        for side in range(2):
            rows = pl.ds(side * half, half)
            acc = acc_in[j, rows]
            for b, s in enumerate(near):
                acc += jnp.dot(scaled[side, b], held_ref[s, j], preferred_element_type=jnp.float32)
            acc_ref[j, rows] = acc


def near_part(near, me, blocks, gain, held, acc, ss):
    blocks = [b if isinstance(b, tuple) else (b,) for b in blocks]
    pieces = [len(b) for b in blocks]
    return pl.pallas_call(
        functools.partial(near_kernel, near, pieces),
        out_shape=(
            jax.ShapeDtypeStruct(acc.shape, jnp.float32),
            jax.ShapeDtypeStruct(ss.shape, jnp.float32),
        ),
        in_specs=[pl.BlockSpec(memory_space=pltpu.SMEM)]
        + vmem_specs(sum(pieces) + 4),
        out_specs=tuple(vmem_specs(2)),
        compiler_params=params(12),
        cost_estimate=pl.CostEstimate(flops=10**11, bytes_accessed=0, transcendentals=0),
    )(me, *[h for b in blocks for h in b], gain, held, acc, ss)


def image_kernel(n_rows, n_blk, me_ref, *refs):
    x_refs, refs = refs[:n_blk], refs[n_blk:]
    gain_ref, sel_ref, held_ref, w_out_ref, qkv_ref, own_ref, w_out_held, sem_ref = refs
    copy = pltpu.make_async_copy(w_out_ref, w_out_held, sem_ref)
    copy.start()
    is_img = jnp.sum(sel_ref[...].astype(jnp.float32), axis=1, keepdims=True) > 0.5
    total = 0.0
    for s in range(n_blk):
        xf = x_refs[s][...].astype(jnp.float32)
        total += jnp.sum(xf * xf, axis=1, keepdims=True)
    scale = lax.rsqrt(total / D + EPS)
    total = 0.0
    scaled = []
    for s in range(n_blk):
        xf = x_refs[s][...].astype(jnp.float32)
        merged = jnp.where(is_img, xf * scale * xf[n_rows : n_rows + 1], xf).astype(jnp.bfloat16)
        if s == 0:
            own_ref[...] = merged
        mf = merged.astype(jnp.float32)
        total += jnp.sum(mf * mf, axis=1, keepdims=True)
        scaled.append((mf * gain_ref[me_ref[0] ^ s]).astype(jnp.bfloat16))
    scale = lax.rsqrt(total / D + EPS)
    for j in range(3):
        acc = 0.0
        for s in range(n_blk):
            acc += jnp.dot(scaled[s], held_ref[s, j], preferred_element_type=jnp.float32)
        qkv_ref[j] = (acc * scale).astype(jnp.bfloat16)
    copy.wait()


def image_part(me, blocks, gain, sel, held, w_out, n_rows):
    n_img, width = blocks[0].shape
    return pl.pallas_call(
        functools.partial(image_kernel, n_rows, len(blocks)),
        out_shape=(
            jax.ShapeDtypeStruct((3, n_img, held.shape[3]), jnp.bfloat16),
            jax.ShapeDtypeStruct((n_img, width), jnp.bfloat16),
            pltpu.VMEM(w_out.shape, w_out.dtype),
        ),
        in_specs=[pl.BlockSpec(memory_space=pltpu.SMEM)]
        + vmem_specs(len(blocks) + 3)
        + [pl.BlockSpec(memory_space=pltpu.HBM)],
        out_specs=tuple(vmem_specs(3)),
        scratch_shapes=[pltpu.SemaphoreType.DMA],
        compiler_params=params(12),
        cost_estimate=pl.CostEstimate(flops=3*10**9, bytes_accessed=0, transcendentals=0),
    )(me, *blocks, gain, sel, held, in_hbm(w_out))


def project_side(side, far, me_ref, x_ref, gain_ref, held_ref, acc_ref, ss_ref, out_ref):
    half = x_ref.shape[0]
    part = pl.ds(side * half, half)
    x, total = scale_rows(x_ref[...], gain_ref[me_ref[0] ^ far])
    scale = lax.rsqrt((ss_ref[part] + total) / D + EPS)[:, :1]
    for j in range(3):
        prod = jnp.dot(x, held_ref[far, j], preferred_element_type=jnp.float32)
        out_ref[j, part] = ((prod + acc_ref[j, part]) * scale).astype(jnp.bfloat16)


def attend(edges, first, qkv_ref, key_ref, ctx_ref):
    heads = [pl.ds(h * HD, HD) for h in range(ctx_ref.shape[1] // HD)]
    for low, last in zip(edges, edges[1:]):
        here, step = pl.ds(low, last - low), last - low
        row = lax.broadcasted_iota(jnp.int32, (step, last), 0) + low
        col = lax.broadcasted_iota(jnp.int32, (step, last), 1)
        bias = jnp.where((row >= col) & (key_ref[0:1, pl.ds(0, last)] > 0.5), 0.0, -1e30)
        scores = [
            lax.dot_general(
                qkv_ref[0, here, lanes],
                qkv_ref[1, pl.ds(0, last), lanes],
                (((1,), (1,)), ((), ())),
                preferred_element_type=jnp.float32,
            )
            for lanes in heads
        ]
        scores = [x * (LOG2E / HD**0.5) + bias for x in scores]
        tops = [jnp.max(x, axis=1, keepdims=True) for x in scores]
        expo = [jnp.exp2(x - top) for x, top in zip(scores, tops)]
        sums = [jnp.sum(x, axis=1, keepdims=True) for x in expo]
        outs = [
            jnp.dot(x.astype(jnp.bfloat16), qkv_ref[2, pl.ds(0, last), lanes], preferred_element_type=jnp.float32)
            for x, lanes in zip(expo, heads)
        ]
        for lanes, out, total in zip(heads, outs, sums):
            ctx_ref[pl.ds(low - first, step), lanes] = (out / total).astype(jnp.bfloat16)


def put_columns(product, outs):
    half = outs[0].shape[1]
    for i, out_ref in enumerate(outs):
        out_ref[...] = product[:, i * half : (i + 1) * half].astype(out_ref.dtype)


def head_kernel(far, me_ref, top_ref, gain_ref, held_ref, acc_ref, ss_ref, img_ref, text_at_ref, img_at_ref, key_ref,
                w_out_ref, text_qkv_ref, qkv_ref, ctx_ref, left_ref, right_ref):
    rows = ctx_ref.shape[0]
    width = 2 * left_ref.shape[1]
    project_side(0, far, me_ref, top_ref, gain_ref, held_ref, acc_ref, ss_ref, text_qkv_ref)
    for j in range(3):
        qkv = jnp.dot(text_at_ref[:rows, :rows], text_qkv_ref[j], preferred_element_type=jnp.float32)
        qkv += jnp.dot(img_at_ref[:rows], img_ref[j], preferred_element_type=jnp.float32)
        qkv_ref[j] = qkv.astype(jnp.bfloat16)
    attend([0, rows], 0, qkv_ref, key_ref, ctx_ref)
    weight = cols_of(w_out_ref, me_ref[0] ^ far, width)
    put_columns(jnp.dot(ctx_ref[...], weight, preferred_element_type=jnp.float32), (left_ref, right_ref))


def head_part(far, me, top, gain, held, acc, ss, img, text_at, img_at, key_ok, w_out):
    width, cols = held.shape[2:]
    rows = top.shape[0]
    bf16 = jnp.bfloat16
    return pl.pallas_call(
        functools.partial(head_kernel, far),
        out_shape=(
            jax.ShapeDtypeStruct((3, rows, cols), bf16),
            jax.ShapeDtypeStruct((3, rows, cols), bf16),
            jax.ShapeDtypeStruct((rows, cols), bf16),
            jax.ShapeDtypeStruct((rows, width // 2), bf16),
            jax.ShapeDtypeStruct((rows, width // 2), bf16),
        ),
        in_specs=[pl.BlockSpec(memory_space=pltpu.SMEM)] + vmem_specs(10),
        out_specs=tuple(vmem_specs(5)),
        compiler_params=params(12),
        cost_estimate=TINY,
    )(me, top, gain, held, acc, ss, img, text_at, img_at, key_ok, w_out)


def tail_kernel(far, me_ref, bottom_ref, gain_ref, held_ref, acc_ref, ss_ref, img_ref, text_at_ref, img_at_ref,
                key_ref, w_out_ref, top_qkv_ref, head_qkv_ref, ctx_ref, left_ref, right_ref, text_qkv_ref, qkv_ref):
    first = top_qkv_ref.shape[1]
    length = text_at_ref.shape[0]
    width = 2 * left_ref.shape[1]
    project_side(1, far, me_ref, bottom_ref, gain_ref, held_ref, acc_ref, ss_ref, text_qkv_ref)
    for j in range(3):
        text_qkv_ref[j, :first] = top_qkv_ref[j]
        qkv_ref[j, :first] = head_qkv_ref[j]
        qkv = jnp.dot(text_at_ref[first:], text_qkv_ref[j], preferred_element_type=jnp.float32)
        qkv += jnp.dot(img_at_ref[first:], img_ref[j], preferred_element_type=jnp.float32)
        qkv_ref[j, first:] = qkv.astype(jnp.bfloat16)
    edges = [first] + [at for at in range(128, length, 128) if at > first] + [length]
    attend(edges, first, qkv_ref, key_ref, ctx_ref)
    weight = cols_of(w_out_ref, me_ref[0] ^ far, width)
    put_columns(jnp.dot(ctx_ref[...], weight, preferred_element_type=jnp.float32), (left_ref, right_ref))


def tail_part(far, me, bottom, gain, held, acc, ss, img, text_at, img_at, key_ok, w_out, top_qkv, head_qkv):
    width, cols = held.shape[2:]
    length, n_text = text_at.shape
    rows = length - top_qkv.shape[1]
    bf16 = jnp.bfloat16
    return pl.pallas_call(
        functools.partial(tail_kernel, far),
        out_shape=(
            jax.ShapeDtypeStruct((rows, cols), bf16),
            jax.ShapeDtypeStruct((rows, width // 2), bf16),
            jax.ShapeDtypeStruct((rows, width // 2), bf16),
        ),
        in_specs=[pl.BlockSpec(memory_space=pltpu.SMEM)] + vmem_specs(12),
        out_specs=tuple(vmem_specs(3)),
        scratch_shapes=[pltpu.VMEM((3, n_text, cols), bf16), pltpu.VMEM((3, length, cols), bf16)],
        compiler_params=params(12),
        cost_estimate=pl.CostEstimate(flops=10**10, bytes_accessed=0, transcendentals=0),
    )(me, bottom, gain, held, acc, ss, img, text_at, img_at, key_ok, w_out, top_qkv, head_qkv)


def out_kernel(away, me_ref, head_ref, tail_ref, w_ref, left_ref, right_ref):
    first = head_ref.shape[0]
    weight = cols_of(w_ref, me_ref[0] ^ away, 2 * left_ref.shape[1])
    for ctx_ref, rows in ((head_ref, slice(None, first)), (tail_ref, slice(first, None))):
        product = jnp.dot(ctx_ref[...], weight, preferred_element_type=jnp.float32)
        put_columns(product, (left_ref.at[rows], right_ref.at[rows]))


def out_part(away, me, head, tail, w, width, dtype=jnp.bfloat16):
    rows = head.shape[0] + tail.shape[0]
    return pl.pallas_call(
        functools.partial(out_kernel, away),
        out_shape=(jax.ShapeDtypeStruct((rows, width // 2), dtype),) * 2,
        in_specs=[pl.BlockSpec(memory_space=pltpu.SMEM)] + vmem_specs(3),
        out_specs=tuple(vmem_specs(2)),
        compiler_params=params(12),
        cost_estimate=pl.CostEstimate(flops=10**9, bytes_accessed=0, transcendentals=0),
    )(me, head, tail, w)


def sum_of(refs):
    return functools.reduce(lambda a, b: a + b, [ref[...].astype(jnp.float32) for ref in refs])


def first_kernel(n_left, base_ref, *refs):
    out_ref = refs[-1]
    half = base_ref.shape[1] // 2
    for side, terms in enumerate((refs[:n_left], refs[n_left:-1])):
        part = pl.ds(side * half, half)
        out_ref[:, part] = base_ref[:, part].astype(jnp.float32) + sum_of(terms)


def add_first(base, left, right):
    return pl.pallas_call(
        functools.partial(first_kernel, len(left)),
        out_shape=jax.ShapeDtypeStruct(base.shape, jnp.float32),
        in_specs=vmem_specs(1 + len(left) + len(right)),
        out_specs=pl.BlockSpec(memory_space=pltpu.VMEM),
        compiler_params=params(12),
        cost_estimate=TINY,
    )(base, *left, *right)


def last_kernel(n_left, base_ref, *refs):
    refs, (out_ref, tmp_ref, sem_ref) = refs[:-3], refs[-3:]
    half = base_ref.shape[1] // 2
    copies = []
    for side, terms in enumerate((refs[:n_left], refs[n_left:])):
        part = pl.ds(side * half, half)
        tmp_ref[:, part] = (base_ref[:, part] + sum_of(terms)).astype(tmp_ref.dtype)
        copy = pltpu.make_async_copy(tmp_ref.at[:, part], out_ref.at[:, part], sem_ref.at[side])
        copy.start()
        copies.append(copy)
    for copy in copies:
        copy.wait()


def add_last(base, left, right):
    return pl.pallas_call(
        functools.partial(last_kernel, len(left)),
        out_shape=jax.ShapeDtypeStruct(base.shape, jnp.bfloat16),
        in_specs=vmem_specs(1 + len(left) + len(right)),
        out_specs=pl.BlockSpec(memory_space=pl.ANY),
        scratch_shapes=[pltpu.VMEM(base.shape, jnp.bfloat16), pltpu.SemaphoreType.DMA((2,))],
        compiler_params=params(12),
        cost_estimate=TINY,
    )(base, *left, *right)


def scatter_terms(parts, got, n):
    acc = {s: [[parts[s][0]], [parts[s][1]]] for s in parts}
    far = n - 1
    acc[far ^ low_bit(far)][0].append(got[0])
    acc[far ^ high_bit(far)][1].append(got[1])
    early, late = [[], []], [[], []]
    for s in by_bits(n, reverse=True)[1:]:
        for side, bit in ((0, low_bit(s)), (1, high_bit(s))):
            terms = [t.astype(jnp.float32) for t in acc[s][side]]
            out = swap(functools.reduce(lambda a, b: a + b, terms).astype(jnp.bfloat16), bit)
            if s == bit:
                (early if len(terms) == 1 else late)[side].append(out)
            else:
                acc[s ^ bit][side].append(out)
    return early, late


def body(text, patches, grids, image_request, slot_start, vis_gain, dec_gain, w_qkv, w_out):
    n_req = lax.axis_size("req")
    n_ten = lax.axis_size("tensor")
    me_req = lax.axis_index("req")
    me_ten = lax.axis_index("tensor")
    img_dev, side, _, width = patches.shape
    half = side // 2
    region = half * half
    length = text.shape[0]
    w3 = jnp.transpose(w_qkv, (1, 0, 2))
    req_at = me_req.astype(jnp.int32)[None]
    ten_at = me_ten.astype(jnp.int32)[None]
    order = by_bits(n_ten)
    near_at, far = order[:-1], order[-1]

    n_rows = n_req * region
    n_img = round_up(n_rows + 1, 16)
    n_text = round_up(length - (n_rows if img_dev == n_req else 0), 32)
    ctext, *kept = gather_text(
        req_at, image_request, slot_start, text, jnp.transpose(patches, (1, 2, 0, 3)), dec_gain, vis_gain, n_req, region,
        n_text
    )
    blocks = near_blocks(ctext, n_ten)

    even, odd, rtext, sel, table, key_ok, gains, vis_row = prepare(
        req_at, image_request, slot_start, grids, *kept, n_req, n_img
    )
    pairs = mix_pairs(even, swap(odd, 1, "req"), region)
    received = [pairs[0]] + [swap(pairs[i], 2 * i, "req") for i in range(1, n_req // 2)]
    ctext, table, pairs = lax.optimization_barrier((ctext, table, pairs))
    acc, ss, held = own_part(ten_at, ctext, gains, w3)
    text_at, img_at, text_row = placement(table, region, length, n_text, n_img)
    received, acc, text_at = lax.optimization_barrier((received, acc, text_at))
    img_own = pack_images(received, vis_row, rtext, sel, region)
    img_blocks = [img_own] + [swap(img_own, s) for s in range(1, n_ten)]

    one_bit = sorted(blocks)
    between = [s for s in near_at if s not in one_bit]
    blocks, img_own = lax.optimization_barrier((blocks, img_own))
    acc, ss = near_part(one_bit, ten_at, [blocks[s] for s in one_bit], gains, held, acc, ss)
    blocks, acc = lax.optimization_barrier((blocks, acc))
    blocks = far_blocks(blocks, n_ten)
    if between:
        acc, ss = near_part(between, ten_at, [blocks[s] for s in between], gains, held, acc, ss)
    img_qkv, merged, w_out = image_part(ten_at, img_blocks, gains, sel, held, w_out, n_rows)

    shared = (gains, held, acc, ss, img_qkv, text_at, img_at, key_ok, w_out)
    top_qkv, head_qkv, head_ctx, *head_far = head_part(far, ten_at, blocks[far][0], *shared)
    tail_ctx, *tail_far = tail_part(far, ten_at, blocks[far][1], *shared, top_qkv, head_qkv)

    img_here = jnp.dot(img_at, merged, preferred_element_type=jnp.float32)
    x_in = (text.astype(jnp.float32) * text_row[:, :1] + img_here).astype(jnp.bfloat16)

    bits = (low_bit(far), high_bit(far))
    head_got = [swap(t, bit) for t, bit in zip(head_far, bits)]
    tail_got = [swap(t, bit) for t, bit in zip(tail_far, bits)]
    head_got, head_ctx, tail_ctx = lax.optimization_barrier((head_got, head_ctx, tail_ctx))
    parts = {}
    for s in reversed([0] + near_at):
        parts[s] = out_part(s, ten_at, head_ctx, tail_ctx, w_out, width, jnp.float32 if s == 0 else jnp.bfloat16)
    got = [jnp.concatenate(pair, axis=0) for pair in zip(head_got, tail_got)]
    early, late = scatter_terms(parts, got, n_ten)
    base = add_first(x_in, [parts[0][0]] + early[0], [parts[0][1]] + early[1])
    return add_last(base, late[0], late[1])


def solution(mesh):
    in_specs = (
        P("req", "tensor"),
        P("req", None, None, "tensor"),
        P(),
        P(),
        P(),
        P("tensor"),
        P(),
        P(None, None, "tensor"),
        P("tensor", None),
    )
    out_specs = P("req", "tensor")
    return jax.shard_map(body, mesh=mesh, in_specs=in_specs, out_specs=out_specs, check_vma=False)
```

```python
import functools

import jax
import jax.numpy as jnp
from jax import lax
from jax.experimental import pallas as pl
from jax.experimental.pallas import tpu as pltpu
from jax.sharding import PartitionSpec as P

D = 4096
HD = 128
EPS = 1e-05
LOG2E = 1.4426950408889634
TINY = pl.CostEstimate(flops=0, bytes_accessed=0, transcendentals=0)


def round_up(n, m):
    return -(-n // m) * m


def swap(x, s, axis="tensor"):
    n = lax.axis_size(axis)
    return lax.ppermute(x, axis, [(i, i ^ s) for i in range(n)])


def in_hbm(x):
    return pltpu.with_memory_space_constraint(x, pltpu.HBM)


def low_bit(s):
    return s & -s


def high_bit(s):
    return 1 << (s.bit_length() - 1)


def by_bits(n, reverse=False):
    return sorted(range(1, n), key=lambda s: (bin(s).count("1"), s), reverse=reverse)


def sides(n):
    half = round_up(n // 2, 16)
    return (0, half), (half, n - half)


def halves(block):
    if isinstance(block, tuple):
        return block
    return tuple(block[first : first + rows] for first, rows in sides(block.shape[0]))


def near_blocks(x, n):
    return {s: swap(x, s) for s in by_bits(n) if s & (s - 1) == 0}


def far_blocks(blocks, n):
    blocks = dict(blocks)
    for s in by_bits(n):
        if s not in blocks:
            low, high = low_bit(s), high_bit(s)
            blocks[s] = (swap(halves(blocks[s ^ low])[0], low), swap(halves(blocks[s ^ high])[1], high))
    return blocks


def vmem_specs(n):
    return [pl.BlockSpec(memory_space=pltpu.VMEM)] * n


def params(mib):
    return pltpu.CompilerParams(vmem_limit_bytes=mib * 1024 * 1024)


def fetch(pairs, sem_ref):
    copies = [pltpu.make_async_copy(src, dst, sem_ref.at[i]) for i, (src, dst) in enumerate(pairs)]
    for copy in copies:
        copy.start()
    return copies


NOWHERE = 1 << 20


def prep_kernel(n_req, me_ref, req_hbm, start_hbm, grid_hbm, text_hbm, x_hbm, dec_hbm, vis_hbm, *refs):
    (even_out, odd_out, ctext_out, rtext_out, sel_out, table_out, key_out, dec_out, vis_out, req_ref, start_ref, grid_ref,
     text_ref, x_ref, dec_ref, vis_ref, tmp_ref, sem_ref) = refs
    pairs = (
        (req_hbm, req_ref),
        (start_hbm, start_ref),
        (grid_hbm, grid_ref),
        (text_hbm, text_ref),
        (x_hbm, x_ref),
        (dec_hbm, dec_ref),
        (vis_hbm, vis_ref),
    )
    copies = fetch(pairs, sem_ref)
    side, img_dev = x_ref.shape[0], x_ref.shape[2]
    half = side // 2
    region = half * half
    n_img, n_text, length = sel_out.shape[0], ctext_out.shape[0], text_ref.shape[0]
    me = me_ref[0]
    for copy in copies[:3]:
        copy.wait()

    found = []
    for s in range(n_req):
        source = (me ^ s) * img_dev

        def one_image(k, found, source=source):
            hit = req_ref[source + k] == me
            values = (start_ref[source + k], grid_ref[0, source + k] // 2, grid_ref[1, source + k] // 2)
            return tuple(jnp.where(hit, new, old) for new, old in zip(values, found))

        none = (jnp.int32(NOWHERE), jnp.int32(0), jnp.int32(1))
        found.append(lax.fori_loop(0, img_dev, one_image, none, unroll=img_dev <= 8))

    spot = lax.broadcasted_iota(jnp.int32, (8, length), 1)
    before = jnp.zeros((8, length), jnp.int32)
    closed = jnp.zeros((8, length), jnp.int32)
    inside = jnp.zeros((8, length), jnp.int32)
    row = lax.broadcasted_iota(jnp.int32, (n_img, 128), 0)
    pos = jnp.full((n_img, 128), -1, jnp.int32)
    target = jnp.full((n_img, 128), -1, jnp.int32)
    line = lax.broadcasted_iota(jnp.int32, (n_req, 128), 0)
    table = jnp.zeros((n_req, 128), jnp.int32)
    for s, (start, high, wide) in enumerate(found):
        count = high * wide
        c = spot - start
        here = (c >= 0) & (c < region)
        before += jnp.clip(c, 0, region)
        inside = jnp.where(here, 1, inside)
        closed = jnp.where(here & (c >= count), 1, closed)
        c = row - s * region
        here = (c >= 0) & (c < region)
        pos = jnp.where(here, start + c, pos)
        cell = c
        for w in range(1, half):
            cell = jnp.where(wide == w, c // w * half + c % w, cell)
        target = jnp.where(here & (c < count), s * region + cell, target)
        table = jnp.where(line == s, start, table)
    table_out[...] = table
    key_out[...] = 1.0 - closed.astype(jnp.float32)
    rank = jnp.where(inside == 1, -1, spot - before)[0:1]
    gather = (lax.broadcasted_iota(jnp.int32, (n_text, length), 0) == rank).astype(jnp.bfloat16)
    stays = jnp.where(target >= 0, -1, pos)[:, :1]
    keep = (lax.broadcasted_iota(jnp.int32, (n_img, length), 1) == stays).astype(jnp.bfloat16)
    sel = lax.broadcasted_iota(jnp.int32, (n_img, n_img), 1) == target[:, :1]
    sel_out[...] = sel.astype(jnp.bfloat16)
    copies[3].wait()
    text = text_ref[...]
    ctext_out[...] = jnp.dot(gather, text, preferred_element_type=jnp.float32).astype(jnp.bfloat16)
    rtext_out[...] = jnp.dot(keep, text, preferred_element_type=jnp.float32).astype(jnp.bfloat16)

    for copy in copies[4:]:
        copy.wait()
    rows = lax.broadcasted_iota(jnp.int32, (n_req, img_dev), 0)
    cols = lax.broadcasted_iota(jnp.int32, (n_req, img_dev), 1)
    goal = jnp.full((n_req, img_dev), -1, jnp.int32)
    for k in range(img_dev):
        goal = jnp.where(cols == k, req_ref[me * img_dev + k] ^ me, goal)
    onehot = (rows == goal).astype(jnp.bfloat16)
    tmp_ref[...] = jnp.zeros_like(tmp_ref)
    for i in range(half):
        for j in range(half):
            total = x_ref[2 * i, 2 * j].astype(jnp.float32)
            for a, b in ((0, 1), (1, 0), (1, 1)):
                total += x_ref[2 * i + a, 2 * j + b].astype(jnp.float32)
            pooled = (total * 0.25).astype(jnp.bfloat16)
            tmp_ref[:, i * half + j, :] = jnp.dot(onehot, pooled, preferred_element_type=jnp.float32)
    for s in range(n_req):
        (even_out, odd_out)[s % 2][s // 2] = tmp_ref[s].astype(jnp.bfloat16)
    per = vis_ref.shape[0]
    for i in range(per):
        lanes = pl.ds(i * 128, 128)
        vis_out[:, lanes] = vis_ref[i : i + 1, :].astype(jnp.float32)
        for t in range(dec_out.shape[0]):
            at = t * per + i
            dec_out[t, :, lanes] = dec_ref[at : at + 1, :].astype(jnp.float32)


def prepare(me, image_request, slot_start, grids, text, patches, dec_gain, vis_gain, n_req, n_text, n_img):
    side, _, img_dev, width = patches.shape
    padded = round_up((side // 2) ** 2, 16)
    inputs = (
        image_request,
        slot_start,
        grids.T,
        text,
        patches,
        dec_gain.reshape(-1, 128),
        vis_gain.reshape(-1, 128),
    )
    bf16, f32 = jnp.bfloat16, jnp.float32
    outputs = [((n_req // 2, padded, width), bf16)] * 2 + [
        ((n_text, width), bf16),
        ((n_img, width), bf16),
        ((n_img, n_img), bf16),
        ((n_req, 128), jnp.int32),
        ((8, text.shape[0]), f32),
        ((dec_gain.size // width, 1, width), f32),
        ((1, width), f32),
    ]
    return pl.pallas_call(
        functools.partial(prep_kernel, n_req),
        out_shape=tuple(jax.ShapeDtypeStruct(shape, kind) for shape, kind in outputs),
        in_specs=[pl.BlockSpec(memory_space=pltpu.SMEM)] + [pl.BlockSpec(memory_space=pltpu.HBM)] * len(inputs),
        out_specs=tuple(vmem_specs(len(outputs))),
        scratch_shapes=[pltpu.SMEM(x.shape, jnp.int32) for x in inputs[:3]]
        + [pltpu.VMEM(x.shape, x.dtype) for x in inputs[3:]]
        + [pltpu.VMEM((n_req, padded, width), f32), pltpu.SemaphoreType.DMA((len(inputs),))],
        compiler_params=params(12),
        cost_estimate=TINY,
    )(me, *[in_hbm(x) for x in inputs])


def mix_kernel(even_ref, odd_ref, *outs):
    rows = even_ref.shape[1]
    for i, out_ref in enumerate(outs):
        out_ref[:rows] = even_ref[i]
        out_ref[rows:] = odd_ref[i]


def mix_pairs(even, odd):
    n, rows, width = even.shape
    return pl.pallas_call(
        mix_kernel,
        out_shape=(jax.ShapeDtypeStruct((2 * rows, width), jnp.bfloat16),) * n,
        in_specs=vmem_specs(2),
        out_specs=tuple(vmem_specs(n)),
        compiler_params=params(4),
        cost_estimate=TINY,
    )(even, odd)


def pack_kernel(region, gain_ref, rtext_ref, sel_ref, *refs):
    recs, (out_ref, tmp_ref) = refs[:-2], refs[-2:]
    done = 0
    for rec_ref in recs:
        rows = rec_ref.shape[0] // 2
        pair = rec_ref[...].astype(jnp.float32)
        for first in (0, rows):
            tmp_ref[done : done + region] = pair[first : first + region]
            done += region
    rest = tmp_ref.shape[0] - done
    tmp_ref[done:] = jnp.zeros((rest, tmp_ref.shape[1]), jnp.float32)
    picked = jnp.dot(sel_ref[...], tmp_ref[...].astype(jnp.bfloat16), preferred_element_type=jnp.float32)
    tmp_ref[...] = picked + rtext_ref[...].astype(jnp.float32)
    tmp_ref[done:] = jnp.broadcast_to(gain_ref[0:1, :], (rest, gain_ref.shape[1]))
    out_ref[...] = tmp_ref[...].astype(jnp.bfloat16)


def pack_images(received, gain, rtext, sel, region):
    n_img, width = rtext.shape
    return pl.pallas_call(
        functools.partial(pack_kernel, region),
        out_shape=jax.ShapeDtypeStruct((n_img, width), jnp.bfloat16),
        in_specs=vmem_specs(3 + len(received)),
        out_specs=pl.BlockSpec(memory_space=pltpu.VMEM),
        scratch_shapes=[pltpu.VMEM((n_img, width), jnp.float32)],
        compiler_params=params(4),
        cost_estimate=TINY,
    )(gain, rtext, sel, *received)


def place_kernel(region, table_ref, text_at_ref, img_at_ref, text_row_ref):
    length, n_text = text_at_ref.shape
    spot = lax.broadcasted_iota(jnp.int32, (length, 128), 0)
    before = jnp.zeros((length, 128), jnp.int32)
    at = jnp.full((length, 128), -1, jnp.int32)
    for s in range(table_ref.shape[0]):
        c = spot - table_ref[s : s + 1, :]
        before += jnp.clip(c, 0, region)
        at = jnp.where((c >= 0) & (c < region), s * region + c, at)
    text_row_ref[...] = jnp.where(at < 0, 1.0, 0.0)
    rank = jnp.where(at < 0, spot - before, -1)[:, :1]
    text_at_ref[...] = (lax.broadcasted_iota(jnp.int32, (length, n_text), 1) == rank).astype(jnp.bfloat16)
    lane = lax.broadcasted_iota(jnp.int32, img_at_ref.shape, 1)
    img_at_ref[...] = (lane == at[:, :1]).astype(jnp.bfloat16)


def placement(table, region, length, n_text, n_img):
    return pl.pallas_call(
        functools.partial(place_kernel, region),
        out_shape=(
            jax.ShapeDtypeStruct((length, n_text), jnp.bfloat16),
            jax.ShapeDtypeStruct((length, n_img), jnp.bfloat16),
            jax.ShapeDtypeStruct((length, 128), jnp.float32),
        ),
        in_specs=vmem_specs(1),
        out_specs=tuple(vmem_specs(3)),
        compiler_params=params(8),
        cost_estimate=TINY,
    )(table)


def cols_of(ref, owner, width):
    return ref[:, pl.ds(pl.multiple_of(owner * width, width), width)]


def scale_rows(x, gain):
    xf = x.astype(jnp.float32)
    return (xf * gain).astype(jnp.bfloat16), jnp.sum(xf * xf, axis=1, keepdims=True)


def own_kernel(me_ref, x_ref, gain_ref, w_ref, acc_ref, ss_ref, held_ref, sem_ref):
    n_ten, _, width, _ = held_ref.shape
    copies = []
    for s in range(n_ten):
        rows = pl.ds(pl.multiple_of((me_ref[0] ^ s) * width, width), width)
        copies += [pltpu.make_async_copy(w_ref.at[j, rows], held_ref.at[s, j], sem_ref.at[s, j]) for j in range(3)]
    for copy in copies:
        copy.start()
    scaled = []
    for first, count in sides(x_ref.shape[0]):
        rows = pl.ds(first, count)
        x, total = scale_rows(x_ref[rows], gain_ref[me_ref[0]])
        scaled.append(x)
        ss_ref[rows] = jnp.broadcast_to(total, (count, 128))
    for j in range(3):
        copies[j].wait()
        for side, (first, count) in enumerate(sides(x_ref.shape[0])):
            acc_ref[j, pl.ds(first, count)] = jnp.dot(
                scaled[side], held_ref[0, j], preferred_element_type=jnp.float32
            )
    for copy in copies[3:]:
        copy.wait()


def own_part(me, x, gain, w):
    rows, width = x.shape
    n_ten, cols = gain.shape[0], w.shape[2]
    return pl.pallas_call(
        own_kernel,
        out_shape=(
            jax.ShapeDtypeStruct((3, rows, cols), jnp.float32),
            jax.ShapeDtypeStruct((rows, 128), jnp.float32),
            pltpu.VMEM((n_ten, 3, width, cols), w.dtype),
        ),
        in_specs=[pl.BlockSpec(memory_space=pltpu.SMEM)] + vmem_specs(2) + [pl.BlockSpec(memory_space=pltpu.HBM)],
        out_specs=tuple(vmem_specs(3)),
        scratch_shapes=[pltpu.SemaphoreType.DMA((n_ten, 3))],
        compiler_params=params(12),
        cost_estimate=TINY,
    )(me, x, gain, in_hbm(w))


def near_kernel(near, pieces, me_ref, *refs):
    n_x = sum(pieces)
    x_refs, refs = list(refs[:n_x]), refs[n_x:]
    gain_ref, held_ref, acc_in, ss_in, acc_ref, ss_ref = refs
    parts = [pl.ds(first, count) for first, count in sides(acc_ref.shape[1])]
    views = []
    for n in pieces:
        mine, x_refs = x_refs[:n], x_refs[n:]
        views.append([mine[0].at[parts[side]] if n == 1 else mine[side] for side in range(2)])
    scaled = {}
    for side in range(2):
        rows = parts[side]
        total = ss_in[rows]
        for b, s in enumerate(near):
            scaled[side, b], part = scale_rows(views[b][side][...], gain_ref[me_ref[0] ^ s])
            total += part
        ss_ref[rows] = total
    for j in range(3):
        for side in range(2):
            rows = parts[side]
            acc = acc_in[j, rows]
            for b, s in enumerate(near):
                acc += jnp.dot(scaled[side, b], held_ref[s, j], preferred_element_type=jnp.float32)
            acc_ref[j, rows] = acc


def near_part(near, me, blocks, gain, held, acc, ss):
    blocks = [b if isinstance(b, tuple) else (b,) for b in blocks]
    pieces = [len(b) for b in blocks]
    return pl.pallas_call(
        functools.partial(near_kernel, near, pieces),
        out_shape=(
            jax.ShapeDtypeStruct(acc.shape, jnp.float32),
            jax.ShapeDtypeStruct(ss.shape, jnp.float32),
        ),
        in_specs=[pl.BlockSpec(memory_space=pltpu.SMEM)]
        + vmem_specs(sum(pieces) + 4),
        out_specs=tuple(vmem_specs(2)),
        compiler_params=params(12),
        cost_estimate=pl.CostEstimate(flops=10**11, bytes_accessed=0, transcendentals=0),
    )(me, *[h for b in blocks for h in b], gain, held, acc, ss)


def image_kernel(n_rows, n_blk, me_ref, *refs):
    x_refs, refs = refs[:n_blk], refs[n_blk:]
    gain_ref, sel_ref, held_ref, w_out_ref, qkv_ref, own_ref, w_out_held, sem_ref = refs
    copy = pltpu.make_async_copy(w_out_ref, w_out_held, sem_ref)
    copy.start()
    is_img = jnp.sum(sel_ref[...].astype(jnp.float32), axis=1, keepdims=True) > 0.5
    total = 0.0
    for s in range(n_blk):
        xf = x_refs[s][...].astype(jnp.float32)
        total += jnp.sum(xf * xf, axis=1, keepdims=True)
    scale = lax.rsqrt(total / D + EPS)
    total = 0.0
    scaled = []
    for s in range(n_blk):
        xf = x_refs[s][...].astype(jnp.float32)
        merged = jnp.where(is_img, xf * scale * xf[n_rows : n_rows + 1], xf).astype(jnp.bfloat16)
        if s == 0:
            own_ref[...] = merged
        mf = merged.astype(jnp.float32)
        total += jnp.sum(mf * mf, axis=1, keepdims=True)
        scaled.append((mf * gain_ref[me_ref[0] ^ s]).astype(jnp.bfloat16))
    scale = lax.rsqrt(total / D + EPS)
    for j in range(3):
        acc = 0.0
        for s in range(n_blk):
            acc += jnp.dot(scaled[s], held_ref[s, j], preferred_element_type=jnp.float32)
        qkv_ref[j] = (acc * scale).astype(jnp.bfloat16)
    copy.wait()


def image_part(me, blocks, gain, sel, held, w_out, n_rows):
    n_img, width = blocks[0].shape
    return pl.pallas_call(
        functools.partial(image_kernel, n_rows, len(blocks)),
        out_shape=(
            jax.ShapeDtypeStruct((3, n_img, held.shape[3]), jnp.bfloat16),
            jax.ShapeDtypeStruct((n_img, width), jnp.bfloat16),
            pltpu.VMEM(w_out.shape, w_out.dtype),
        ),
        in_specs=[pl.BlockSpec(memory_space=pltpu.SMEM)]
        + vmem_specs(len(blocks) + 3)
        + [pl.BlockSpec(memory_space=pltpu.HBM)],
        out_specs=tuple(vmem_specs(3)),
        scratch_shapes=[pltpu.SemaphoreType.DMA],
        compiler_params=params(12),
        cost_estimate=pl.CostEstimate(flops=0, bytes_accessed=0, transcendentals=0),
    )(me, *blocks, gain, sel, held, in_hbm(w_out))


def project_side(side, far, me_ref, x_ref, gain_ref, held_ref, acc_ref, ss_ref, out_ref):
    first, count = sides(acc_ref.shape[1])[side]
    part = pl.ds(first, count)
    x, total = scale_rows(x_ref[...], gain_ref[me_ref[0] ^ far])
    scale = lax.rsqrt((ss_ref[part] + total) / D + EPS)[:, :1]
    for j in range(3):
        prod = jnp.dot(x, held_ref[far, j], preferred_element_type=jnp.float32)
        out_ref[j, part] = ((prod + acc_ref[j, part]) * scale).astype(jnp.bfloat16)


def attend(edges, first, qkv_ref, key_ref, ctx_ref):
    heads = [pl.ds(h * HD, HD) for h in range(ctx_ref.shape[1] // HD)]
    for low, last in zip(edges, edges[1:]):
        here, step = pl.ds(low, last - low), last - low
        row = lax.broadcasted_iota(jnp.int32, (step, last), 0) + low
        col = lax.broadcasted_iota(jnp.int32, (step, last), 1)
        bias = jnp.where((row >= col) & (key_ref[0:1, pl.ds(0, last)] > 0.5), 0.0, -1e30)
        scores = [
            lax.dot_general(
                qkv_ref[0, here, lanes],
                qkv_ref[1, pl.ds(0, last), lanes],
                (((1,), (1,)), ((), ())),
                preferred_element_type=jnp.float32,
            )
            for lanes in heads
        ]
        scores = [x * (LOG2E / HD**0.5) + bias for x in scores]
        tops = [jnp.max(x, axis=1, keepdims=True) for x in scores]
        expo = [jnp.exp2(x - top) for x, top in zip(scores, tops)]
        sums = [jnp.sum(x, axis=1, keepdims=True) for x in expo]
        outs = [
            jnp.dot(x.astype(jnp.bfloat16), qkv_ref[2, pl.ds(0, last), lanes], preferred_element_type=jnp.float32)
            for x, lanes in zip(expo, heads)
        ]
        for lanes, out, total in zip(heads, outs, sums):
            ctx_ref[pl.ds(low - first, step), lanes] = (out / total).astype(jnp.bfloat16)


def put_columns(product, outs):
    half = outs[0].shape[1]
    for i, out_ref in enumerate(outs):
        out_ref[...] = product[:, i * half : (i + 1) * half].astype(out_ref.dtype)


def head_kernel(far, me_ref, top_ref, gain_ref, held_ref, acc_ref, ss_ref, img_ref, text_at_ref, img_at_ref, key_ref,
                w_out_ref, text_qkv_ref, qkv_ref, ctx_ref, left_ref, right_ref):
    rows = ctx_ref.shape[0]
    width = 2 * left_ref.shape[1]
    project_side(0, far, me_ref, top_ref, gain_ref, held_ref, acc_ref, ss_ref, text_qkv_ref)
    for j in range(3):
        qkv = jnp.dot(text_at_ref[:rows, :rows], text_qkv_ref[j], preferred_element_type=jnp.float32)
        qkv += jnp.dot(img_at_ref[:rows], img_ref[j], preferred_element_type=jnp.float32)
        qkv_ref[j] = qkv.astype(jnp.bfloat16)
    attend([0, rows], 0, qkv_ref, key_ref, ctx_ref)
    weight = cols_of(w_out_ref, me_ref[0] ^ far, width)
    put_columns(jnp.dot(ctx_ref[...], weight, preferred_element_type=jnp.float32), (left_ref, right_ref))


def head_part(far, me, top, gain, held, acc, ss, img, text_at, img_at, key_ok, w_out):
    width, cols = held.shape[2:]
    rows = top.shape[0]
    bf16 = jnp.bfloat16
    return pl.pallas_call(
        functools.partial(head_kernel, far),
        out_shape=(
            jax.ShapeDtypeStruct((3, rows, cols), bf16),
            jax.ShapeDtypeStruct((3, rows, cols), bf16),
            jax.ShapeDtypeStruct((rows, cols), bf16),
            jax.ShapeDtypeStruct((rows, width // 2), bf16),
            jax.ShapeDtypeStruct((rows, width // 2), bf16),
        ),
        in_specs=[pl.BlockSpec(memory_space=pltpu.SMEM)] + vmem_specs(10),
        out_specs=tuple(vmem_specs(5)),
        compiler_params=params(12),
        cost_estimate=TINY,
    )(me, top, gain, held, acc, ss, img, text_at, img_at, key_ok, w_out)


def tail_kernel(far, me_ref, bottom_ref, gain_ref, held_ref, acc_ref, ss_ref, img_ref, text_at_ref, img_at_ref,
                key_ref, w_out_ref, top_qkv_ref, head_qkv_ref, ctx_ref, left_ref, right_ref, text_qkv_ref, qkv_ref):
    first = top_qkv_ref.shape[1]
    length = text_at_ref.shape[0]
    width = 2 * left_ref.shape[1]
    project_side(1, far, me_ref, bottom_ref, gain_ref, held_ref, acc_ref, ss_ref, text_qkv_ref)
    for j in range(3):
        text_qkv_ref[j, :first] = top_qkv_ref[j]
        qkv_ref[j, :first] = head_qkv_ref[j]
        qkv = jnp.dot(text_at_ref[first:], text_qkv_ref[j], preferred_element_type=jnp.float32)
        qkv += jnp.dot(img_at_ref[first:], img_ref[j], preferred_element_type=jnp.float32)
        qkv_ref[j, first:] = qkv.astype(jnp.bfloat16)
    edges = [first] + [at for at in range(128, length, 128) if at > first] + [length]
    attend(edges, first, qkv_ref, key_ref, ctx_ref)
    weight = cols_of(w_out_ref, me_ref[0] ^ far, width)
    put_columns(jnp.dot(ctx_ref[...], weight, preferred_element_type=jnp.float32), (left_ref, right_ref))


def tail_part(far, me, bottom, gain, held, acc, ss, img, text_at, img_at, key_ok, w_out, top_qkv, head_qkv):
    width, cols = held.shape[2:]
    length, n_text = text_at.shape
    rows = length - top_qkv.shape[1]
    bf16 = jnp.bfloat16
    return pl.pallas_call(
        functools.partial(tail_kernel, far),
        out_shape=(
            jax.ShapeDtypeStruct((rows, cols), bf16),
            jax.ShapeDtypeStruct((rows, width // 2), bf16),
            jax.ShapeDtypeStruct((rows, width // 2), bf16),
        ),
        in_specs=[pl.BlockSpec(memory_space=pltpu.SMEM)] + vmem_specs(12),
        out_specs=tuple(vmem_specs(3)),
        scratch_shapes=[pltpu.VMEM((3, n_text, cols), bf16), pltpu.VMEM((3, length, cols), bf16)],
        compiler_params=params(12),
        cost_estimate=pl.CostEstimate(flops=10**10, bytes_accessed=0, transcendentals=0),
    )(me, bottom, gain, held, acc, ss, img, text_at, img_at, key_ok, w_out, top_qkv, head_qkv)


def out_kernel(away, me_ref, head_ref, tail_ref, w_ref, left_ref, right_ref):
    first = head_ref.shape[0]
    weight = cols_of(w_ref, me_ref[0] ^ away, 2 * left_ref.shape[1])
    for ctx_ref, rows in ((head_ref, slice(None, first)), (tail_ref, slice(first, None))):
        product = jnp.dot(ctx_ref[...], weight, preferred_element_type=jnp.float32)
        put_columns(product, (left_ref.at[rows], right_ref.at[rows]))


def out_part(away, me, head, tail, w, width, dtype=jnp.bfloat16):
    rows = head.shape[0] + tail.shape[0]
    return pl.pallas_call(
        functools.partial(out_kernel, away),
        out_shape=(jax.ShapeDtypeStruct((rows, width // 2), dtype),) * 2,
        in_specs=[pl.BlockSpec(memory_space=pltpu.SMEM)] + vmem_specs(3),
        out_specs=tuple(vmem_specs(2)),
        compiler_params=params(12),
        cost_estimate=pl.CostEstimate(flops=10**9, bytes_accessed=0, transcendentals=0),
    )(me, head, tail, w)


def sum_of(refs):
    return functools.reduce(lambda a, b: a + b, [ref[...].astype(jnp.float32) for ref in refs])


def first_kernel(n_left, base_ref, *refs):
    out_ref = refs[-1]
    half = base_ref.shape[1] // 2
    for side, terms in enumerate((refs[:n_left], refs[n_left:-1])):
        part = pl.ds(side * half, half)
        out_ref[:, part] = base_ref[:, part].astype(jnp.float32) + sum_of(terms)


def add_first(base, left, right):
    return pl.pallas_call(
        functools.partial(first_kernel, len(left)),
        out_shape=jax.ShapeDtypeStruct(base.shape, jnp.float32),
        in_specs=vmem_specs(1 + len(left) + len(right)),
        out_specs=pl.BlockSpec(memory_space=pltpu.VMEM),
        compiler_params=params(12),
        cost_estimate=TINY,
    )(base, *left, *right)


def last_kernel(n_left, base_ref, *refs):
    refs, (out_ref, tmp_ref, sem_ref) = refs[:-3], refs[-3:]
    half = base_ref.shape[1] // 2
    copies = []
    for side, terms in enumerate((refs[:n_left], refs[n_left:])):
        part = pl.ds(side * half, half)
        tmp_ref[:, part] = (base_ref[:, part] + sum_of(terms)).astype(tmp_ref.dtype)
        copy = pltpu.make_async_copy(tmp_ref.at[:, part], out_ref.at[:, part], sem_ref.at[side])
        copy.start()
        copies.append(copy)
    for copy in copies:
        copy.wait()


def add_last(base, left, right):
    return pl.pallas_call(
        functools.partial(last_kernel, len(left)),
        out_shape=jax.ShapeDtypeStruct(base.shape, jnp.bfloat16),
        in_specs=vmem_specs(1 + len(left) + len(right)),
        out_specs=pl.BlockSpec(memory_space=pl.ANY),
        scratch_shapes=[pltpu.VMEM(base.shape, jnp.bfloat16), pltpu.SemaphoreType.DMA((2,))],
        compiler_params=params(12),
        cost_estimate=TINY,
    )(base, *left, *right)


def scatter_terms(parts, got, n):
    acc = {s: [[parts[s][0]], [parts[s][1]]] for s in parts}
    far = n - 1
    acc[far ^ low_bit(far)][0].append(got[0])
    acc[far ^ high_bit(far)][1].append(got[1])
    early, late = [[], []], [[], []]
    for s in by_bits(n, reverse=True)[1:]:
        for side, bit in ((0, low_bit(s)), (1, high_bit(s))):
            terms = [t.astype(jnp.float32) for t in acc[s][side]]
            out = swap(functools.reduce(lambda a, b: a + b, terms).astype(jnp.bfloat16), bit)
            if s == bit:
                (early if len(terms) == 1 else late)[side].append(out)
            else:
                acc[s ^ bit][side].append(out)
    return early, late


def body(text, patches, grids, image_request, slot_start, vis_gain, dec_gain, w_qkv, w_out):
    n_req = lax.axis_size("req")
    n_ten = lax.axis_size("tensor")
    me_req = lax.axis_index("req")
    me_ten = lax.axis_index("tensor")
    img_dev, side, _, width = patches.shape
    half = side // 2
    region = half * half
    length = text.shape[0]
    w3 = jnp.transpose(w_qkv, (1, 0, 2))
    req_at = me_req.astype(jnp.int32)[None]
    ten_at = me_ten.astype(jnp.int32)[None]
    order = by_bits(n_ten)
    near_at, far = order[:-1], order[-1]

    n_rows = n_req * region
    n_img = round_up(n_rows + 1, 16)
    n_text = length - (n_rows if img_dev == n_req else 0)
    even, odd, ctext, rtext, sel, table, key_ok, gains, vis_row = prepare(
        req_at, image_request, slot_start, grids, text, jnp.transpose(patches, (1, 2, 0, 3)), dec_gain, vis_gain, n_req,
        n_text, n_img
    )
    blocks = near_blocks(ctext, n_ten)

    pairs = mix_pairs(even, swap(odd, 1, "req"))
    received = [pairs[0]] + [swap(pairs[i], 2 * i, "req") for i in range(1, n_req // 2)]
    img_own = pack_images(received, vis_row, rtext, sel, region)
    img_blocks = [img_own] + [swap(img_own, s) for s in range(1, n_ten)]
    own, img_own = lax.optimization_barrier((ctext, img_own))
    acc, ss, held = own_part(ten_at, own, gains, w3)
    handed, img_own = lax.optimization_barrier((blocks, img_own))
    blocks = {**far_blocks(handed, n_ten), **blocks}

    near = [blocks[s] for s in near_at]
    acc, ss = near_part(near_at, ten_at, near, gains, held, acc, ss)
    table, acc = lax.optimization_barrier((table, acc))
    text_at, img_at, text_row = placement(table, region, length, n_text, n_img)
    img_blocks, text_at = lax.optimization_barrier((img_blocks, text_at))
    img_qkv, merged, w_out = image_part(ten_at, img_blocks, gains, sel, held, w_out, n_rows)

    shared = (gains, held, acc, ss, img_qkv, text_at, img_at, key_ok, w_out)
    top_qkv, head_qkv, head_ctx, *head_far = head_part(far, ten_at, blocks[far][0], *shared)
    tail_ctx, *tail_far = tail_part(far, ten_at, blocks[far][1], *shared, top_qkv, head_qkv)

    img_here = jnp.dot(img_at, merged, preferred_element_type=jnp.float32)
    x_in = (text.astype(jnp.float32) * text_row[:, :1] + img_here).astype(jnp.bfloat16)

    bits = (low_bit(far), high_bit(far))
    head_got = [swap(t, bit) for t, bit in zip(head_far, bits)]
    tail_got = [swap(t, bit) for t, bit in zip(tail_far, bits)]
    head_got, head_ctx, tail_ctx = lax.optimization_barrier((head_got, head_ctx, tail_ctx))
    parts = {}
    for s in reversed([0] + near_at):
        parts[s] = out_part(s, ten_at, head_ctx, tail_ctx, w_out, width, jnp.float32 if s == 0 else jnp.bfloat16)
    got = [jnp.concatenate(pair, axis=0) for pair in zip(head_got, tail_got)]
    early, late = scatter_terms(parts, got, n_ten)
    base = add_first(x_in, [parts[0][0]] + early[0], [parts[0][1]] + early[1])
    return add_last(base, late[0], late[1])


def solution(mesh):
    in_specs = (
        P("req", "tensor"),
        P("req", None, None, "tensor"),
        P(),
        P(),
        P(),
        P("tensor"),
        P(),
        P(None, None, "tensor"),
        P("tensor", None),
    )
    out_specs = P("req", "tensor")
    return jax.shard_map(body, mesh=mesh, in_specs=in_specs, out_specs=out_specs, check_vma=False)
```

```python
import functools

import jax
import jax.numpy as jnp
from jax import lax
from jax.experimental import pallas as pl
from jax.experimental.pallas import tpu as pltpu
from jax.sharding import PartitionSpec as P

D = 4096
HD = 128
EPS = 1e-05
LOG2E = 1.4426950408889634
TINY = pl.CostEstimate(flops=0, bytes_accessed=0, transcendentals=0)


def round_up(n, m):
    return -(-n // m) * m


def swap(x, s, axis="tensor"):
    n = lax.axis_size(axis)
    return lax.ppermute(x, axis, [(i, i ^ s) for i in range(n)])


def in_hbm(x):
    return pltpu.with_memory_space_constraint(x, pltpu.HBM)


def low_bit(s):
    return s & -s


def high_bit(s):
    return 1 << (s.bit_length() - 1)


def by_bits(n, reverse=False):
    return sorted(range(1, n), key=lambda s: (bin(s).count("1"), s), reverse=reverse)


def sides(n):
    half = round_up(n // 2, 16)
    return (0, half), (half, n - half)


def halves(block):
    if isinstance(block, tuple):
        return block
    return tuple(block[first : first + rows] for first, rows in sides(block.shape[0]))


def near_blocks(x, n):
    return {s: swap(x, s) for s in by_bits(n) if s & (s - 1) == 0}


def far_blocks(blocks, n):
    blocks = dict(blocks)
    for s in by_bits(n):
        if s not in blocks:
            low, high = low_bit(s), high_bit(s)
            blocks[s] = (swap(halves(blocks[s ^ low])[0], low), swap(halves(blocks[s ^ high])[1], high))
    return blocks


def vmem_specs(n):
    return [pl.BlockSpec(memory_space=pltpu.VMEM)] * n


def params(mib):
    return pltpu.CompilerParams(vmem_limit_bytes=mib * 1024 * 1024)


def fetch(pairs, sem_ref):
    copies = [pltpu.make_async_copy(src, dst, sem_ref.at[i]) for i, (src, dst) in enumerate(pairs)]
    for copy in copies:
        copy.start()
    return copies


NOWHERE = 1 << 20


def prep_kernel(n_req, me_ref, req_hbm, start_hbm, grid_hbm, text_hbm, x_hbm, dec_hbm, vis_hbm, *refs):
    (even_out, odd_out, ctext_out, rtext_out, sel_out, table_out, key_out, dec_out, vis_out, req_ref, start_ref, grid_ref,
     text_ref, x_ref, dec_ref, vis_ref, tmp_ref, sem_ref) = refs
    pairs = (
        (req_hbm, req_ref),
        (start_hbm, start_ref),
        (grid_hbm, grid_ref),
        (text_hbm, text_ref),
        (x_hbm, x_ref),
        (dec_hbm, dec_ref),
        (vis_hbm, vis_ref),
    )
    copies = fetch(pairs, sem_ref)
    side, img_dev = x_ref.shape[0], x_ref.shape[2]
    half = side // 2
    region = half * half
    n_img, n_text, length = sel_out.shape[0], ctext_out.shape[0], text_ref.shape[0]
    me = me_ref[0]
    for copy in copies[:3]:
        copy.wait()

    found = []
    for s in range(n_req):
        source = (me ^ s) * img_dev

        def one_image(k, found, source=source):
            hit = req_ref[source + k] == me
            values = (start_ref[source + k], grid_ref[0, source + k] // 2, grid_ref[1, source + k] // 2)
            return tuple(jnp.where(hit, new, old) for new, old in zip(values, found))

        none = (jnp.int32(NOWHERE), jnp.int32(0), jnp.int32(1))
        found.append(lax.fori_loop(0, img_dev, one_image, none, unroll=img_dev <= 8))

    spot = lax.broadcasted_iota(jnp.int32, (8, length), 1)
    before = jnp.zeros((8, length), jnp.int32)
    closed = jnp.zeros((8, length), jnp.int32)
    inside = jnp.zeros((8, length), jnp.int32)
    row = lax.broadcasted_iota(jnp.int32, (n_img, 128), 0)
    pos = jnp.full((n_img, 128), -1, jnp.int32)
    target = jnp.full((n_img, 128), -1, jnp.int32)
    line = lax.broadcasted_iota(jnp.int32, (n_req, 128), 0)
    table = jnp.zeros((n_req, 128), jnp.int32)
    for s, (start, high, wide) in enumerate(found):
        count = high * wide
        c = spot - start
        here = (c >= 0) & (c < region)
        before += jnp.clip(c, 0, region)
        inside = jnp.where(here, 1, inside)
        closed = jnp.where(here & (c >= count), 1, closed)
        c = row - s * region
        here = (c >= 0) & (c < region)
        pos = jnp.where(here, start + c, pos)
        cell = c
        for w in range(1, half):
            cell = jnp.where(wide == w, c // w * half + c % w, cell)
        target = jnp.where(here & (c < count), s * region + cell, target)
        table = jnp.where(line == s, start, table)
    table_out[...] = table
    key_out[...] = 1.0 - closed.astype(jnp.float32)
    rank = jnp.where(inside == 1, -1, spot - before)[0:1]
    gather = (lax.broadcasted_iota(jnp.int32, (n_text, length), 0) == rank).astype(jnp.bfloat16)
    stays = jnp.where(target >= 0, -1, pos)[:, :1]
    keep = (lax.broadcasted_iota(jnp.int32, (n_img, length), 1) == stays).astype(jnp.bfloat16)
    sel = lax.broadcasted_iota(jnp.int32, (n_img, n_img), 1) == target[:, :1]
    sel_out[...] = sel.astype(jnp.bfloat16)
    copies[3].wait()
    text = text_ref[...]
    ctext_out[...] = jnp.dot(gather, text, preferred_element_type=jnp.float32).astype(jnp.bfloat16)
    rtext_out[...] = jnp.dot(keep, text, preferred_element_type=jnp.float32).astype(jnp.bfloat16)

    for copy in copies[4:]:
        copy.wait()
    rows = lax.broadcasted_iota(jnp.int32, (n_req, img_dev), 0)
    cols = lax.broadcasted_iota(jnp.int32, (n_req, img_dev), 1)
    goal = jnp.full((n_req, img_dev), -1, jnp.int32)
    for k in range(img_dev):
        goal = jnp.where(cols == k, req_ref[me * img_dev + k] ^ me, goal)
    onehot = (rows == goal).astype(jnp.bfloat16)
    tmp_ref[...] = jnp.zeros_like(tmp_ref)
    for i in range(half):
        for j in range(half):
            total = x_ref[2 * i, 2 * j].astype(jnp.float32)
            for a, b in ((0, 1), (1, 0), (1, 1)):
                total += x_ref[2 * i + a, 2 * j + b].astype(jnp.float32)
            pooled = (total * 0.25).astype(jnp.bfloat16)
            tmp_ref[:, i * half + j, :] = jnp.dot(onehot, pooled, preferred_element_type=jnp.float32)
    for s in range(n_req):
        (even_out, odd_out)[s % 2][s // 2] = tmp_ref[s].astype(jnp.bfloat16)
    per = vis_ref.shape[0]
    for i in range(per):
        lanes = pl.ds(i * 128, 128)
        vis_out[:, lanes] = vis_ref[i : i + 1, :].astype(jnp.float32)
        for t in range(dec_out.shape[0]):
            at = t * per + i
            dec_out[t, :, lanes] = dec_ref[at : at + 1, :].astype(jnp.float32)


def prepare(me, image_request, slot_start, grids, text, patches, dec_gain, vis_gain, n_req, n_text, n_img):
    side, _, img_dev, width = patches.shape
    padded = round_up((side // 2) ** 2, 16)
    inputs = (
        image_request,
        slot_start,
        grids.T,
        text,
        patches,
        dec_gain.reshape(-1, 128),
        vis_gain.reshape(-1, 128),
    )
    bf16, f32 = jnp.bfloat16, jnp.float32
    outputs = [((n_req // 2, padded, width), bf16)] * 2 + [
        ((n_text, width), bf16),
        ((n_img, width), bf16),
        ((n_img, n_img), bf16),
        ((n_req, 128), jnp.int32),
        ((8, text.shape[0]), f32),
        ((dec_gain.size // width, 1, width), f32),
        ((1, width), f32),
    ]
    return pl.pallas_call(
        functools.partial(prep_kernel, n_req),
        out_shape=tuple(jax.ShapeDtypeStruct(shape, kind) for shape, kind in outputs),
        in_specs=[pl.BlockSpec(memory_space=pltpu.SMEM)] + [pl.BlockSpec(memory_space=pltpu.HBM)] * len(inputs),
        out_specs=tuple(vmem_specs(len(outputs))),
        scratch_shapes=[pltpu.SMEM(x.shape, jnp.int32) for x in inputs[:3]]
        + [pltpu.VMEM(x.shape, x.dtype) for x in inputs[3:]]
        + [pltpu.VMEM((n_req, padded, width), f32), pltpu.SemaphoreType.DMA((len(inputs),))],
        compiler_params=params(12),
        cost_estimate=TINY,
    )(me, *[in_hbm(x) for x in inputs])


def mix_kernel(region, even_ref, odd_ref, *refs):
    outs, tmp_ref = refs[:-1], refs[-1]
    for i, out_ref in enumerate(outs):
        tmp_ref[:region] = even_ref[i].astype(jnp.float32)[:region]
        tmp_ref[region : 2 * region] = odd_ref[i].astype(jnp.float32)[:region]
        tmp_ref[2 * region :] = jnp.zeros((tmp_ref.shape[0] - 2 * region, tmp_ref.shape[1]), jnp.float32)
        out_ref[...] = tmp_ref[...].astype(jnp.bfloat16)


def mix_pairs(even, odd, region):
    n, _, width = even.shape
    rows = round_up(2 * region, 8)
    return pl.pallas_call(
        functools.partial(mix_kernel, region),
        out_shape=(jax.ShapeDtypeStruct((rows, width), jnp.bfloat16),) * n,
        in_specs=vmem_specs(2),
        out_specs=tuple(vmem_specs(n)),
        scratch_shapes=[pltpu.VMEM((rows, width), jnp.float32)],
        compiler_params=params(4),
        cost_estimate=TINY,
    )(even, odd)


def pack_kernel(region, gain_ref, rtext_ref, sel_ref, *refs):
    recs, (out_ref, tmp_ref) = refs[:-2], refs[-2:]
    done = 0
    for rec_ref in recs:
        tmp_ref[done : done + 2 * region] = rec_ref[...].astype(jnp.float32)[: 2 * region]
        done += 2 * region
    rest = tmp_ref.shape[0] - done
    tmp_ref[done:] = jnp.zeros((rest, tmp_ref.shape[1]), jnp.float32)
    picked = jnp.dot(sel_ref[...], tmp_ref[...].astype(jnp.bfloat16), preferred_element_type=jnp.float32)
    tmp_ref[...] = picked + rtext_ref[...].astype(jnp.float32)
    tmp_ref[done:] = jnp.broadcast_to(gain_ref[0:1, :], (rest, gain_ref.shape[1]))
    out_ref[...] = tmp_ref[...].astype(jnp.bfloat16)


def pack_images(received, gain, rtext, sel, region):
    n_img, width = rtext.shape
    return pl.pallas_call(
        functools.partial(pack_kernel, region),
        out_shape=jax.ShapeDtypeStruct((n_img, width), jnp.bfloat16),
        in_specs=vmem_specs(3 + len(received)),
        out_specs=pl.BlockSpec(memory_space=pltpu.VMEM),
        scratch_shapes=[pltpu.VMEM((n_img, width), jnp.float32)],
        compiler_params=params(4),
        cost_estimate=TINY,
    )(gain, rtext, sel, *received)


def place_kernel(region, table_ref, text_at_ref, img_at_ref, text_row_ref):
    length, n_text = text_at_ref.shape
    spot = lax.broadcasted_iota(jnp.int32, (length, 128), 0)
    before = jnp.zeros((length, 128), jnp.int32)
    at = jnp.full((length, 128), -1, jnp.int32)
    for s in range(table_ref.shape[0]):
        c = spot - table_ref[s : s + 1, :]
        before += jnp.clip(c, 0, region)
        at = jnp.where((c >= 0) & (c < region), s * region + c, at)
    text_row_ref[...] = jnp.where(at < 0, 1.0, 0.0)
    rank = jnp.where(at < 0, spot - before, -1)[:, :1]
    text_at_ref[...] = (lax.broadcasted_iota(jnp.int32, (length, n_text), 1) == rank).astype(jnp.bfloat16)
    lane = lax.broadcasted_iota(jnp.int32, img_at_ref.shape, 1)
    img_at_ref[...] = (lane == at[:, :1]).astype(jnp.bfloat16)


def placement(table, region, length, n_text, n_img):
    return pl.pallas_call(
        functools.partial(place_kernel, region),
        out_shape=(
            jax.ShapeDtypeStruct((length, n_text), jnp.bfloat16),
            jax.ShapeDtypeStruct((length, n_img), jnp.bfloat16),
            jax.ShapeDtypeStruct((length, 128), jnp.float32),
        ),
        in_specs=vmem_specs(1),
        out_specs=tuple(vmem_specs(3)),
        compiler_params=params(8),
        cost_estimate=TINY,
    )(table)


def cols_of(ref, owner, width):
    return ref[:, pl.ds(pl.multiple_of(owner * width, width), width)]


def scale_rows(x, gain):
    xf = x.astype(jnp.float32)
    return (xf * gain).astype(jnp.bfloat16), jnp.sum(xf * xf, axis=1, keepdims=True)


def own_kernel(me_ref, x_ref, gain_ref, w_ref, acc_ref, ss_ref, held_ref, sem_ref):
    n_ten, _, width, _ = held_ref.shape
    copies = []
    for s in range(n_ten):
        rows = pl.ds(pl.multiple_of((me_ref[0] ^ s) * width, width), width)
        copies += [pltpu.make_async_copy(w_ref.at[j, rows], held_ref.at[s, j], sem_ref.at[s, j]) for j in range(3)]
    for copy in copies:
        copy.start()
    scaled = []
    for first, count in sides(x_ref.shape[0]):
        rows = pl.ds(first, count)
        x, total = scale_rows(x_ref[rows], gain_ref[me_ref[0]])
        scaled.append(x)
        ss_ref[rows] = jnp.broadcast_to(total, (count, 128))
    for j in range(3):
        copies[j].wait()
        for side, (first, count) in enumerate(sides(x_ref.shape[0])):
            acc_ref[j, pl.ds(first, count)] = jnp.dot(
                scaled[side], held_ref[0, j], preferred_element_type=jnp.float32
            )
    for copy in copies[3:]:
        copy.wait()


def own_part(me, x, gain, w):
    rows, width = x.shape
    n_ten, cols = gain.shape[0], w.shape[2]
    return pl.pallas_call(
        own_kernel,
        out_shape=(
            jax.ShapeDtypeStruct((3, rows, cols), jnp.float32),
            jax.ShapeDtypeStruct((rows, 128), jnp.float32),
            pltpu.VMEM((n_ten, 3, width, cols), w.dtype),
        ),
        in_specs=[pl.BlockSpec(memory_space=pltpu.SMEM)] + vmem_specs(2) + [pl.BlockSpec(memory_space=pltpu.HBM)],
        out_specs=tuple(vmem_specs(3)),
        scratch_shapes=[pltpu.SemaphoreType.DMA((n_ten, 3))],
        compiler_params=params(12),
        cost_estimate=TINY,
    )(me, x, gain, in_hbm(w))


def near_kernel(near, pieces, me_ref, *refs):
    n_x = sum(pieces)
    x_refs, refs = list(refs[:n_x]), refs[n_x:]
    gain_ref, held_ref, acc_in, ss_in, acc_ref, ss_ref = refs
    parts = [pl.ds(first, count) for first, count in sides(acc_ref.shape[1])]
    views = []
    for n in pieces:
        mine, x_refs = x_refs[:n], x_refs[n:]
        views.append([mine[0].at[parts[side]] if n == 1 else mine[side] for side in range(2)])
    scaled = {}
    for side in range(2):
        rows = parts[side]
        total = ss_in[rows]
        for b, s in enumerate(near):
            scaled[side, b], part = scale_rows(views[b][side][...], gain_ref[me_ref[0] ^ s])
            total += part
        ss_ref[rows] = total
    for j in range(3):
        for side in range(2):
            rows = parts[side]
            acc = acc_in[j, rows]
            for b, s in enumerate(near):
                acc += jnp.dot(scaled[side, b], held_ref[s, j], preferred_element_type=jnp.float32)
            acc_ref[j, rows] = acc


def near_part(near, me, blocks, gain, held, acc, ss):
    blocks = [b if isinstance(b, tuple) else (b,) for b in blocks]
    pieces = [len(b) for b in blocks]
    return pl.pallas_call(
        functools.partial(near_kernel, near, pieces),
        out_shape=(
            jax.ShapeDtypeStruct(acc.shape, jnp.float32),
            jax.ShapeDtypeStruct(ss.shape, jnp.float32),
        ),
        in_specs=[pl.BlockSpec(memory_space=pltpu.SMEM)]
        + vmem_specs(sum(pieces) + 4),
        out_specs=tuple(vmem_specs(2)),
        compiler_params=params(12),
        cost_estimate=pl.CostEstimate(flops=10**11, bytes_accessed=0, transcendentals=0),
    )(me, *[h for b in blocks for h in b], gain, held, acc, ss)


def image_kernel(n_rows, n_blk, me_ref, *refs):
    x_refs, refs = refs[:n_blk], refs[n_blk:]
    gain_ref, sel_ref, held_ref, w_out_ref, qkv_ref, own_ref, w_out_held, sem_ref = refs
    copy = pltpu.make_async_copy(w_out_ref, w_out_held, sem_ref)
    copy.start()
    is_img = jnp.sum(sel_ref[...].astype(jnp.float32), axis=1, keepdims=True) > 0.5
    total = 0.0
    for s in range(n_blk):
        xf = x_refs[s][...].astype(jnp.float32)
        total += jnp.sum(xf * xf, axis=1, keepdims=True)
    scale = lax.rsqrt(total / D + EPS)
    total = 0.0
    scaled = []
    for s in range(n_blk):
        xf = x_refs[s][...].astype(jnp.float32)
        merged = jnp.where(is_img, xf * scale * xf[n_rows : n_rows + 1], xf).astype(jnp.bfloat16)
        if s == 0:
            own_ref[...] = merged
        mf = merged.astype(jnp.float32)
        total += jnp.sum(mf * mf, axis=1, keepdims=True)
        scaled.append((mf * gain_ref[me_ref[0] ^ s]).astype(jnp.bfloat16))
    scale = lax.rsqrt(total / D + EPS)
    for j in range(3):
        acc = 0.0
        for s in range(n_blk):
            acc += jnp.dot(scaled[s], held_ref[s, j], preferred_element_type=jnp.float32)
        qkv_ref[j] = (acc * scale).astype(jnp.bfloat16)
    copy.wait()


def image_part(me, blocks, gain, sel, held, w_out, n_rows):
    n_img, width = blocks[0].shape
    return pl.pallas_call(
        functools.partial(image_kernel, n_rows, len(blocks)),
        out_shape=(
            jax.ShapeDtypeStruct((3, n_img, held.shape[3]), jnp.bfloat16),
            jax.ShapeDtypeStruct((n_img, width), jnp.bfloat16),
            pltpu.VMEM(w_out.shape, w_out.dtype),
        ),
        in_specs=[pl.BlockSpec(memory_space=pltpu.SMEM)]
        + vmem_specs(len(blocks) + 3)
        + [pl.BlockSpec(memory_space=pltpu.HBM)],
        out_specs=tuple(vmem_specs(3)),
        scratch_shapes=[pltpu.SemaphoreType.DMA],
        compiler_params=params(12),
        cost_estimate=pl.CostEstimate(flops=0, bytes_accessed=0, transcendentals=0),
    )(me, *blocks, gain, sel, held, in_hbm(w_out))


def project_side(side, far, me_ref, x_ref, gain_ref, held_ref, acc_ref, ss_ref, out_ref):
    first, count = sides(acc_ref.shape[1])[side]
    part = pl.ds(first, count)
    x, total = scale_rows(x_ref[...], gain_ref[me_ref[0] ^ far])
    scale = lax.rsqrt((ss_ref[part] + total) / D + EPS)[:, :1]
    for j in range(3):
        prod = jnp.dot(x, held_ref[far, j], preferred_element_type=jnp.float32)
        out_ref[j, part] = ((prod + acc_ref[j, part]) * scale).astype(jnp.bfloat16)


def attend(edges, first, qkv_ref, key_ref, ctx_ref):
    heads = [pl.ds(h * HD, HD) for h in range(ctx_ref.shape[1] // HD)]
    for low, last in zip(edges, edges[1:]):
        here, step = pl.ds(low, last - low), last - low
        row = lax.broadcasted_iota(jnp.int32, (step, last), 0) + low
        col = lax.broadcasted_iota(jnp.int32, (step, last), 1)
        bias = jnp.where((row >= col) & (key_ref[0:1, pl.ds(0, last)] > 0.5), 0.0, -1e30)
        scores = [
            lax.dot_general(
                qkv_ref[0, here, lanes],
                qkv_ref[1, pl.ds(0, last), lanes],
                (((1,), (1,)), ((), ())),
                preferred_element_type=jnp.float32,
            )
            for lanes in heads
        ]
        scores = [x * (LOG2E / HD**0.5) + bias for x in scores]
        tops = [jnp.max(x, axis=1, keepdims=True) for x in scores]
        expo = [jnp.exp2(x - top) for x, top in zip(scores, tops)]
        sums = [jnp.sum(x, axis=1, keepdims=True) for x in expo]
        outs = [
            jnp.dot(x.astype(jnp.bfloat16), qkv_ref[2, pl.ds(0, last), lanes], preferred_element_type=jnp.float32)
            for x, lanes in zip(expo, heads)
        ]
        for lanes, out, total in zip(heads, outs, sums):
            ctx_ref[pl.ds(low - first, step), lanes] = (out / total).astype(jnp.bfloat16)


def put_columns(product, outs):
    half = outs[0].shape[1]
    for i, out_ref in enumerate(outs):
        out_ref[...] = product[:, i * half : (i + 1) * half].astype(out_ref.dtype)


def head_kernel(far, me_ref, top_ref, gain_ref, held_ref, acc_ref, ss_ref, img_ref, text_at_ref, img_at_ref, key_ref,
                w_out_ref, text_qkv_ref, qkv_ref, ctx_ref, left_ref, right_ref):
    rows = ctx_ref.shape[0]
    width = 2 * left_ref.shape[1]
    project_side(0, far, me_ref, top_ref, gain_ref, held_ref, acc_ref, ss_ref, text_qkv_ref)
    for j in range(3):
        qkv = jnp.dot(text_at_ref[:rows, :rows], text_qkv_ref[j], preferred_element_type=jnp.float32)
        qkv += jnp.dot(img_at_ref[:rows], img_ref[j], preferred_element_type=jnp.float32)
        qkv_ref[j] = qkv.astype(jnp.bfloat16)
    attend([0, rows], 0, qkv_ref, key_ref, ctx_ref)
    weight = cols_of(w_out_ref, me_ref[0] ^ far, width)
    put_columns(jnp.dot(ctx_ref[...], weight, preferred_element_type=jnp.float32), (left_ref, right_ref))


def head_part(far, me, top, gain, held, acc, ss, img, text_at, img_at, key_ok, w_out):
    width, cols = held.shape[2:]
    rows = top.shape[0]
    bf16 = jnp.bfloat16
    return pl.pallas_call(
        functools.partial(head_kernel, far),
        out_shape=(
            jax.ShapeDtypeStruct((3, rows, cols), bf16),
            jax.ShapeDtypeStruct((3, rows, cols), bf16),
            jax.ShapeDtypeStruct((rows, cols), bf16),
            jax.ShapeDtypeStruct((rows, width // 2), bf16),
            jax.ShapeDtypeStruct((rows, width // 2), bf16),
        ),
        in_specs=[pl.BlockSpec(memory_space=pltpu.SMEM)] + vmem_specs(10),
        out_specs=tuple(vmem_specs(5)),
        compiler_params=params(12),
        cost_estimate=TINY,
    )(me, top, gain, held, acc, ss, img, text_at, img_at, key_ok, w_out)


def tail_kernel(far, me_ref, bottom_ref, gain_ref, held_ref, acc_ref, ss_ref, img_ref, text_at_ref, img_at_ref,
                key_ref, w_out_ref, top_qkv_ref, head_qkv_ref, ctx_ref, left_ref, right_ref, text_qkv_ref, qkv_ref):
    first = top_qkv_ref.shape[1]
    length = text_at_ref.shape[0]
    width = 2 * left_ref.shape[1]
    project_side(1, far, me_ref, bottom_ref, gain_ref, held_ref, acc_ref, ss_ref, text_qkv_ref)
    for j in range(3):
        text_qkv_ref[j, :first] = top_qkv_ref[j]
        qkv_ref[j, :first] = head_qkv_ref[j]
        qkv = jnp.dot(text_at_ref[first:], text_qkv_ref[j], preferred_element_type=jnp.float32)
        qkv += jnp.dot(img_at_ref[first:], img_ref[j], preferred_element_type=jnp.float32)
        qkv_ref[j, first:] = qkv.astype(jnp.bfloat16)
    edges = [first] + [at for at in range(128, length, 128) if at > first] + [length]
    attend(edges, first, qkv_ref, key_ref, ctx_ref)
    weight = cols_of(w_out_ref, me_ref[0] ^ far, width)
    put_columns(jnp.dot(ctx_ref[...], weight, preferred_element_type=jnp.float32), (left_ref, right_ref))


def tail_part(far, me, bottom, gain, held, acc, ss, img, text_at, img_at, key_ok, w_out, top_qkv, head_qkv):
    width, cols = held.shape[2:]
    length, n_text = text_at.shape
    rows = length - top_qkv.shape[1]
    bf16 = jnp.bfloat16
    return pl.pallas_call(
        functools.partial(tail_kernel, far),
        out_shape=(
            jax.ShapeDtypeStruct((rows, cols), bf16),
            jax.ShapeDtypeStruct((rows, width // 2), bf16),
            jax.ShapeDtypeStruct((rows, width // 2), bf16),
        ),
        in_specs=[pl.BlockSpec(memory_space=pltpu.SMEM)] + vmem_specs(12),
        out_specs=tuple(vmem_specs(3)),
        scratch_shapes=[pltpu.VMEM((3, n_text, cols), bf16), pltpu.VMEM((3, length, cols), bf16)],
        compiler_params=params(12),
        cost_estimate=pl.CostEstimate(flops=10**10, bytes_accessed=0, transcendentals=0),
    )(me, bottom, gain, held, acc, ss, img, text_at, img_at, key_ok, w_out, top_qkv, head_qkv)


def out_kernel(away, me_ref, head_ref, tail_ref, w_ref, left_ref, right_ref):
    first = head_ref.shape[0]
    weight = cols_of(w_ref, me_ref[0] ^ away, 2 * left_ref.shape[1])
    for ctx_ref, rows in ((head_ref, slice(None, first)), (tail_ref, slice(first, None))):
        product = jnp.dot(ctx_ref[...], weight, preferred_element_type=jnp.float32)
        put_columns(product, (left_ref.at[rows], right_ref.at[rows]))


def out_part(away, me, head, tail, w, width, dtype=jnp.bfloat16):
    rows = head.shape[0] + tail.shape[0]
    return pl.pallas_call(
        functools.partial(out_kernel, away),
        out_shape=(jax.ShapeDtypeStruct((rows, width // 2), dtype),) * 2,
        in_specs=[pl.BlockSpec(memory_space=pltpu.SMEM)] + vmem_specs(3),
        out_specs=tuple(vmem_specs(2)),
        compiler_params=params(12),
        cost_estimate=pl.CostEstimate(flops=10**9, bytes_accessed=0, transcendentals=0),
    )(me, head, tail, w)


def sum_of(refs):
    return functools.reduce(lambda a, b: a + b, [ref[...].astype(jnp.float32) for ref in refs])


def first_kernel(n_left, base_ref, *refs):
    out_ref = refs[-1]
    half = base_ref.shape[1] // 2
    for side, terms in enumerate((refs[:n_left], refs[n_left:-1])):
        part = pl.ds(side * half, half)
        out_ref[:, part] = base_ref[:, part].astype(jnp.float32) + sum_of(terms)


def add_first(base, left, right):
    return pl.pallas_call(
        functools.partial(first_kernel, len(left)),
        out_shape=jax.ShapeDtypeStruct(base.shape, jnp.float32),
        in_specs=vmem_specs(1 + len(left) + len(right)),
        out_specs=pl.BlockSpec(memory_space=pltpu.VMEM),
        compiler_params=params(12),
        cost_estimate=TINY,
    )(base, *left, *right)


def last_kernel(n_left, base_ref, *refs):
    refs, (out_ref, tmp_ref, sem_ref) = refs[:-3], refs[-3:]
    half = base_ref.shape[1] // 2
    copies = []
    for side, terms in enumerate((refs[:n_left], refs[n_left:])):
        part = pl.ds(side * half, half)
        tmp_ref[:, part] = (base_ref[:, part] + sum_of(terms)).astype(tmp_ref.dtype)
        copy = pltpu.make_async_copy(tmp_ref.at[:, part], out_ref.at[:, part], sem_ref.at[side])
        copy.start()
        copies.append(copy)
    for copy in copies:
        copy.wait()


def add_last(base, left, right):
    return pl.pallas_call(
        functools.partial(last_kernel, len(left)),
        out_shape=jax.ShapeDtypeStruct(base.shape, jnp.bfloat16),
        in_specs=vmem_specs(1 + len(left) + len(right)),
        out_specs=pl.BlockSpec(memory_space=pl.ANY),
        scratch_shapes=[pltpu.VMEM(base.shape, jnp.bfloat16), pltpu.SemaphoreType.DMA((2,))],
        compiler_params=params(12),
        cost_estimate=TINY,
    )(base, *left, *right)


def scatter_terms(parts, got, n):
    acc = {s: [[parts[s][0]], [parts[s][1]]] for s in parts}
    far = n - 1
    acc[far ^ low_bit(far)][0].append(got[0])
    acc[far ^ high_bit(far)][1].append(got[1])
    early, late = [[], []], [[], []]
    for s in by_bits(n, reverse=True)[1:]:
        for side, bit in ((0, low_bit(s)), (1, high_bit(s))):
            terms = [t.astype(jnp.float32) for t in acc[s][side]]
            out = swap(functools.reduce(lambda a, b: a + b, terms).astype(jnp.bfloat16), bit)
            if s == bit:
                (early if len(terms) == 1 else late)[side].append(out)
            else:
                acc[s ^ bit][side].append(out)
    return early, late


def body(text, patches, grids, image_request, slot_start, vis_gain, dec_gain, w_qkv, w_out):
    n_req = lax.axis_size("req")
    n_ten = lax.axis_size("tensor")
    me_req = lax.axis_index("req")
    me_ten = lax.axis_index("tensor")
    img_dev, side, _, width = patches.shape
    half = side // 2
    region = half * half
    length = text.shape[0]
    w3 = jnp.transpose(w_qkv, (1, 0, 2))
    req_at = me_req.astype(jnp.int32)[None]
    ten_at = me_ten.astype(jnp.int32)[None]
    order = by_bits(n_ten)
    near_at, far = order[:-1], order[-1]

    n_rows = n_req * region
    n_img = round_up(n_rows + 1, 16)
    n_text = length - (n_rows if img_dev == n_req else 0)
    even, odd, ctext, rtext, sel, table, key_ok, gains, vis_row = prepare(
        req_at, image_request, slot_start, grids, text, jnp.transpose(patches, (1, 2, 0, 3)), dec_gain, vis_gain, n_req,
        n_text, n_img
    )
    blocks = near_blocks(ctext, n_ten)

    pairs = mix_pairs(even, swap(odd, 1, "req"), region)
    received = [pairs[0]] + [swap(pairs[i], 2 * i, "req") for i in range(1, n_req // 2)]
    table, pairs = lax.optimization_barrier((table, pairs))
    text_at, img_at, text_row = placement(table, region, length, n_text, n_img)
    received, text_at = lax.optimization_barrier((received, text_at))
    img_own = pack_images(received, vis_row, rtext, sel, region)
    img_blocks = [img_own] + [swap(img_own, s) for s in range(1, n_ten)]
    own, img_own = lax.optimization_barrier((ctext, img_own))
    acc, ss, held = own_part(ten_at, own, gains, w3)
    handed, img_own = lax.optimization_barrier((blocks, img_own))
    blocks = {**far_blocks(handed, n_ten), **blocks}

    near = [blocks[s] for s in near_at]
    acc, ss = near_part(near_at, ten_at, near, gains, held, acc, ss)
    img_blocks, acc = lax.optimization_barrier((img_blocks, acc))
    img_qkv, merged, w_out = image_part(ten_at, img_blocks, gains, sel, held, w_out, n_rows)

    shared = (gains, held, acc, ss, img_qkv, text_at, img_at, key_ok, w_out)
    top_qkv, head_qkv, head_ctx, *head_far = head_part(far, ten_at, blocks[far][0], *shared)
    tail_ctx, *tail_far = tail_part(far, ten_at, blocks[far][1], *shared, top_qkv, head_qkv)

    img_here = jnp.dot(img_at, merged, preferred_element_type=jnp.float32)
    x_in = (text.astype(jnp.float32) * text_row[:, :1] + img_here).astype(jnp.bfloat16)

    bits = (low_bit(far), high_bit(far))
    head_got = [swap(t, bit) for t, bit in zip(head_far, bits)]
    tail_got = [swap(t, bit) for t, bit in zip(tail_far, bits)]
    head_got, head_ctx, tail_ctx = lax.optimization_barrier((head_got, head_ctx, tail_ctx))
    parts = {}
    for s in reversed([0] + near_at):
        parts[s] = out_part(s, ten_at, head_ctx, tail_ctx, w_out, width, jnp.float32 if s == 0 else jnp.bfloat16)
    got = [jnp.concatenate(pair, axis=0) for pair in zip(head_got, tail_got)]
    early, late = scatter_terms(parts, got, n_ten)
    base = add_first(x_in, [parts[0][0]] + early[0], [parts[0][1]] + early[1])
    return add_last(base, late[0], late[1])


def solution(mesh):
    in_specs = (
        P("req", "tensor"),
        P("req", None, None, "tensor"),
        P(),
        P(),
        P(),
        P("tensor"),
        P(),
        P(None, None, "tensor"),
        P("tensor", None),
    )
    out_specs = P("req", "tensor")
    return jax.shard_map(body, mesh=mesh, in_specs=in_specs, out_specs=out_specs, check_vma=False)
```

```python
import functools

import jax
import jax.numpy as jnp
from jax import lax
from jax.experimental import pallas as pl
from jax.experimental.pallas import tpu as pltpu
from jax.sharding import PartitionSpec as P

D = 4096
HD = 128
EPS = 1e-05
LOG2E = 1.4426950408889634
TINY = pl.CostEstimate(flops=0, bytes_accessed=0, transcendentals=0)


def round_up(n, m):
    return -(-n // m) * m


def swap(x, s, axis="tensor"):
    n = lax.axis_size(axis)
    return lax.ppermute(x, axis, [(i, i ^ s) for i in range(n)])


def in_hbm(x):
    return pltpu.with_memory_space_constraint(x, pltpu.HBM)


def low_bit(s):
    return s & -s


def high_bit(s):
    return 1 << (s.bit_length() - 1)


def by_bits(n, reverse=False):
    return sorted(range(1, n), key=lambda s: (bin(s).count("1"), s), reverse=reverse)


def halves(block):
    if isinstance(block, tuple):
        return block
    half = block.shape[0] // 2
    return block[:half], block[half:]


def near_blocks(x, n):
    return {s: swap(x, s) for s in by_bits(n) if s & (s - 1) == 0}


def far_blocks(blocks, n):
    blocks = dict(blocks)
    for s in by_bits(n):
        if s not in blocks:
            low, high = low_bit(s), high_bit(s)
            blocks[s] = (swap(halves(blocks[s ^ low])[0], low), swap(halves(blocks[s ^ high])[1], high))
    return blocks


def vmem_specs(n):
    return [pl.BlockSpec(memory_space=pltpu.VMEM)] * n


def params(mib):
    return pltpu.CompilerParams(vmem_limit_bytes=mib * 1024 * 1024)


def fetch(pairs, sem_ref):
    copies = [pltpu.make_async_copy(src, dst, sem_ref.at[i]) for i, (src, dst) in enumerate(pairs)]
    for copy in copies:
        copy.start()
    return copies


NOWHERE = 1 << 20


def find_images(n_req, img_dev, me, req_ref, start_ref, grid_ref=None):
    found = []
    for s in range(n_req):
        source = (me ^ s) * img_dev

        def one_image(k, found, source=source):
            hit = req_ref[source + k] == me
            values = (start_ref[source + k],)
            if grid_ref is not None:
                values += (grid_ref[0, source + k] // 2, grid_ref[1, source + k] // 2)
            return tuple(jnp.where(hit, new, old) for new, old in zip(values, found))

        none = (jnp.int32(NOWHERE), jnp.int32(0), jnp.int32(1))[: 1 if grid_ref is None else 3]
        found.append(lax.fori_loop(0, img_dev, one_image, none, unroll=img_dev <= 8))
    return found


def text_kernel(n_req, region, me_ref, req_hbm, start_hbm, text_hbm, *refs):
    others, (ctext_out, text_ref, *kept), (req_ref, start_ref, sem_ref) = refs[:3], refs[3:8], refs[8:]
    pairs = ((req_hbm, req_ref), (start_hbm, start_ref), (text_hbm, text_ref)) + tuple(zip(others, kept))
    copies = fetch(pairs, sem_ref)
    n_text, length = ctext_out.shape[0], text_ref.shape[0]
    spot = lax.broadcasted_iota(jnp.int32, (8, length), 1)
    before = jnp.zeros((8, length), jnp.int32)
    inside = jnp.zeros((8, length), jnp.int32)
    copies[0].wait()
    copies[1].wait()
    for (start,) in find_images(n_req, req_ref.shape[0] // n_req, me_ref[0], req_ref, start_ref):
        c = spot - start
        before += jnp.clip(c, 0, region)
        inside = jnp.where((c >= 0) & (c < region), 1, inside)
    rank = jnp.where(inside == 1, -1, spot - before)[0:1]
    gather = (lax.broadcasted_iota(jnp.int32, (n_text, length), 0) == rank).astype(jnp.bfloat16)
    copies[2].wait()
    ctext_out[...] = jnp.dot(gather, text_ref[...], preferred_element_type=jnp.float32).astype(jnp.bfloat16)
    for copy in copies[3:]:
        copy.wait()


def gather_text(me, image_request, slot_start, text, patches, dec_gain, vis_gain, n_req, region, n_text):
    inputs = (image_request, slot_start, text, patches, dec_gain.reshape(-1, 128), vis_gain.reshape(-1, 128))
    return pl.pallas_call(
        functools.partial(text_kernel, n_req, region),
        out_shape=(jax.ShapeDtypeStruct((n_text, text.shape[1]), text.dtype),)
        + tuple(pltpu.VMEM(x.shape, x.dtype) for x in inputs[2:]),
        in_specs=[pl.BlockSpec(memory_space=pltpu.SMEM)] + [pl.BlockSpec(memory_space=pltpu.HBM)] * len(inputs),
        out_specs=tuple(vmem_specs(len(inputs) - 1)),
        scratch_shapes=[pltpu.SMEM(x.shape, jnp.int32) for x in inputs[:2]] + [pltpu.SemaphoreType.DMA((len(inputs),))],
        compiler_params=params(8),
        cost_estimate=TINY,
    )(me, *[in_hbm(x) for x in inputs])


def prep_kernel(n_req, me_ref, req_hbm, start_hbm, grid_hbm, text_ref, x_ref, dec_ref, vis_ref, *refs):
    (even_out, odd_out, rtext_out, sel_out, table_out, key_out, dec_out, vis_out, req_ref, start_ref, grid_ref,
     pool_ref, tmp_ref, sem_ref) = refs
    copies = fetch(((req_hbm, req_ref), (start_hbm, start_ref), (grid_hbm, grid_ref)), sem_ref)
    side, img_dev = x_ref.shape[0], x_ref.shape[2]
    half = side // 2
    region = half * half
    n_img, length = sel_out.shape[0], text_ref.shape[0]
    me = me_ref[0]
    for i in range(half):
        for j in range(half):
            total = x_ref[2 * i, 2 * j].astype(jnp.float32)
            for a, b in ((0, 1), (1, 0), (1, 1)):
                total += x_ref[2 * i + a, 2 * j + b].astype(jnp.float32)
            pool_ref[i * half + j] = total * 0.25
    tmp_ref[...] = jnp.zeros_like(tmp_ref)
    for copy in copies:
        copy.wait()

    spot = lax.broadcasted_iota(jnp.int32, (8, length), 1)
    closed = jnp.zeros((8, length), jnp.int32)
    row = lax.broadcasted_iota(jnp.int32, (n_img, 128), 0)
    pos = jnp.full((n_img, 128), -1, jnp.int32)
    target = jnp.full((n_img, 128), -1, jnp.int32)
    line = lax.broadcasted_iota(jnp.int32, (n_req, 128), 0)
    table = jnp.zeros((n_req, 128), jnp.int32)
    for s, (start, high, wide) in enumerate(find_images(n_req, img_dev, me, req_ref, start_ref, grid_ref)):
        count = high * wide
        c = spot - start
        closed = jnp.where((c >= count) & (c < region) & (c >= 0), 1, closed)
        c = row - s * region
        here = (c >= 0) & (c < region)
        pos = jnp.where(here, start + c, pos)
        cell = c
        for w in range(1, half):
            cell = jnp.where(wide == w, c // w * half + c % w, cell)
        target = jnp.where(here & (c < count), s * region + cell, target)
        table = jnp.where(line == s, start, table)
    table_out[...] = table
    key_out[...] = 1.0 - closed.astype(jnp.float32)
    stays = jnp.where(target >= 0, -1, pos)[:, :1]
    keep = (lax.broadcasted_iota(jnp.int32, (n_img, length), 1) == stays).astype(jnp.bfloat16)
    sel = lax.broadcasted_iota(jnp.int32, (n_img, n_img), 1) == target[:, :1]
    sel_out[...] = sel.astype(jnp.bfloat16)
    rows = lax.broadcasted_iota(jnp.int32, (n_req, img_dev), 0)
    cols = lax.broadcasted_iota(jnp.int32, (n_req, img_dev), 1)
    goal = jnp.full((n_req, img_dev), -1, jnp.int32)
    for k in range(img_dev):
        goal = jnp.where(cols == k, req_ref[me * img_dev + k] ^ me, goal)
    onehot = (rows == goal).astype(jnp.bfloat16)

    rtext_out[...] = jnp.dot(keep, text_ref[...], preferred_element_type=jnp.float32).astype(jnp.bfloat16)
    for cell in range(region):
        pooled = pool_ref[cell].astype(jnp.bfloat16)
        tmp_ref[:, cell, :] = jnp.dot(onehot, pooled, preferred_element_type=jnp.float32)
    for s in range(n_req):
        (even_out, odd_out)[s % 2][s // 2] = tmp_ref[s].astype(jnp.bfloat16)
    per = vis_ref.shape[0]
    for i in range(per):
        lanes = pl.ds(i * 128, 128)
        vis_out[:, lanes] = vis_ref[i : i + 1, :].astype(jnp.float32)
        for t in range(dec_out.shape[0]):
            at = t * per + i
            dec_out[t, :, lanes] = dec_ref[at : at + 1, :].astype(jnp.float32)


def prepare(me, image_request, slot_start, grids, text, patches, dec_rows, vis_rows, n_req, n_img):
    side, _, img_dev, width = patches.shape
    padded = round_up((side // 2) ** 2, 16)
    inputs = (image_request, slot_start, grids.T)
    bf16, f32 = jnp.bfloat16, jnp.float32
    outputs = [((n_req // 2, padded, width), bf16)] * 2 + [
        ((n_img, width), bf16),
        ((n_img, n_img), bf16),
        ((n_req, 128), jnp.int32),
        ((8, text.shape[0]), f32),
        ((dec_rows.size // width, 1, width), f32),
        ((1, width), f32),
    ]
    return pl.pallas_call(
        functools.partial(prep_kernel, n_req),
        out_shape=tuple(jax.ShapeDtypeStruct(shape, kind) for shape, kind in outputs),
        in_specs=[pl.BlockSpec(memory_space=pltpu.SMEM)]
        + [pl.BlockSpec(memory_space=pltpu.HBM)] * 3
        + vmem_specs(4),
        out_specs=tuple(vmem_specs(len(outputs))),
        scratch_shapes=[pltpu.SMEM(x.shape, jnp.int32) for x in inputs]
        + [
            pltpu.VMEM(((side // 2) ** 2, img_dev, width), f32),
            pltpu.VMEM((n_req, padded, width), f32),
            pltpu.SemaphoreType.DMA((3,)),
        ],
        compiler_params=params(12),
        cost_estimate=TINY,
    )(me, *[in_hbm(x) for x in inputs], text, patches, dec_rows, vis_rows)


def mix_kernel(region, even_ref, odd_ref, *refs):
    outs, tmp_ref = refs[:-1], refs[-1]
    for i, out_ref in enumerate(outs):
        tmp_ref[:region] = even_ref[i].astype(jnp.float32)[:region]
        tmp_ref[region : 2 * region] = odd_ref[i].astype(jnp.float32)[:region]
        tmp_ref[2 * region :] = jnp.zeros((tmp_ref.shape[0] - 2 * region, tmp_ref.shape[1]), jnp.float32)
        out_ref[...] = tmp_ref[...].astype(jnp.bfloat16)


def mix_pairs(even, odd, region):
    n, _, width = even.shape
    rows = round_up(2 * region, 8)
    return pl.pallas_call(
        functools.partial(mix_kernel, region),
        out_shape=(jax.ShapeDtypeStruct((rows, width), jnp.bfloat16),) * n,
        in_specs=vmem_specs(2),
        out_specs=tuple(vmem_specs(n)),
        scratch_shapes=[pltpu.VMEM((rows, width), jnp.float32)],
        compiler_params=params(4),
        cost_estimate=TINY,
    )(even, odd)


def pack_kernel(region, gain_ref, rtext_ref, sel_ref, *refs):
    recs, (out_ref, tmp_ref) = refs[:-2], refs[-2:]
    done = 0
    for rec_ref in recs:
        tmp_ref[done : done + 2 * region] = rec_ref[...].astype(jnp.float32)[: 2 * region]
        done += 2 * region
    rest = tmp_ref.shape[0] - done
    tmp_ref[done:] = jnp.zeros((rest, tmp_ref.shape[1]), jnp.float32)
    picked = jnp.dot(sel_ref[...], tmp_ref[...].astype(jnp.bfloat16), preferred_element_type=jnp.float32)
    tmp_ref[...] = picked + rtext_ref[...].astype(jnp.float32)
    tmp_ref[done:] = jnp.broadcast_to(gain_ref[0:1, :], (rest, gain_ref.shape[1]))
    out_ref[...] = tmp_ref[...].astype(jnp.bfloat16)


def pack_images(received, gain, rtext, sel, region):
    n_img, width = rtext.shape
    return pl.pallas_call(
        functools.partial(pack_kernel, region),
        out_shape=jax.ShapeDtypeStruct((n_img, width), jnp.bfloat16),
        in_specs=vmem_specs(3 + len(received)),
        out_specs=pl.BlockSpec(memory_space=pltpu.VMEM),
        scratch_shapes=[pltpu.VMEM((n_img, width), jnp.float32)],
        compiler_params=params(4),
        cost_estimate=TINY,
    )(gain, rtext, sel, *received)


def place_kernel(region, table_ref, text_at_ref, img_at_ref, text_row_ref):
    length, n_text = text_at_ref.shape
    spot = lax.broadcasted_iota(jnp.int32, (length, 128), 0)
    before = jnp.zeros((length, 128), jnp.int32)
    at = jnp.full((length, 128), -1, jnp.int32)
    for s in range(table_ref.shape[0]):
        c = spot - table_ref[s : s + 1, :]
        before += jnp.clip(c, 0, region)
        at = jnp.where((c >= 0) & (c < region), s * region + c, at)
    text_row_ref[...] = jnp.where(at < 0, 1.0, 0.0)
    rank = jnp.where(at < 0, spot - before, -1)[:, :1]
    text_at_ref[...] = (lax.broadcasted_iota(jnp.int32, (length, n_text), 1) == rank).astype(jnp.bfloat16)
    lane = lax.broadcasted_iota(jnp.int32, img_at_ref.shape, 1)
    img_at_ref[...] = (lane == at[:, :1]).astype(jnp.bfloat16)


def placement(table, region, length, n_text, n_img):
    return pl.pallas_call(
        functools.partial(place_kernel, region),
        out_shape=(
            jax.ShapeDtypeStruct((length, n_text), jnp.bfloat16),
            jax.ShapeDtypeStruct((length, n_img), jnp.bfloat16),
            jax.ShapeDtypeStruct((length, 128), jnp.float32),
        ),
        in_specs=vmem_specs(1),
        out_specs=tuple(vmem_specs(3)),
        compiler_params=params(8),
        cost_estimate=TINY,
    )(table)


def cols_of(ref, owner, width):
    return ref[:, pl.ds(pl.multiple_of(owner * width, width), width)]


def scale_rows(x, gain):
    xf = x.astype(jnp.float32)
    return (xf * gain).astype(jnp.bfloat16), jnp.sum(xf * xf, axis=1, keepdims=True)


def own_kernel(me_ref, x_ref, gain_ref, w_ref, acc_ref, ss_ref, held_ref, sem_ref):
    n_ten, _, width, _ = held_ref.shape
    half = x_ref.shape[0] // 2
    copies = []
    for s in range(n_ten):
        rows = pl.ds(pl.multiple_of((me_ref[0] ^ s) * width, width), width)
        copies += [pltpu.make_async_copy(w_ref.at[j, rows], held_ref.at[s, j], sem_ref.at[s, j]) for j in range(3)]
    for copy in copies:
        copy.start()
    scaled = []
    for side in range(2):
        rows = pl.ds(side * half, half)
        x, total = scale_rows(x_ref[rows], gain_ref[me_ref[0]])
        scaled.append(x)
        ss_ref[rows] = jnp.broadcast_to(total, (half, 128))
    for j in range(3):
        copies[j].wait()
        for side in range(2):
            acc_ref[j, pl.ds(side * half, half)] = jnp.dot(
                scaled[side], held_ref[0, j], preferred_element_type=jnp.float32
            )
    for copy in copies[3:]:
        copy.wait()


def own_part(me, x, gain, w):
    rows, width = x.shape
    n_ten, cols = gain.shape[0], w.shape[2]
    return pl.pallas_call(
        own_kernel,
        out_shape=(
            jax.ShapeDtypeStruct((3, rows, cols), jnp.float32),
            jax.ShapeDtypeStruct((rows, 128), jnp.float32),
            pltpu.VMEM((n_ten, 3, width, cols), w.dtype),
        ),
        in_specs=[pl.BlockSpec(memory_space=pltpu.SMEM)] + vmem_specs(2) + [pl.BlockSpec(memory_space=pltpu.HBM)],
        out_specs=tuple(vmem_specs(3)),
        scratch_shapes=[pltpu.SemaphoreType.DMA((n_ten, 3))],
        compiler_params=params(12),
        cost_estimate=TINY,
    )(me, x, gain, in_hbm(w))


def near_kernel(near, pieces, me_ref, *refs):
    n_x = sum(pieces)
    x_refs, refs = list(refs[:n_x]), refs[n_x:]
    gain_ref, held_ref, acc_in, ss_in, acc_ref, ss_ref = refs
    half = acc_ref.shape[1] // 2
    views = []
    for n in pieces:
        mine, x_refs = x_refs[:n], x_refs[n:]
        views.append([mine[0].at[pl.ds(side * half, half)] if n == 1 else mine[side] for side in range(2)])
    scaled = {}
    for side in range(2):
        rows = pl.ds(side * half, half)
        total = ss_in[rows]
        for b, s in enumerate(near):
            scaled[side, b], part = scale_rows(views[b][side][...], gain_ref[me_ref[0] ^ s])
            total += part
        ss_ref[rows] = total
    for j in range(3):
        for side in range(2):
            rows = pl.ds(side * half, half)
            acc = acc_in[j, rows]
            for b, s in enumerate(near):
                acc += jnp.dot(scaled[side, b], held_ref[s, j], preferred_element_type=jnp.float32)
            acc_ref[j, rows] = acc


def near_part(near, me, blocks, gain, held, acc, ss):
    blocks = [b if isinstance(b, tuple) else (b,) for b in blocks]
    pieces = [len(b) for b in blocks]
    return pl.pallas_call(
        functools.partial(near_kernel, near, pieces),
        out_shape=(
            jax.ShapeDtypeStruct(acc.shape, jnp.float32),
            jax.ShapeDtypeStruct(ss.shape, jnp.float32),
        ),
        in_specs=[pl.BlockSpec(memory_space=pltpu.SMEM)]
        + vmem_specs(sum(pieces) + 4),
        out_specs=tuple(vmem_specs(2)),
        compiler_params=params(12),
        cost_estimate=pl.CostEstimate(flops=10**11, bytes_accessed=0, transcendentals=0),
    )(me, *[h for b in blocks for h in b], gain, held, acc, ss)


def image_kernel(n_rows, n_blk, me_ref, *refs):
    x_refs, refs = refs[:n_blk][::-1], refs[n_blk:]
    gain_ref, sel_ref, held_ref, w_out_ref, qkv_ref, own_ref, w_out_held, sem_ref = refs
    copy = pltpu.make_async_copy(w_out_ref, w_out_held, sem_ref)
    copy.start()
    is_img = jnp.sum(sel_ref[...].astype(jnp.float32), axis=1, keepdims=True) > 0.5
    total = 0.0
    for s in range(n_blk):
        xf = x_refs[s][...].astype(jnp.float32)
        total += jnp.sum(xf * xf, axis=1, keepdims=True)
    scale = lax.rsqrt(total / D + EPS)
    total = 0.0
    scaled = []
    for s in range(n_blk):
        xf = x_refs[s][...].astype(jnp.float32)
        merged = jnp.where(is_img, xf * scale * xf[n_rows : n_rows + 1], xf).astype(jnp.bfloat16)
        if s == 0:
            own_ref[...] = merged
        mf = merged.astype(jnp.float32)
        total += jnp.sum(mf * mf, axis=1, keepdims=True)
        scaled.append((mf * gain_ref[me_ref[0] ^ s]).astype(jnp.bfloat16))
    scale = lax.rsqrt(total / D + EPS)
    for j in range(3):
        acc = 0.0
        for s in range(n_blk):
            acc += jnp.dot(scaled[s], held_ref[s, j], preferred_element_type=jnp.float32)
        qkv_ref[j] = (acc * scale).astype(jnp.bfloat16)
    copy.wait()


def image_part(me, blocks, gain, sel, held, w_out, n_rows):
    n_img, width = blocks[0].shape
    return pl.pallas_call(
        functools.partial(image_kernel, n_rows, len(blocks)),
        out_shape=(
            jax.ShapeDtypeStruct((3, n_img, held.shape[3]), jnp.bfloat16),
            jax.ShapeDtypeStruct((n_img, width), jnp.bfloat16),
            pltpu.VMEM(w_out.shape, w_out.dtype),
        ),
        in_specs=[pl.BlockSpec(memory_space=pltpu.SMEM)]
        + vmem_specs(len(blocks) + 3)
        + [pl.BlockSpec(memory_space=pltpu.HBM)],
        out_specs=tuple(vmem_specs(3)),
        scratch_shapes=[pltpu.SemaphoreType.DMA],
        compiler_params=params(12),
        cost_estimate=pl.CostEstimate(flops=3*10**9, bytes_accessed=0, transcendentals=0),
    )(me, *blocks, gain, sel, held, in_hbm(w_out))


def project_side(side, far, me_ref, x_ref, gain_ref, held_ref, acc_ref, ss_ref, out_ref):
    half = x_ref.shape[0]
    part = pl.ds(side * half, half)
    x, total = scale_rows(x_ref[...], gain_ref[me_ref[0] ^ far])
    scale = lax.rsqrt((ss_ref[part] + total) / D + EPS)[:, :1]
    for j in range(3):
        prod = jnp.dot(x, held_ref[far, j], preferred_element_type=jnp.float32)
        out_ref[j, part] = ((prod + acc_ref[j, part]) * scale).astype(jnp.bfloat16)


def attend(edges, first, qkv_ref, key_ref, ctx_ref):
    heads = [pl.ds(h * HD, HD) for h in range(ctx_ref.shape[1] // HD)]
    for low, last in zip(edges, edges[1:]):
        here, step = pl.ds(low, last - low), last - low
        row = lax.broadcasted_iota(jnp.int32, (step, last), 0) + low
        col = lax.broadcasted_iota(jnp.int32, (step, last), 1)
        bias = jnp.where((row >= col) & (key_ref[0:1, pl.ds(0, last)] > 0.5), 0.0, -1e30)
        scores = [
            lax.dot_general(
                qkv_ref[0, here, lanes],
                qkv_ref[1, pl.ds(0, last), lanes],
                (((1,), (1,)), ((), ())),
                preferred_element_type=jnp.float32,
            )
            for lanes in heads
        ]
        scores = [x * (LOG2E / HD**0.5) + bias for x in scores]
        tops = [jnp.max(x, axis=1, keepdims=True) for x in scores]
        expo = [jnp.exp2(x - top) for x, top in zip(scores, tops)]
        sums = [jnp.sum(x, axis=1, keepdims=True) for x in expo]
        outs = [
            jnp.dot(x.astype(jnp.bfloat16), qkv_ref[2, pl.ds(0, last), lanes], preferred_element_type=jnp.float32)
            for x, lanes in zip(expo, heads)
        ]
        for lanes, out, total in zip(heads, outs, sums):
            ctx_ref[pl.ds(low - first, step), lanes] = (out / total).astype(jnp.bfloat16)


def put_columns(product, outs):
    half = outs[0].shape[1]
    for i, out_ref in enumerate(outs):
        out_ref[...] = product[:, i * half : (i + 1) * half].astype(out_ref.dtype)


def head_kernel(far, me_ref, top_ref, gain_ref, held_ref, acc_ref, ss_ref, img_ref, text_at_ref, img_at_ref, key_ref,
                w_out_ref, text_qkv_ref, qkv_ref, ctx_ref, left_ref, right_ref):
    rows = ctx_ref.shape[0]
    width = 2 * left_ref.shape[1]
    project_side(0, far, me_ref, top_ref, gain_ref, held_ref, acc_ref, ss_ref, text_qkv_ref)
    for j in range(3):
        qkv = jnp.dot(text_at_ref[:rows, :rows], text_qkv_ref[j], preferred_element_type=jnp.float32)
        qkv += jnp.dot(img_at_ref[:rows], img_ref[j], preferred_element_type=jnp.float32)
        qkv_ref[j] = qkv.astype(jnp.bfloat16)
    attend([0, rows], 0, qkv_ref, key_ref, ctx_ref)
    weight = cols_of(w_out_ref, me_ref[0] ^ far, width)
    put_columns(jnp.dot(ctx_ref[...], weight, preferred_element_type=jnp.float32), (left_ref, right_ref))


def head_part(far, me, top, gain, held, acc, ss, img, text_at, img_at, key_ok, w_out):
    width, cols = held.shape[2:]
    rows = top.shape[0]
    bf16 = jnp.bfloat16
    return pl.pallas_call(
        functools.partial(head_kernel, far),
        out_shape=(
            jax.ShapeDtypeStruct((3, rows, cols), bf16),
            jax.ShapeDtypeStruct((3, rows, cols), bf16),
            jax.ShapeDtypeStruct((rows, cols), bf16),
            jax.ShapeDtypeStruct((rows, width // 2), bf16),
            jax.ShapeDtypeStruct((rows, width // 2), bf16),
        ),
        in_specs=[pl.BlockSpec(memory_space=pltpu.SMEM)] + vmem_specs(10),
        out_specs=tuple(vmem_specs(5)),
        compiler_params=params(12),
        cost_estimate=TINY,
    )(me, top, gain, held, acc, ss, img, text_at, img_at, key_ok, w_out)


def tail_kernel(far, me_ref, bottom_ref, gain_ref, held_ref, acc_ref, ss_ref, img_ref, text_at_ref, img_at_ref,
                key_ref, w_out_ref, top_qkv_ref, head_qkv_ref, ctx_ref, left_ref, right_ref, text_qkv_ref, qkv_ref):
    first = top_qkv_ref.shape[1]
    length = text_at_ref.shape[0]
    width = 2 * left_ref.shape[1]
    project_side(1, far, me_ref, bottom_ref, gain_ref, held_ref, acc_ref, ss_ref, text_qkv_ref)
    for j in range(3):
        text_qkv_ref[j, :first] = top_qkv_ref[j]
        qkv_ref[j, :first] = head_qkv_ref[j]
        qkv = jnp.dot(text_at_ref[first:], text_qkv_ref[j], preferred_element_type=jnp.float32)
        qkv += jnp.dot(img_at_ref[first:], img_ref[j], preferred_element_type=jnp.float32)
        qkv_ref[j, first:] = qkv.astype(jnp.bfloat16)
    edges = [first] + [at for at in range(128, length, 128) if at > first] + [length]
    attend(edges, first, qkv_ref, key_ref, ctx_ref)
    weight = cols_of(w_out_ref, me_ref[0] ^ far, width)
    put_columns(jnp.dot(ctx_ref[...], weight, preferred_element_type=jnp.float32), (left_ref, right_ref))


def tail_part(far, me, bottom, gain, held, acc, ss, img, text_at, img_at, key_ok, w_out, top_qkv, head_qkv):
    width, cols = held.shape[2:]
    length, n_text = text_at.shape
    rows = length - top_qkv.shape[1]
    bf16 = jnp.bfloat16
    return pl.pallas_call(
        functools.partial(tail_kernel, far),
        out_shape=(
            jax.ShapeDtypeStruct((rows, cols), bf16),
            jax.ShapeDtypeStruct((rows, width // 2), bf16),
            jax.ShapeDtypeStruct((rows, width // 2), bf16),
        ),
        in_specs=[pl.BlockSpec(memory_space=pltpu.SMEM)] + vmem_specs(12),
        out_specs=tuple(vmem_specs(3)),
        scratch_shapes=[pltpu.VMEM((3, n_text, cols), bf16), pltpu.VMEM((3, length, cols), bf16)],
        compiler_params=params(12),
        cost_estimate=pl.CostEstimate(flops=10**10, bytes_accessed=0, transcendentals=0),
    )(me, bottom, gain, held, acc, ss, img, text_at, img_at, key_ok, w_out, top_qkv, head_qkv)


def out_kernel(away, me_ref, head_ref, tail_ref, w_ref, left_ref, right_ref):
    first = head_ref.shape[0]
    weight = cols_of(w_ref, me_ref[0] ^ away, 2 * left_ref.shape[1])
    for ctx_ref, rows in ((head_ref, slice(None, first)), (tail_ref, slice(first, None))):
        product = jnp.dot(ctx_ref[...], weight, preferred_element_type=jnp.float32)
        put_columns(product, (left_ref.at[rows], right_ref.at[rows]))


def out_part(away, me, head, tail, w, width, dtype=jnp.bfloat16):
    rows = head.shape[0] + tail.shape[0]
    return pl.pallas_call(
        functools.partial(out_kernel, away),
        out_shape=(jax.ShapeDtypeStruct((rows, width // 2), dtype),) * 2,
        in_specs=[pl.BlockSpec(memory_space=pltpu.SMEM)] + vmem_specs(3),
        out_specs=tuple(vmem_specs(2)),
        compiler_params=params(12),
        cost_estimate=pl.CostEstimate(flops=10**9, bytes_accessed=0, transcendentals=0),
    )(me, head, tail, w)


def sum_of(refs):
    return functools.reduce(lambda a, b: a + b, [ref[...].astype(jnp.float32) for ref in refs])


def first_kernel(n_left, base_ref, *refs):
    out_ref = refs[-1]
    half = base_ref.shape[1] // 2
    for side, terms in enumerate((refs[:n_left], refs[n_left:-1])):
        part = pl.ds(side * half, half)
        out_ref[:, part] = base_ref[:, part].astype(jnp.float32) + sum_of(terms)


def add_first(base, left, right):
    return pl.pallas_call(
        functools.partial(first_kernel, len(left)),
        out_shape=jax.ShapeDtypeStruct(base.shape, jnp.float32),
        in_specs=vmem_specs(1 + len(left) + len(right)),
        out_specs=pl.BlockSpec(memory_space=pltpu.VMEM),
        compiler_params=params(12),
        cost_estimate=TINY,
    )(base, *left, *right)


def last_kernel(n_left, base_ref, *refs):
    refs, (out_ref, tmp_ref, sem_ref) = refs[:-3], refs[-3:]
    half = base_ref.shape[1] // 2
    copies = []
    for side, terms in enumerate((refs[:n_left], refs[n_left:])):
        part = pl.ds(side * half, half)
        tmp_ref[:, part] = (base_ref[:, part] + sum_of(terms)).astype(tmp_ref.dtype)
        copy = pltpu.make_async_copy(tmp_ref.at[:, part], out_ref.at[:, part], sem_ref.at[side])
        copy.start()
        copies.append(copy)
    for copy in copies:
        copy.wait()


def add_last(base, left, right):
    return pl.pallas_call(
        functools.partial(last_kernel, len(left)),
        out_shape=jax.ShapeDtypeStruct(base.shape, jnp.bfloat16),
        in_specs=vmem_specs(1 + len(left) + len(right)),
        out_specs=pl.BlockSpec(memory_space=pl.ANY),
        scratch_shapes=[pltpu.VMEM(base.shape, jnp.bfloat16), pltpu.SemaphoreType.DMA((2,))],
        compiler_params=params(12),
        cost_estimate=TINY,
    )(base, *left, *right)


def scatter_terms(parts, got, n):
    acc = {s: [[parts[s][0]], [parts[s][1]]] for s in parts}
    far = n - 1
    acc[far ^ low_bit(far)][0].append(got[0])
    acc[far ^ high_bit(far)][1].append(got[1])
    early, late = [[], []], [[], []]
    for s in by_bits(n, reverse=True)[1:]:
        for side, bit in ((0, low_bit(s)), (1, high_bit(s))):
            terms = [t.astype(jnp.float32) for t in acc[s][side]]
            out = swap(functools.reduce(lambda a, b: a + b, terms).astype(jnp.bfloat16), bit)
            if s == bit:
                (early if len(terms) == 1 else late)[side].append(out)
            else:
                acc[s ^ bit][side].append(out)
    return early, late


def body(text, patches, grids, image_request, slot_start, vis_gain, dec_gain, w_qkv, w_out):
    n_req = lax.axis_size("req")
    n_ten = lax.axis_size("tensor")
    me_req = lax.axis_index("req")
    me_ten = lax.axis_index("tensor")
    img_dev, side, _, width = patches.shape
    half = side // 2
    region = half * half
    length = text.shape[0]
    w3 = jnp.transpose(w_qkv, (1, 0, 2))
    req_at = me_req.astype(jnp.int32)[None]
    ten_at = me_ten.astype(jnp.int32)[None]
    order = by_bits(n_ten)
    near_at, far = order[:-1], order[-1]

    n_rows = n_req * region
    n_img = round_up(n_rows + 1, 16)
    n_text = round_up(length - (n_rows if img_dev == n_req else 0), 32)
    ctext, *kept = gather_text(
        req_at, image_request, slot_start, text, jnp.transpose(patches, (1, 2, 0, 3)), dec_gain, vis_gain, n_req, region,
        n_text
    )
    blocks = near_blocks(ctext, n_ten)

    even, odd, rtext, sel, table, key_ok, gains, vis_row = prepare(
        req_at, image_request, slot_start, grids, *kept, n_req, n_img
    )
    pairs = mix_pairs(even, swap(odd, 1, "req"), region)
    received = [pairs[0]] + [swap(pairs[i], 2 * i, "req") for i in range(1, n_req // 2)]
    ctext, table, pairs = lax.optimization_barrier((ctext, table, pairs))
    acc, ss, held = own_part(ten_at, ctext, gains, w3)
    text_at, img_at, text_row = placement(table, region, length, n_text, n_img)
    received, acc, text_at = lax.optimization_barrier((received, acc, text_at))
    img_own = pack_images(received, vis_row, rtext, sel, region)
    img_far_first = {s: swap(img_own, s) for s in reversed(order)}
    img_blocks = [img_own] + [img_far_first[s] for s in range(1, n_ten)]

    one_bit = sorted(blocks)
    between = [s for s in near_at if s not in one_bit]
    blocks, img_own = lax.optimization_barrier((blocks, img_own))
    acc, ss = near_part(one_bit, ten_at, [blocks[s] for s in one_bit], gains, held, acc, ss)
    blocks, acc = lax.optimization_barrier((blocks, acc))
    blocks = far_blocks(blocks, n_ten)
    if between:
        acc, ss = near_part(between, ten_at, [blocks[s] for s in between], gains, held, acc, ss)
    img_qkv, merged, w_out = image_part(ten_at, img_blocks[::-1], gains, sel, held, w_out, n_rows)

    shared = (gains, held, acc, ss, img_qkv, text_at, img_at, key_ok, w_out)
    top_qkv, head_qkv, head_ctx, *head_far = head_part(far, ten_at, blocks[far][0], *shared)
    tail_ctx, *tail_far = tail_part(far, ten_at, blocks[far][1], *shared, top_qkv, head_qkv)

    img_here = jnp.dot(img_at, merged, preferred_element_type=jnp.float32)
    x_in = (text.astype(jnp.float32) * text_row[:, :1] + img_here).astype(jnp.bfloat16)

    bits = (low_bit(far), high_bit(far))
    head_got = [swap(t, bit) for t, bit in zip(head_far, bits)]
    tail_got = [swap(t, bit) for t, bit in zip(tail_far, bits)]
    head_got, head_ctx, tail_ctx = lax.optimization_barrier((head_got, head_ctx, tail_ctx))
    parts = {}
    for s in reversed([0] + near_at):
        parts[s] = out_part(s, ten_at, head_ctx, tail_ctx, w_out, width, jnp.float32 if s == 0 else jnp.bfloat16)
    got = [jnp.concatenate(pair, axis=0) for pair in zip(head_got, tail_got)]
    early, late = scatter_terms(parts, got, n_ten)
    base = add_first(x_in, [parts[0][0]] + early[0], [parts[0][1]] + early[1])
    return add_last(base, late[0], late[1])


def solution(mesh):
    in_specs = (
        P("req", "tensor"),
        P("req", None, None, "tensor"),
        P(),
        P(),
        P(),
        P("tensor"),
        P(),
        P(None, None, "tensor"),
        P("tensor", None),
    )
    out_specs = P("req", "tensor")
    return jax.shard_map(body, mesh=mesh, in_specs=in_specs, out_specs=out_specs, check_vma=False)
```
